32 devices in a mesh: seq: 16 (over z, y, core), section: 2 (over x).
Axes of the slice: x: 2, y: 2, z: 4, core: 2. Of those that a mesh axis runs over, the one named last changes fastest.
Arguments:
- stream_in: bfloat16 [2, 2048, 2048], P('section', 'seq'), may hold values from -20 to 20
- keys_values: bfloat16 [2, 2, 2048, 512], P('section', None, 'seq'), may hold values from -6 to 6
- out_weight: bfloat16 [2, 2048, 2048], P('section'), may hold values from -1 to 1
- tile_mask: int32 [2, 16, 16], P('section'), may hold values 0 or 1
- cotangent: bfloat16 [2, 2048, 2048], P('section', 'seq'), may hold values from -6 to 6
Outputs:
- stream_out: bfloat16 [2, 2048, 2048], P('section', 'seq')
- stream_grads: bfloat16 [2, 2048, 2048], P('section', 'seq')
- kv_grads: float32 [2, 2, 2048, 512], P('section', None, 'seq')
The draws below stay inside these ranges and needn't reach their ends.
All inputs are finite; a program needn't handle non-finite values. No bound on the sum of `tile_mask` on one device may be relied on, other than what follows from the above.
Results may differ from the reference program's by a relative error of at most 0.013.
Values may be sent and summed in bfloat16 or wider, within the bound.
No kernel may reach another device: no remote copies, remote signals or barrier semaphores. Data moves between devices by JAX's collectives and lax.ppermute only.
A program may use at most 64 MiB of HBM per device.

```python
import jax
import jax.numpy as jnp
from jax import lax

HEADS = 16
KVH = 4
HD = 128
TILE = 128
TOK_DEV = 128
HID = 2048
KVW = 512
NT = 16
TOKENS = 2048
WINDOW = 256
LAYERS = 2


def draw_stream_in(key, part):
    shape = (LAYERS, TOKENS, HID)
    base = jnp.clip(jax.random.normal(key, shape, jnp.float32), -6.0, 6.0)
    return base.astype(jnp.bfloat16)


def draw_keys_values(key, part):
    shape = (LAYERS, 2, TOKENS, KVW)
    base = jnp.clip(jax.random.normal(key, shape, jnp.float32), -6.0, 6.0)
    return base.astype(jnp.bfloat16)


def with_ends(values, own_key, low, largest):
    dims = values.shape
    spot = [jax.random.randint(jax.random.fold_in(own_key, axis), (), 0, dims[axis]) for axis in range(len(dims))]
    values = values.at[tuple(spot)].set(low)
    longest = dims.index(max(dims))
    spot[longest] = (spot[longest] + 1) % dims[longest]
    return values.at[tuple(spot)].set(largest)


def level_of(stream_key, shape, pieces, smallest, top_value):
    def one(position, blocks):
        draws = jax.random.uniform(jax.random.fold_in(jax.random.fold_in(stream_key, 6), position), (blocks,), jnp.float32, smallest / len(pieces), top_value / len(pieces))
        return jnp.repeat(jnp.exp(draws), shape[position] // blocks).reshape((-1,) + (1,) * (len(shape) - position - 1))

    factor_of = one(*pieces[0])
    for cut in pieces[1:]:
        factor_of = factor_of * one(*cut)
    return factor_of


def noise(key, extent, scale, most, pieces=(), kind=jnp.bfloat16):
    entries = scale * jax.random.normal(key, extent, jnp.float32)
    if pieces:
        entries = entries * level_of(key, extent, pieces, -0.22, 0.18)
    return jnp.clip(entries, -most, most).astype(kind)


def setup_inputs(seed: int = 0) -> dict:
    seeds = jax.random.split(jax.random.key(seed), 6)
    return {
        "stream_in": draw_stream_in(jax.random.fold_in(seeds[5], 71), 0),
        "keys_values": draw_keys_values(jax.random.fold_in(seeds[5], 71), 0),
        "out_weight": noise(seeds[2], (LAYERS, HID, HID), (HID // 64) ** -0.5, 1.0, ((0, 2),)),
        "tile_mask": with_ends((jax.random.randint(seeds[3], (LAYERS, NT, NT), 0, 2) < 1).astype(jnp.int32), jax.random.fold_in(seeds[3], 1), 0, 1),
        "cotangent": noise(seeds[4], (LAYERS, TOKENS, HID), 1.0, 6.0, ((0, 2), (1, 16))),
    }


def pruned_weight(weight, tiles):
    tile_count = tiles.shape[0]
    shaped = weight.reshape(tile_count, TILE, tile_count, TILE)
    kept = jnp.where(tiles[:, None, :, None] > 0, shaped, jnp.zeros_like(shaped))
    return kept.reshape(weight.shape)


def band_softmax(q_heads, key_rows, row_pos, key_pos):
    logits = jnp.einsum('rkgd,jkd->kgrj', q_heads.astype(jnp.float32), key_rows.astype(jnp.float32)) * (HD ** -0.5)
    distance = row_pos[:, None] - key_pos[None, :]
    inside = (distance >= 0) & (distance < WINDOW) & (key_pos[None, :] >= 0)
    logits = jnp.where(inside[None, None], logits, -jnp.inf)
    row_top = jnp.max(logits, axis=-1, keepdims=True)
    exp_terms = jnp.exp(logits - row_top)
    return exp_terms / jnp.sum(exp_terms, axis=-1, keepdims=True)


def reference(stream_in, keys_values, out_weight, tile_mask, cotangent):
    block_rows = 4 * TOK_DEV
    block_total = TOKENS // block_rows
    block_ids = jnp.arange(block_total, dtype=jnp.int32)
    layer_outs = []
    in_grads = []
    kv_grads = []
    for layer in range(LAYERS):
        weight = pruned_weight(out_weight[layer], tile_mask[layer])
        padded = jnp.concatenate([jnp.zeros((2, WINDOW, KVW), jnp.bfloat16), keys_values[layer]], axis=1)
        stream = stream_in[layer]
        grad_in = cotangent[layer]
        d_attended = jnp.dot(grad_in, weight.T, preferred_element_type=jnp.float32).astype(jnp.bfloat16)

        def block_step(accum, block_id):
            row_start = (block_id * block_rows).astype(jnp.int32)
            queries = lax.dynamic_slice_in_dim(stream, row_start, block_rows, 0)
            kv_block = lax.dynamic_slice_in_dim(padded, row_start, block_rows + WINDOW, 1)
            row_pos = row_start + jnp.arange(block_rows, dtype=jnp.int32)
            key_pos = row_start - WINDOW + jnp.arange(block_rows + WINDOW, dtype=jnp.int32)
            q_heads = queries.reshape(block_rows, KVH, HEADS // KVH, HD)
            key_rows = kv_block[0].reshape(block_rows + WINDOW, KVH, HD)
            value_rows = kv_block[1].reshape(block_rows + WINDOW, KVH, HD)
            probs = band_softmax(q_heads, key_rows, row_pos, key_pos)
            prob_b = lax.optimization_barrier(probs.astype(jnp.bfloat16)).astype(jnp.float32)
            attended = jnp.einsum('kgrj,jkd->rkgd', prob_b, value_rows.astype(jnp.float32))
            attended = attended.astype(jnp.bfloat16).reshape(block_rows, HID)
            d_block = lax.dynamic_slice_in_dim(d_attended, row_start, block_rows, 0)
            d_heads = lax.optimization_barrier(d_block).astype(jnp.float32).reshape(block_rows, KVH, HEADS // KVH, HD)
            d_probs = jnp.einsum('rkgd,jkd->kgrj', d_heads, value_rows.astype(jnp.float32))
            d_values = jnp.einsum('kgrj,rkgd->jkd', prob_b, d_heads)
            row_dot = jnp.sum(probs * d_probs, axis=-1, keepdims=True)
            d_logits = (probs * (d_probs - row_dot)).astype(jnp.bfloat16)
            d_logits = lax.optimization_barrier(d_logits).astype(jnp.float32)
            d_queries = jnp.einsum('kgrj,jkd->rkgd', d_logits, key_rows.astype(jnp.float32)) * (HD ** -0.5)
            d_keys = jnp.einsum('kgrj,rkgd->jkd', d_logits, q_heads.astype(jnp.float32)) * (HD ** -0.5)
            update = jnp.stack([d_keys, d_values]).reshape(2, block_rows + WINDOW, KVW)
            current = lax.dynamic_slice_in_dim(accum, row_start, block_rows + WINDOW, 1)
            accum = lax.dynamic_update_slice_in_dim(accum, current + update, row_start, 1)
            return accum, (attended, d_queries.reshape(block_rows, HID))

        accum_zero = jnp.zeros((2, WINDOW + TOKENS, KVW), jnp.float32)
        accum, results = lax.scan(block_step, accum_zero, block_ids)
        attended = results[0].reshape(TOKENS, HID)
        d_queries = results[1].reshape(TOKENS, HID)
        mixed_rows = jnp.dot(attended, weight, preferred_element_type=jnp.float32)
        layer_outs.append((stream.astype(jnp.float32) + mixed_rows).astype(jnp.bfloat16))
        in_grads.append((grad_in.astype(jnp.float32) + d_queries).astype(jnp.bfloat16))
        kv_grads.append(accum[:, WINDOW:])
    stream_out = jnp.roll(jnp.stack(layer_outs), 1, axis=0)
    stream_grads = jnp.roll(jnp.stack(in_grads), -1, axis=0)
    return stream_out, stream_grads, jnp.stack(kv_grads)
```

```python
import functools

import jax
import jax.numpy as jnp
from jax import lax
from jax.experimental import pallas as pl
from jax.experimental.pallas import tpu as pltpu
from jax.sharding import PartitionSpec as P

HD = 128
TILE = 128
SPAN = 2
CHUNKS = ((0, 1), (1, 4))
VMEM_LIMIT = 48 * 1024 * 1024
NT = (((1,), (1,)), ((), ()))


def from_behind(block, axis, distance):
    devices = range(lax.axis_size(axis))
    route = [(i - distance, i) for i in devices if i - distance in devices]
    return lax.ppermute(block, axis, route)


def around(value, axis, by):
    length = lax.axis_size(axis)
    return lax.ppermute(value, axis, [(i, (i + by) % length) for i in range(length)])


def f32_dot(a, b, dims=(((1,), (0,)), ((), ()))):
    return lax.dot_general(a, b, dims, preferred_element_type=jnp.float32)


def prune(weight, mask_ref, row_tile, column_tile):
    rows, columns = weight.shape
    strips = []
    for a in range(rows // TILE):
        blocks = []
        for b in range(columns // TILE):
            block = weight[a * TILE : (a + 1) * TILE, b * TILE : (b + 1) * TILE]
            kept = mask_ref[row_tile + a, column_tile + b] > 0
            blocks.append(jnp.where(kept, block, jnp.zeros_like(block)))
        strips.append(jnp.concatenate(blocks, axis=1))
    return jnp.concatenate(strips, axis=0)


def d_attended_kernel(mask_ref, cot_ref, weight_ref, out_ref):
    rows = weight_ref.shape[0]
    step = pl.program_id(0)
    weight = prune(weight_ref[...], mask_ref, step * (rows // TILE), 0)
    out_ref[...] = f32_dot(cot_ref[...], weight, NT).astype(jnp.bfloat16)


def d_attended_of(cot, weight, mask, block=512):
    tok, width = cot.shape
    return pl.pallas_call(
        d_attended_kernel,
        grid=(width // block,),
        in_specs=[
            pl.BlockSpec(memory_space=pltpu.SMEM),
            pl.BlockSpec((tok, width), lambda i: (0, 0)),
            pl.BlockSpec((block, width), lambda i: (i, 0)),
        ],
        out_specs=pl.BlockSpec((tok, block), lambda i: (0, i)),
        out_shape=jax.ShapeDtypeStruct((tok, width), jnp.bfloat16),
        compiler_params=pltpu.CompilerParams(vmem_limit_bytes=VMEM_LIMIT),
        cost_estimate=pl.CostEstimate(
            flops=2 * tok * width * width, bytes_accessed=2 * width * width, transcendentals=0
        ),
        name="d_attended",
    )(mask, cot, weight)


def layer_out_kernel(mask_ref, q_ref, *refs):
    attended_refs, weight_ref, out_ref = refs[:-2], refs[-2], refs[-1]
    columns = weight_ref.shape[1]
    step = pl.program_id(0)
    weight = prune(weight_ref[...], mask_ref, 0, step * (columns // TILE))
    attended = jnp.concatenate([ref[...] for ref in attended_refs], axis=1)
    mixed = f32_dot(attended, weight)
    out_ref[...] = (q_ref[...].astype(jnp.float32) + mixed).astype(jnp.bfloat16)


def layer_out_of(queries, attended, weight, mask, block=512):
    tok, width = queries.shape
    return pl.pallas_call(
        layer_out_kernel,
        grid=(width // block,),
        in_specs=[
            pl.BlockSpec(memory_space=pltpu.SMEM),
            pl.BlockSpec((tok, block), lambda i: (0, i)),
            *[pl.BlockSpec(part.shape, lambda i: (0, 0)) for part in attended],
            pl.BlockSpec((width, block), lambda i: (0, i)),
        ],
        out_specs=pl.BlockSpec((tok, block), lambda i: (0, i)),
        out_shape=jax.ShapeDtypeStruct((tok, width), jnp.bfloat16),
        compiler_params=pltpu.CompilerParams(vmem_limit_bytes=VMEM_LIMIT),
        cost_estimate=pl.CostEstimate(
            flops=2 * tok * width * width, bytes_accessed=2 * width * width, transcendentals=0
        ),
        name="layer_out",
    )(mask, queries, *attended, weight)


def attention_kernel(
    shard_ref, q_ref, d_ref, cot_ref, own_ref, near_ref, far_ref,
    att_ref, grad_ref, own_grad_ref, near_grad_ref, far_grad_ref,
):
    tok = q_ref.shape[0]
    heads = q_ref.shape[1] // HD
    scaling = HD ** (-0.5)
    shard = shard_ref[0]
    floor = jnp.float32(-1e30)
    near_ok = shard >= 1
    far_ok = shard >= 2
    key_at = lax.broadcasted_iota(jnp.int32, (tok, tok), 0)
    row_at = lax.broadcasted_iota(jnp.int32, (tok, tok), 1)
    causal = key_at <= row_at

    def stacked(ref):
        return jnp.concatenate([ref[:, h * HD : (h + 1) * HD] for h in range(heads)], axis=0)

    q_rows = stacked(q_ref)
    d_rows = stacked(d_ref)
    keys = jnp.concatenate([own_ref[0], near_ref[0], far_ref[0]], axis=0)
    values = jnp.concatenate([own_ref[1], near_ref[1], far_ref[1]], axis=0)
    logits = f32_dot(keys, q_rows, NT)
    d_probs = f32_dot(values, d_rows, NT)
    probs_parts, d_logit_parts = [], []
    zeros = jnp.zeros((tok, tok), jnp.float32)
    for h in range(heads):
        at = slice(h * tok, (h + 1) * tok)
        own, near, far = (logits[i * tok : (i + 1) * tok, at] for i in range(3))
        edge = jnp.where(causal, own, jnp.where(far_ok, far, floor))
        near = jnp.where(near_ok, near, floor)
        top = jnp.max(jnp.maximum(edge, near), axis=0, keepdims=True)
        edge = jnp.exp((edge - top) * scaling)
        near = jnp.exp((near - top) * scaling)
        total = jnp.sum(edge + near, axis=0, keepdims=True)
        inverse = 1.0 / total
        edge = edge * inverse
        near = near * inverse
        own_d, near_d, far_d = (d_probs[i * tok : (i + 1) * tok, at] for i in range(3))
        edge_d = jnp.where(causal, own_d, far_d)
        row_dot = jnp.sum(edge * edge_d + near * near_d, axis=0, keepdims=True)
        d_edge = edge * (edge_d - row_dot)
        d_near = near * (near_d - row_dot)
        probs_parts.append(
            jnp.concatenate(
                [jnp.where(causal, edge, zeros), near, jnp.where(causal, zeros, edge)], axis=0
            ).astype(jnp.bfloat16)
        )
        d_logit_parts.append(
            jnp.concatenate(
                [jnp.where(causal, d_edge, zeros), d_near, jnp.where(causal, zeros, d_edge)], axis=0
            ).astype(jnp.bfloat16)
        )
    probs = jnp.concatenate(probs_parts, axis=1)
    d_logits = jnp.concatenate(d_logit_parts, axis=1)
    d_queries = f32_dot(keys.T, d_logits) * scaling
    for h in range(heads):
        at = slice(h * HD, (h + 1) * HD)
        grad_ref[:, at] = (
            cot_ref[:, at].astype(jnp.float32) + d_queries[:, h * tok : (h + 1) * tok].T
        ).astype(jnp.bfloat16)
    attended = f32_dot(values.T, probs)
    for h in range(heads):
        at = slice(h * HD, (h + 1) * HD)
        att_ref[:, at] = attended[:, h * tok : (h + 1) * tok].T.astype(jnp.bfloat16)
    d_keys = f32_dot(d_logits, q_rows) * scaling
    d_values = f32_dot(probs, d_rows)
    for index, grad in enumerate((d_keys, d_values)):
        own_grad_ref[index] = grad[:tok]
        near_grad_ref[index] = grad[tok : 2 * tok].astype(jnp.bfloat16)
        far_grad_ref[index] = grad[2 * tok :].astype(jnp.bfloat16)


def attention_of(shard, queries, d_attended, cot, own, near, far, first, last):
    tok, width = queries.shape
    kv_heads = own.shape[-1] // HD
    group = width // kv_heads
    count = last - first
    wide = pl.BlockSpec((tok, group), lambda i: (0, i + first))
    own_kv = pl.BlockSpec((2, tok, HD), lambda i: (0, 0, i + first))
    part_wide = pl.BlockSpec((tok, group), lambda i: (0, i))
    part_kv = pl.BlockSpec((2, tok, HD), lambda i: (0, 0, i))
    return pl.pallas_call(
        attention_kernel,
        grid=(count,),
        in_specs=[
            pl.BlockSpec(memory_space=pltpu.SMEM), wide, wide, wide, own_kv, part_kv, part_kv,
        ],
        out_specs=[part_wide, part_wide, part_kv, part_kv, part_kv],
        out_shape=[
            jax.ShapeDtypeStruct((tok, count * group), jnp.bfloat16),
            jax.ShapeDtypeStruct((tok, count * group), jnp.bfloat16),
            jax.ShapeDtypeStruct((2, tok, count * HD), jnp.float32),
            jax.ShapeDtypeStruct((2, tok, count * HD), jnp.bfloat16),
            jax.ShapeDtypeStruct((2, tok, count * HD), jnp.bfloat16),
        ],
        compiler_params=pltpu.CompilerParams(vmem_limit_bytes=VMEM_LIMIT),
        cost_estimate=pl.CostEstimate(
            flops=12 * tok * 3 * tok * count * group, bytes_accessed=8 * tok * count * group,
            transcendentals=0,
        ),
        name="attention",
    )(shard, queries, d_attended, cot, own, near, far)


def per_device(stream_in, keys_values, out_weight, tile_mask, cotangent):
    queries, own, weight = stream_in[0], keys_values[0], out_weight[0]
    mask, cot = tile_mask[0], cotangent[0]
    shard = lax.axis_index("seq").astype(jnp.int32).reshape(1)
    halos = []
    for first, last in CHUNKS:
        piece = own[:, :, first * HD : last * HD]
        halos.append([from_behind(piece, "seq", offset + 1) for offset in range(SPAN)])
    d_attended = d_attended_of(cot, weight, mask)
    attended, grads_back, own_grads = [], [], []
    kv_back = []
    for (first, last), (near, far) in zip(CHUNKS, halos):
        att, grad, own_grad, near_grad, far_grad = attention_of(
            shard, queries, d_attended, cot, own, near, far, first, last
        )
        attended.append(att)
        grads_back.append(around(grad, "section", -1))
        own_grads.append(own_grad)
        kv_back.append([from_behind(near_grad, "seq", -1), from_behind(far_grad, "seq", -2)])
    result = layer_out_of(queries, attended, weight, mask)
    next_input = around(result, "section", 1)
    kv_total = jnp.concatenate(
        [
            own_grad + near.astype(jnp.float32) + far.astype(jnp.float32)
            for own_grad, (near, far) in zip(own_grads, kv_back)
        ],
        axis=-1,
    )
    return (next_input[None], jnp.concatenate(grads_back, axis=-1)[None], kv_total[None])


def solution(mesh):
    return jax.shard_map(
        per_device,
        mesh=mesh,
        in_specs=(
            P("section", "seq", None),
            P("section", None, "seq", None),
            P("section", None, None),
            P("section", None, None),
            P("section", "seq", None),
        ),
        out_specs=(
            P("section", "seq", None),
            P("section", "seq", None),
            P("section", None, "seq", None),
        ),
        check_vma=False,
    )
```

```python
import functools

import jax
import jax.numpy as jnp
from jax import lax
from jax.experimental import pallas as pl
from jax.experimental.pallas import tpu as pltpu
from jax.sharding import PartitionSpec as P

HD = 128
TILE = 128
CHUNKS = ((0, 2), (2, 4))
VMEM_LIMIT = 48 * 1024 * 1024
NT = (((1,), (1,)), ((), ()))


def from_behind(block, axis, distance):
    devices = range(lax.axis_size(axis))
    route = [(i - distance, i) for i in devices if i - distance in devices]
    return lax.ppermute(block, axis, route)


def around(value, axis, by):
    length = lax.axis_size(axis)
    return lax.ppermute(value, axis, [(i, (i + by) % length) for i in range(length)])


def f32_dot(a, b, dims=(((1,), (0,)), ((), ()))):
    return lax.dot_general(a, b, dims, preferred_element_type=jnp.float32)


def prune(weight, mask_ref, row_tile, column_tile):
    rows, columns = weight.shape
    strips = []
    for a in range(rows // TILE):
        blocks = []
        for b in range(columns // TILE):
            block = weight[a * TILE : (a + 1) * TILE, b * TILE : (b + 1) * TILE]
            kept = mask_ref[row_tile + a, column_tile + b] > 0
            blocks.append(jnp.where(kept, block, jnp.zeros_like(block)))
        strips.append(jnp.concatenate(blocks, axis=1))
    return jnp.concatenate(strips, axis=0)


def d_attended_kernel(mask_ref, cot_ref, weight_ref, out_ref):
    rows = weight_ref.shape[0]
    step = pl.program_id(0)
    weight = prune(weight_ref[...], mask_ref, step * (rows // TILE), 0)
    out_ref[...] = f32_dot(weight, cot_ref[...], NT).astype(jnp.bfloat16)


def d_attended_of(cot, weight, mask, block=512):
    tok, width = cot.shape
    return pl.pallas_call(
        d_attended_kernel,
        grid=(width // block,),
        in_specs=[
            pl.BlockSpec(memory_space=pltpu.SMEM),
            pl.BlockSpec((tok, width), lambda i: (0, 0)),
            pl.BlockSpec((block, width), lambda i: (i, 0)),
        ],
        out_specs=pl.BlockSpec((block, tok), lambda i: (i, 0)),
        out_shape=jax.ShapeDtypeStruct((width, tok), jnp.bfloat16),
        compiler_params=pltpu.CompilerParams(vmem_limit_bytes=VMEM_LIMIT),
        cost_estimate=pl.CostEstimate(
            flops=2 * tok * width * width, bytes_accessed=2 * width * width, transcendentals=0
        ),
        name="d_attended",
    )(mask, cot, weight)


def layer_out_kernel(mask_ref, q_ref, *refs):
    attended_refs, weight_ref, out_ref = refs[:-2], refs[-2], refs[-1]
    columns = weight_ref.shape[1]
    step = pl.program_id(0)
    weight = prune(weight_ref[...], mask_ref, 0, step * (columns // TILE))
    attended = jnp.concatenate([ref[...] for ref in attended_refs], axis=1)
    mixed = f32_dot(attended, weight)
    out_ref[...] = (q_ref[...].astype(jnp.float32) + mixed).astype(jnp.bfloat16)


def layer_out_of(queries, attended, weight, mask, block=512):
    tok, width = queries.shape
    return pl.pallas_call(
        layer_out_kernel,
        grid=(width // block,),
        in_specs=[
            pl.BlockSpec(memory_space=pltpu.SMEM),
            pl.BlockSpec((tok, block), lambda i: (0, i)),
            *[pl.BlockSpec(part.shape, lambda i: (0, 0)) for part in attended],
            pl.BlockSpec((width, block), lambda i: (0, i)),
        ],
        out_specs=pl.BlockSpec((tok, block), lambda i: (0, i)),
        out_shape=jax.ShapeDtypeStruct((tok, width), jnp.bfloat16),
        compiler_params=pltpu.CompilerParams(vmem_limit_bytes=VMEM_LIMIT),
        cost_estimate=pl.CostEstimate(
            flops=2 * tok * width * width, bytes_accessed=2 * width * width, transcendentals=0
        ),
        name="layer_out",
    )(mask, queries, *attended, weight)


def attention_group(near_ok, far_ok, q_heads, d_heads, own, near, far):
    tok = q_heads[0].shape[0]
    scaling = HD ** (-0.5)
    floor = jnp.float32(-1e30)
    key_at = lax.broadcasted_iota(jnp.int32, (tok, tok), 0)
    row_at = lax.broadcasted_iota(jnp.int32, (tok, tok), 1)
    causal = key_at <= row_at
    q_rows = jnp.concatenate(q_heads, axis=0)
    d_columns = jnp.concatenate(d_heads, axis=1)
    keys = jnp.concatenate([own[0], near[0], far[0]], axis=0)
    values = jnp.concatenate([own[1], near[1], far[1]], axis=0)
    logits = f32_dot(keys, q_rows, NT)
    d_probs = f32_dot(values, d_columns)
    probs_parts, d_logit_parts = [], []
    zeros = jnp.zeros((tok, tok), jnp.float32)
    for h in range(len(q_heads)):
        at = slice(h * tok, (h + 1) * tok)
        own_l, near_l, far_l = (logits[i * tok : (i + 1) * tok, at] for i in range(3))
        edge = jnp.where(causal, own_l, jnp.where(far_ok, far_l, floor))
        near_l = jnp.where(near_ok, near_l, floor)
        top = jnp.max(jnp.maximum(edge, near_l), axis=0, keepdims=True)
        edge = jnp.exp((edge - top) * scaling)
        near_l = jnp.exp((near_l - top) * scaling)
        inverse = 1.0 / jnp.sum(edge + near_l, axis=0, keepdims=True)
        edge = edge * inverse
        near_l = near_l * inverse
        own_d, near_d, far_d = (d_probs[i * tok : (i + 1) * tok, at] for i in range(3))
        edge_d = jnp.where(causal, own_d, far_d)
        row_dot = jnp.sum(edge * edge_d + near_l * near_d, axis=0, keepdims=True)
        d_edge = edge * (edge_d - row_dot)
        d_near = near_l * (near_d - row_dot)
        probs_parts.append(
            jnp.concatenate(
                [jnp.where(causal, edge, zeros), near_l, jnp.where(causal, zeros, edge)], axis=0
            ).astype(jnp.bfloat16)
        )
        d_logit_parts.append(
            jnp.concatenate(
                [jnp.where(causal, d_edge, zeros), d_near, jnp.where(causal, zeros, d_edge)], axis=0
            ).astype(jnp.bfloat16)
        )
    probs = jnp.concatenate(probs_parts, axis=1)
    d_logits = jnp.concatenate(d_logit_parts, axis=1)
    d_queries = f32_dot(keys.T, d_logits) * scaling
    attended = f32_dot(values.T, probs)
    d_keys = f32_dot(d_logits, q_rows) * scaling
    d_values = f32_dot(probs, d_columns, NT)
    return d_queries, attended, d_keys, d_values


def attention_kernel(first, last, shard_ref, q_ref, d_ref, cot_ref, own_ref, near_ref, far_ref, *refs):
    kv_heads = own_ref.shape[-1] // HD
    tok, width = q_ref.shape
    group = width // kv_heads
    heads = group // HD
    shard = shard_ref[0]
    att_ref, grad_ref, *kv_refs = refs[-5:]
    for done_ref, kv_ref in zip(refs[:-5], kv_refs):
        kv_ref[:, :, : first * HD] = done_ref[...]
    for g in range(first, last):
        at_kv = slice(g * HD, (g + 1) * HD)
        own, near, far = (
            [ref[0, :, at_kv], ref[1, :, at_kv]] for ref in (own_ref, near_ref, far_ref)
        )
        columns = [g * group + h * HD for h in range(heads)]
        d_queries, attended, d_keys, d_values = attention_group(
            shard >= 1,
            shard >= 2,
            [q_ref[:, c : c + HD] for c in columns],
            [d_ref[c : c + HD, :] for c in columns],
            own, near, far,
        )
        for h, c in enumerate(columns):
            rows = slice(h * tok, (h + 1) * tok)
            at = slice(c - first * group, c - first * group + HD)
            grad_ref[:, at] = (
                cot_ref[:, c : c + HD].astype(jnp.float32) + d_queries[:, rows].T
            ).astype(jnp.bfloat16)
            att_ref[:, at] = attended[:, rows].T.astype(jnp.bfloat16)
        for index, grad in enumerate((d_keys, d_values)):
            for part, ref in enumerate(kv_refs):
                ref[index, :, at_kv] = grad[part * tok : (part + 1) * tok].astype(ref.dtype)


def attention_of(shard, queries, d_attended, cot, own, near, far, first, last, done):
    tok, width = queries.shape
    kv_heads = own.shape[-1] // HD
    group = width // kv_heads
    count = last - first
    vmem = pl.BlockSpec(memory_space=pltpu.VMEM)
    rows = jax.ShapeDtypeStruct((tok, count * group), jnp.bfloat16)
    return pl.pallas_call(
        functools.partial(attention_kernel, first, last),
        in_specs=[pl.BlockSpec(memory_space=pltpu.SMEM)] + [vmem] * (6 + len(done)),
        out_specs=[vmem] * 5,
        out_shape=[rows, rows]
        + [jax.ShapeDtypeStruct((2, tok, last * HD), t) for t in (jnp.float32, jnp.bfloat16, jnp.bfloat16)],
        compiler_params=pltpu.CompilerParams(vmem_limit_bytes=VMEM_LIMIT),
        cost_estimate=pl.CostEstimate(
            flops=12 * tok * 3 * tok * count * group, bytes_accessed=8 * tok * count * group,
            transcendentals=0,
        ),
        name="attention",
    )(shard, queries, d_attended, cot, own, near, far, *done)


def core_swap(value, axis):
    return lax.ppermute(value, axis, [(i, i ^ 1) for i in range(lax.axis_size(axis))])


def per_device(stream_in, keys_values, out_weight, tile_mask, cotangent):
    queries, own, weight = stream_in[0], keys_values[0], out_weight[0]
    mask, cot = tile_mask[0], cotangent[0]
    seq_index = lax.axis_index("seq").astype(jnp.int32)
    shard = seq_index.reshape(1)
    odd = seq_index % 2 == 1
    far = from_behind(own, "seq", 2)
    near = from_behind(own, "seq", 1)
    d_attended = d_attended_of(cot, weight, mask)
    attended, grads_back, kv_grads = [], [], []
    for first, last in CHUNKS:
        att, grad, *kv_grads = attention_of(
            shard, queries, d_attended, cot, own, near, far, first, last, kv_grads
        )
        attended.append(att)
        grads_back.append(around(grad, "section", -1))
    own_grad, near_grad, far_grad = kv_grads
    beside = core_swap(near_grad, "seq").astype(jnp.float32)
    behind = jnp.where(odd, far_grad.astype(jnp.float32) + beside, far_grad.astype(jnp.float32))
    result = layer_out_of(queries, attended, weight, mask)
    next_input = around(result, "section", 1)
    ahead = from_behind(behind.astype(jnp.bfloat16), "seq", -2).astype(jnp.float32)
    kv_total = own_grad + ahead + jnp.where(odd, jnp.zeros_like(beside), beside)
    return (next_input[None], jnp.concatenate(grads_back, axis=-1)[None], kv_total[None])


def solution(mesh):
    return jax.shard_map(
        per_device,
        mesh=mesh,
        in_specs=(
            P("section", "seq", None),
            P("section", None, "seq", None),
            P("section", None, None),
            P("section", None, None),
            P("section", "seq", None),
        ),
        out_specs=(
            P("section", "seq", None),
            P("section", "seq", None),
            P("section", None, "seq", None),
        ),
        check_vma=False,
    )
```

```python
import functools

import jax
import jax.numpy as jnp
from jax import lax
from jax.experimental import pallas as pl
from jax.experimental.pallas import tpu as pltpu
from jax.sharding import PartitionSpec as P

HD = 128
TILE = 128
CHUNKS = ((0, 2), (2, 4))
OUT_CUT = 2
VMEM_LIMIT = 48 * 1024 * 1024
NT = (((1,), (1,)), ((), ()))


def from_behind(block, axis, distance):
    devices = range(lax.axis_size(axis))
    route = [(i - distance, i) for i in devices if i - distance in devices]
    return lax.ppermute(block, axis, route)


def around(value, axis, by):
    length = lax.axis_size(axis)
    return lax.ppermute(value, axis, [(i, (i + by) % length) for i in range(length)])


def f32_dot(a, b, dims=(((1,), (0,)), ((), ()))):
    return lax.dot_general(a, b, dims, preferred_element_type=jnp.float32)


def prune(weight, mask_ref, row_tile, column_tile):
    rows, columns = weight.shape
    strips = []
    for a in range(rows // TILE):
        blocks = []
        for b in range(columns // TILE):
            block = weight[a * TILE : (a + 1) * TILE, b * TILE : (b + 1) * TILE]
            kept = mask_ref[row_tile + a, column_tile + b] > 0
            blocks.append(jnp.where(kept, block, jnp.zeros_like(block)))
        strips.append(jnp.concatenate(blocks, axis=1))
    return jnp.concatenate(strips, axis=0)


def d_attended_kernel(mask_ref, cot_ref, weight_ref, out_ref):
    rows = weight_ref.shape[0]
    step = pl.program_id(0)
    weight = prune(weight_ref[...], mask_ref, step * (rows // TILE), 0)
    out_ref[...] = f32_dot(weight, cot_ref[...], NT).astype(jnp.bfloat16)


def d_attended_of(cot, weight, mask, block=512):
    tok, width = cot.shape
    return pl.pallas_call(
        d_attended_kernel,
        grid=(width // block,),
        in_specs=[
            pl.BlockSpec(memory_space=pltpu.SMEM),
            pl.BlockSpec((tok, width), lambda i: (0, 0)),
            pl.BlockSpec((block, width), lambda i: (i, 0)),
        ],
        out_specs=pl.BlockSpec((block, tok), lambda i: (i, 0)),
        out_shape=jax.ShapeDtypeStruct((width, tok), jnp.bfloat16),
        compiler_params=pltpu.CompilerParams(vmem_limit_bytes=VMEM_LIMIT),
        cost_estimate=pl.CostEstimate(
            flops=2 * tok * width * width, bytes_accessed=2 * width * width, transcendentals=0
        ),
        name="d_attended",
    )(mask, cot, weight)


def layer_out_kernel(first, part, column, mask_ref, q_ref, *refs):
    *attended_refs, weight_ref, piece_ref, out_ref, whole_ref, sem = refs
    columns = weight_ref.shape[1]
    step = pl.program_id(0)
    if part:
        refs = attended_refs[:-1]
    else:
        refs = attended_refs
    target = whole_ref.at[:, column : column + piece_ref.shape[1]]
    store = pltpu.make_async_copy(piece_ref, target, sem)

    @pl.when(step == 0)
    def _():
        store.start()

    weight = prune(weight_ref[...], mask_ref, 0, (first + step) * (columns // TILE))
    attended = jnp.concatenate([ref[...] for ref in refs], axis=1)
    mixed = f32_dot(attended, weight)
    out_ref[...] = (q_ref[...].astype(jnp.float32) + mixed).astype(jnp.bfloat16)

    @pl.when(step == pl.num_programs(0) - 1)
    def _():
        store.wait()


def layer_out_of(queries, attended, weight, mask, first, last, piece, column, whole, block=512):
    tok, width = queries.shape
    count = last - first
    part = whole is not None
    hbm = pl.BlockSpec(memory_space=pltpu.HBM)
    anywhere = pl.BlockSpec(memory_space=pl.ANY)
    given = [whole] if part else []
    return pl.pallas_call(
        functools.partial(layer_out_kernel, first, part, column),
        grid=(count,),
        in_specs=[
            pl.BlockSpec(memory_space=pltpu.SMEM),
            pl.BlockSpec((tok, block), lambda i: (0, i + first)),
            *[pl.BlockSpec(a.shape, lambda i: (0, 0)) for a in attended],
            *[hbm for _ in given],
            pl.BlockSpec((width, block), lambda i: (0, i + first)),
            anywhere,
        ],
        out_specs=[pl.BlockSpec((tok, block), lambda i: (0, i)), hbm],
        out_shape=[
            jax.ShapeDtypeStruct((tok, count * block), jnp.bfloat16),
            jax.ShapeDtypeStruct((tok, width), jnp.bfloat16),
        ],
        scratch_shapes=[pltpu.SemaphoreType.DMA],
        input_output_aliases={2 + len(attended): 1} if part else {},
        compiler_params=pltpu.CompilerParams(vmem_limit_bytes=VMEM_LIMIT),
        cost_estimate=pl.CostEstimate(
            flops=2 * tok * width * count * block,
            bytes_accessed=2 * width * count * block,
            transcendentals=0,
        ),
        name="layer_out",
    )(mask, queries, *attended, *given, weight, piece)


def store_first_kernel(piece_ref, whole_ref, sem):
    store = pltpu.make_async_copy(piece_ref, whole_ref.at[:, : piece_ref.shape[1]], sem)
    store.start()
    store.wait()


def store_first(piece, width):
    return pl.pallas_call(
        store_first_kernel,
        in_specs=[pl.BlockSpec(memory_space=pl.ANY)],
        out_specs=pl.BlockSpec(memory_space=pltpu.HBM),
        out_shape=jax.ShapeDtypeStruct((piece.shape[0], width), piece.dtype),
        scratch_shapes=[pltpu.SemaphoreType.DMA],
        name="store_first",
    )(piece)


def store_last_kernel(piece_ref, given_ref, beside_ref, whole_ref, kept_ref, sem):
    column = whole_ref.shape[1] - piece_ref.shape[1]
    store = pltpu.make_async_copy(piece_ref, whole_ref.at[:, column:], sem)
    store.start()
    store.wait()


def store_last(piece, whole, beside):
    hbm = pl.BlockSpec(memory_space=pltpu.HBM)
    return pl.pallas_call(
        store_last_kernel,
        in_specs=[pl.BlockSpec(memory_space=pl.ANY), hbm, hbm],
        out_specs=[hbm, hbm],
        out_shape=[
            jax.ShapeDtypeStruct(whole.shape, whole.dtype),
            jax.ShapeDtypeStruct(beside.shape, beside.dtype),
        ],
        scratch_shapes=[pltpu.SemaphoreType.DMA],
        input_output_aliases={1: 0, 2: 1},
        name="store_last",
    )(piece, whole, beside)


def attention_group(near_ok, far_ok, q_heads, d_heads, own, near, far):
    tok = q_heads[0].shape[0]
    scaling = HD ** (-0.5)
    floor = jnp.float32(-1e30)
    key_at = lax.broadcasted_iota(jnp.int32, (tok, tok), 0)
    row_at = lax.broadcasted_iota(jnp.int32, (tok, tok), 1)
    causal = key_at <= row_at
    q_rows = jnp.concatenate(q_heads, axis=0)
    d_columns = jnp.concatenate(d_heads, axis=1)
    keys = jnp.concatenate([own[0], near[0], far[0]], axis=0)
    values = jnp.concatenate([own[1], near[1], far[1]], axis=0)
    logits = f32_dot(keys, q_rows, NT)
    d_probs = f32_dot(values, d_columns)
    probs_parts, d_logit_parts = [], []
    zeros = jnp.zeros((tok, tok), jnp.float32)
    for h in range(len(q_heads)):
        at = slice(h * tok, (h + 1) * tok)
        own_l, near_l, far_l = (logits[i * tok : (i + 1) * tok, at] for i in range(3))
        edge = jnp.where(causal, own_l, jnp.where(far_ok, far_l, floor))
        near_l = jnp.where(near_ok, near_l, floor)
        top = jnp.max(jnp.maximum(edge, near_l), axis=0, keepdims=True)
        edge = jnp.exp((edge - top) * scaling)
        near_l = jnp.exp((near_l - top) * scaling)
        inverse = 1.0 / jnp.sum(edge + near_l, axis=0, keepdims=True)
        edge = edge * inverse
        near_l = near_l * inverse
        own_d, near_d, far_d = (d_probs[i * tok : (i + 1) * tok, at] for i in range(3))
        edge_d = jnp.where(causal, own_d, far_d)
        row_dot = jnp.sum(edge * edge_d + near_l * near_d, axis=0, keepdims=True)
        d_edge = edge * (edge_d - row_dot)
        d_near = near_l * (near_d - row_dot)
        probs_parts.append(
            jnp.concatenate(
                [jnp.where(causal, edge, zeros), near_l, jnp.where(causal, zeros, edge)], axis=0
            ).astype(jnp.bfloat16)
        )
        d_logit_parts.append(
            jnp.concatenate(
                [jnp.where(causal, d_edge, zeros), d_near, jnp.where(causal, zeros, d_edge)], axis=0
            ).astype(jnp.bfloat16)
        )
    probs = jnp.concatenate(probs_parts, axis=1)
    d_logits = jnp.concatenate(d_logit_parts, axis=1)
    d_queries = f32_dot(keys.T, d_logits) * scaling
    attended = f32_dot(values.T, probs)
    d_keys = f32_dot(d_logits, q_rows) * scaling
    d_values = f32_dot(probs, d_columns, NT)
    return d_queries, attended, d_keys, d_values


def attention_kernel(first, last, shard_ref, q_ref, d_ref, cot_ref, own_ref, near_ref, far_ref, *refs):
    kv_heads = own_ref.shape[-1] // HD
    tok, width = q_ref.shape
    group = width // kv_heads
    heads = group // HD
    shard = shard_ref[0]
    att_ref, grad_ref, *kv_refs = refs[-5:]
    for done_ref, kv_ref in zip(refs[:-5], kv_refs):
        kv_ref[:, :, : first * HD] = done_ref[...]
    for g in range(first, last):
        at_kv = slice(g * HD, (g + 1) * HD)
        own, near, far = (
            [ref[0, :, at_kv], ref[1, :, at_kv]] for ref in (own_ref, near_ref, far_ref)
        )
        columns = [g * group + h * HD for h in range(heads)]
        d_queries, attended, d_keys, d_values = attention_group(
            shard >= 1,
            shard >= 2,
            [q_ref[:, c : c + HD] for c in columns],
            [d_ref[c : c + HD, :] for c in columns],
            own, near, far,
        )
        for h, c in enumerate(columns):
            rows = slice(h * tok, (h + 1) * tok)
            at = slice(c - first * group, c - first * group + HD)
            grad_ref[:, at] = (
                cot_ref[:, c : c + HD].astype(jnp.float32) + d_queries[:, rows].T
            ).astype(jnp.bfloat16)
            att_ref[:, at] = attended[:, rows].T.astype(jnp.bfloat16)
        for index, grad in enumerate((d_keys, d_values)):
            for part, ref in enumerate(kv_refs):
                ref[index, :, at_kv] = grad[part * tok : (part + 1) * tok].astype(ref.dtype)


def attention_of(shard, queries, d_attended, cot, own, near, far, first, last, done):
    tok, width = queries.shape
    kv_heads = own.shape[-1] // HD
    group = width // kv_heads
    count = last - first
    vmem = pl.BlockSpec(memory_space=pltpu.VMEM)
    rows = jax.ShapeDtypeStruct((tok, count * group), jnp.bfloat16)
    return pl.pallas_call(
        functools.partial(attention_kernel, first, last),
        in_specs=[pl.BlockSpec(memory_space=pltpu.SMEM)] + [vmem] * (6 + len(done)),
        out_specs=[vmem] * 5,
        out_shape=[rows, rows]
        + [jax.ShapeDtypeStruct((2, tok, last * HD), t) for t in (jnp.float32, jnp.bfloat16, jnp.bfloat16)],
        compiler_params=pltpu.CompilerParams(vmem_limit_bytes=VMEM_LIMIT),
        cost_estimate=pl.CostEstimate(
            flops=12 * tok * 3 * tok * count * group, bytes_accessed=8 * tok * count * group,
            transcendentals=0,
        ),
        name="attention",
    )(shard, queries, d_attended, cot, own, near, far, *done)


def core_swap(value, axis):
    return lax.ppermute(value, axis, [(i, i ^ 1) for i in range(lax.axis_size(axis))])


def per_device(stream_in, keys_values, out_weight, tile_mask, cotangent):
    queries, own, weight = stream_in[0], keys_values[0], out_weight[0]
    mask, cot = tile_mask[0], cotangent[0]
    seq_index = lax.axis_index("seq").astype(jnp.int32)
    shard = seq_index.reshape(1)
    odd = seq_index % 2 == 1
    far = from_behind(own, "seq", 2)
    near = from_behind(own, "seq", 1)
    d_attended = d_attended_of(cot, weight, mask)
    attended, grads_back, kv_grads = [], [], []
    for first, last in CHUNKS:
        att, grad, *kv_grads = attention_of(
            shard, queries, d_attended, cot, own, near, far, first, last, kv_grads
        )
        attended.append(att)
        grads_back.append(around(grad, "section", -1))
    own_grad, near_grad, far_grad = kv_grads
    beside = core_swap(near_grad, "seq").astype(jnp.float32)
    behind = jnp.where(odd, far_grad.astype(jnp.float32) + beside, far_grad.astype(jnp.float32))
    cut = OUT_CUT
    steps = queries.shape[1] // 512
    result, prev_grad = layer_out_of(
        queries, attended, weight, mask, 0, cut, grads_back[0], 0, None
    )
    early = around(result, "section", 1)
    ahead = from_behind(behind.astype(jnp.bfloat16), "seq", -2).astype(jnp.float32)
    result, prev_grad = layer_out_of(
        queries, attended, weight, mask, cut, steps, grads_back[1], grads_back[0].shape[1], prev_grad
    )
    late = around(result, "section", 1)
    next_input = store_first(early, queries.shape[1])
    kv_total = own_grad + ahead + jnp.where(odd, jnp.zeros_like(beside), beside)
    next_input, kv_total = store_last(late, next_input, kv_total)
    return (next_input[None], prev_grad[None], kv_total[None])


def solution(mesh):
    return jax.shard_map(
        per_device,
        mesh=mesh,
        in_specs=(
            P("section", "seq", None),
            P("section", None, "seq", None),
            P("section", None, None),
            P("section", None, None),
            P("section", "seq", None),
        ),
        out_specs=(
            P("section", "seq", None),
            P("section", "seq", None),
            P("section", None, "seq", None),
        ),
        check_vma=False,
    )
```

```python
import functools

import jax
import jax.numpy as jnp
from jax import lax
from jax.experimental import pallas as pl
from jax.experimental.pallas import tpu as pltpu
from jax.sharding import PartitionSpec as P

HD = 128
TILE = 128
CHUNKS = ((0, 1), (1, 2), (2, 4))
OUT_CUT = 3
VMEM_LIMIT = 32 * 1024 * 1024
NT = (((1,), (1,)), ((), ()))


def from_behind(block, axis, distance):
    devices = range(lax.axis_size(axis))
    route = [(i - distance, i) for i in devices if i - distance in devices]
    return lax.ppermute(block, axis, route)


def around(value, axis, by):
    length = lax.axis_size(axis)
    return lax.ppermute(value, axis, [(i, (i + by) % length) for i in range(length)])


def f32_dot(a, b, dims=(((1,), (0,)), ((), ()))):
    return lax.dot_general(a, b, dims, preferred_element_type=jnp.float32)


def prune(weight, mask_ref, row_tile, column_tile):
    rows, columns = weight.shape
    strips = []
    for a in range(rows // TILE):
        blocks = []
        for b in range(columns // TILE):
            block = weight[a * TILE : (a + 1) * TILE, b * TILE : (b + 1) * TILE]
            kept = mask_ref[row_tile + a, column_tile + b] > 0
            blocks.append(jnp.where(kept, block, jnp.zeros_like(block)))
        strips.append(jnp.concatenate(blocks, axis=1))
    return jnp.concatenate(strips, axis=0)


def d_attended_kernel(mask_hbm, cot_hbm, weight_hbm, out_ref, mask_ref, cot_ref, weight_ref, sems):
    rows = weight_ref.shape[1]
    count = weight_ref.shape[0]
    small = [
        pltpu.make_async_copy(mask_hbm, mask_ref, sems.at[count]),
        pltpu.make_async_copy(cot_hbm, cot_ref, sems.at[count + 1]),
    ]
    large = [
        pltpu.make_async_copy(weight_hbm.at[pl.ds(i * rows, rows)], weight_ref.at[i], sems.at[i])
        for i in range(count)
    ]
    for copy in small + large:
        copy.start()
    for copy in small:
        copy.wait()
    cot = cot_ref[...].T
    for i, copy in enumerate(large):
        copy.wait()
        weight = prune(weight_ref[i], mask_ref, i * (rows // TILE), 0)
        out_ref[i * rows : (i + 1) * rows, :] = f32_dot(weight, cot).astype(jnp.bfloat16)


def d_attended_of(cot, weight, mask, block=256):
    tok, width = cot.shape
    count = width // block
    hbm = pl.BlockSpec(memory_space=pltpu.HBM)
    return pl.pallas_call(
        d_attended_kernel,
        in_specs=[hbm, hbm, hbm],
        out_specs=pl.BlockSpec(memory_space=pltpu.VMEM),
        out_shape=jax.ShapeDtypeStruct((width, tok), jnp.bfloat16),
        scratch_shapes=[
            pltpu.SMEM(mask.shape, mask.dtype),
            pltpu.VMEM(cot.shape, cot.dtype),
            pltpu.VMEM((count, block, width), weight.dtype),
            pltpu.SemaphoreType.DMA((count + 2,)),
        ],
        compiler_params=pltpu.CompilerParams(vmem_limit_bytes=VMEM_LIMIT),
        cost_estimate=pl.CostEstimate(
            flops=2 * tok * width * width, bytes_accessed=2 * width * width, transcendentals=0
        ),
        name="d_attended",
    )(*[pltpu.with_memory_space_constraint(x, pltpu.HBM) for x in (mask, cot, weight)])


def pick_kernel(shard_ref, own_ref, far_ref, after_ref, out_ref):
    odd = shard_ref[0] % 2 == 1

    @pl.when(odd)
    def _():
        out_ref[...] = far_ref[...]

    @pl.when(jnp.logical_not(odd))
    def _():
        out_ref[...] = own_ref[...]


def pick(shard, own, far, after):
    vmem = pl.BlockSpec(memory_space=pltpu.VMEM)
    return pl.pallas_call(
        pick_kernel,
        in_specs=[
            pl.BlockSpec(memory_space=pltpu.SMEM), vmem, vmem, pl.BlockSpec(memory_space=pl.ANY),
        ],
        out_specs=vmem,
        out_shape=jax.ShapeDtypeStruct(own.shape, own.dtype),
        compiler_params=pltpu.CompilerParams(vmem_limit_bytes=VMEM_LIMIT),
        name="pick",
    )(shard, own, far, after)


def behind_kernel(shard_ref, far_ref, beside_ref, out_ref):
    far = far_ref[...].astype(jnp.float32)
    both = far + beside_ref[...].astype(jnp.float32)
    out_ref[...] = jnp.where(shard_ref[0] % 2 == 1, both, far).astype(jnp.bfloat16)


def behind_of(shard, far, beside):
    vmem = pl.BlockSpec(memory_space=pltpu.VMEM)
    return pl.pallas_call(
        behind_kernel,
        in_specs=[pl.BlockSpec(memory_space=pltpu.SMEM), vmem, vmem],
        out_specs=vmem,
        out_shape=jax.ShapeDtypeStruct(far.shape, far.dtype),
        compiler_params=pltpu.CompilerParams(vmem_limit_bytes=VMEM_LIMIT),
        name="behind",
    )(shard, far, beside)


def pieces_into(whole_ref, piece_refs, columns, sems):
    return [
        pltpu.make_async_copy(ref, whole_ref.at[:, c : c + ref.shape[1]], sems.at[i])
        for i, (ref, c) in enumerate(zip(piece_refs, columns))
    ]


def layer_out_kernel(first, columns, parts, *refs):
    mask_ref, q_ref, weight_ref = refs[:3]
    attended_refs = refs[3 : 3 + parts]
    piece_refs = refs[3 + parts : 3 + parts + len(columns)]
    refs = refs[3 + parts + len(columns) :]
    out_ref, whole_ref, sems = refs[-3:]
    step = pl.program_id(0)
    stores = pieces_into(whole_ref, piece_refs, columns, sems)

    @pl.when(step == 0)
    def _():
        for store in stores:
            store.start()

    weight = prune(weight_ref[...], mask_ref, 0, (first + step) * (weight_ref.shape[1] // TILE))
    attended = jnp.concatenate([ref[...] for ref in attended_refs], axis=1)
    mixed = f32_dot(attended, weight)
    out_ref[...] = (q_ref[...].astype(jnp.float32) + mixed).astype(jnp.bfloat16)

    @pl.when(step == pl.num_programs(0) - 1)
    def _():
        for store in stores:
            store.wait()


def layer_out_of(queries, attended, weight, mask, first, last, pieces, whole, block=512):
    tok, width = queries.shape
    count = last - first
    hbm = pl.BlockSpec(memory_space=pltpu.HBM)
    anywhere = pl.BlockSpec(memory_space=pl.ANY)
    columns = [c for _, c in pieces]
    return pl.pallas_call(
        functools.partial(layer_out_kernel, first, columns, len(attended)),
        grid=(count,),
        in_specs=[
            pl.BlockSpec(memory_space=pltpu.SMEM),
            pl.BlockSpec((tok, block), lambda i: (0, i + first)),
            pl.BlockSpec((width, block), lambda i: (0, i + first)),
            *[pl.BlockSpec(a.shape, lambda i: (0, 0)) for a in attended],
            *[anywhere for _ in pieces],
            *[hbm for _ in whole],
        ],
        out_specs=[pl.BlockSpec((tok, block), lambda i: (0, i)), hbm],
        out_shape=[
            jax.ShapeDtypeStruct((tok, count * block), jnp.bfloat16),
            jax.ShapeDtypeStruct((tok, width), jnp.bfloat16),
        ],
        scratch_shapes=[pltpu.SemaphoreType.DMA((len(pieces),))],
        input_output_aliases={3 + len(attended) + len(pieces): 1} if whole else {},
        compiler_params=pltpu.CompilerParams(vmem_limit_bytes=VMEM_LIMIT),
        cost_estimate=pl.CostEstimate(
            flops=2 * tok * width * count * block,
            bytes_accessed=2 * width * count * block,
            transcendentals=0,
        ),
        name="layer_out",
    )(mask, queries, weight, *attended, *[p for p, _ in pieces], *whole)


def store_first_kernel(shard_ref, piece_ref, own_ref, ahead_ref, beside_ref, whole_ref, kv_ref, sum_ref, sems):
    (store,) = pieces_into(whole_ref, [piece_ref], [0], sems)
    store.start()
    total = own_ref[...] + ahead_ref[...].astype(jnp.float32)
    both = total + beside_ref[...].astype(jnp.float32)
    sum_ref[...] = jnp.where(shard_ref[0] % 2 == 0, both, total)
    kv_store = pltpu.make_async_copy(sum_ref, kv_ref, sems.at[1])
    kv_store.start()
    store.wait()
    kv_store.wait()


def store_first(shard, piece, own, ahead, beside, width):
    hbm = pl.BlockSpec(memory_space=pltpu.HBM)
    vmem = pl.BlockSpec(memory_space=pltpu.VMEM)
    return pl.pallas_call(
        store_first_kernel,
        in_specs=[pl.BlockSpec(memory_space=pltpu.SMEM), vmem, vmem, vmem, vmem],
        out_specs=[hbm, hbm],
        out_shape=[
            jax.ShapeDtypeStruct((piece.shape[0], width), piece.dtype),
            jax.ShapeDtypeStruct(own.shape, own.dtype),
        ],
        scratch_shapes=[pltpu.VMEM(own.shape, own.dtype), pltpu.SemaphoreType.DMA((2,))],
        compiler_params=pltpu.CompilerParams(vmem_limit_bytes=VMEM_LIMIT),
        name="store_first",
    )(shard, piece, own, ahead, beside)


def store_last_kernel(piece_ref, given_ref, kept_ref, whole_ref, same_ref, sems):
    (store,) = pieces_into(whole_ref, [piece_ref], [whole_ref.shape[1] - piece_ref.shape[1]], sems)
    store.start()
    store.wait()


def store_last(piece, whole, kept):
    hbm = pl.BlockSpec(memory_space=pltpu.HBM)
    return pl.pallas_call(
        store_last_kernel,
        in_specs=[pl.BlockSpec(memory_space=pltpu.VMEM), hbm, hbm],
        out_specs=[hbm, hbm],
        out_shape=[
            jax.ShapeDtypeStruct(whole.shape, whole.dtype),
            jax.ShapeDtypeStruct(kept.shape, kept.dtype),
        ],
        scratch_shapes=[pltpu.SemaphoreType.DMA((1,))],
        input_output_aliases={1: 0, 2: 1},
        compiler_params=pltpu.CompilerParams(vmem_limit_bytes=VMEM_LIMIT),
        name="store_last",
    )(piece, whole, kept)


def attention_group(near_ok, far_ok, q_heads, d_heads, own, near, far):
    tok = q_heads[0].shape[0]
    scaling = HD ** (-0.5)
    floor = jnp.float32(-1e30)
    key_at = lax.broadcasted_iota(jnp.int32, (tok, tok), 0)
    row_at = lax.broadcasted_iota(jnp.int32, (tok, tok), 1)
    causal = key_at <= row_at
    q_rows = jnp.concatenate(q_heads, axis=0)
    d_columns = jnp.concatenate(d_heads, axis=1)
    keys = jnp.concatenate([own[0], near[0], far[0]], axis=0)
    values = jnp.concatenate([own[1], near[1], far[1]], axis=0)
    logits = f32_dot(keys, q_rows, NT)
    d_probs = f32_dot(values, d_columns)
    probs_parts, d_logit_parts = [], []
    zeros = jnp.zeros((tok, tok), jnp.float32)
    for h in range(len(q_heads)):
        at = slice(h * tok, (h + 1) * tok)
        own_l, near_l, far_l = (logits[i * tok : (i + 1) * tok, at] for i in range(3))
        edge = jnp.where(causal, own_l, jnp.where(far_ok, far_l, floor))
        near_l = jnp.where(near_ok, near_l, floor)
        top = jnp.max(jnp.maximum(edge, near_l), axis=0, keepdims=True)
        edge = jnp.exp((edge - top) * scaling)
        near_l = jnp.exp((near_l - top) * scaling)
        inverse = 1.0 / jnp.sum(edge + near_l, axis=0, keepdims=True)
        edge = edge * inverse
        near_l = near_l * inverse
        own_d, near_d, far_d = (d_probs[i * tok : (i + 1) * tok, at] for i in range(3))
        edge_d = jnp.where(causal, own_d, far_d)
        row_dot = jnp.sum(edge * edge_d + near_l * near_d, axis=0, keepdims=True)
        d_edge = edge * (edge_d - row_dot)
        d_near = near_l * (near_d - row_dot)
        probs_parts.append(
            jnp.concatenate(
                [jnp.where(causal, edge, zeros), near_l, jnp.where(causal, zeros, edge)], axis=0
            ).astype(jnp.bfloat16)
        )
        d_logit_parts.append(
            jnp.concatenate(
                [jnp.where(causal, d_edge, zeros), d_near, jnp.where(causal, zeros, d_edge)], axis=0
            ).astype(jnp.bfloat16)
        )
    probs = jnp.concatenate(probs_parts, axis=1)
    d_logits = jnp.concatenate(d_logit_parts, axis=1)
    d_queries = f32_dot(keys.T, d_logits) * scaling
    attended = f32_dot(values.T, probs)
    d_keys = f32_dot(d_logits, q_rows) * scaling
    d_values = f32_dot(probs, d_columns, NT)
    return d_queries, attended, d_keys, d_values


def attention_kernel(first, last, shard_ref, q_ref, d_ref, cot_ref, own_ref, near_ref, far_ref, *refs):
    kv_heads = own_ref.shape[-1] // HD
    tok, width = q_ref.shape
    group = width // kv_heads
    heads = group // HD
    shard = shard_ref[0]
    att_ref, grad_ref, *kv_refs = refs[-5:]
    for done_ref, kv_ref in zip(refs[:-5], kv_refs):
        kv_ref[:, :, : first * HD] = done_ref[...]
    for g in range(first, last):
        at_kv = slice(g * HD, (g + 1) * HD)
        own, near, far = (
            [ref[0, :, at_kv], ref[1, :, at_kv]] for ref in (own_ref, near_ref, far_ref)
        )
        columns = [g * group + h * HD for h in range(heads)]
        d_queries, attended, d_keys, d_values = attention_group(
            shard >= 1,
            shard >= 2,
            [q_ref[:, c : c + HD] for c in columns],
            [d_ref[c : c + HD, :] for c in columns],
            own, near, far,
        )
        for h, c in enumerate(columns):
            rows = slice(h * tok, (h + 1) * tok)
            at = slice(c - first * group, c - first * group + HD)
            grad_ref[:, at] = (
                cot_ref[:, c : c + HD].astype(jnp.float32) + d_queries[:, rows].T
            ).astype(jnp.bfloat16)
            att_ref[:, at] = attended[:, rows].T.astype(jnp.bfloat16)
        for index, grad in enumerate((d_keys, d_values)):
            for part, ref in enumerate(kv_refs):
                ref[index, :, at_kv] = grad[part * tok : (part + 1) * tok].astype(ref.dtype)


def attention_of(shard, queries, d_attended, cot, own, near, far, first, last, done):
    tok, width = queries.shape
    kv_heads = own.shape[-1] // HD
    group = width // kv_heads
    count = last - first
    vmem = pl.BlockSpec(memory_space=pltpu.VMEM)
    rows = jax.ShapeDtypeStruct((tok, count * group), jnp.bfloat16)
    return pl.pallas_call(
        functools.partial(attention_kernel, first, last),
        in_specs=[pl.BlockSpec(memory_space=pltpu.SMEM)] + [vmem] * (6 + len(done)),
        out_specs=[vmem] * 5,
        out_shape=[rows, rows]
        + [jax.ShapeDtypeStruct((2, tok, last * HD), t) for t in (jnp.float32, jnp.bfloat16, jnp.bfloat16)],
        compiler_params=pltpu.CompilerParams(vmem_limit_bytes=VMEM_LIMIT),
        cost_estimate=pl.CostEstimate(
            flops=12 * tok * 3 * tok * count * group, bytes_accessed=8 * tok * count * group,
            transcendentals=0,
        ),
        name="attention",
    )(shard, queries, d_attended, cot, own, near, far, *done)


def core_swap(value, axis):
    return lax.ppermute(value, axis, [(i, i ^ 1) for i in range(lax.axis_size(axis))])


def per_device(stream_in, keys_values, out_weight, tile_mask, cotangent):
    queries, own, weight = stream_in[0], keys_values[0], out_weight[0]
    mask, cot = tile_mask[0], cotangent[0]
    seq_index = lax.axis_index("seq").astype(jnp.int32)
    shard = seq_index.reshape(1)
    far = from_behind(own, "seq", 2)
    d_attended = d_attended_of(cot, weight, mask)
    near = core_swap(pick(shard, own, far, d_attended), "seq")
    group = queries.shape[1] // (own.shape[-1] // HD)
    attended, pieces, kv_grads = [], [], []
    for first, last in CHUNKS:
        att, grad, *kv_grads = attention_of(
            shard, queries, d_attended, cot, own, near, far, first, last, kv_grads
        )
        attended.append(att)
        pieces.append((around(grad, "section", -1), first * group))
    own_grad, near_grad, far_grad = kv_grads
    beside = core_swap(near_grad, "seq")
    steps = queries.shape[1] // 512
    result, prev_grad = layer_out_of(
        queries, attended, weight, mask, 0, OUT_CUT, pieces[:-1], []
    )
    early = around(result, "section", 1)
    ahead = from_behind(behind_of(shard, far_grad, beside), "seq", -2)
    result, prev_grad = layer_out_of(
        queries, attended, weight, mask, OUT_CUT, steps, pieces[-1:], [prev_grad]
    )
    late = around(result, "section", 1)
    next_input, kv_total = store_first(shard, early, own_grad, ahead, beside, queries.shape[1])
    next_input, kv_total = store_last(late, next_input, kv_total)
    return (next_input[None], prev_grad[None], kv_total[None])


def solution(mesh):
    return jax.shard_map(
        per_device,
        mesh=mesh,
        in_specs=(
            P("section", "seq", None),
            P("section", None, "seq", None),
            P("section", None, None),
            P("section", None, None),
            P("section", "seq", None),
        ),
        out_specs=(
            P("section", "seq", None),
            P("section", "seq", None),
            P("section", None, "seq", None),
        ),
        check_vma=False,
    )
```

```python
import functools

import jax
import jax.numpy as jnp
from jax import lax
from jax.experimental import pallas as pl
from jax.experimental.pallas import tpu as pltpu
from jax.sharding import PartitionSpec as P

HD = 128
TILE = 128
CHUNKS = ((0, 1), (1, 2), (2, 4))
OUT_CUT = 3
VMEM_LIMIT = 32 * 1024 * 1024
NT = (((1,), (1,)), ((), ()))


def around(value, axis, by):
    length = lax.axis_size(axis)
    return lax.ppermute(value, axis, [(i, (i + by) % length) for i in range(length)])


def f32_dot(a, b, dims=(((1,), (0,)), ((), ()))):
    return lax.dot_general(a, b, dims, preferred_element_type=jnp.float32)


def prune(weight, mask_ref, row_tile, column_tile):
    rows, columns = weight.shape
    strips = []
    for a in range(rows // TILE):
        blocks = []
        for b in range(columns // TILE):
            block = weight[a * TILE : (a + 1) * TILE, b * TILE : (b + 1) * TILE]
            kept = mask_ref[row_tile + a, column_tile + b] > 0
            blocks.append(jnp.where(kept, block, jnp.zeros_like(block)))
        strips.append(jnp.concatenate(blocks, axis=1))
    return jnp.concatenate(strips, axis=0)


def d_attended_kernel(mask_hbm, cot_hbm, weight_hbm, out_ref, weight_ref, mask_ref, cot_ref, sems):
    rows = 2 * TILE
    count = weight_ref.shape[0] // rows
    small = [
        pltpu.make_async_copy(mask_hbm, mask_ref, sems.at[count]),
        pltpu.make_async_copy(cot_hbm, cot_ref, sems.at[count + 1]),
    ]
    large = [
        pltpu.make_async_copy(
            weight_hbm.at[i * rows : (i + 1) * rows], weight_ref.at[i * rows : (i + 1) * rows], sems.at[i]
        )
        for i in range(count)
    ]
    for copy in small + large:
        copy.start()
    for copy in small:
        copy.wait()
    cot = cot_ref[...].T
    for i, copy in enumerate(large):
        at = slice(i * rows, (i + 1) * rows)
        copy.wait()
        weight = prune(weight_ref[at, :], mask_ref, i * (rows // TILE), 0)
        out_ref[at, :] = f32_dot(weight, cot).astype(jnp.bfloat16)


def d_attended_of(cot, weight, mask):
    tok, width = cot.shape
    hbm = pl.BlockSpec(memory_space=pltpu.HBM)
    vmem = pl.BlockSpec(memory_space=pltpu.VMEM)
    return pl.pallas_call(
        d_attended_kernel,
        in_specs=[hbm, hbm, hbm],
        out_specs=[vmem, vmem],
        out_shape=[
            jax.ShapeDtypeStruct((width, tok), jnp.bfloat16),
            jax.ShapeDtypeStruct(weight.shape, weight.dtype),
        ],
        scratch_shapes=[
            pltpu.SMEM(mask.shape, mask.dtype),
            pltpu.VMEM(cot.shape, cot.dtype),
            pltpu.SemaphoreType.DMA((width // (2 * TILE) + 2,)),
        ],
        compiler_params=pltpu.CompilerParams(vmem_limit_bytes=VMEM_LIMIT),
        cost_estimate=pl.CostEstimate(
            flops=2 * tok * width * width, bytes_accessed=2 * width * width, transcendentals=0
        ),
        name="d_attended",
    )(*[pltpu.with_memory_space_constraint(x, pltpu.HBM) for x in (mask, cot, weight)])


def pick_kernel(shard_ref, own_ref, far_ref, after_ref, out_ref):
    odd = shard_ref[0] % 2 == 1

    @pl.when(odd)
    def _():
        out_ref[...] = far_ref[...]

    @pl.when(jnp.logical_not(odd))
    def _():
        out_ref[...] = own_ref[...]


def pick(shard, own, far, after):
    vmem = pl.BlockSpec(memory_space=pltpu.VMEM)
    return pl.pallas_call(
        pick_kernel,
        in_specs=[
            pl.BlockSpec(memory_space=pltpu.SMEM), vmem, vmem, pl.BlockSpec(memory_space=pl.ANY),
        ],
        out_specs=vmem,
        out_shape=jax.ShapeDtypeStruct(own.shape, own.dtype),
        compiler_params=pltpu.CompilerParams(vmem_limit_bytes=VMEM_LIMIT),
        name="pick",
    )(shard, own, far, after)


def behind_kernel(shard_ref, far_ref, beside_ref, out_ref):
    far = far_ref[...].astype(jnp.float32)
    both = far + beside_ref[...].astype(jnp.float32)
    out_ref[...] = jnp.where(shard_ref[0] % 2 == 1, both, far).astype(jnp.bfloat16)


def behind_of(shard, far, beside):
    vmem = pl.BlockSpec(memory_space=pltpu.VMEM)
    return pl.pallas_call(
        behind_kernel,
        in_specs=[pl.BlockSpec(memory_space=pltpu.SMEM), vmem, vmem],
        out_specs=vmem,
        out_shape=jax.ShapeDtypeStruct(far.shape, far.dtype),
        compiler_params=pltpu.CompilerParams(vmem_limit_bytes=VMEM_LIMIT),
        name="behind",
    )(shard, far, beside)


def pieces_into(whole_ref, piece_refs, columns, sems):
    return [
        pltpu.make_async_copy(ref, whole_ref.at[:, c : c + ref.shape[1]], sems.at[i])
        for i, (ref, c) in enumerate(zip(piece_refs, columns))
    ]


def layer_out_kernel(first, columns, parts, *refs):
    mask_ref, q_ref, weight_ref = refs[:3]
    attended_refs = refs[3 : 3 + parts]
    piece_refs = refs[3 + parts : 3 + parts + len(columns)]
    refs = refs[3 + parts + len(columns) :]
    out_ref, whole_ref, sems = refs[-3:]
    stores = pieces_into(whole_ref, piece_refs, columns, sems)
    for store in stores:
        store.start()
    attended = jnp.concatenate([ref[...] for ref in attended_refs], axis=1)
    columns = 4 * TILE
    for i in range(out_ref.shape[1] // columns):
        at = slice(i * columns, (i + 1) * columns)
        from_all = slice((first + i) * columns, (first + i + 1) * columns)
        weight = prune(weight_ref[:, from_all], mask_ref, 0, (first + i) * (columns // TILE))
        mixed = f32_dot(attended, weight)
        out_ref[:, at] = (q_ref[:, from_all].astype(jnp.float32) + mixed).astype(jnp.bfloat16)
    for store in stores:
        store.wait()


def layer_out_of(queries, attended, weight, mask, first, last, pieces, whole, block=512):
    tok, width = queries.shape
    count = last - first
    hbm = pl.BlockSpec(memory_space=pltpu.HBM)
    vmem = pl.BlockSpec(memory_space=pltpu.VMEM)
    anywhere = pl.BlockSpec(memory_space=pl.ANY)
    columns = [c for _, c in pieces]
    return pl.pallas_call(
        functools.partial(layer_out_kernel, first, columns, len(attended)),
        in_specs=[
            pl.BlockSpec(memory_space=pltpu.SMEM),
            vmem,
            vmem,
            *[vmem for _ in attended],
            *[anywhere for _ in pieces],
            *[hbm for _ in whole],
        ],
        out_specs=[vmem, hbm],
        out_shape=[
            jax.ShapeDtypeStruct((tok, count * block), jnp.bfloat16),
            jax.ShapeDtypeStruct((tok, width), jnp.bfloat16),
        ],
        scratch_shapes=[pltpu.SemaphoreType.DMA((len(pieces),))],
        input_output_aliases={3 + len(attended) + len(pieces): 1} if whole else {},
        compiler_params=pltpu.CompilerParams(vmem_limit_bytes=VMEM_LIMIT),
        cost_estimate=pl.CostEstimate(
            flops=2 * tok * width * count * block,
            bytes_accessed=2 * width * count * block,
            transcendentals=0,
        ),
        name="layer_out",
    )(mask, queries, weight, *attended, *[p for p, _ in pieces], *whole)


def store_first_kernel(shard_ref, piece_ref, own_ref, ahead_ref, beside_ref, whole_ref, kv_ref, sum_ref, sems):
    (store,) = pieces_into(whole_ref, [piece_ref], [0], sems)
    store.start()
    total = own_ref[...] + ahead_ref[...].astype(jnp.float32)
    both = total + beside_ref[...].astype(jnp.float32)
    sum_ref[...] = jnp.where(shard_ref[0] % 2 == 0, both, total)
    kv_store = pltpu.make_async_copy(sum_ref, kv_ref, sems.at[1])
    kv_store.start()
    store.wait()
    kv_store.wait()


def store_first(shard, piece, own, ahead, beside, width):
    hbm = pl.BlockSpec(memory_space=pltpu.HBM)
    vmem = pl.BlockSpec(memory_space=pltpu.VMEM)
    return pl.pallas_call(
        store_first_kernel,
        in_specs=[pl.BlockSpec(memory_space=pltpu.SMEM), vmem, vmem, vmem, vmem],
        out_specs=[hbm, hbm],
        out_shape=[
            jax.ShapeDtypeStruct((piece.shape[0], width), piece.dtype),
            jax.ShapeDtypeStruct(own.shape, own.dtype),
        ],
        scratch_shapes=[pltpu.VMEM(own.shape, own.dtype), pltpu.SemaphoreType.DMA((2,))],
        compiler_params=pltpu.CompilerParams(vmem_limit_bytes=VMEM_LIMIT),
        name="store_first",
    )(shard, piece, own, ahead, beside)


def store_last_kernel(piece_ref, given_ref, kept_ref, whole_ref, same_ref, sems):
    (store,) = pieces_into(whole_ref, [piece_ref], [whole_ref.shape[1] - piece_ref.shape[1]], sems)
    store.start()
    store.wait()


def store_last(piece, whole, kept):
    hbm = pl.BlockSpec(memory_space=pltpu.HBM)
    return pl.pallas_call(
        store_last_kernel,
        in_specs=[pl.BlockSpec(memory_space=pltpu.VMEM), hbm, hbm],
        out_specs=[hbm, hbm],
        out_shape=[
            jax.ShapeDtypeStruct(whole.shape, whole.dtype),
            jax.ShapeDtypeStruct(kept.shape, kept.dtype),
        ],
        scratch_shapes=[pltpu.SemaphoreType.DMA((1,))],
        input_output_aliases={1: 0, 2: 1},
        compiler_params=pltpu.CompilerParams(vmem_limit_bytes=VMEM_LIMIT),
        name="store_last",
    )(piece, whole, kept)


def attention_group(near_ok, far_ok, q_heads, d_heads, own, near, far):
    tok = q_heads[0].shape[0]
    scaling = HD ** (-0.5)
    floor = jnp.float32(-1e30)
    key_at = lax.broadcasted_iota(jnp.int32, (tok, tok), 0)
    row_at = lax.broadcasted_iota(jnp.int32, (tok, tok), 1)
    causal = key_at <= row_at
    q_rows = jnp.concatenate(q_heads, axis=0)
    d_columns = jnp.concatenate(d_heads, axis=1)
    keys = jnp.concatenate([own[0], near[0], far[0]], axis=0)
    values = jnp.concatenate([own[1], near[1], far[1]], axis=0)
    logits = f32_dot(keys, q_rows, NT)
    d_probs = f32_dot(values, d_columns)
    probs_parts, d_logit_parts = [], []
    zeros = jnp.zeros((tok, tok), jnp.float32)
    for h in range(len(q_heads)):
        at = slice(h * tok, (h + 1) * tok)
        own_l, near_l, far_l = (logits[i * tok : (i + 1) * tok, at] for i in range(3))
        edge = jnp.where(causal, own_l, jnp.where(far_ok, far_l, floor))
        near_l = jnp.where(near_ok, near_l, floor)
        top = jnp.max(jnp.maximum(edge, near_l), axis=0, keepdims=True)
        edge = jnp.exp((edge - top) * scaling)
        near_l = jnp.exp((near_l - top) * scaling)
        inverse = 1.0 / jnp.sum(edge + near_l, axis=0, keepdims=True)
        edge = edge * inverse
        near_l = near_l * inverse
        own_d, near_d, far_d = (d_probs[i * tok : (i + 1) * tok, at] for i in range(3))
        edge_d = jnp.where(causal, own_d, far_d)
        row_dot = jnp.sum(edge * edge_d + near_l * near_d, axis=0, keepdims=True)
        d_edge = edge * (edge_d - row_dot)
        d_near = near_l * (near_d - row_dot)
        probs_parts.append(
            jnp.concatenate(
                [jnp.where(causal, edge, zeros), near_l, jnp.where(causal, zeros, edge)], axis=0
            ).astype(jnp.bfloat16)
        )
        d_logit_parts.append(
            jnp.concatenate(
                [jnp.where(causal, d_edge, zeros), d_near, jnp.where(causal, zeros, d_edge)], axis=0
            ).astype(jnp.bfloat16)
        )
    probs = jnp.concatenate(probs_parts, axis=1)
    d_logits = jnp.concatenate(d_logit_parts, axis=1)
    d_queries = f32_dot(keys.T, d_logits) * scaling
    attended = f32_dot(values.T, probs)
    d_keys = f32_dot(d_logits, q_rows) * scaling
    d_values = f32_dot(probs, d_columns, NT)
    return d_queries, attended, d_keys, d_values


def attention_kernel(first, last, shard_ref, q_ref, d_ref, cot_ref, own_ref, near_ref, far_ref, *refs):
    kv_heads = own_ref.shape[-1] // HD
    tok, width = q_ref.shape
    group = width // kv_heads
    heads = group // HD
    shard = shard_ref[0]
    att_ref, grad_ref, *kv_refs = refs[-5:]
    for done_ref, kv_ref in zip(refs[:-5], kv_refs):
        kv_ref[:, :, : first * HD] = done_ref[...]
    for g in range(first, last):
        at_kv = slice(g * HD, (g + 1) * HD)
        own, near, far = (
            [ref[0, :, at_kv], ref[1, :, at_kv]] for ref in (own_ref, near_ref, far_ref)
        )
        columns = [g * group + h * HD for h in range(heads)]
        d_queries, attended, d_keys, d_values = attention_group(
            shard >= 1,
            shard >= 2,
            [q_ref[:, c : c + HD] for c in columns],
            [d_ref[c : c + HD, :] for c in columns],
            own, near, far,
        )
        for h, c in enumerate(columns):
            rows = slice(h * tok, (h + 1) * tok)
            at = slice(c - first * group, c - first * group + HD)
            grad_ref[:, at] = (
                cot_ref[:, c : c + HD].astype(jnp.float32) + d_queries[:, rows].T
            ).astype(jnp.bfloat16)
            att_ref[:, at] = attended[:, rows].T.astype(jnp.bfloat16)
        for index, grad in enumerate((d_keys, d_values)):
            for part, ref in enumerate(kv_refs):
                ref[index, :, at_kv] = grad[part * tok : (part + 1) * tok].astype(ref.dtype)


def attention_of(shard, queries, d_attended, cot, own, near, far, first, last, done):
    tok, width = queries.shape
    kv_heads = own.shape[-1] // HD
    group = width // kv_heads
    count = last - first
    vmem = pl.BlockSpec(memory_space=pltpu.VMEM)
    rows = jax.ShapeDtypeStruct((tok, count * group), jnp.bfloat16)
    return pl.pallas_call(
        functools.partial(attention_kernel, first, last),
        in_specs=[pl.BlockSpec(memory_space=pltpu.SMEM)] + [vmem] * (6 + len(done)),
        out_specs=[vmem] * 5,
        out_shape=[rows, rows]
        + [jax.ShapeDtypeStruct((2, tok, last * HD), t) for t in (jnp.float32, jnp.bfloat16, jnp.bfloat16)],
        compiler_params=pltpu.CompilerParams(vmem_limit_bytes=VMEM_LIMIT),
        cost_estimate=pl.CostEstimate(
            flops=12 * tok * 3 * tok * count * group, bytes_accessed=8 * tok * count * group,
            transcendentals=0,
        ),
        name="attention",
    )(shard, queries, d_attended, cot, own, near, far, *done)


def core_swap(value, axis):
    return lax.ppermute(value, axis, [(i, i ^ 1) for i in range(lax.axis_size(axis))])


def per_device(stream_in, keys_values, out_weight, tile_mask, cotangent):
    queries, own, weight = stream_in[0], keys_values[0], out_weight[0]
    mask, cot = tile_mask[0], cotangent[0]
    seq_index = lax.axis_index("seq").astype(jnp.int32)
    shard = seq_index.reshape(1)
    far = around(own, "seq", 2)
    d_attended, weight = d_attended_of(cot, weight, mask)
    near = core_swap(pick(shard, own, far, d_attended), "seq")
    group = queries.shape[1] // (own.shape[-1] // HD)
    attended, pieces, kv_grads = [], [], []
    for first, last in CHUNKS:
        att, grad, *kv_grads = attention_of(
            shard, queries, d_attended, cot, own, near, far, first, last, kv_grads
        )
        attended.append(att)
        pieces.append((around(grad, "section", -1), first * group))
    own_grad, near_grad, far_grad = kv_grads
    beside = core_swap(near_grad, "seq")
    steps = queries.shape[1] // 512
    result, prev_grad = layer_out_of(
        queries, attended, weight, mask, 0, OUT_CUT, pieces[:-1], []
    )
    early = around(result, "section", 1)
    ahead = around(behind_of(shard, far_grad, beside), "seq", -2)
    result, prev_grad = layer_out_of(
        queries, attended, weight, mask, OUT_CUT, steps, pieces[-1:], [prev_grad]
    )
    late = around(result, "section", 1)
    next_input, kv_total = store_first(shard, early, own_grad, ahead, beside, queries.shape[1])
    next_input, kv_total = store_last(late, next_input, kv_total)
    return (next_input[None], prev_grad[None], kv_total[None])


def solution(mesh):
    return jax.shard_map(
        per_device,
        mesh=mesh,
        in_specs=(
            P("section", "seq", None),
            P("section", None, "seq", None),
            P("section", None, None),
            P("section", None, None),
            P("section", "seq", None),
        ),
        out_specs=(
            P("section", "seq", None),
            P("section", "seq", None),
            P("section", None, "seq", None),
        ),
        check_vma=False,
    )
```

```python
import functools

import jax
import jax.numpy as jnp
from jax import lax
from jax.experimental import pallas as pl
from jax.experimental.pallas import tpu as pltpu
from jax.sharding import PartitionSpec as P

HD = 128
TILE = 128
HALOS = ((0, 1), (1, 4))
CHUNKS = ((0, 1), (1, 2), (2, 4))
OUT_CUT = 3
CUT_FLOPS = 10**10
ATT_FLOPS = {0: 10**9, 1: 1, 2: 10**10}
VMEM_LIMIT = 32 * 1024 * 1024
NT = (((1,), (1,)), ((), ()))


def around(value, axis, by):
    length = lax.axis_size(axis)
    return lax.ppermute(value, axis, [(i, (i + by) % length) for i in range(length)])


def f32_dot(a, b, dims=(((1,), (0,)), ((), ()))):
    return lax.dot_general(a, b, dims, preferred_element_type=jnp.float32)


def prune(weight, mask_ref, row_tile, column_tile):
    rows, columns = weight.shape
    strips = []
    for a in range(rows // TILE):
        blocks = []
        for b in range(columns // TILE):
            block = weight[a * TILE : (a + 1) * TILE, b * TILE : (b + 1) * TILE]
            kept = mask_ref[row_tile + a, column_tile + b] > 0
            blocks.append(jnp.where(kept, block, jnp.zeros_like(block)))
        strips.append(jnp.concatenate(blocks, axis=1))
    return jnp.concatenate(strips, axis=0)


def cut_kernel(own_hbm, *refs):
    *piece_refs, sems = refs
    copies, column = [], 0
    for i, ref in enumerate(piece_refs):
        width = ref.shape[-1]
        source = own_hbm.at[:, :, column : column + width]
        copies.append(pltpu.make_async_copy(source, ref, sems.at[i]))
        column += width
    for copy in copies:
        copy.start()
    for copy in copies:
        copy.wait()


def cut(own):
    shapes = [own.shape[:2] + ((last - first) * HD,) for first, last in HALOS]
    return pl.pallas_call(
        cut_kernel,
        in_specs=[pl.BlockSpec(memory_space=pltpu.HBM)],
        out_specs=[pl.BlockSpec(memory_space=pltpu.VMEM) for _ in shapes],
        out_shape=[jax.ShapeDtypeStruct(shape, own.dtype) for shape in shapes],
        scratch_shapes=[pltpu.SemaphoreType.DMA((len(shapes),))],
        compiler_params=pltpu.CompilerParams(vmem_limit_bytes=VMEM_LIMIT),
        cost_estimate=pl.CostEstimate(flops=CUT_FLOPS, bytes_accessed=0, transcendentals=0),
        name="cut",
    )(pltpu.with_memory_space_constraint(own, pltpu.HBM))


def d_attended_kernel(mask_hbm, cot_hbm, weight_ref, out_ref, mask_ref, cot_ref, sems):
    small = [
        pltpu.make_async_copy(mask_hbm, mask_ref, sems.at[0]),
        pltpu.make_async_copy(cot_hbm, cot_ref, sems.at[1]),
    ]
    for copy in small:
        copy.start()
    for copy in small:
        copy.wait()
    rows = 4 * TILE
    for i in range(weight_ref.shape[0] // rows):
        at = slice(i * rows, (i + 1) * rows)
        weight = prune(weight_ref[at, :], mask_ref, i * (rows // TILE), 0)
        out_ref[:, at] = f32_dot(cot_ref[...], weight, NT).astype(jnp.bfloat16)


def d_attended_of(cot, weight, mask):
    tok, width = cot.shape
    hbm = pl.BlockSpec(memory_space=pltpu.HBM)
    vmem = pl.BlockSpec(memory_space=pltpu.VMEM)
    return pl.pallas_call(
        d_attended_kernel,
        in_specs=[hbm, hbm, vmem],
        out_specs=vmem,
        out_shape=jax.ShapeDtypeStruct((tok, width), jnp.bfloat16),
        scratch_shapes=[
            pltpu.SMEM(mask.shape, mask.dtype),
            pltpu.VMEM(cot.shape, cot.dtype),
            pltpu.SemaphoreType.DMA((2,)),
        ],
        compiler_params=pltpu.CompilerParams(vmem_limit_bytes=VMEM_LIMIT),
        cost_estimate=pl.CostEstimate(
            flops=1, bytes_accessed=1, transcendentals=0
        ),
        name="d_attended",
    )(
        *[pltpu.with_memory_space_constraint(x, pltpu.HBM) for x in (mask, cot)],
        pltpu.with_memory_space_constraint(weight, pltpu.VMEM),
    )


def pick_kernel(shard_ref, own_ref, far_ref, after_ref, key_ref, value_ref):
    odd = shard_ref[0] % 2 == 1
    for index, ref in enumerate((key_ref, value_ref)):

        @pl.when(odd)
        def _():
            ref[...] = far_ref[index]

        @pl.when(jnp.logical_not(odd))
        def _():
            ref[...] = own_ref[index]


def pick(shard, own, far, after):
    vmem = pl.BlockSpec(memory_space=pltpu.VMEM)
    return pl.pallas_call(
        pick_kernel,
        in_specs=[
            pl.BlockSpec(memory_space=pltpu.SMEM), vmem, vmem, pl.BlockSpec(memory_space=pl.ANY),
        ],
        out_specs=[vmem, vmem],
        out_shape=[jax.ShapeDtypeStruct(own.shape[1:], own.dtype)] * 2,
        compiler_params=pltpu.CompilerParams(vmem_limit_bytes=VMEM_LIMIT),
        cost_estimate=pl.CostEstimate(flops=1, bytes_accessed=1, transcendentals=0),
        name="pick",
    )(shard, own, far, after)


def behind_kernel(shard_ref, far_ref, beside_ref, out_ref):
    far = far_ref[...].astype(jnp.float32)
    both = far + beside_ref[...].astype(jnp.float32)
    out_ref[...] = jnp.where(shard_ref[0] % 2 == 1, both, far).astype(jnp.bfloat16)


def behind_of(shard, far, beside):
    vmem = pl.BlockSpec(memory_space=pltpu.VMEM)
    return pl.pallas_call(
        behind_kernel,
        in_specs=[pl.BlockSpec(memory_space=pltpu.SMEM), vmem, vmem],
        out_specs=vmem,
        out_shape=jax.ShapeDtypeStruct(far.shape, far.dtype),
        compiler_params=pltpu.CompilerParams(vmem_limit_bytes=VMEM_LIMIT),
        name="behind",
    )(shard, far, beside)


def pieces_into(whole_ref, piece_refs, columns, sems):
    return [
        pltpu.make_async_copy(ref, whole_ref.at[:, c : c + ref.shape[1]], sems.at[i])
        for i, (ref, c) in enumerate(zip(piece_refs, columns))
    ]


def layer_out_kernel(first, columns, parts, *refs):
    mask_ref, q_ref, weight_ref = refs[:3]
    attended_refs = refs[3 : 3 + parts]
    piece_refs = refs[3 + parts : 3 + parts + len(columns)]
    refs = refs[3 + parts + len(columns) :]
    out_ref, whole_ref, sems = refs[-3:]
    stores = pieces_into(whole_ref, piece_refs, columns, sems)
    for store in stores:
        store.start()
    attended = jnp.concatenate([ref[...] for ref in attended_refs], axis=1)
    columns = 4 * TILE
    for i in range(out_ref.shape[1] // columns):
        at = slice(i * columns, (i + 1) * columns)
        from_all = slice((first + i) * columns, (first + i + 1) * columns)
        weight = prune(weight_ref[:, from_all], mask_ref, 0, (first + i) * (columns // TILE))
        mixed = f32_dot(attended, weight)
        out_ref[:, at] = (q_ref[:, from_all].astype(jnp.float32) + mixed).astype(jnp.bfloat16)
    for store in stores:
        store.wait()


def layer_out_of(queries, attended, weight, mask, first, last, pieces, whole, block=512):
    tok, width = queries.shape
    count = last - first
    hbm = pl.BlockSpec(memory_space=pltpu.HBM)
    vmem = pl.BlockSpec(memory_space=pltpu.VMEM)
    anywhere = pl.BlockSpec(memory_space=pl.ANY)
    columns = [c for _, c in pieces]
    return pl.pallas_call(
        functools.partial(layer_out_kernel, first, columns, len(attended)),
        in_specs=[
            pl.BlockSpec(memory_space=pltpu.SMEM),
            vmem,
            vmem,
            *[vmem for _ in attended],
            *[anywhere for _ in pieces],
            *[hbm for _ in whole],
        ],
        out_specs=[vmem, hbm],
        out_shape=[
            jax.ShapeDtypeStruct((tok, count * block), jnp.bfloat16),
            jax.ShapeDtypeStruct((tok, width), jnp.bfloat16),
        ],
        scratch_shapes=[pltpu.SemaphoreType.DMA((len(pieces),))],
        input_output_aliases={3 + len(attended) + len(pieces): 1} if whole else {},
        compiler_params=pltpu.CompilerParams(vmem_limit_bytes=VMEM_LIMIT),
        cost_estimate=pl.CostEstimate(
            flops=2 * tok * width * count * block,
            bytes_accessed=2 * width * count * block,
            transcendentals=0,
        ),
        name="layer_out",
    )(mask, queries, weight, *attended, *[p for p, _ in pieces], *whole)


def store_first_kernel(shard_ref, piece_ref, own_ref, ahead_ref, beside_ref, whole_ref, kv_ref, sum_ref, sems):
    (store,) = pieces_into(whole_ref, [piece_ref], [0], sems)
    store.start()
    total = own_ref[...] + ahead_ref[...].astype(jnp.float32)
    both = total + beside_ref[...].astype(jnp.float32)
    sum_ref[...] = jnp.where(shard_ref[0] % 2 == 0, both, total)
    kv_store = pltpu.make_async_copy(sum_ref, kv_ref, sems.at[1])
    kv_store.start()
    store.wait()
    kv_store.wait()


def store_first(shard, piece, own, ahead, beside, width):
    hbm = pl.BlockSpec(memory_space=pltpu.HBM)
    vmem = pl.BlockSpec(memory_space=pltpu.VMEM)
    return pl.pallas_call(
        store_first_kernel,
        in_specs=[pl.BlockSpec(memory_space=pltpu.SMEM), vmem, vmem, vmem, vmem],
        out_specs=[hbm, hbm],
        out_shape=[
            jax.ShapeDtypeStruct((piece.shape[0], width), piece.dtype),
            jax.ShapeDtypeStruct(own.shape, own.dtype),
        ],
        scratch_shapes=[pltpu.VMEM(own.shape, own.dtype), pltpu.SemaphoreType.DMA((2,))],
        compiler_params=pltpu.CompilerParams(vmem_limit_bytes=VMEM_LIMIT),
        name="store_first",
    )(shard, piece, own, ahead, beside)


def store_last_kernel(piece_ref, given_ref, kept_ref, whole_ref, same_ref, sems):
    (store,) = pieces_into(whole_ref, [piece_ref], [whole_ref.shape[1] - piece_ref.shape[1]], sems)
    store.start()
    store.wait()


def store_last(piece, whole, kept):
    hbm = pl.BlockSpec(memory_space=pltpu.HBM)
    return pl.pallas_call(
        store_last_kernel,
        in_specs=[pl.BlockSpec(memory_space=pltpu.VMEM), hbm, hbm],
        out_specs=[hbm, hbm],
        out_shape=[
            jax.ShapeDtypeStruct(whole.shape, whole.dtype),
            jax.ShapeDtypeStruct(kept.shape, kept.dtype),
        ],
        scratch_shapes=[pltpu.SemaphoreType.DMA((1,))],
        input_output_aliases={1: 0, 2: 1},
        compiler_params=pltpu.CompilerParams(vmem_limit_bytes=VMEM_LIMIT),
        name="store_last",
    )(piece, whole, kept)


def attention_group(near_ok, far_ok, q_heads, d_heads, own, near, far):
    tok = q_heads[0].shape[0]
    scaling = HD ** (-0.5)
    floor = jnp.float32(-1e30)
    key_at = lax.broadcasted_iota(jnp.int32, (tok, tok), 0)
    row_at = lax.broadcasted_iota(jnp.int32, (tok, tok), 1)
    causal = key_at <= row_at
    q_rows = jnp.concatenate(q_heads, axis=0)
    d_rows = jnp.concatenate(d_heads, axis=0)
    keys = jnp.concatenate([own[0], near[0], far[0]], axis=0)
    values = jnp.concatenate([own[1], near[1], far[1]], axis=0)
    logits = f32_dot(keys, q_rows, NT)
    d_probs = f32_dot(values, d_rows, NT)
    probs_parts, d_logit_parts = [], []
    zeros = jnp.zeros((tok, tok), jnp.float32)
    for h in range(len(q_heads)):
        at = slice(h * tok, (h + 1) * tok)
        own_l, near_l, far_l = (logits[i * tok : (i + 1) * tok, at] for i in range(3))
        edge = jnp.where(causal, own_l, jnp.where(far_ok, far_l, floor))
        near_l = jnp.where(near_ok, near_l, floor)
        top = jnp.max(jnp.maximum(edge, near_l), axis=0, keepdims=True)
        edge = jnp.exp((edge - top) * scaling)
        near_l = jnp.exp((near_l - top) * scaling)
        inverse = 1.0 / jnp.sum(edge + near_l, axis=0, keepdims=True)
        edge = edge * inverse
        near_l = near_l * inverse
        own_d, near_d, far_d = (d_probs[i * tok : (i + 1) * tok, at] for i in range(3))
        edge_d = jnp.where(causal, own_d, far_d)
        row_dot = jnp.sum(edge * edge_d + near_l * near_d, axis=0, keepdims=True)
        d_edge = edge * (edge_d - row_dot)
        d_near = near_l * (near_d - row_dot)
        probs_parts.append(
            jnp.concatenate(
                [jnp.where(causal, edge, zeros), near_l, jnp.where(causal, zeros, edge)], axis=0
            ).astype(jnp.bfloat16)
        )
        d_logit_parts.append(
            jnp.concatenate(
                [jnp.where(causal, d_edge, zeros), d_near, jnp.where(causal, zeros, d_edge)], axis=0
            ).astype(jnp.bfloat16)
        )
    probs = jnp.concatenate(probs_parts, axis=1)
    d_logits = jnp.concatenate(d_logit_parts, axis=1)
    d_queries = f32_dot(keys.T, d_logits) * scaling
    attended = f32_dot(values.T, probs)
    d_keys = f32_dot(d_logits, q_rows) * scaling
    d_values = f32_dot(probs, d_rows)
    return d_queries, attended, d_keys, d_values


def attention_kernel(low, first, last, group, column, shard_ref, q_ref, d_ref, cot_ref, *refs):
    own_ref, keys_ref, values_ref, far_ref, *refs = refs
    tok = q_ref.shape[0]
    heads = group // HD
    shard = shard_ref[0]
    stores = []
    if column is not None:
        piece_ref, *refs, whole_ref, sems = refs
        stores = pieces_into(whole_ref, [piece_ref], [column], sems)
    for store in stores:
        store.start()
    att_ref, grad_ref, *kv_refs = refs[-5:]
    for done_ref, kv_ref in zip(refs[:-5], kv_refs):
        kv_ref[:, :, : first * HD] = done_ref[...]
    for g in range(first, last):
        at_kv = slice(g * HD, (g + 1) * HD)
        in_piece = slice((g - low) * HD, (g - low + 1) * HD)
        own, far = ([ref[0, :, in_piece], ref[1, :, in_piece]] for ref in (own_ref, far_ref))
        near = [keys_ref[:, in_piece], values_ref[:, in_piece]]
        columns = [g * group + h * HD for h in range(heads)]
        d_queries, attended, d_keys, d_values = attention_group(
            shard >= 1,
            shard >= 2,
            [q_ref[:, c : c + HD] for c in columns],
            [d_ref[:, c : c + HD] for c in columns],
            own, near, far,
        )
        for h, c in enumerate(columns):
            rows = slice(h * tok, (h + 1) * tok)
            at = slice(c - first * group, c - first * group + HD)
            grad_ref[:, at] = (
                cot_ref[:, c : c + HD].astype(jnp.float32) + d_queries[:, rows].T
            ).astype(jnp.bfloat16)
            att_ref[:, at] = attended[:, rows].T.astype(jnp.bfloat16)
        for index, grad in enumerate((d_keys, d_values)):
            for part, ref in enumerate(kv_refs):
                ref[index, :, at_kv] = grad[part * tok : (part + 1) * tok].astype(ref.dtype)
    for store in stores:
        store.wait()


def attention_of(shard, queries, d_attended, cot, block, low, first, last, group, done, piece=None):
    tok, width = queries.shape
    count = last - first
    vmem = pl.BlockSpec(memory_space=pltpu.VMEM)
    rows = jax.ShapeDtypeStruct((tok, count * group), jnp.bfloat16)
    out_specs = [vmem] * 5
    out_shape = [rows, rows] + [
        jax.ShapeDtypeStruct((2, tok, last * HD), t) for t in (jnp.float32, jnp.bfloat16, jnp.bfloat16)
    ]
    pieces, column, scratch = [], None, []
    if piece is not None:
        pieces, column = [piece[0]], piece[1]
        out_specs.append(pl.BlockSpec(memory_space=pltpu.HBM))
        out_shape.append(jax.ShapeDtypeStruct((tok, width), jnp.bfloat16))
        scratch.append(pltpu.SemaphoreType.DMA((1,)))
    return pl.pallas_call(
        functools.partial(attention_kernel, low, first, last, group, column),
        in_specs=[pl.BlockSpec(memory_space=pltpu.SMEM)] + [vmem] * (7 + len(done) + len(pieces)),
        out_specs=out_specs,
        out_shape=out_shape,
        scratch_shapes=scratch,
        compiler_params=pltpu.CompilerParams(vmem_limit_bytes=VMEM_LIMIT),
        cost_estimate=pl.CostEstimate(
            flops=ATT_FLOPS[first], bytes_accessed=1, transcendentals=0,
        ),
        name="attention",
    )(shard, queries, d_attended, cot, *block, *pieces, *done)


def core_swap(value, axis):
    return lax.ppermute(value, axis, [(i, i ^ 1) for i in range(lax.axis_size(axis))])


def per_device(stream_in, keys_values, out_weight, tile_mask, cotangent):
    queries, own, weight = stream_in[0], keys_values[0], out_weight[0]
    mask, cot = tile_mask[0], cotangent[0]
    seq_index = lax.axis_index("seq").astype(jnp.int32)
    shard = seq_index.reshape(1)
    group = queries.shape[1] // (own.shape[-1] // HD)
    owns = cut(own)
    fars = [around(piece, "seq", 2) for piece in owns]
    d_attended = d_attended_of(cot, weight, mask)
    attended, pieces, kv_grads = [], [], []
    attended, pieces, kv_grads, blocks = [], [], [], []
    after = d_attended
    for first, last in CHUNKS:
        halo = [i for i, (low, high) in enumerate(HALOS) if low <= first < high][0]
        if halo == len(blocks):
            near = [core_swap(x, "seq") for x in pick(shard, owns[halo], fars[halo], after)]
            blocks.append((owns[halo], *near, fars[halo]))
        stored = pieces[0] if first == CHUNKS[-1][0] else None
        att, grad, *kv_grads = attention_of(
            shard, queries, d_attended, cot, blocks[halo], HALOS[halo][0], first, last, group, kv_grads, stored
        )
        attended.append(att)
        pieces.append((around(grad, "section", -1), first * group))
        after = grad
    own_grad, near_grad, far_grad, prev_grad = kv_grads
    beside = core_swap(near_grad, "seq")
    steps = queries.shape[1] // 512
    result, prev_grad = layer_out_of(
        queries, attended, weight, mask, 0, OUT_CUT, pieces[1:2], [prev_grad]
    )
    early = around(result, "section", 1)
    ahead = around(behind_of(shard, far_grad, beside), "seq", -2)
    result, prev_grad = layer_out_of(
        queries, attended, weight, mask, OUT_CUT, steps, pieces[2:], [prev_grad]
    )
    late = around(result, "section", 1)
    next_input, kv_total = store_first(shard, early, own_grad, ahead, beside, queries.shape[1])
    next_input, kv_total = store_last(late, next_input, kv_total)
    return (next_input[None], prev_grad[None], kv_total[None])


def solution(mesh):
    return jax.shard_map(
        per_device,
        mesh=mesh,
        in_specs=(
            P("section", "seq", None),
            P("section", None, "seq", None),
            P("section", None, None),
            P("section", None, None),
            P("section", "seq", None),
        ),
        out_specs=(
            P("section", "seq", None),
            P("section", "seq", None),
            P("section", None, "seq", None),
        ),
        check_vma=False,
    )
```

```python
import functools

import jax
import jax.numpy as jnp
from jax import lax
from jax.experimental import pallas as pl
from jax.experimental.pallas import tpu as pltpu
from jax.sharding import PartitionSpec as P

HD = 128
TILE = 128
HALOS = ((0, 1), (1, 4))
CHUNKS = ((0, 1), (1, 2), (2, 4))
OUT_CUT = 3
CUT_FLOPS = 10**10
ATT_FLOPS = {0: 10**9, 1: 1, 2: 10**10}
VMEM = pl.BlockSpec(memory_space=pltpu.VMEM)
HBM = pl.BlockSpec(memory_space=pltpu.HBM)
SMEM = pl.BlockSpec(memory_space=pltpu.SMEM)
VMEM_LIMIT = 32 * 1024 * 1024
NT = (((1,), (1,)), ((), ()))


def around(value, axis, by):
    length = lax.axis_size(axis)
    return lax.ppermute(value, axis, [(i, (i + by) % length) for i in range(length)])


def f32_dot(a, b, dims=(((1,), (0,)), ((), ()))):
    return lax.dot_general(a, b, dims, preferred_element_type=jnp.float32)


def params():
    return pltpu.CompilerParams(vmem_limit_bytes=VMEM_LIMIT)


def cost(flops):
    return pl.CostEstimate(flops=flops, bytes_accessed=1, transcendentals=0)


def prune(weight, kept_ref, row_tile, columns):
    strips = []
    for a in range(weight.shape[0] // TILE):
        row = kept_ref[row_tile + a : row_tile + a + 1, columns]
        kept = jnp.broadcast_to(row, (16, row.shape[1])).astype(weight.dtype)
        strip = weight[a * TILE : (a + 1) * TILE, :]
        strips.append(strip * jnp.concatenate([kept] * (TILE // 16), axis=0))
    return jnp.concatenate(strips, axis=0)


def cut_kernel(own_hbm, *refs):
    *piece_refs, sems = refs
    copies, column = [], 0
    for i, ref in enumerate(piece_refs):
        width = ref.shape[-1]
        source = own_hbm.at[:, :, column : column + width]
        copies.append(pltpu.make_async_copy(source, ref, sems.at[i]))
        column += width
    for copy in copies:
        copy.start()
    for copy in copies:
        copy.wait()


def cut(own):
    shapes = [own.shape[:2] + ((last - first) * HD,) for first, last in HALOS]
    return pl.pallas_call(
        cut_kernel,
        in_specs=[HBM],
        out_specs=[VMEM for _ in shapes],
        out_shape=[jax.ShapeDtypeStruct(shape, own.dtype) for shape in shapes],
        scratch_shapes=[pltpu.SemaphoreType.DMA((len(shapes),))],
        compiler_params=params(),
        cost_estimate=cost(CUT_FLOPS),
        name="cut",
    )(pltpu.with_memory_space_constraint(own, pltpu.HBM))


def d_attended_first_kernel(last, mask_ref, cot_ref, weight_ref, out_ref, turned_ref, kept_ref):
    tiles = mask_ref.shape[0]
    width = kept_ref.shape[1]
    tile = lax.broadcasted_iota(jnp.int32, (tiles, width), 1) // TILE
    spread = (tile == lax.broadcasted_iota(jnp.int32, (tiles, width), 0)).astype(jnp.float32)
    kept_ref[...] = f32_dot((mask_ref[...] > 0).astype(jnp.float32), spread)
    d_attended_rows(0, last, cot_ref, weight_ref, kept_ref, out_ref)
    turned_ref[...] = cot_ref[...].T


def d_attended_second_kernel(first, last, kept_ref, cot_ref, weight_ref, after_ref, out_ref):
    d_attended_rows(first, last, cot_ref, weight_ref, kept_ref, out_ref)


def d_attended_rows(first, last, cot_ref, weight_ref, kept_ref, out_ref):
    rows = 4 * TILE
    for row in range(first, last, rows):
        weight = prune(weight_ref[row : row + rows, :], kept_ref, row // TILE, slice(None))
        at = slice(row - first, row - first + rows)
        out_ref[:, at] = f32_dot(cot_ref[...], weight, NT).astype(jnp.bfloat16)


def d_attended_first(cot, weight, mask, last):
    tok, width = cot.shape
    return pl.pallas_call(
        functools.partial(d_attended_first_kernel, last),
        in_specs=[VMEM, VMEM, VMEM],
        out_specs=[VMEM, VMEM, VMEM],
        out_shape=[
            jax.ShapeDtypeStruct((tok, last), jnp.bfloat16),
            jax.ShapeDtypeStruct((width, tok), jnp.bfloat16),
            jax.ShapeDtypeStruct((mask.shape[0], width), jnp.float32),
        ],
        compiler_params=params(),
        cost_estimate=cost(1),
        name="d_attended_first",
    )(mask, cot, weight)


def d_attended_second(cot, weight, kept, first, after):
    tok, width = cot.shape
    return pl.pallas_call(
        functools.partial(d_attended_second_kernel, first, width),
        in_specs=[VMEM, VMEM, VMEM, pl.BlockSpec(memory_space=pl.ANY)],
        out_specs=VMEM,
        out_shape=jax.ShapeDtypeStruct((tok, width - first), jnp.bfloat16),
        compiler_params=params(),
        cost_estimate=cost(1),
        name="d_attended_second",
    )(kept, cot, weight, after)


def pick_kernel(shard_ref, own_ref, far_ref, after_ref, *out_refs):
    odd = shard_ref[0] % 2 == 1
    split = len(out_refs) == 2

    @pl.when(odd)
    def _():
        for index, ref in enumerate(out_refs):
            ref[...] = far_ref[index] if split else far_ref[...]

    @pl.when(jnp.logical_not(odd))
    def _():
        for index, ref in enumerate(out_refs):
            ref[...] = own_ref[index] if split else own_ref[...]


def pick(shard, own, far, after, split):
    shape = jax.ShapeDtypeStruct(own.shape[1:] if split else own.shape, own.dtype)
    return pl.pallas_call(
        pick_kernel,
        in_specs=[SMEM, VMEM, VMEM, pl.BlockSpec(memory_space=pl.ANY)],
        out_specs=[VMEM] * (2 if split else 1),
        out_shape=[shape] * (2 if split else 1),
        compiler_params=params(),
        cost_estimate=cost(1),
        name="pick",
    )(shard, own, far, after)


def behind_kernel(shard_ref, far_ref, *refs):
    *beside_refs, out_ref = refs
    for index, beside_ref in enumerate(beside_refs):
        far = far_ref[index].astype(jnp.float32)
        both = far + beside_ref[...].astype(jnp.float32)
        out_ref[index] = jnp.where(shard_ref[0] % 2 == 1, both, far).astype(jnp.bfloat16)


def behind_of(shard, far, beside):
    return pl.pallas_call(
        behind_kernel,
        in_specs=[SMEM, VMEM, VMEM, VMEM],
        out_specs=VMEM,
        out_shape=jax.ShapeDtypeStruct(far.shape, far.dtype),
        compiler_params=params(),
        cost_estimate=cost(1),
        name="behind",
    )(shard, far, *beside)


def store_piece(piece, column, turned_ref, whole_ref, sem):
    turned_ref[...] = piece.T
    store = pltpu.make_async_copy(
        turned_ref, whole_ref.at[:, column : column + turned_ref.shape[1]], sem
    )
    store.start()
    return store


def stacked(parts, axis=0):
    return jnp.concatenate(parts, axis=axis)


def blocks_of(own_ref, near_refs, far_ref, index, at):
    near = near_refs[index][:, at] if len(near_refs) == 2 else near_refs[0][index, :, at]
    return stacked([own_ref[index, :, at], near, far_ref[index, :, at]])


def in_grad_group(near_ok, far_ok, q_rows, d_rows, keys, values):
    tok = keys.shape[0] // 3
    scaling = HD ** (-0.5)
    floor = jnp.float32(-1e30)
    key_at = lax.broadcasted_iota(jnp.int32, (tok, tok), 0)
    row_at = lax.broadcasted_iota(jnp.int32, (tok, tok), 1)
    causal = key_at <= row_at
    logits = f32_dot(keys, q_rows, NT)
    d_probs = f32_dot(values, d_rows, NT)
    probs_parts, d_logit_parts = [], []
    zeros = jnp.zeros((tok, tok), jnp.float32)
    for h in range(q_rows.shape[0] // tok):
        at = slice(h * tok, (h + 1) * tok)
        own_l, near_l, far_l = (logits[i * tok : (i + 1) * tok, at] for i in range(3))
        edge = jnp.where(causal, own_l, jnp.where(far_ok, far_l, floor))
        near_l = jnp.where(near_ok, near_l, floor)
        top = jnp.max(jnp.maximum(edge, near_l), axis=0, keepdims=True)
        edge = jnp.exp((edge - top) * scaling)
        near_l = jnp.exp((near_l - top) * scaling)
        inverse = 1.0 / jnp.sum(edge + near_l, axis=0, keepdims=True)
        edge = edge * inverse
        near_l = near_l * inverse
        own_d, near_d, far_d = (d_probs[i * tok : (i + 1) * tok, at] for i in range(3))
        edge_d = jnp.where(causal, own_d, far_d)
        row_dot = jnp.sum(edge * edge_d + near_l * near_d, axis=0, keepdims=True)
        d_edge = edge * (edge_d - row_dot)
        d_near = near_l * (near_d - row_dot)
        probs_parts.append(
            stacked([jnp.where(causal, edge, zeros), near_l, jnp.where(causal, zeros, edge)])
            .astype(jnp.bfloat16)
        )
        d_logit_parts.append(
            stacked([jnp.where(causal, d_edge, zeros), d_near, jnp.where(causal, zeros, d_edge)])
            .astype(jnp.bfloat16)
        )
    probs = stacked(probs_parts, axis=1)
    d_logits = stacked(d_logit_parts, axis=1)
    return f32_dot(keys.T, d_logits) * scaling, probs, d_logits


def in_grad_kernel(low, d_low, first, last, group, nears, column, shard_ref, q_ref, d_ref, turned_cot_ref, *refs):
    own_ref, *refs = refs
    near_refs, (far_ref, *refs) = refs[:nears], refs[nears:]
    tok = q_ref.shape[0]
    store = None
    if column is not None:
        piece_ref, *refs, whole_ref, turned_ref, sem = refs
        store = store_piece(piece_ref[...], column, turned_ref, whole_ref, sem)
    grad_ref, probs_ref, d_logits_ref = refs
    shard = shard_ref[0]
    for g in range(first, last):
        at = slice((g - low) * HD, (g - low + 1) * HD)
        columns = [g * group + c for c in range(0, group, HD)]
        d_queries, probs, d_logits = in_grad_group(
            shard >= 1,
            shard >= 2,
            stacked([q_ref[:, c : c + HD] for c in columns]),
            stacked([d_ref[:, c - d_low : c - d_low + HD] for c in columns]),
            blocks_of(own_ref, near_refs, far_ref, 0, at),
            blocks_of(own_ref, near_refs, far_ref, 1, at),
        )
        probs_ref[g - first] = probs
        d_logits_ref[g - first] = d_logits
        for h, c in enumerate(columns):
            out = slice(c - first * group, c - first * group + HD)
            grad_ref[out, :] = (
                turned_cot_ref[c : c + HD, :].astype(jnp.float32)
                + d_queries[:, h * tok : (h + 1) * tok]
            ).astype(jnp.bfloat16)
    if store is not None:
        store.wait()


def in_grad_of(shard, queries, d_attended, turned_cot, block, low, d_low, first, last, group, piece=None):
    tok, width = queries.shape
    count = last - first
    inside = jax.ShapeDtypeStruct((count, 3 * tok, tok * group // HD), jnp.bfloat16)
    out_specs = [VMEM] * 3
    out_shape = [jax.ShapeDtypeStruct((count * group, tok), jnp.bfloat16), inside, inside]
    pieces, column, scratch = [], None, []
    if piece is not None:
        pieces, column = [piece[0]], piece[1]
        out_specs.append(HBM)
        out_shape.append(jax.ShapeDtypeStruct((tok, width), jnp.bfloat16))
        scratch = [pltpu.VMEM(piece[0].shape[::-1], jnp.bfloat16), pltpu.SemaphoreType.DMA]
    own, near, far = block
    return pl.pallas_call(
        functools.partial(in_grad_kernel, low, d_low, first, last, group, len(near), column),
        in_specs=[SMEM] + [VMEM] * (5 + len(near) + len(pieces)),
        out_specs=out_specs,
        out_shape=out_shape,
        scratch_shapes=scratch,
        compiler_params=params(),
        cost_estimate=cost(ATT_FLOPS[first]),
        name="in_grad",
    )(shard, queries, d_attended, turned_cot, own, *near, far, *pieces)


def mixed_columns(attended, weight_ref, kept_ref, q_ref, out_ref, first):
    step = 4 * TILE
    for column in range(0, out_ref.shape[1], step):
        at = slice(column, column + step)
        of_all = slice(first + column, first + column + step)
        weight = prune(weight_ref[:, of_all], kept_ref, 0, of_all)
        mixed = f32_dot(attended, weight)
        out_ref[:, at] = (q_ref[:, of_all].astype(jnp.float32) + mixed).astype(jnp.bfloat16)


def layer_out_first_kernel(group, chunks, halos, nears, cut_at, column, *refs):
    kept_ref, q_ref, weight_ref, piece_ref, given_ref, *refs = refs
    d_refs, refs = refs[:2], refs[2:]
    owns, nears_refs, fars = [], [], []
    for count in nears:
        own_ref, *refs = refs
        near, (far_ref, *refs) = refs[:count], refs[count:]
        owns.append(own_ref)
        nears_refs.append(near)
        fars.append(far_ref)
    probs_refs, refs = refs[: len(chunks)], refs[len(chunks) :]
    d_logits_refs, refs = refs[: len(chunks)], refs[len(chunks) :]
    out_ref, whole_ref, attended_ref, own_grad_ref, *near_grad_refs, far_grad_ref, turned_ref, sem = refs
    tok = q_ref.shape[0]
    scaling = HD ** (-0.5)
    store = store_piece(piece_ref[...], column, turned_ref, whole_ref, sem)
    for i, (first, last) in enumerate(chunks):
        for g in range(first, last):
            halo = [j for j, (low, high) in enumerate(halos) if low <= g < high][0]
            at = slice((g - halos[halo][0]) * HD, (g - halos[halo][0] + 1) * HD)
            at_kv = slice(g * HD, (g + 1) * HD)
            columns = [g * group + c for c in range(0, group, HD)]
            half = 0 if columns[0] < cut_at else 1
            d_rows = stacked([d_refs[half][:, c - half * cut_at : c - half * cut_at + HD] for c in columns])
            q_rows = stacked([q_ref[:, c : c + HD] for c in columns])
            values = blocks_of(owns[halo], nears_refs[halo], fars[halo], 1, at)
            probs = probs_refs[i][g - first]
            d_logits = d_logits_refs[i][g - first]
            attended = f32_dot(values.T, probs).astype(jnp.bfloat16)
            for h, c in enumerate(columns):
                attended_ref[:, c : c + HD] = attended[:, h * tok : (h + 1) * tok].T
            d_keys = f32_dot(d_logits, q_rows) * scaling
            d_values = f32_dot(probs, d_rows)
            for index, grad in enumerate((d_keys, d_values)):
                own_grad_ref[index, :, at_kv] = grad[:tok]
                near_grad_refs[index][:, at_kv] = grad[tok : 2 * tok].astype(jnp.bfloat16)
                far_grad_ref[index, :, at_kv] = grad[2 * tok :].astype(jnp.bfloat16)
    mixed_columns(attended_ref[...], weight_ref, kept_ref, q_ref, out_ref, 0)
    store.wait()


def layer_out_first(kept, queries, weight, piece, given, d_parts, blocks, chunks, probs, d_logits, group, last):
    tok, width = queries.shape
    kv_width = sum(own.shape[-1] for own, _, _ in blocks)
    flat = [x for own, near, far in blocks for x in (own, *near, far)]
    operands = [kept, queries, weight, piece[0], given, *d_parts, *flat, *probs, *d_logits]
    near_grad = jax.ShapeDtypeStruct((tok, kv_width), jnp.bfloat16)
    own_grad, far_grad = (jax.ShapeDtypeStruct((2, tok, kv_width), t) for t in (jnp.float32, jnp.bfloat16))
    return pl.pallas_call(
        functools.partial(
            layer_out_first_kernel, group, chunks, HALOS, [len(near) for _, near, _ in blocks],
            d_parts[0].shape[1], piece[1],
        ),
        in_specs=[VMEM] * 4 + [HBM] + [VMEM] * (len(operands) - 5),
        out_specs=[VMEM, HBM] + [VMEM] * 5,
        out_shape=[
            jax.ShapeDtypeStruct((tok, last), jnp.bfloat16),
            jax.ShapeDtypeStruct((tok, width), jnp.bfloat16),
            jax.ShapeDtypeStruct((tok, width), jnp.bfloat16),
            own_grad, near_grad, near_grad, far_grad,
        ],
        scratch_shapes=[pltpu.VMEM(piece[0].shape[::-1], jnp.bfloat16), pltpu.SemaphoreType.DMA],
        input_output_aliases={4: 1},
        compiler_params=params(),
        cost_estimate=cost(10**10),
        name="layer_out_first",
    )(*operands)


def layer_out_second_kernel(first, column, *refs):
    kept_ref, q_ref, weight_ref, piece_ref, given_ref, attended_ref, out_ref, whole_ref, turned_ref, sem = refs
    store = store_piece(piece_ref[...], column, turned_ref, whole_ref, sem)
    mixed_columns(attended_ref[...], weight_ref, kept_ref, q_ref, out_ref, first)
    store.wait()


def layer_out_second(kept, queries, weight, piece, given, attended, first):
    tok, width = queries.shape
    return pl.pallas_call(
        functools.partial(layer_out_second_kernel, first, piece[1]),
        in_specs=[VMEM] * 4 + [HBM, VMEM],
        out_specs=[VMEM, HBM],
        out_shape=[
            jax.ShapeDtypeStruct((tok, width - first), jnp.bfloat16),
            jax.ShapeDtypeStruct((tok, width), jnp.bfloat16),
        ],
        scratch_shapes=[pltpu.VMEM(piece[0].shape[::-1], jnp.bfloat16), pltpu.SemaphoreType.DMA],
        input_output_aliases={4: 1},
        compiler_params=params(),
        cost_estimate=cost(10**10),
        name="layer_out_second",
    )(kept, queries, weight, piece[0], given, attended)


def store_first_kernel(shard_ref, piece_ref, own_ref, ahead_ref, *refs):
    *beside_refs, whole_ref, kv_ref, sum_ref, sems = refs
    store = pltpu.make_async_copy(piece_ref, whole_ref.at[:, : piece_ref.shape[1]], sems.at[0])
    store.start()
    for index, beside_ref in enumerate(beside_refs):
        total = own_ref[index] + ahead_ref[index].astype(jnp.float32)
        both = total + beside_ref[...].astype(jnp.float32)
        sum_ref[index] = jnp.where(shard_ref[0] % 2 == 0, both, total)
    kv_store = pltpu.make_async_copy(sum_ref, kv_ref, sems.at[1])
    kv_store.start()
    store.wait()
    kv_store.wait()


def store_first(shard, piece, own, ahead, beside, width):
    return pl.pallas_call(
        store_first_kernel,
        in_specs=[SMEM] + [VMEM] * 5,
        out_specs=[HBM, HBM],
        out_shape=[
            jax.ShapeDtypeStruct((piece.shape[0], width), piece.dtype),
            jax.ShapeDtypeStruct(own.shape, own.dtype),
        ],
        scratch_shapes=[pltpu.VMEM(own.shape, own.dtype), pltpu.SemaphoreType.DMA((2,))],
        compiler_params=params(),
        name="store_first",
    )(shard, piece, own, ahead, *beside)


def store_last_kernel(piece_ref, given_ref, kept_ref, whole_ref, same_ref, sem):
    column = whole_ref.shape[1] - piece_ref.shape[1]
    store = pltpu.make_async_copy(piece_ref, whole_ref.at[:, column:], sem)
    store.start()
    store.wait()


def store_last(piece, whole, kept):
    return pl.pallas_call(
        store_last_kernel,
        in_specs=[VMEM, HBM, HBM],
        out_specs=[HBM, HBM],
        out_shape=[
            jax.ShapeDtypeStruct(whole.shape, whole.dtype),
            jax.ShapeDtypeStruct(kept.shape, kept.dtype),
        ],
        scratch_shapes=[pltpu.SemaphoreType.DMA],
        input_output_aliases={1: 0, 2: 1},
        compiler_params=params(),
        name="store_last",
    )(piece, whole, kept)


def core_swap(value, axis):
    return lax.ppermute(value, axis, [(i, i ^ 1) for i in range(lax.axis_size(axis))])


def per_device(stream_in, keys_values, out_weight, tile_mask, cotangent):
    queries, own, mask, cot = stream_in[0], keys_values[0], tile_mask[0], cotangent[0]
    weight = pltpu.with_memory_space_constraint(out_weight[0], pltpu.VMEM)
    width = queries.shape[1]
    group = width // (own.shape[-1] // HD)
    shard = lax.axis_index("seq").astype(jnp.int32).reshape(1)
    owns = cut(own)
    fars = [around(piece, "seq", 2) for piece in owns]
    d_cut = CHUNKS[-1][0] * group
    d_first, turned_cot, kept = d_attended_first(cot, weight, mask, d_cut)
    pieces, probs, d_logits, blocks = [], [], [], []
    after = d_first
    for first, last in CHUNKS:
        halo = [i for i, (low, high) in enumerate(HALOS) if low <= first < high][0]
        if halo == len(blocks):
            near = [core_swap(x, "seq") for x in pick(shard, owns[halo], fars[halo], after, halo > 0)]
            blocks.append((owns[halo], near, fars[halo]))
        late = first == CHUNKS[-1][0]
        if late:
            d_second = d_attended_second(cot, weight, kept, d_cut, after)
        grad, p, d, *stored = in_grad_of(
            shard, queries, d_second if late else d_first, turned_cot, blocks[halo], HALOS[halo][0],
            d_cut if late else 0, first, last, group, pieces[0] if late else None,
        )
        probs.append(p)
        d_logits.append(d)
        pieces.append((around(grad, "section", -1), first * group))
        after = grad
    out_cut = OUT_CUT * 4 * TILE
    result, prev_grad, attended, own_grad, *near_grad, far_grad = layer_out_first(
        kept, queries, weight, pieces[1], stored[0], [d_first, d_second], blocks, CHUNKS, probs,
        d_logits, group, out_cut,
    )
    early = around(result, "section", 1)
    beside = [core_swap(x, "seq") for x in near_grad]
    ahead = around(behind_of(shard, far_grad, beside), "seq", -2)
    result, prev_grad = layer_out_second(kept, queries, weight, pieces[2], prev_grad, attended, out_cut)
    late = around(result, "section", 1)
    next_input, kv_total = store_first(shard, early, own_grad, ahead, beside, width)
    next_input, kv_total = store_last(late, next_input, kv_total)
    return (next_input[None], prev_grad[None], kv_total[None])


def solution(mesh):
    return jax.shard_map(
        per_device,
        mesh=mesh,
        in_specs=(
            P("section", "seq", None),
            P("section", None, "seq", None),
            P("section", None, None),
            P("section", None, None),
            P("section", "seq", None),
        ),
        out_specs=(
            P("section", "seq", None),
            P("section", "seq", None),
            P("section", None, "seq", None),
        ),
        check_vma=False,
    )
```

```python
import functools

import jax
import jax.numpy as jnp
from jax import lax
from jax.experimental import pallas as pl
from jax.experimental.pallas import tpu as pltpu
from jax.sharding import PartitionSpec as P

HD = 128
TILE = 128
HALOS = ((0, 1), (1, 4))
CHUNKS = ((0, 1), (1, 2), (2, 4))
OUT_CUT = 3
CUT_FLOPS = 10**10
ATT_FLOPS = {0: 10**9, 1: 1, 2: 10**10}
VMEM = pl.BlockSpec(memory_space=pltpu.VMEM)
HBM = pl.BlockSpec(memory_space=pltpu.HBM)
SMEM = pl.BlockSpec(memory_space=pltpu.SMEM)
VMEM_LIMIT = 32 * 1024 * 1024
NT = (((1,), (1,)), ((), ()))


def around(value, axis, by):
    length = lax.axis_size(axis)
    return lax.ppermute(value, axis, [(i, (i + by) % length) for i in range(length)])


def f32_dot(a, b, dims=(((1,), (0,)), ((), ()))):
    return lax.dot_general(a, b, dims, preferred_element_type=jnp.float32)


def params():
    return pltpu.CompilerParams(vmem_limit_bytes=VMEM_LIMIT)


def cost(flops):
    return pl.CostEstimate(flops=flops, bytes_accessed=1, transcendentals=0)


def prune(weight, kept_ref, row_tile, columns):
    strips = []
    for a in range(weight.shape[0] // TILE):
        row = kept_ref[row_tile + a : row_tile + a + 1, columns]
        kept = jnp.broadcast_to(row, (16, row.shape[1])).astype(weight.dtype)
        strip = weight[a * TILE : (a + 1) * TILE, :]
        strips.append(strip * jnp.concatenate([kept] * (TILE // 16), axis=0))
    return jnp.concatenate(strips, axis=0)


def cut_kernel(own_hbm, *refs):
    *piece_refs, sems = refs
    copies, column = [], 0
    for i, ref in enumerate(piece_refs):
        width = ref.shape[-1]
        source = own_hbm.at[:, :, column : column + width]
        copies.append(pltpu.make_async_copy(source, ref, sems.at[i]))
        column += width
    for copy in copies:
        copy.start()
    for copy in copies:
        copy.wait()


def cut(own):
    shapes = [own.shape[:2] + ((last - first) * HD,) for first, last in HALOS]
    return pl.pallas_call(
        cut_kernel,
        in_specs=[HBM],
        out_specs=[VMEM for _ in shapes],
        out_shape=[jax.ShapeDtypeStruct(shape, own.dtype) for shape in shapes],
        scratch_shapes=[pltpu.SemaphoreType.DMA((len(shapes),))],
        compiler_params=params(),
        cost_estimate=cost(CUT_FLOPS),
        name="cut",
    )(pltpu.with_memory_space_constraint(own, pltpu.HBM))


def d_attended_kernel(mask_ref, cot_ref, weight_ref, out_ref, turned_ref, kept_ref):
    tiles = mask_ref.shape[0]
    width = kept_ref.shape[1]
    tile = lax.broadcasted_iota(jnp.int32, (tiles, width), 1) // TILE
    spread = (tile == lax.broadcasted_iota(jnp.int32, (tiles, width), 0)).astype(jnp.float32)
    kept_ref[...] = f32_dot((mask_ref[...] > 0).astype(jnp.float32), spread)
    rows = 4 * TILE
    for row in range(0, width, rows):
        weight = prune(weight_ref[row : row + rows, :], kept_ref, row // TILE, slice(None))
        out_ref[:, row : row + rows] = f32_dot(cot_ref[...], weight, NT).astype(jnp.bfloat16)
    turned_ref[...] = cot_ref[...].T


def d_attended_of(cot, weight, mask):
    tok, width = cot.shape
    return pl.pallas_call(
        d_attended_kernel,
        in_specs=[VMEM, VMEM, VMEM],
        out_specs=[VMEM, VMEM, VMEM],
        out_shape=[
            jax.ShapeDtypeStruct((tok, width), jnp.bfloat16),
            jax.ShapeDtypeStruct((width, tok), jnp.bfloat16),
            jax.ShapeDtypeStruct((mask.shape[0], width), jnp.float32),
        ],
        compiler_params=params(),
        cost_estimate=cost(1),
        name="d_attended",
    )(mask, cot, weight)


def pick_kernel(shard_ref, own_ref, far_ref, after_ref, *out_refs):
    odd = shard_ref[0] % 2 == 1
    split = len(out_refs) == 2

    @pl.when(odd)
    def _():
        for index, ref in enumerate(out_refs):
            ref[...] = far_ref[index] if split else far_ref[...]

    @pl.when(jnp.logical_not(odd))
    def _():
        for index, ref in enumerate(out_refs):
            ref[...] = own_ref[index] if split else own_ref[...]


def pick(shard, own, far, after, split):
    shape = jax.ShapeDtypeStruct(own.shape[1:] if split else own.shape, own.dtype)
    return pl.pallas_call(
        pick_kernel,
        in_specs=[SMEM, VMEM, VMEM, pl.BlockSpec(memory_space=pl.ANY)],
        out_specs=[VMEM] * (2 if split else 1),
        out_shape=[shape] * (2 if split else 1),
        compiler_params=params(),
        cost_estimate=cost(1),
        name="pick",
    )(shard, own, far, after)


def behind_kernel(shard_ref, far_ref, *refs):
    *beside_refs, out_ref = refs
    for index, beside_ref in enumerate(beside_refs):
        far = far_ref[index].astype(jnp.float32)
        both = far + beside_ref[...].astype(jnp.float32)
        out_ref[index] = jnp.where(shard_ref[0] % 2 == 1, both, far).astype(jnp.bfloat16)


def behind_of(shard, far, beside):
    return pl.pallas_call(
        behind_kernel,
        in_specs=[SMEM, VMEM, VMEM, VMEM],
        out_specs=VMEM,
        out_shape=jax.ShapeDtypeStruct(far.shape, far.dtype),
        compiler_params=params(),
        cost_estimate=cost(1),
        name="behind",
    )(shard, far, *beside)


def store_piece(piece, column, turned_ref, whole_ref, sem):
    turned_ref[...] = piece.T
    store = pltpu.make_async_copy(
        turned_ref, whole_ref.at[:, column : column + turned_ref.shape[1]], sem
    )
    store.start()
    return store


def stacked(parts, axis=0):
    return jnp.concatenate(parts, axis=axis)


def blocks_of(own_ref, near_refs, far_ref, index, at):
    near = near_refs[index][:, at] if len(near_refs) == 2 else near_refs[0][index, :, at]
    return stacked([own_ref[index, :, at], near, far_ref[index, :, at]])


def in_grad_group(near_ok, far_ok, q_rows, d_rows, keys, values):
    tok = keys.shape[0] // 3
    scaling = HD ** (-0.5)
    floor = jnp.float32(-1e30)
    key_at = lax.broadcasted_iota(jnp.int32, (tok, tok), 0)
    row_at = lax.broadcasted_iota(jnp.int32, (tok, tok), 1)
    causal = key_at <= row_at
    logits = f32_dot(keys, q_rows, NT)
    d_probs = f32_dot(values, d_rows, NT)
    probs_parts, d_logit_parts = [], []
    zeros = jnp.zeros((tok, tok), jnp.float32)
    for h in range(q_rows.shape[0] // tok):
        at = slice(h * tok, (h + 1) * tok)
        own_l, near_l, far_l = (logits[i * tok : (i + 1) * tok, at] for i in range(3))
        edge = jnp.where(causal, own_l, jnp.where(far_ok, far_l, floor))
        near_l = jnp.where(near_ok, near_l, floor)
        top = jnp.max(jnp.maximum(edge, near_l), axis=0, keepdims=True)
        edge = jnp.exp((edge - top) * scaling)
        near_l = jnp.exp((near_l - top) * scaling)
        inverse = 1.0 / jnp.sum(edge + near_l, axis=0, keepdims=True)
        edge = edge * inverse
        near_l = near_l * inverse
        own_d, near_d, far_d = (d_probs[i * tok : (i + 1) * tok, at] for i in range(3))
        edge_d = jnp.where(causal, own_d, far_d)
        row_dot = jnp.sum(edge * edge_d + near_l * near_d, axis=0, keepdims=True)
        d_edge = edge * (edge_d - row_dot)
        d_near = near_l * (near_d - row_dot)
        probs_parts.append(
            stacked([jnp.where(causal, edge, zeros), near_l, jnp.where(causal, zeros, edge)])
            .astype(jnp.bfloat16)
        )
        d_logit_parts.append(
            stacked([jnp.where(causal, d_edge, zeros), d_near, jnp.where(causal, zeros, d_edge)])
            .astype(jnp.bfloat16)
        )
    probs = stacked(probs_parts, axis=1)
    d_logits = stacked(d_logit_parts, axis=1)
    return f32_dot(keys.T, d_logits) * scaling, probs, d_logits


def in_grad_kernel(low, first, last, group, nears, column, shard_ref, q_ref, d_ref, turned_cot_ref, *refs):
    own_ref, *refs = refs
    near_refs, (far_ref, *refs) = refs[:nears], refs[nears:]
    tok = q_ref.shape[0]
    store = None
    if column is not None:
        piece_ref, *refs, whole_ref, turned_ref, sem = refs
        store = store_piece(piece_ref[...], column, turned_ref, whole_ref, sem)
    grad_ref, probs_ref, d_logits_ref = refs
    shard = shard_ref[0]
    for g in range(first, last):
        at = slice((g - low) * HD, (g - low + 1) * HD)
        columns = [g * group + c for c in range(0, group, HD)]
        d_queries, probs, d_logits = in_grad_group(
            shard >= 1,
            shard >= 2,
            stacked([q_ref[:, c : c + HD] for c in columns]),
            stacked([d_ref[:, c : c + HD] for c in columns]),
            blocks_of(own_ref, near_refs, far_ref, 0, at),
            blocks_of(own_ref, near_refs, far_ref, 1, at),
        )
        probs_ref[g - first] = probs
        d_logits_ref[g - first] = d_logits
        for h, c in enumerate(columns):
            out = slice(c - first * group, c - first * group + HD)
            grad_ref[out, :] = (
                turned_cot_ref[c : c + HD, :].astype(jnp.float32)
                + d_queries[:, h * tok : (h + 1) * tok]
            ).astype(jnp.bfloat16)
    if store is not None:
        store.wait()


def in_grad_of(shard, queries, d_attended, turned_cot, block, low, first, last, group, piece=None):
    tok, width = queries.shape
    count = last - first
    inside = jax.ShapeDtypeStruct((count, 3 * tok, tok * group // HD), jnp.bfloat16)
    out_specs = [VMEM] * 3
    out_shape = [jax.ShapeDtypeStruct((count * group, tok), jnp.bfloat16), inside, inside]
    pieces, column, scratch = [], None, []
    if piece is not None:
        pieces, column = [piece[0]], piece[1]
        out_specs.append(HBM)
        out_shape.append(jax.ShapeDtypeStruct((tok, width), jnp.bfloat16))
        scratch = [pltpu.VMEM(piece[0].shape[::-1], jnp.bfloat16), pltpu.SemaphoreType.DMA]
    own, near, far = block
    return pl.pallas_call(
        functools.partial(in_grad_kernel, low, first, last, group, len(near), column),
        in_specs=[SMEM] + [VMEM] * (5 + len(near) + len(pieces)),
        out_specs=out_specs,
        out_shape=out_shape,
        scratch_shapes=scratch,
        compiler_params=params(),
        cost_estimate=cost(ATT_FLOPS[first]),
        name="in_grad",
    )(shard, queries, d_attended, turned_cot, own, *near, far, *pieces)


def mixed_columns(attended, weight_ref, kept_ref, q_ref, out_ref, first):
    step = 4 * TILE
    for column in range(0, out_ref.shape[1], step):
        at = slice(column, column + step)
        of_all = slice(first + column, first + column + step)
        weight = prune(weight_ref[:, of_all], kept_ref, 0, of_all)
        mixed = f32_dot(attended, weight)
        out_ref[:, at] = (q_ref[:, of_all].astype(jnp.float32) + mixed).astype(jnp.bfloat16)


def layer_out_first_kernel(group, chunks, halos, nears, column, *refs):
    kept_ref, q_ref, weight_ref, piece_ref, given_ref, *refs = refs
    d_ref, *refs = refs
    owns, nears_refs, fars = [], [], []
    for count in nears:
        own_ref, *refs = refs
        near, (far_ref, *refs) = refs[:count], refs[count:]
        owns.append(own_ref)
        nears_refs.append(near)
        fars.append(far_ref)
    probs_refs, refs = refs[: len(chunks)], refs[len(chunks) :]
    d_logits_refs, refs = refs[: len(chunks)], refs[len(chunks) :]
    out_ref, whole_ref, attended_ref, own_grad_ref, *near_grad_refs, far_grad_ref, turned_ref, sem = refs
    tok = q_ref.shape[0]
    scaling = HD ** (-0.5)
    store = store_piece(piece_ref[...], column, turned_ref, whole_ref, sem)
    for i, (first, last) in enumerate(chunks):
        for g in range(first, last):
            halo = [j for j, (low, high) in enumerate(halos) if low <= g < high][0]
            at = slice((g - halos[halo][0]) * HD, (g - halos[halo][0] + 1) * HD)
            at_kv = slice(g * HD, (g + 1) * HD)
            columns = [g * group + c for c in range(0, group, HD)]
            d_rows = stacked([d_ref[:, c : c + HD] for c in columns])
            q_rows = stacked([q_ref[:, c : c + HD] for c in columns])
            values = blocks_of(owns[halo], nears_refs[halo], fars[halo], 1, at)
            probs = probs_refs[i][g - first]
            d_logits = d_logits_refs[i][g - first]
            attended = f32_dot(values.T, probs).astype(jnp.bfloat16)
            for h, c in enumerate(columns):
                attended_ref[:, c : c + HD] = attended[:, h * tok : (h + 1) * tok].T
            d_keys = f32_dot(d_logits, q_rows) * scaling
            d_values = f32_dot(probs, d_rows)
            for index, grad in enumerate((d_keys, d_values)):
                own_grad_ref[index, :, at_kv] = grad[:tok]
                near_grad_refs[index][:, at_kv] = grad[tok : 2 * tok].astype(jnp.bfloat16)
                far_grad_ref[index, :, at_kv] = grad[2 * tok :].astype(jnp.bfloat16)
    mixed_columns(attended_ref[...], weight_ref, kept_ref, q_ref, out_ref, 0)
    store.wait()


def layer_out_first(kept, queries, weight, piece, given, d_attended, blocks, chunks, probs, d_logits, group, last):
    tok, width = queries.shape
    kv_width = sum(own.shape[-1] for own, _, _ in blocks)
    flat = [x for own, near, far in blocks for x in (own, *near, far)]
    operands = [kept, queries, weight, piece[0], given, d_attended, *flat, *probs, *d_logits]
    near_grad = jax.ShapeDtypeStruct((tok, kv_width), jnp.bfloat16)
    own_grad, far_grad = (jax.ShapeDtypeStruct((2, tok, kv_width), t) for t in (jnp.float32, jnp.bfloat16))
    return pl.pallas_call(
        functools.partial(
            layer_out_first_kernel, group, chunks, HALOS, [len(near) for _, near, _ in blocks],
            piece[1],
        ),
        in_specs=[VMEM] * 4 + [HBM] + [VMEM] * (len(operands) - 5),
        out_specs=[VMEM, HBM] + [VMEM] * 5,
        out_shape=[
            jax.ShapeDtypeStruct((tok, last), jnp.bfloat16),
            jax.ShapeDtypeStruct((tok, width), jnp.bfloat16),
            jax.ShapeDtypeStruct((tok, width), jnp.bfloat16),
            own_grad, near_grad, near_grad, far_grad,
        ],
        scratch_shapes=[pltpu.VMEM(piece[0].shape[::-1], jnp.bfloat16), pltpu.SemaphoreType.DMA],
        input_output_aliases={4: 1},
        compiler_params=params(),
        cost_estimate=cost(10**10),
        name="layer_out_first",
    )(*operands)


def layer_out_second_kernel(first, column, *refs):
    kept_ref, q_ref, weight_ref, piece_ref, given_ref, attended_ref, out_ref, whole_ref, turned_ref, sem = refs
    store = store_piece(piece_ref[...], column, turned_ref, whole_ref, sem)
    mixed_columns(attended_ref[...], weight_ref, kept_ref, q_ref, out_ref, first)
    store.wait()


def layer_out_second(kept, queries, weight, piece, given, attended, first):
    tok, width = queries.shape
    return pl.pallas_call(
        functools.partial(layer_out_second_kernel, first, piece[1]),
        in_specs=[VMEM] * 4 + [HBM, VMEM],
        out_specs=[VMEM, HBM],
        out_shape=[
            jax.ShapeDtypeStruct((tok, width - first), jnp.bfloat16),
            jax.ShapeDtypeStruct((tok, width), jnp.bfloat16),
        ],
        scratch_shapes=[pltpu.VMEM(piece[0].shape[::-1], jnp.bfloat16), pltpu.SemaphoreType.DMA],
        input_output_aliases={4: 1},
        compiler_params=params(),
        cost_estimate=cost(10**10),
        name="layer_out_second",
    )(kept, queries, weight, piece[0], given, attended)


def store_first_kernel(shard_ref, piece_ref, own_ref, ahead_ref, *refs):
    *beside_refs, whole_ref, kv_ref, sum_ref, sems = refs
    store = pltpu.make_async_copy(piece_ref, whole_ref.at[:, : piece_ref.shape[1]], sems.at[0])
    store.start()
    for index, beside_ref in enumerate(beside_refs):
        total = own_ref[index] + ahead_ref[index].astype(jnp.float32)
        both = total + beside_ref[...].astype(jnp.float32)
        sum_ref[index] = jnp.where(shard_ref[0] % 2 == 0, both, total)
    kv_store = pltpu.make_async_copy(sum_ref, kv_ref, sems.at[1])
    kv_store.start()
    store.wait()
    kv_store.wait()


def store_first(shard, piece, own, ahead, beside, width):
    return pl.pallas_call(
        store_first_kernel,
        in_specs=[SMEM] + [VMEM] * 5,
        out_specs=[HBM, HBM],
        out_shape=[
            jax.ShapeDtypeStruct((piece.shape[0], width), piece.dtype),
            jax.ShapeDtypeStruct(own.shape, own.dtype),
        ],
        scratch_shapes=[pltpu.VMEM(own.shape, own.dtype), pltpu.SemaphoreType.DMA((2,))],
        compiler_params=params(),
        name="store_first",
    )(shard, piece, own, ahead, *beside)


def store_last_kernel(piece_ref, given_ref, kept_ref, whole_ref, same_ref, sem):
    column = whole_ref.shape[1] - piece_ref.shape[1]
    store = pltpu.make_async_copy(piece_ref, whole_ref.at[:, column:], sem)
    store.start()
    store.wait()


def store_last(piece, whole, kept):
    return pl.pallas_call(
        store_last_kernel,
        in_specs=[VMEM, HBM, HBM],
        out_specs=[HBM, HBM],
        out_shape=[
            jax.ShapeDtypeStruct(whole.shape, whole.dtype),
            jax.ShapeDtypeStruct(kept.shape, kept.dtype),
        ],
        scratch_shapes=[pltpu.SemaphoreType.DMA],
        input_output_aliases={1: 0, 2: 1},
        compiler_params=params(),
        name="store_last",
    )(piece, whole, kept)


def core_swap(value, axis):
    return lax.ppermute(value, axis, [(i, i ^ 1) for i in range(lax.axis_size(axis))])


def per_device(stream_in, keys_values, out_weight, tile_mask, cotangent):
    queries, own, mask, cot = stream_in[0], keys_values[0], tile_mask[0], cotangent[0]
    weight = pltpu.with_memory_space_constraint(out_weight[0], pltpu.VMEM)
    width = queries.shape[1]
    group = width // (own.shape[-1] // HD)
    shard = lax.axis_index("seq").astype(jnp.int32).reshape(1)
    owns = cut(own)
    fars = [around(piece, "seq", 2) for piece in owns]
    d_attended, turned_cot, kept = d_attended_of(cot, weight, mask)
    pieces, probs, d_logits, blocks = [], [], [], []
    after = d_attended
    for first, last in CHUNKS:
        halo = [i for i, (low, high) in enumerate(HALOS) if low <= first < high][0]
        if halo == len(blocks):
            near = [core_swap(x, "seq") for x in pick(shard, owns[halo], fars[halo], after, halo > 0)]
            blocks.append((owns[halo], near, fars[halo]))
        late = first == CHUNKS[-1][0]
        grad, p, d, *stored = in_grad_of(
            shard, queries, d_attended, turned_cot, blocks[halo], HALOS[halo][0], first, last, group,
            pieces[0] if late else None,
        )
        probs.append(p)
        d_logits.append(d)
        pieces.append((around(grad, "section", -1), first * group))
        after = grad
    out_cut = OUT_CUT * 4 * TILE
    result, prev_grad, attended, own_grad, *near_grad, far_grad = layer_out_first(
        kept, queries, weight, pieces[1], stored[0], d_attended, blocks, CHUNKS, probs,
        d_logits, group, out_cut,
    )
    early = around(result, "section", 1)
    beside = [core_swap(x, "seq") for x in near_grad]
    ahead = around(behind_of(shard, far_grad, beside), "seq", -2)
    result, prev_grad = layer_out_second(kept, queries, weight, pieces[2], prev_grad, attended, out_cut)
    late = around(result, "section", 1)
    next_input, kv_total = store_first(shard, early, own_grad, ahead, beside, width)
    next_input, kv_total = store_last(late, next_input, kv_total)
    return (next_input[None], prev_grad[None], kv_total[None])


def solution(mesh):
    return jax.shard_map(
        per_device,
        mesh=mesh,
        in_specs=(
            P("section", "seq", None),
            P("section", None, "seq", None),
            P("section", None, None),
            P("section", None, None),
            P("section", "seq", None),
        ),
        out_specs=(
            P("section", "seq", None),
            P("section", "seq", None),
            P("section", None, "seq", None),
        ),
        check_vma=False,
    )
```

```python
import functools

import jax
import jax.numpy as jnp
from jax import lax
from jax.experimental import pallas as pl
from jax.experimental.pallas import tpu as pltpu
from jax.sharding import PartitionSpec as P

HD = 128
TILE = 128
HALOS = ((0, 1), (1, 4))
CHUNKS = ((0, 1), (1, 2), (2, 4))
OUT_CUT = 3
CUT_FLOPS = 10**10
ATT_FLOPS = {0: 10**9, 1: 1, 2: 10**10}
VMEM = pl.BlockSpec(memory_space=pltpu.VMEM)
HBM = pl.BlockSpec(memory_space=pltpu.HBM)
SMEM = pl.BlockSpec(memory_space=pltpu.SMEM)
VMEM_LIMIT = 32 * 1024 * 1024
NT = (((1,), (1,)), ((), ()))


def around(value, axis, by):
    length = lax.axis_size(axis)
    return lax.ppermute(value, axis, [(i, (i + by) % length) for i in range(length)])


def f32_dot(a, b, dims=(((1,), (0,)), ((), ()))):
    return lax.dot_general(a, b, dims, preferred_element_type=jnp.float32)


def params():
    return pltpu.CompilerParams(vmem_limit_bytes=VMEM_LIMIT)


def cost(flops):
    return pl.CostEstimate(flops=flops, bytes_accessed=1, transcendentals=0)


def prune(weight, kept_ref, row_tile, columns):
    strips = []
    for a in range(weight.shape[0] // TILE):
        row = kept_ref[row_tile + a : row_tile + a + 1, columns]
        kept = jnp.broadcast_to(row, (16, row.shape[1])).astype(weight.dtype)
        strip = weight[a * TILE : (a + 1) * TILE, :]
        strips.append(strip * jnp.concatenate([kept] * (TILE // 16), axis=0))
    return jnp.concatenate(strips, axis=0)


def cut_kernel(own_hbm, *refs):
    *piece_refs, sems = refs
    copies, column = [], 0
    for i, ref in enumerate(piece_refs):
        width = ref.shape[-1]
        source = own_hbm.at[:, :, column : column + width]
        copies.append(pltpu.make_async_copy(source, ref, sems.at[i]))
        column += width
    for copy in copies:
        copy.start()
    for copy in copies:
        copy.wait()


def cut(own):
    shapes = [own.shape[:2] + ((last - first) * HD,) for first, last in HALOS]
    return pl.pallas_call(
        cut_kernel,
        in_specs=[HBM],
        out_specs=[VMEM for _ in shapes],
        out_shape=[jax.ShapeDtypeStruct(shape, own.dtype) for shape in shapes],
        scratch_shapes=[pltpu.SemaphoreType.DMA((len(shapes),))],
        compiler_params=params(),
        cost_estimate=cost(CUT_FLOPS),
        name="cut",
    )(pltpu.with_memory_space_constraint(own, pltpu.HBM))


def d_attended_kernel(mask_ref, cot_ref, weight_ref, out_ref, turned_ref, kept_ref):
    tiles = mask_ref.shape[0]
    width = kept_ref.shape[1]
    tile = lax.broadcasted_iota(jnp.int32, (tiles, width), 1) // TILE
    spread = (tile == lax.broadcasted_iota(jnp.int32, (tiles, width), 0)).astype(jnp.float32)
    kept_ref[...] = f32_dot((mask_ref[...] > 0).astype(jnp.float32), spread)
    rows = 4 * TILE
    for row in range(0, width, rows):
        weight = prune(weight_ref[row : row + rows, :], kept_ref, row // TILE, slice(None))
        out_ref[:, row : row + rows] = f32_dot(cot_ref[...], weight, NT).astype(jnp.bfloat16)
    turned_ref[...] = cot_ref[...].T


def d_attended_of(cot, weight, mask):
    tok, width = cot.shape
    return pl.pallas_call(
        d_attended_kernel,
        in_specs=[VMEM, VMEM, VMEM],
        out_specs=[VMEM, VMEM, VMEM],
        out_shape=[
            jax.ShapeDtypeStruct((tok, width), jnp.bfloat16),
            jax.ShapeDtypeStruct((width, tok), jnp.bfloat16),
            jax.ShapeDtypeStruct((mask.shape[0], width), jnp.float32),
        ],
        compiler_params=params(),
        cost_estimate=cost(1),
        name="d_attended",
    )(mask, cot, weight)


def pick_kernel(shard_ref, own_ref, far_ref, after_ref, *out_refs):
    odd = shard_ref[0] % 2 == 1
    split = len(out_refs) == 2

    @pl.when(odd)
    def _():
        for index, ref in enumerate(out_refs):
            ref[...] = far_ref[index] if split else far_ref[...]

    @pl.when(jnp.logical_not(odd))
    def _():
        for index, ref in enumerate(out_refs):
            ref[...] = own_ref[index] if split else own_ref[...]


def pick(shard, own, far, after, split):
    shape = jax.ShapeDtypeStruct(own.shape[1:] if split else own.shape, own.dtype)
    return pl.pallas_call(
        pick_kernel,
        in_specs=[SMEM, VMEM, VMEM, pl.BlockSpec(memory_space=pl.ANY)],
        out_specs=[VMEM] * (2 if split else 1),
        out_shape=[shape] * (2 if split else 1),
        compiler_params=params(),
        cost_estimate=cost(1),
        name="pick",
    )(shard, own, far, after)


def behind_kernel(shard_ref, far_ref, *refs):
    *beside_refs, out_ref = refs
    for index, beside_ref in enumerate(beside_refs):
        far = far_ref[index].astype(jnp.float32)
        both = far + beside_ref[...].astype(jnp.float32)
        out_ref[index] = jnp.where(shard_ref[0] % 2 == 1, both, far).astype(jnp.bfloat16)


def behind_of(shard, far, beside):
    return pl.pallas_call(
        behind_kernel,
        in_specs=[SMEM, VMEM, VMEM, VMEM],
        out_specs=VMEM,
        out_shape=jax.ShapeDtypeStruct(far.shape, far.dtype),
        compiler_params=params(),
        cost_estimate=cost(1),
        name="behind",
    )(shard, far, *beside)


def store_piece(piece, column, turned_ref, whole_ref, sem):
    turned_ref[...] = piece.T
    store = pltpu.make_async_copy(
        turned_ref, whole_ref.at[:, column : column + turned_ref.shape[1]], sem
    )
    store.start()
    return store


def stacked(parts, axis=0):
    return jnp.concatenate(parts, axis=axis)


def blocks_of(own_ref, near_refs, far_ref, index, at):
    near = near_refs[index][:, at] if len(near_refs) == 2 else near_refs[0][index, :, at]
    return stacked([own_ref[index, :, at], near, far_ref[index, :, at]])


def in_grad_group(near_ok, far_ok, q_rows, d_rows, keys, values):
    tok = keys.shape[0] // 3
    scaling = HD ** (-0.5)
    floor = jnp.float32(-1e30)
    key_at = lax.broadcasted_iota(jnp.int32, (tok, tok), 0)
    row_at = lax.broadcasted_iota(jnp.int32, (tok, tok), 1)
    causal = key_at <= row_at
    logits = f32_dot(keys, q_rows, NT)
    d_probs = f32_dot(values, d_rows, NT)
    probs_parts, d_logit_parts = [], []
    zeros = jnp.zeros((tok, tok), jnp.float32)
    for h in range(q_rows.shape[0] // tok):
        at = slice(h * tok, (h + 1) * tok)
        own_l, near_l, far_l = (logits[i * tok : (i + 1) * tok, at] for i in range(3))
        edge = jnp.where(causal, own_l, jnp.where(far_ok, far_l, floor))
        near_l = jnp.where(near_ok, near_l, floor)
        top = jnp.max(jnp.maximum(edge, near_l), axis=0, keepdims=True)
        edge = jnp.exp((edge - top) * scaling)
        near_l = jnp.exp((near_l - top) * scaling)
        inverse = 1.0 / jnp.sum(edge + near_l, axis=0, keepdims=True)
        edge = edge * inverse
        near_l = near_l * inverse
        own_d, near_d, far_d = (d_probs[i * tok : (i + 1) * tok, at] for i in range(3))
        edge_d = jnp.where(causal, own_d, far_d)
        row_dot = jnp.sum(edge * edge_d + near_l * near_d, axis=0, keepdims=True)
        d_edge = edge * (edge_d - row_dot)
        d_near = near_l * (near_d - row_dot)
        probs_parts.append(
            stacked([jnp.where(causal, edge, zeros), near_l, jnp.where(causal, zeros, edge)])
            .astype(jnp.bfloat16)
        )
        d_logit_parts.append(
            stacked([jnp.where(causal, d_edge, zeros), d_near, jnp.where(causal, zeros, d_edge)])
            .astype(jnp.bfloat16)
        )
    probs = stacked(probs_parts, axis=1)
    d_logits = stacked(d_logit_parts, axis=1)
    return f32_dot(keys.T, d_logits) * scaling, probs, d_logits


def in_grad_kernel(low, first, last, group, nears, column, shard_ref, q_ref, d_ref, turned_cot_ref, *refs):
    own_ref, *refs = refs
    near_refs, (far_ref, *refs) = refs[:nears], refs[nears:]
    tok = q_ref.shape[0]
    store = None
    if column is not None:
        piece_ref, *refs, whole_ref, turned_ref, sem = refs
        store = store_piece(piece_ref[shard_ref[1]], column, turned_ref, whole_ref, sem)
    grad_ref, probs_ref, d_logits_ref = refs
    shard = shard_ref[0]
    for g in range(first, last):
        at = slice((g - low) * HD, (g - low + 1) * HD)
        columns = [g * group + c for c in range(0, group, HD)]
        d_queries, probs, d_logits = in_grad_group(
            shard >= 1,
            shard >= 2,
            stacked([q_ref[:, c : c + HD] for c in columns]),
            stacked([d_ref[:, c : c + HD] for c in columns]),
            blocks_of(own_ref, near_refs, far_ref, 0, at),
            blocks_of(own_ref, near_refs, far_ref, 1, at),
        )
        probs_ref[g - first] = probs
        d_logits_ref[g - first] = d_logits
        for h, c in enumerate(columns):
            out = slice(c - first * group, c - first * group + HD)
            grad_ref[out, :] = (
                turned_cot_ref[c : c + HD, :].astype(jnp.float32)
                + d_queries[:, h * tok : (h + 1) * tok]
            ).astype(jnp.bfloat16)
    if store is not None:
        store.wait()


def in_grad_of(shard, queries, d_attended, turned_cot, block, low, first, last, group, piece=None):
    tok, width = queries.shape
    count = last - first
    inside = jax.ShapeDtypeStruct((count, 3 * tok, tok * group // HD), jnp.bfloat16)
    out_specs = [VMEM] * 3
    out_shape = [jax.ShapeDtypeStruct((count * group, tok), jnp.bfloat16), inside, inside]
    pieces, column, scratch = [], None, []
    if piece is not None:
        pieces, column = [piece[0]], piece[1]
        out_specs.append(HBM)
        out_shape.append(jax.ShapeDtypeStruct((tok, width), jnp.bfloat16))
        scratch = [pltpu.VMEM(piece[0].shape[:0:-1], jnp.bfloat16), pltpu.SemaphoreType.DMA]
    own, near, far = block
    return pl.pallas_call(
        functools.partial(in_grad_kernel, low, first, last, group, len(near), column),
        in_specs=[SMEM] + [VMEM] * (5 + len(near) + len(pieces)),
        out_specs=out_specs,
        out_shape=out_shape,
        scratch_shapes=scratch,
        compiler_params=params(),
        cost_estimate=cost(ATT_FLOPS[first]),
        name="in_grad",
    )(shard, queries, d_attended, turned_cot, own, *near, far, *pieces)


def mixed_columns(attended, weight_ref, kept_ref, q_ref, out_ref, first):
    step = 4 * TILE
    for column in range(0, out_ref.shape[1], step):
        at = slice(column, column + step)
        of_all = slice(first + column, first + column + step)
        weight = prune(weight_ref[:, of_all], kept_ref, 0, of_all)
        mixed = f32_dot(attended, weight)
        out_ref[:, at] = (q_ref[:, of_all].astype(jnp.float32) + mixed).astype(jnp.bfloat16)


def layer_out_first_kernel(group, chunks, halos, nears, column, *refs):
    shard_ref, kept_ref, q_ref, weight_ref, piece_ref, given_ref, *refs = refs
    d_ref, *refs = refs
    owns, nears_refs, fars = [], [], []
    for count in nears:
        own_ref, *refs = refs
        near, (far_ref, *refs) = refs[:count], refs[count:]
        owns.append(own_ref)
        nears_refs.append(near)
        fars.append(far_ref)
    probs_refs, refs = refs[: len(chunks)], refs[len(chunks) :]
    d_logits_refs, refs = refs[: len(chunks)], refs[len(chunks) :]
    out_ref, whole_ref, attended_ref, own_grad_ref, *near_grad_refs, far_grad_ref, turned_ref, sem = refs
    tok = q_ref.shape[0]
    scaling = HD ** (-0.5)
    store = store_piece(piece_ref[shard_ref[1]], column, turned_ref, whole_ref, sem)
    for i, (first, last) in enumerate(chunks):
        for g in range(first, last):
            halo = [j for j, (low, high) in enumerate(halos) if low <= g < high][0]
            at = slice((g - halos[halo][0]) * HD, (g - halos[halo][0] + 1) * HD)
            at_kv = slice(g * HD, (g + 1) * HD)
            columns = [g * group + c for c in range(0, group, HD)]
            d_rows = stacked([d_ref[:, c : c + HD] for c in columns])
            q_rows = stacked([q_ref[:, c : c + HD] for c in columns])
            values = blocks_of(owns[halo], nears_refs[halo], fars[halo], 1, at)
            probs = probs_refs[i][g - first]
            d_logits = d_logits_refs[i][g - first]
            attended = f32_dot(values.T, probs).astype(jnp.bfloat16)
            for h, c in enumerate(columns):
                attended_ref[:, c : c + HD] = attended[:, h * tok : (h + 1) * tok].T
            d_keys = f32_dot(d_logits, q_rows) * scaling
            d_values = f32_dot(probs, d_rows)
            for index, grad in enumerate((d_keys, d_values)):
                own_grad_ref[index, :, at_kv] = grad[:tok]
                near_grad_refs[index][:, at_kv] = grad[tok : 2 * tok].astype(jnp.bfloat16)
                far_grad_ref[index, :, at_kv] = grad[2 * tok :].astype(jnp.bfloat16)
    mixed_columns(attended_ref[...], weight_ref, kept_ref, q_ref, out_ref, 0)
    store.wait()


def layer_out_first(shard, kept, queries, weight, piece, given, d_attended, blocks, chunks, probs, d_logits, group, last):
    tok, width = queries.shape
    kv_width = sum(own.shape[-1] for own, _, _ in blocks)
    flat = [x for own, near, far in blocks for x in (own, *near, far)]
    operands = [shard, kept, queries, weight, piece[0], given, d_attended, *flat, *probs, *d_logits]
    near_grad = jax.ShapeDtypeStruct((tok, kv_width), jnp.bfloat16)
    own_grad, far_grad = (jax.ShapeDtypeStruct((2, tok, kv_width), t) for t in (jnp.float32, jnp.bfloat16))
    return pl.pallas_call(
        functools.partial(
            layer_out_first_kernel, group, chunks, HALOS, [len(near) for _, near, _ in blocks],
            piece[1],
        ),
        in_specs=[SMEM] + [VMEM] * 4 + [HBM] + [VMEM] * (len(operands) - 6),
        out_specs=[VMEM, HBM] + [VMEM] * 5,
        out_shape=[
            jax.ShapeDtypeStruct((tok, last), jnp.bfloat16),
            jax.ShapeDtypeStruct((tok, width), jnp.bfloat16),
            jax.ShapeDtypeStruct((tok, width), jnp.bfloat16),
            own_grad, near_grad, near_grad, far_grad,
        ],
        scratch_shapes=[pltpu.VMEM(piece[0].shape[:0:-1], jnp.bfloat16), pltpu.SemaphoreType.DMA],
        input_output_aliases={5: 1},
        compiler_params=params(),
        cost_estimate=cost(10**10),
        name="layer_out_first",
    )(*operands)


def layer_out_second_kernel(first, column, *refs):
    shard_ref, kept_ref, q_ref, weight_ref, piece_ref, given_ref, attended_ref, out_ref, whole_ref, turned_ref, sem = refs
    store = store_piece(piece_ref[shard_ref[1]], column, turned_ref, whole_ref, sem)
    mixed_columns(attended_ref[...], weight_ref, kept_ref, q_ref, out_ref, first)
    store.wait()


def layer_out_second(shard, kept, queries, weight, piece, given, attended, first):
    tok, width = queries.shape
    return pl.pallas_call(
        functools.partial(layer_out_second_kernel, first, piece[1]),
        in_specs=[SMEM] + [VMEM] * 4 + [HBM, VMEM],
        out_specs=[VMEM, HBM],
        out_shape=[
            jax.ShapeDtypeStruct((tok, width - first), jnp.bfloat16),
            jax.ShapeDtypeStruct((tok, width), jnp.bfloat16),
        ],
        scratch_shapes=[pltpu.VMEM(piece[0].shape[:0:-1], jnp.bfloat16), pltpu.SemaphoreType.DMA],
        input_output_aliases={5: 1},
        compiler_params=params(),
        cost_estimate=cost(10**10),
        name="layer_out_second",
    )(shard, kept, queries, weight, piece[0], given, attended)


def store_first_kernel(shard_ref, piece_ref, own_ref, ahead_ref, *refs):
    *beside_refs, whole_ref, kv_ref, sum_ref, sems = refs
    store = pltpu.make_async_copy(
        piece_ref.at[shard_ref[2]], whole_ref.at[:, : piece_ref.shape[2]], sems.at[0]
    )
    store.start()
    for index, beside_ref in enumerate(beside_refs):
        total = own_ref[index] + ahead_ref[index].astype(jnp.float32)
        both = total + beside_ref[...].astype(jnp.float32)
        sum_ref[index] = jnp.where(shard_ref[0] % 2 == 0, both, total)
    kv_store = pltpu.make_async_copy(sum_ref, kv_ref, sems.at[1])
    kv_store.start()
    store.wait()
    kv_store.wait()


def store_first(shard, piece, own, ahead, beside, width):
    return pl.pallas_call(
        store_first_kernel,
        in_specs=[SMEM] + [VMEM] * 5,
        out_specs=[HBM, HBM],
        out_shape=[
            jax.ShapeDtypeStruct((piece.shape[1], width), piece.dtype),
            jax.ShapeDtypeStruct(own.shape, own.dtype),
        ],
        scratch_shapes=[pltpu.VMEM(own.shape, own.dtype), pltpu.SemaphoreType.DMA((2,))],
        compiler_params=params(),
        name="store_first",
    )(shard, piece, own, ahead, *beside)


def store_last_kernel(shard_ref, piece_ref, given_ref, kept_ref, whole_ref, same_ref, sem):
    column = whole_ref.shape[1] - piece_ref.shape[2]
    store = pltpu.make_async_copy(piece_ref.at[shard_ref[2]], whole_ref.at[:, column:], sem)
    store.start()
    store.wait()


def store_last(shard, piece, whole, kept):
    return pl.pallas_call(
        store_last_kernel,
        in_specs=[SMEM, VMEM, HBM, HBM],
        out_specs=[HBM, HBM],
        out_shape=[
            jax.ShapeDtypeStruct(whole.shape, whole.dtype),
            jax.ShapeDtypeStruct(kept.shape, kept.dtype),
        ],
        scratch_shapes=[pltpu.SemaphoreType.DMA],
        input_output_aliases={2: 0, 3: 1},
        compiler_params=params(),
        name="store_last",
    )(shard, piece, whole, kept)


def core_swap(value, axis):
    return lax.ppermute(value, axis, [(i, i ^ 1) for i in range(lax.axis_size(axis))])


def per_device(stream_in, keys_values, out_weight, tile_mask, cotangent):
    queries, own, mask, cot = stream_in[0], keys_values[0], tile_mask[0], cotangent[0]
    weight = pltpu.with_memory_space_constraint(out_weight[0], pltpu.VMEM)
    width = queries.shape[1]
    group = width // (own.shape[-1] // HD)
    sections = lax.axis_size("section")
    section = lax.axis_index("section")
    shard = jnp.stack(
        [lax.axis_index("seq"), (section + 1) % sections, (section + sections - 1) % sections]
    ).astype(jnp.int32)
    owns = cut(own)
    fars = [around(piece, "seq", 2) for piece in owns]
    d_attended, turned_cot, kept = d_attended_of(cot, weight, mask)
    pieces, probs, d_logits, blocks = [], [], [], []
    after = d_attended
    for first, last in CHUNKS:
        halo = [i for i, (low, high) in enumerate(HALOS) if low <= first < high][0]
        if halo == len(blocks):
            near = [core_swap(x, "seq") for x in pick(shard, owns[halo], fars[halo], after, halo > 0)]
            blocks.append((owns[halo], near, fars[halo]))
        late = first == CHUNKS[-1][0]
        grad, p, d, *stored = in_grad_of(
            shard, queries, d_attended, turned_cot, blocks[halo], HALOS[halo][0], first, last, group,
            pieces[0] if late else None,
        )
        probs.append(p)
        d_logits.append(d)
        pieces.append((lax.all_gather(grad, "section"), first * group))
        after = grad
    out_cut = OUT_CUT * 4 * TILE
    result, prev_grad, attended, own_grad, *near_grad, far_grad = layer_out_first(
        shard, kept, queries, weight, pieces[1], stored[0], d_attended, blocks, CHUNKS, probs,
        d_logits, group, out_cut,
    )
    early = lax.all_gather(result, "section")
    beside = [core_swap(x, "seq") for x in near_grad]
    ahead = around(behind_of(shard, far_grad, beside), "seq", -2)
    result, prev_grad = layer_out_second(shard, kept, queries, weight, pieces[2], prev_grad, attended, out_cut)
    late = lax.all_gather(result, "section")
    next_input, kv_total = store_first(shard, early, own_grad, ahead, beside, width)
    next_input, kv_total = store_last(shard, late, next_input, kv_total)
    return (next_input[None], prev_grad[None], kv_total[None])


def solution(mesh):
    return jax.shard_map(
        per_device,
        mesh=mesh,
        in_specs=(
            P("section", "seq", None),
            P("section", None, "seq", None),
            P("section", None, None),
            P("section", None, None),
            P("section", "seq", None),
        ),
        out_specs=(
            P("section", "seq", None),
            P("section", "seq", None),
            P("section", None, "seq", None),
        ),
        check_vma=False,
    )
```

```python
import functools
import math

import jax
import jax.numpy as jnp
from jax import lax
from jax.experimental import pallas as pl
from jax.experimental.pallas import tpu as pltpu
from jax.sharding import PartitionSpec as P

HD = 128
TILE = 128
HALOS = ((0, 1), (1, 4))
CHUNKS = ((0, 1), (1, 2), (2, 4))
OUT_CUT = 3
CUT_FLOPS = 10**10
ATT_FLOPS = {0: 10**9, 1: 1, 2: 10**10}
VMEM = pl.BlockSpec(memory_space=pltpu.VMEM)
HBM = pl.BlockSpec(memory_space=pltpu.HBM)
SMEM = pl.BlockSpec(memory_space=pltpu.SMEM)
VMEM_LIMIT = 32 * 1024 * 1024
NT = (((1,), (1,)), ((), ()))


def around(value, axis, by):
    length = lax.axis_size(axis)
    return lax.ppermute(value, axis, [(i, (i + by) % length) for i in range(length)])


def f32_dot(a, b, dims=(((1,), (0,)), ((), ()))):
    return lax.dot_general(a, b, dims, preferred_element_type=jnp.float32)


def params():
    return pltpu.CompilerParams(vmem_limit_bytes=VMEM_LIMIT)


def cost(flops):
    return pl.CostEstimate(flops=flops, bytes_accessed=1, transcendentals=0)


def prune(weight, kept_ref, row_tile, columns):
    strips = []
    for a in range(weight.shape[0] // TILE):
        row = kept_ref[row_tile + a : row_tile + a + 1, columns]
        kept = jnp.broadcast_to(row, (16, row.shape[1])).astype(weight.dtype)
        strip = weight[a * TILE : (a + 1) * TILE, :]
        strips.append(strip * jnp.concatenate([kept] * (TILE // 16), axis=0))
    return jnp.concatenate(strips, axis=0)


def cut_kernel(own_hbm, *refs):
    *piece_refs, sems = refs
    copies, column = [], 0
    for i, ref in enumerate(piece_refs):
        width = ref.shape[-1]
        source = own_hbm.at[:, :, column : column + width]
        copies.append(pltpu.make_async_copy(source, ref, sems.at[i]))
        column += width
    for copy in copies:
        copy.start()
    for copy in copies:
        copy.wait()


def cut(own):
    shapes = [own.shape[:2] + ((last - first) * HD,) for first, last in HALOS]
    return pl.pallas_call(
        cut_kernel,
        in_specs=[HBM],
        out_specs=[VMEM for _ in shapes],
        out_shape=[jax.ShapeDtypeStruct(shape, own.dtype) for shape in shapes],
        scratch_shapes=[pltpu.SemaphoreType.DMA((len(shapes),))],
        compiler_params=params(),
        cost_estimate=cost(CUT_FLOPS),
        name="cut",
    )(pltpu.with_memory_space_constraint(own, pltpu.HBM))


def d_attended_kernel(mask_ref, cot_ref, weight_ref, out_ref, turned_ref, kept_ref):
    tiles = mask_ref.shape[0]
    width = kept_ref.shape[1]
    tile = lax.broadcasted_iota(jnp.int32, (tiles, width), 1) // TILE
    spread = (tile == lax.broadcasted_iota(jnp.int32, (tiles, width), 0)).astype(jnp.float32)
    kept_ref[...] = f32_dot((mask_ref[...] > 0).astype(jnp.float32), spread)
    rows = 4 * TILE
    for row in range(0, width, rows):
        weight = prune(weight_ref[row : row + rows, :], kept_ref, row // TILE, slice(None))
        out_ref[:, row : row + rows] = f32_dot(cot_ref[...], weight, NT).astype(jnp.bfloat16)
    turned_ref[...] = cot_ref[...].T


def d_attended_of(cot, weight, mask):
    tok, width = cot.shape
    return pl.pallas_call(
        d_attended_kernel,
        in_specs=[VMEM, VMEM, VMEM],
        out_specs=[VMEM, VMEM, VMEM],
        out_shape=[
            jax.ShapeDtypeStruct((tok, width), jnp.bfloat16),
            jax.ShapeDtypeStruct((width, tok), jnp.bfloat16),
            jax.ShapeDtypeStruct((mask.shape[0], width), jnp.float32),
        ],
        compiler_params=params(),
        cost_estimate=cost(1),
        name="d_attended",
    )(mask, cot, weight)


def pick_kernel(shard_ref, own_ref, far_ref, after_ref, *out_refs):
    odd = shard_ref[0] % 2 == 1
    split = len(out_refs) == 2

    @pl.when(odd)
    def _():
        for index, ref in enumerate(out_refs):
            ref[...] = far_ref[index] if split else far_ref[...]

    @pl.when(jnp.logical_not(odd))
    def _():
        for index, ref in enumerate(out_refs):
            ref[...] = own_ref[index] if split else own_ref[...]


def pick(shard, own, far, after, split):
    shape = jax.ShapeDtypeStruct(own.shape[1:] if split else own.shape, own.dtype)
    return pl.pallas_call(
        pick_kernel,
        in_specs=[SMEM, VMEM, VMEM, pl.BlockSpec(memory_space=pl.ANY)],
        out_specs=[VMEM] * (2 if split else 1),
        out_shape=[shape] * (2 if split else 1),
        compiler_params=params(),
        cost_estimate=cost(1),
        name="pick",
    )(shard, own, far, after)


def behind_kernel(shard_ref, far_ref, *refs):
    *beside_refs, out_ref = refs
    for index, beside_ref in enumerate(beside_refs):
        far = far_ref[index].astype(jnp.float32)
        both = far + beside_ref[...].astype(jnp.float32)
        out_ref[index] = jnp.where(shard_ref[0] % 2 == 1, both, far).astype(jnp.bfloat16)


def behind_of(shard, far, beside):
    return pl.pallas_call(
        behind_kernel,
        in_specs=[SMEM, VMEM, VMEM, VMEM],
        out_specs=VMEM,
        out_shape=jax.ShapeDtypeStruct(far.shape, far.dtype),
        compiler_params=params(),
        cost_estimate=cost(1),
        name="behind",
    )(shard, far, *beside)


def store_piece(piece, column, turned_ref, whole_ref, sem):
    turned_ref[...] = piece.T
    store = pltpu.make_async_copy(
        turned_ref, whole_ref.at[:, column : column + turned_ref.shape[1]], sem
    )
    store.start()
    return store


def stacked(parts, axis=0):
    return jnp.concatenate(parts, axis=axis)


def blocks_of(own_ref, near_refs, far_ref, index, at):
    near = near_refs[index][:, at] if len(near_refs) == 2 else near_refs[0][index, :, at]
    return [own_ref[index, :, at], near, far_ref[index, :, at]]


def in_grad_group(near_ok, far_ok, q_rows, d_rows, keys, values):
    own_k, near_k, far_k = keys
    tok = own_k.shape[0]
    scaling = HD ** (-0.5)
    factor = scaling * math.log2(math.e)
    floor = jnp.float32(-1e30)
    key_at = lax.broadcasted_iota(jnp.int32, (tok, tok), 0)
    row_at = lax.broadcasted_iota(jnp.int32, (tok, tok), 1)
    causal = key_at <= row_at
    lower = causal.astype(jnp.float32).astype(jnp.bfloat16)
    upper = (1.0 - causal.astype(jnp.float32)).astype(jnp.bfloat16)
    own_l, near_l, far_l = (f32_dot(k, q_rows, NT) for k in keys)
    own_d, near_d, far_d = (f32_dot(v, d_rows, NT) for v in values)
    parts = []
    for h in range(q_rows.shape[0] // tok):
        at = slice(h * tok, (h + 1) * tok)
        edge = jnp.where(causal, own_l[:, at], jnp.where(far_ok, far_l[:, at], floor))
        near = jnp.where(near_ok, near_l[:, at], floor)
        top = jnp.max(jnp.maximum(edge, near), axis=0, keepdims=True)
        edge = jnp.exp2((edge - top) * factor)
        near = jnp.exp2((near - top) * factor)
        inverse = 1.0 / jnp.sum(edge + near, axis=0, keepdims=True)
        edge = edge * inverse
        near = near * inverse
        edge_d = jnp.where(causal, own_d[:, at], far_d[:, at])
        row_dot = jnp.sum(edge * edge_d + near * near_d[:, at], axis=0, keepdims=True)
        d_edge = (edge * (edge_d - row_dot)).astype(jnp.bfloat16)
        d_near = (near * (near_d[:, at] - row_dot)).astype(jnp.bfloat16)
        edge = edge.astype(jnp.bfloat16)
        parts.append(
            (
                stacked([edge * lower, near.astype(jnp.bfloat16), edge * upper]),
                stacked([d_edge * lower, d_near, d_edge * upper]),
            )
        )
    probs = stacked([p for p, _ in parts], axis=1)
    d_logits = stacked([d for _, d in parts], axis=1)
    turned = stacked([k.T for k in keys], axis=1)
    return f32_dot(turned, d_logits) * scaling, probs, d_logits


def in_grad_kernel(low, first, last, group, nears, column, shard_ref, q_ref, d_ref, turned_cot_ref, *refs):
    own_ref, *refs = refs
    near_refs, (far_ref, *refs) = refs[:nears], refs[nears:]
    tok = q_ref.shape[0]
    store = None
    if column is not None:
        piece_ref, *refs, whole_ref, turned_ref, sem = refs
        store = store_piece(piece_ref[...], column, turned_ref, whole_ref, sem)
    grad_ref, probs_ref, d_logits_ref = refs
    shard = shard_ref[0]
    for g in range(first, last):
        at = slice((g - low) * HD, (g - low + 1) * HD)
        columns = [g * group + c for c in range(0, group, HD)]
        d_queries, probs, d_logits = in_grad_group(
            shard >= 1,
            shard >= 2,
            stacked([q_ref[:, c : c + HD] for c in columns]),
            stacked([d_ref[:, c : c + HD] for c in columns]),
            blocks_of(own_ref, near_refs, far_ref, 0, at),
            blocks_of(own_ref, near_refs, far_ref, 1, at),
        )
        probs_ref[g - first] = probs
        d_logits_ref[g - first] = d_logits
        for h, c in enumerate(columns):
            out = slice(c - first * group, c - first * group + HD)
            grad_ref[out, :] = (
                turned_cot_ref[c : c + HD, :].astype(jnp.float32)
                + d_queries[:, h * tok : (h + 1) * tok]
            ).astype(jnp.bfloat16)
    if store is not None:
        store.wait()


def in_grad_of(shard, queries, d_attended, turned_cot, block, low, first, last, group, piece=None):
    tok, width = queries.shape
    count = last - first
    inside = jax.ShapeDtypeStruct((count, 3 * tok, tok * group // HD), jnp.bfloat16)
    out_specs = [VMEM] * 3
    out_shape = [jax.ShapeDtypeStruct((count * group, tok), jnp.bfloat16), inside, inside]
    pieces, column, scratch = [], None, []
    if piece is not None:
        pieces, column = [piece[0]], piece[1]
        out_specs.append(HBM)
        out_shape.append(jax.ShapeDtypeStruct((tok, width), jnp.bfloat16))
        scratch = [pltpu.VMEM(piece[0].shape[::-1], jnp.bfloat16), pltpu.SemaphoreType.DMA]
    own, near, far = block
    return pl.pallas_call(
        functools.partial(in_grad_kernel, low, first, last, group, len(near), column),
        in_specs=[SMEM] + [VMEM] * (5 + len(near) + len(pieces)),
        out_specs=out_specs,
        out_shape=out_shape,
        scratch_shapes=scratch,
        compiler_params=params(),
        cost_estimate=cost(ATT_FLOPS[first]),
        name="in_grad",
    )(shard, queries, d_attended, turned_cot, own, *near, far, *pieces)


def mixed_columns(attended, weight_ref, kept_ref, q_ref, out_ref, first):
    step = 4 * TILE
    for column in range(0, out_ref.shape[1], step):
        at = slice(column, column + step)
        of_all = slice(first + column, first + column + step)
        weight = prune(weight_ref[:, of_all], kept_ref, 0, of_all)
        mixed = f32_dot(attended, weight)
        out_ref[:, at] = (q_ref[:, of_all].astype(jnp.float32) + mixed).astype(jnp.bfloat16)


def layer_out_first_kernel(group, chunks, halos, nears, column, *refs):
    kept_ref, q_ref, weight_ref, piece_ref, given_ref, *refs = refs
    d_ref, *refs = refs
    owns, nears_refs, fars = [], [], []
    for count in nears:
        own_ref, *refs = refs
        near, (far_ref, *refs) = refs[:count], refs[count:]
        owns.append(own_ref)
        nears_refs.append(near)
        fars.append(far_ref)
    probs_refs, refs = refs[: len(chunks)], refs[len(chunks) :]
    d_logits_refs, refs = refs[: len(chunks)], refs[len(chunks) :]
    out_ref, whole_ref, attended_ref, own_grad_ref, *near_grad_refs, far_grad_ref, turned_ref, sem = refs
    tok = q_ref.shape[0]
    scaling = HD ** (-0.5)
    store = store_piece(piece_ref[...], column, turned_ref, whole_ref, sem)
    for i, (first, last) in enumerate(chunks):
        for g in range(first, last):
            halo = [j for j, (low, high) in enumerate(halos) if low <= g < high][0]
            at = slice((g - halos[halo][0]) * HD, (g - halos[halo][0] + 1) * HD)
            at_kv = slice(g * HD, (g + 1) * HD)
            columns = [g * group + c for c in range(0, group, HD)]
            d_rows = stacked([d_ref[:, c : c + HD] for c in columns])
            q_rows = stacked([q_ref[:, c : c + HD] for c in columns])
            values = stacked(blocks_of(owns[halo], nears_refs[halo], fars[halo], 1, at))
            probs = probs_refs[i][g - first]
            d_logits = d_logits_refs[i][g - first]
            attended = f32_dot(values.T, probs).astype(jnp.bfloat16)
            for h, c in enumerate(columns):
                attended_ref[:, c : c + HD] = attended[:, h * tok : (h + 1) * tok].T
            d_keys = f32_dot(d_logits, q_rows) * scaling
            d_values = f32_dot(probs, d_rows)
            for index, grad in enumerate((d_keys, d_values)):
                own_grad_ref[index, :, at_kv] = grad[:tok]
                near_grad_refs[index][:, at_kv] = grad[tok : 2 * tok].astype(jnp.bfloat16)
                far_grad_ref[index, :, at_kv] = grad[2 * tok :].astype(jnp.bfloat16)
    mixed_columns(attended_ref[...], weight_ref, kept_ref, q_ref, out_ref, 0)
    store.wait()


def layer_out_first(kept, queries, weight, piece, given, d_attended, blocks, chunks, probs, d_logits, group, last):
    tok, width = queries.shape
    kv_width = sum(own.shape[-1] for own, _, _ in blocks)
    flat = [x for own, near, far in blocks for x in (own, *near, far)]
    operands = [kept, queries, weight, piece[0], given, d_attended, *flat, *probs, *d_logits]
    near_grad = jax.ShapeDtypeStruct((tok, kv_width), jnp.bfloat16)
    own_grad, far_grad = (jax.ShapeDtypeStruct((2, tok, kv_width), t) for t in (jnp.float32, jnp.bfloat16))
    return pl.pallas_call(
        functools.partial(
            layer_out_first_kernel, group, chunks, HALOS, [len(near) for _, near, _ in blocks],
            piece[1],
        ),
        in_specs=[VMEM] * 4 + [HBM] + [VMEM] * (len(operands) - 5),
        out_specs=[VMEM, HBM] + [VMEM] * 5,
        out_shape=[
            jax.ShapeDtypeStruct((tok, last), jnp.bfloat16),
            jax.ShapeDtypeStruct((tok, width), jnp.bfloat16),
            jax.ShapeDtypeStruct((tok, width), jnp.bfloat16),
            own_grad, near_grad, near_grad, far_grad,
        ],
        scratch_shapes=[pltpu.VMEM(piece[0].shape[::-1], jnp.bfloat16), pltpu.SemaphoreType.DMA],
        input_output_aliases={4: 1},
        compiler_params=params(),
        cost_estimate=cost(10**10),
        name="layer_out_first",
    )(*operands)


def layer_out_second_kernel(first, column, *refs):
    kept_ref, q_ref, weight_ref, piece_ref, given_ref, attended_ref, out_ref, whole_ref, turned_ref, sem = refs
    store = store_piece(piece_ref[...], column, turned_ref, whole_ref, sem)
    mixed_columns(attended_ref[...], weight_ref, kept_ref, q_ref, out_ref, first)
    store.wait()


def layer_out_second(kept, queries, weight, piece, given, attended, first):
    tok, width = queries.shape
    return pl.pallas_call(
        functools.partial(layer_out_second_kernel, first, piece[1]),
        in_specs=[VMEM] * 4 + [HBM, VMEM],
        out_specs=[VMEM, HBM],
        out_shape=[
            jax.ShapeDtypeStruct((tok, width - first), jnp.bfloat16),
            jax.ShapeDtypeStruct((tok, width), jnp.bfloat16),
        ],
        scratch_shapes=[pltpu.VMEM(piece[0].shape[::-1], jnp.bfloat16), pltpu.SemaphoreType.DMA],
        input_output_aliases={4: 1},
        compiler_params=params(),
        cost_estimate=cost(10**10),
        name="layer_out_second",
    )(kept, queries, weight, piece[0], given, attended)


def store_first_kernel(shard_ref, piece_ref, own_ref, ahead_ref, *refs):
    *beside_refs, whole_ref, kv_ref, sum_ref, sems = refs
    store = pltpu.make_async_copy(piece_ref, whole_ref.at[:, : piece_ref.shape[1]], sems.at[0])
    store.start()
    for index, beside_ref in enumerate(beside_refs):
        total = own_ref[index] + ahead_ref[index].astype(jnp.float32)
        both = total + beside_ref[...].astype(jnp.float32)
        sum_ref[index] = jnp.where(shard_ref[0] % 2 == 0, both, total)
    kv_store = pltpu.make_async_copy(sum_ref, kv_ref, sems.at[1])
    kv_store.start()
    store.wait()
    kv_store.wait()


def store_first(shard, piece, own, ahead, beside, width):
    return pl.pallas_call(
        store_first_kernel,
        in_specs=[SMEM] + [VMEM] * 5,
        out_specs=[HBM, HBM],
        out_shape=[
            jax.ShapeDtypeStruct((piece.shape[0], width), piece.dtype),
            jax.ShapeDtypeStruct(own.shape, own.dtype),
        ],
        scratch_shapes=[pltpu.VMEM(own.shape, own.dtype), pltpu.SemaphoreType.DMA((2,))],
        compiler_params=params(),
        name="store_first",
    )(shard, piece, own, ahead, *beside)


def store_last_kernel(piece_ref, given_ref, kept_ref, whole_ref, same_ref, sem):
    column = whole_ref.shape[1] - piece_ref.shape[1]
    store = pltpu.make_async_copy(piece_ref, whole_ref.at[:, column:], sem)
    store.start()
    store.wait()


def store_last(piece, whole, kept):
    return pl.pallas_call(
        store_last_kernel,
        in_specs=[VMEM, HBM, HBM],
        out_specs=[HBM, HBM],
        out_shape=[
            jax.ShapeDtypeStruct(whole.shape, whole.dtype),
            jax.ShapeDtypeStruct(kept.shape, kept.dtype),
        ],
        scratch_shapes=[pltpu.SemaphoreType.DMA],
        input_output_aliases={1: 0, 2: 1},
        compiler_params=params(),
        name="store_last",
    )(piece, whole, kept)


def core_swap(value, axis):
    return lax.ppermute(value, axis, [(i, i ^ 1) for i in range(lax.axis_size(axis))])


def per_device(stream_in, keys_values, out_weight, tile_mask, cotangent):
    queries, own, mask, cot = stream_in[0], keys_values[0], tile_mask[0], cotangent[0]
    weight = pltpu.with_memory_space_constraint(out_weight[0], pltpu.VMEM)
    width = queries.shape[1]
    group = width // (own.shape[-1] // HD)
    shard = lax.axis_index("seq").astype(jnp.int32).reshape(1)
    owns = cut(own)
    fars = [around(piece, "seq", 2) for piece in owns]
    d_attended, turned_cot, kept = d_attended_of(cot, weight, mask)
    pieces, probs, d_logits, blocks = [], [], [], []
    after = d_attended
    for first, last in CHUNKS:
        halo = [i for i, (low, high) in enumerate(HALOS) if low <= first < high][0]
        if halo == len(blocks):
            near = [core_swap(x, "seq") for x in pick(shard, owns[halo], fars[halo], after, halo > 0)]
            blocks.append((owns[halo], near, fars[halo]))
        late = first == CHUNKS[-1][0]
        grad, p, d, *stored = in_grad_of(
            shard, queries, d_attended, turned_cot, blocks[halo], HALOS[halo][0], first, last, group,
            pieces[0] if late else None,
        )
        probs.append(p)
        d_logits.append(d)
        pieces.append((around(grad, "section", -1), first * group))
        after = grad
    out_cut = OUT_CUT * 4 * TILE
    result, prev_grad, attended, own_grad, *near_grad, far_grad = layer_out_first(
        kept, queries, weight, pieces[1], stored[0], d_attended, blocks, CHUNKS, probs,
        d_logits, group, out_cut,
    )
    early = around(result, "section", 1)
    beside = [core_swap(x, "seq") for x in near_grad]
    ahead = around(behind_of(shard, far_grad, beside), "seq", -2)
    result, prev_grad = layer_out_second(kept, queries, weight, pieces[2], prev_grad, attended, out_cut)
    late = around(result, "section", 1)
    next_input, kv_total = store_first(shard, early, own_grad, ahead, beside, width)
    next_input, kv_total = store_last(late, next_input, kv_total)
    return (next_input[None], prev_grad[None], kv_total[None])


def solution(mesh):
    return jax.shard_map(
        per_device,
        mesh=mesh,
        in_specs=(
            P("section", "seq", None),
            P("section", None, "seq", None),
            P("section", None, None),
            P("section", None, None),
            P("section", "seq", None),
        ),
        out_specs=(
            P("section", "seq", None),
            P("section", "seq", None),
            P("section", None, "seq", None),
        ),
        check_vma=False,
    )
```

```python
import functools
import math

import jax
import jax.numpy as jnp
from jax import lax
from jax.experimental import pallas as pl
from jax.experimental.pallas import tpu as pltpu
from jax.sharding import PartitionSpec as P

HD = 128
TILE = 128
HALOS = ((0, 1), (1, 4))
CHUNKS = ((0, 1), (1, 2), (2, 4))
OUT_CUT = 3
CUT_FLOPS = 10**10
ATT_FLOPS = {0: 2 * 10**8, 1: 1, 2: 10**10}
VMEM = pl.BlockSpec(memory_space=pltpu.VMEM)
HBM = pl.BlockSpec(memory_space=pltpu.HBM)
SMEM = pl.BlockSpec(memory_space=pltpu.SMEM)
VMEM_LIMIT = 32 * 1024 * 1024
NT = (((1,), (1,)), ((), ()))


def around(value, axis, by):
    length = lax.axis_size(axis)
    return lax.ppermute(value, axis, [(i, (i + by) % length) for i in range(length)])


def f32_dot(a, b, dims=(((1,), (0,)), ((), ()))):
    return lax.dot_general(a, b, dims, preferred_element_type=jnp.float32)


def params():
    return pltpu.CompilerParams(vmem_limit_bytes=VMEM_LIMIT)


def cost(flops):
    return pl.CostEstimate(flops=flops, bytes_accessed=1, transcendentals=0)


def prune(weight, kept_ref, row_tile, columns):
    strips = []
    for a in range(weight.shape[0] // TILE):
        row = kept_ref[row_tile + a : row_tile + a + 1, columns]
        kept = jnp.broadcast_to(row, (16, row.shape[1])).astype(weight.dtype)
        strip = weight[a * TILE : (a + 1) * TILE, :]
        strips.append(strip * jnp.concatenate([kept] * (TILE // 16), axis=0))
    return jnp.concatenate(strips, axis=0)


def cut_kernel(own_hbm, *refs):
    *piece_refs, sems = refs
    copies, column = [], 0
    for i, ref in enumerate(piece_refs):
        width = ref.shape[-1]
        source = own_hbm.at[:, :, column : column + width]
        copies.append(pltpu.make_async_copy(source, ref, sems.at[i]))
        column += width
    for copy in copies:
        copy.start()
    for copy in copies:
        copy.wait()


def cut(own):
    shapes = [own.shape[:2] + ((last - first) * HD,) for first, last in HALOS]
    return pl.pallas_call(
        cut_kernel,
        in_specs=[HBM],
        out_specs=[VMEM for _ in shapes],
        out_shape=[jax.ShapeDtypeStruct(shape, own.dtype) for shape in shapes],
        scratch_shapes=[pltpu.SemaphoreType.DMA((len(shapes),))],
        compiler_params=params(),
        cost_estimate=cost(CUT_FLOPS),
        name="cut",
    )(pltpu.with_memory_space_constraint(own, pltpu.HBM))


def d_attended_kernel(mask_ref, cot_ref, q_ref, weight_ref, out_ref, turned_ref, kept_ref):
    tiles = mask_ref.shape[0]
    width = kept_ref.shape[1]
    tile = lax.broadcasted_iota(jnp.int32, (tiles, width), 1) // TILE
    spread = (tile == lax.broadcasted_iota(jnp.int32, (tiles, width), 0)).astype(jnp.float32)
    kept_ref[...] = f32_dot((mask_ref[...] > 0).astype(jnp.float32), spread)
    rows = 4 * TILE
    for row in range(0, width, rows):
        weight = prune(weight_ref[row : row + rows, :], kept_ref, row // TILE, slice(None))
        part = f32_dot(cot_ref[...], weight, NT).astype(jnp.bfloat16)
        out_ref[:, row : row + rows] = part
        turned_ref[2, row : row + rows, :] = part.T
    turned_ref[0] = cot_ref[...].T
    turned_ref[1] = q_ref[...].T


def d_attended_of(cot, queries, weight, mask):
    tok, width = cot.shape
    return pl.pallas_call(
        d_attended_kernel,
        in_specs=[VMEM, VMEM, VMEM, VMEM],
        out_specs=[VMEM, VMEM, VMEM],
        out_shape=[
            jax.ShapeDtypeStruct((tok, width), jnp.bfloat16),
            jax.ShapeDtypeStruct((3, width, tok), jnp.bfloat16),
            jax.ShapeDtypeStruct((mask.shape[0], width), jnp.float32),
        ],
        compiler_params=params(),
        cost_estimate=cost(1),
        name="d_attended",
    )(mask, cot, queries, weight)


def pick_kernel(cuts, shard_ref, own_ref, far_ref, after_ref, *out_refs):
    odd = shard_ref[0] % 2 == 1

    def copy_from(source_ref):
        refs = list(out_refs)
        for start, width, split in cuts:
            at = slice(start, start + width)
            if split:
                for index in range(2):
                    refs.pop(0)[...] = source_ref[index, :, at]
            else:
                refs.pop(0)[...] = source_ref[:, :, at]

    @pl.when(odd)
    def _():
        copy_from(far_ref)

    @pl.when(jnp.logical_not(odd))
    def _():
        copy_from(own_ref)


def pick(shard, own, far, after, cuts):
    shapes = []
    for _, width, split in cuts:
        shape = (own.shape[1], width)
        shapes += [shape, shape] if split else [(2,) + shape]
    return pl.pallas_call(
        functools.partial(pick_kernel, cuts),
        in_specs=[SMEM, VMEM, VMEM, pl.BlockSpec(memory_space=pl.ANY)],
        out_specs=[VMEM for _ in shapes],
        out_shape=[jax.ShapeDtypeStruct(shape, own.dtype) for shape in shapes],
        compiler_params=params(),
        cost_estimate=cost(1),
        name="pick",
    )(shard, own, far, after)


def behind_kernel(shard_ref, far_ref, *refs):
    *beside_refs, out_ref = refs
    for index, beside_ref in enumerate(beside_refs):
        far = far_ref[index].astype(jnp.float32)
        both = far + beside_ref[...].astype(jnp.float32)
        out_ref[index] = jnp.where(shard_ref[0] % 2 == 1, both, far).astype(jnp.bfloat16)


def behind_of(shard, far, beside):
    return pl.pallas_call(
        behind_kernel,
        in_specs=[SMEM, VMEM, VMEM, VMEM],
        out_specs=VMEM,
        out_shape=jax.ShapeDtypeStruct(far.shape, far.dtype),
        compiler_params=params(),
        cost_estimate=cost(1),
        name="behind",
    )(shard, far, *beside)


def store_piece(piece, column, turned_ref, whole_ref, sem):
    turned_ref[...] = piece.T
    store = pltpu.make_async_copy(
        turned_ref, whole_ref.at[:, column : column + turned_ref.shape[1]], sem
    )
    store.start()
    return store


def stacked(parts, axis=0):
    return jnp.concatenate(parts, axis=axis)


def blocks_of(own_ref, near_refs, far_ref, index, at, near_head):
    near_at = slice(near_head * HD, (near_head + 1) * HD)
    near = near_refs[index][:, near_at] if len(near_refs) == 2 else near_refs[0][index, :, near_at]
    return stacked([own_ref[index, :, at], near, far_ref[index, :, at]])


def in_grad_group(near_ok, far_ok, q_columns, d_columns, keys, values):
    tok = keys.shape[0] // 3
    scaling = HD ** (-0.5)
    factor = scaling * math.log2(math.e)
    floor = jnp.float32(-1e30)
    key_at = lax.broadcasted_iota(jnp.int32, (tok, tok), 0)
    row_at = lax.broadcasted_iota(jnp.int32, (tok, tok), 1)
    causal = key_at <= row_at
    lower = causal.astype(jnp.float32).astype(jnp.bfloat16)
    upper = (1.0 - causal.astype(jnp.float32)).astype(jnp.bfloat16)
    logits = f32_dot(keys, q_columns)
    d_probs = f32_dot(values, d_columns)
    own_l, near_l, far_l = (logits[i * tok : (i + 1) * tok] for i in range(3))
    own_d, near_d, far_d = (d_probs[i * tok : (i + 1) * tok] for i in range(3))
    parts = []
    for h in range(q_columns.shape[1] // tok):
        at = slice(h * tok, (h + 1) * tok)
        edge = jnp.where(causal, own_l[:, at], jnp.where(far_ok, far_l[:, at], floor))
        near = jnp.where(near_ok, near_l[:, at], floor)
        top = jnp.max(jnp.maximum(edge, near), axis=0, keepdims=True)
        edge = jnp.exp2((edge - top) * factor)
        near = jnp.exp2((near - top) * factor)
        inverse = 1.0 / jnp.sum(edge + near, axis=0, keepdims=True)
        edge = edge * inverse
        near = near * inverse
        edge_d = jnp.where(causal, own_d[:, at], far_d[:, at])
        row_dot = jnp.sum(edge * edge_d + near * near_d[:, at], axis=0, keepdims=True)
        d_edge = (edge * (edge_d - row_dot)).astype(jnp.bfloat16)
        d_near = (near * (near_d[:, at] - row_dot)).astype(jnp.bfloat16)
        edge = edge.astype(jnp.bfloat16)
        parts.append(
            (
                stacked([edge * lower, near.astype(jnp.bfloat16), edge * upper]),
                stacked([d_edge * lower, d_near, d_edge * upper]),
            )
        )
    probs = stacked([p for p, _ in parts], axis=1)
    d_logits = stacked([d for _, d in parts], axis=1)
    return f32_dot(keys.T, d_logits) * scaling, probs, d_logits


def in_grad_kernel(low, first, last, group, nears, shard_ref, turned_ref, *refs):
    own_ref, *refs = refs
    near_refs, far_ref = refs[:nears], refs[nears]
    grad_ref, probs_ref, d_logits_ref = refs[-3:]
    tok = own_ref.shape[1]
    shard = shard_ref[0]
    for g in range(first, last):
        at = slice((g - low) * HD, (g - low + 1) * HD)
        rows = [slice(g * group + c, g * group + c + HD) for c in range(0, group, HD)]
        d_queries, probs, d_logits = in_grad_group(
            shard >= 1,
            shard >= 2,
            stacked([turned_ref[1, row, :] for row in rows], axis=1),
            stacked([turned_ref[2, row, :] for row in rows], axis=1),
            blocks_of(own_ref, near_refs, far_ref, 0, at, g - first),
            blocks_of(own_ref, near_refs, far_ref, 1, at, g - first),
        )
        probs_ref[g - first] = probs
        d_logits_ref[g - first] = d_logits
        for h, row in enumerate(rows):
            out = slice(row.start - first * group, row.stop - first * group)
            grad_ref[out, :] = (
                turned_ref[0, row, :].astype(jnp.float32) + d_queries[:, h * tok : (h + 1) * tok]
            ).astype(jnp.bfloat16)


def in_grad_of(shard, turned, block, low, first, last, group, after):
    tok = turned.shape[-1]
    count = last - first
    inside = jax.ShapeDtypeStruct((count, 3 * tok, tok * group // HD), jnp.bfloat16)
    own, near, far = block
    return pl.pallas_call(
        functools.partial(in_grad_kernel, low, first, last, group, len(near)),
        in_specs=[SMEM] + [VMEM] * (3 + len(near)) + [pl.BlockSpec(memory_space=pl.ANY)] * len(after),
        out_specs=[VMEM] * 3,
        out_shape=[jax.ShapeDtypeStruct((count * group, tok), jnp.bfloat16), inside, inside],
        compiler_params=params(),
        cost_estimate=cost(ATT_FLOPS[first]),
        name="in_grad",
    )(shard, turned, own, *near, far, *after)


def mixed_columns(attended, weight_ref, kept_ref, q_ref, out_ref, first):
    step = 4 * TILE
    for column in range(0, out_ref.shape[1], step):
        at = slice(column, column + step)
        of_all = slice(first + column, first + column + step)
        weight = prune(weight_ref[:, of_all], kept_ref, 0, of_all)
        mixed = f32_dot(attended, weight)
        out_ref[:, at] = (q_ref[:, of_all].astype(jnp.float32) + mixed).astype(jnp.bfloat16)


def layer_out_first_kernel(group, chunks, halos, nears, stored, *refs):
    kept_ref, q_ref, weight_ref, d_ref, *refs = refs
    piece_refs, refs = refs[: len(stored)], refs[len(stored) :]
    owns, refs = refs[: len(halos)], refs[len(halos) :]
    fars, refs = refs[: len(halos)], refs[len(halos) :]
    near_refs = []
    for count in nears:
        near_refs.append(refs[:count])
        refs = refs[count:]
    probs_refs, refs = refs[: len(chunks)], refs[len(chunks) :]
    d_logits_refs, refs = refs[: len(chunks)], refs[len(chunks) :]
    out_ref, whole_ref, attended_ref, own_grad_ref, *near_grad_refs, far_grad_ref = refs[:7]
    *turned_refs, sems = refs[7:]
    tok = q_ref.shape[0]
    scaling = HD ** (-0.5)
    stores = [
        store_piece(piece_ref[...], column, turned_ref, whole_ref, sems.at[i])
        for i, (piece_ref, column, turned_ref) in enumerate(zip(piece_refs, stored, turned_refs))
    ]
    for i, (first, last) in enumerate(chunks):
        for g in range(first, last):
            halo = [j for j, (low, high) in enumerate(halos) if low <= g < high][0]
            at = slice((g - halos[halo][0]) * HD, (g - halos[halo][0] + 1) * HD)
            at_kv = slice(g * HD, (g + 1) * HD)
            columns = [g * group + c for c in range(0, group, HD)]
            d_rows = stacked([d_ref[:, c : c + HD] for c in columns])
            q_rows = stacked([q_ref[:, c : c + HD] for c in columns])
            values = blocks_of(owns[halo], near_refs[i], fars[halo], 1, at, g - first)
            probs = probs_refs[i][g - first]
            d_logits = d_logits_refs[i][g - first]
            attended = f32_dot(values.T, probs).astype(jnp.bfloat16)
            for h, c in enumerate(columns):
                attended_ref[:, c : c + HD] = attended[:, h * tok : (h + 1) * tok].T
            d_keys = f32_dot(d_logits, q_rows) * scaling
            d_values = f32_dot(probs, d_rows)
            for index, grad in enumerate((d_keys, d_values)):
                own_grad_ref[index, :, at_kv] = grad[:tok]
                near_grad_refs[index][:, at_kv] = grad[tok : 2 * tok].astype(jnp.bfloat16)
                far_grad_ref[index, :, at_kv] = grad[2 * tok :].astype(jnp.bfloat16)
    mixed_columns(attended_ref[...], weight_ref, kept_ref, q_ref, out_ref, 0)
    for store in stores:
        store.wait()


def layer_out_first(kept, queries, weight, d_attended, pieces, owns, fars, nears, probs, d_logits, group, last):
    tok, width = queries.shape
    kv_width = sum(own.shape[-1] for own in owns)
    operands = [
        kept, queries, weight, d_attended, *[p for p, _ in pieces], *owns, *fars,
        *[x for near in nears for x in near], *probs, *d_logits,
    ]
    near_grad = jax.ShapeDtypeStruct((tok, kv_width), jnp.bfloat16)
    own_grad, far_grad = (jax.ShapeDtypeStruct((2, tok, kv_width), t) for t in (jnp.float32, jnp.bfloat16))
    return pl.pallas_call(
        functools.partial(
            layer_out_first_kernel, group, CHUNKS, HALOS, [len(near) for near in nears],
            [c for _, c in pieces],
        ),
        in_specs=[VMEM] * len(operands),
        out_specs=[VMEM, HBM] + [VMEM] * 5,
        out_shape=[
            jax.ShapeDtypeStruct((tok, last), jnp.bfloat16),
            jax.ShapeDtypeStruct((tok, width), jnp.bfloat16),
            jax.ShapeDtypeStruct((tok, width), jnp.bfloat16),
            own_grad, near_grad, near_grad, far_grad,
        ],
        scratch_shapes=[pltpu.VMEM(p.shape[::-1], jnp.bfloat16) for p, _ in pieces]
        + [pltpu.SemaphoreType.DMA((len(pieces),))],
        compiler_params=params(),
        cost_estimate=cost(10**10),
        name="layer_out_first",
    )(*operands)


def layer_out_second_kernel(first, column, *refs):
    kept_ref, q_ref, weight_ref, piece_ref, given_ref, attended_ref, out_ref, whole_ref, turned_ref, sem = refs
    store = store_piece(piece_ref[...], column, turned_ref, whole_ref, sem)
    mixed_columns(attended_ref[...], weight_ref, kept_ref, q_ref, out_ref, first)
    store.wait()


def layer_out_second(kept, queries, weight, piece, given, attended, first):
    tok, width = queries.shape
    return pl.pallas_call(
        functools.partial(layer_out_second_kernel, first, piece[1]),
        in_specs=[VMEM] * 4 + [HBM, VMEM],
        out_specs=[VMEM, HBM],
        out_shape=[
            jax.ShapeDtypeStruct((tok, width - first), jnp.bfloat16),
            jax.ShapeDtypeStruct((tok, width), jnp.bfloat16),
        ],
        scratch_shapes=[pltpu.VMEM(piece[0].shape[::-1], jnp.bfloat16), pltpu.SemaphoreType.DMA],
        input_output_aliases={4: 1},
        compiler_params=params(),
        cost_estimate=cost(10**10),
        name="layer_out_second",
    )(kept, queries, weight, piece[0], given, attended)


def store_first_kernel(shard_ref, piece_ref, own_ref, ahead_ref, *refs):
    *beside_refs, whole_ref, kv_ref, sum_ref, sems = refs
    store = pltpu.make_async_copy(piece_ref, whole_ref.at[:, : piece_ref.shape[1]], sems.at[0])
    store.start()
    for index, beside_ref in enumerate(beside_refs):
        total = own_ref[index] + ahead_ref[index].astype(jnp.float32)
        both = total + beside_ref[...].astype(jnp.float32)
        sum_ref[index] = jnp.where(shard_ref[0] % 2 == 0, both, total)
    kv_store = pltpu.make_async_copy(sum_ref, kv_ref, sems.at[1])
    kv_store.start()
    store.wait()
    kv_store.wait()


def store_first(shard, piece, own, ahead, beside, width):
    return pl.pallas_call(
        store_first_kernel,
        in_specs=[SMEM] + [VMEM] * 5,
        out_specs=[HBM, HBM],
        out_shape=[
            jax.ShapeDtypeStruct((piece.shape[0], width), piece.dtype),
            jax.ShapeDtypeStruct(own.shape, own.dtype),
        ],
        scratch_shapes=[pltpu.VMEM(own.shape, own.dtype), pltpu.SemaphoreType.DMA((2,))],
        compiler_params=params(),
        name="store_first",
    )(shard, piece, own, ahead, *beside)


def store_last_kernel(piece_ref, given_ref, kept_ref, whole_ref, same_ref, sem):
    column = whole_ref.shape[1] - piece_ref.shape[1]
    store = pltpu.make_async_copy(piece_ref, whole_ref.at[:, column:], sem)
    store.start()
    store.wait()


def store_last(piece, whole, kept):
    return pl.pallas_call(
        store_last_kernel,
        in_specs=[VMEM, HBM, HBM],
        out_specs=[HBM, HBM],
        out_shape=[
            jax.ShapeDtypeStruct(whole.shape, whole.dtype),
            jax.ShapeDtypeStruct(kept.shape, kept.dtype),
        ],
        scratch_shapes=[pltpu.SemaphoreType.DMA],
        input_output_aliases={1: 0, 2: 1},
        compiler_params=params(),
        name="store_last",
    )(piece, whole, kept)


def core_swap(value, axis):
    return lax.ppermute(value, axis, [(i, i ^ 1) for i in range(lax.axis_size(axis))])


def per_device(stream_in, keys_values, out_weight, tile_mask, cotangent):
    queries, own, mask, cot = stream_in[0], keys_values[0], tile_mask[0], cotangent[0]
    weight = pltpu.with_memory_space_constraint(out_weight[0], pltpu.VMEM)
    width = queries.shape[1]
    group = width // (own.shape[-1] // HD)
    shard = lax.axis_index("seq").astype(jnp.int32).reshape(1)
    owns = cut(own)
    fars = [around(piece, "seq", 2) for piece in owns]
    d_attended, turned, kept = d_attended_of(cot, queries, weight, mask)
    pieces, probs, d_logits, nears = [], [], [], []
    after = d_attended
    for halo, (low, high) in enumerate(HALOS):
        chunks = [(first, last) for first, last in CHUNKS if low <= first < high]
        cuts = [((first - low) * HD, (last - first) * HD, last - first > 1) for first, last in chunks]
        picked = pick(shard, owns[halo], fars[halo], after, cuts)
        swapped = [core_swap(x, "seq") for x in picked]
        for first, last in chunks:
            near, swapped = swapped[: 1 + (last - first > 1)], swapped[1 + (last - first > 1) :]
            grad, p, d = in_grad_of(
                shard, turned, (owns[halo], near, fars[halo]), low, first, last, group,
                [pieces[0][0]] if first == CHUNKS[-1][0] else [],
            )
            nears.append(near)
            probs.append(p)
            d_logits.append(d)
            pieces.append((around(grad, "section", -1), first * group))
            after = grad
    out_cut = OUT_CUT * 4 * TILE
    result, prev_grad, attended, own_grad, *near_grad, far_grad = layer_out_first(
        kept, queries, weight, d_attended, pieces[:2], owns, fars, nears, probs, d_logits, group, out_cut
    )
    early = around(result, "section", 1)
    beside = [core_swap(x, "seq") for x in near_grad]
    ahead = around(behind_of(shard, far_grad, beside), "seq", -2)
    result, prev_grad = layer_out_second(kept, queries, weight, pieces[2], prev_grad, attended, out_cut)
    late = around(result, "section", 1)
    next_input, kv_total = store_first(shard, early, own_grad, ahead, beside, width)
    next_input, kv_total = store_last(late, next_input, kv_total)
    return (next_input[None], prev_grad[None], kv_total[None])


def solution(mesh):
    return jax.shard_map(
        per_device,
        mesh=mesh,
        in_specs=(
            P("section", "seq", None),
            P("section", None, "seq", None),
            P("section", None, None),
            P("section", None, None),
            P("section", "seq", None),
        ),
        out_specs=(
            P("section", "seq", None),
            P("section", "seq", None),
            P("section", None, "seq", None),
        ),
        check_vma=False,
    )
```

```python
import functools
import math

import jax
import jax.numpy as jnp
from jax import lax
from jax.experimental import pallas as pl
from jax.experimental.pallas import tpu as pltpu
from jax.sharding import PartitionSpec as P

HD = 128
TILE = 128
HALOS = ((0, 1), (1, 4))
CHUNKS = ((0, 1), (1, 2), (2, 4))
CUT_FLOPS = 10**10
ATT_FLOPS = {0: 2 * 10**8, 1: 1, 2: 10**10}
VMEM = pl.BlockSpec(memory_space=pltpu.VMEM)
HBM = pl.BlockSpec(memory_space=pltpu.HBM)
SMEM = pl.BlockSpec(memory_space=pltpu.SMEM)
VMEM_LIMIT = 32 * 1024 * 1024
NT = (((1,), (1,)), ((), ()))


def around(value, axis, by):
    length = lax.axis_size(axis)
    return lax.ppermute(value, axis, [(i, (i + by) % length) for i in range(length)])


def f32_dot(a, b, dims=(((1,), (0,)), ((), ()))):
    return lax.dot_general(a, b, dims, preferred_element_type=jnp.float32)


def params():
    return pltpu.CompilerParams(vmem_limit_bytes=VMEM_LIMIT)


def cost(flops):
    return pl.CostEstimate(flops=flops, bytes_accessed=1, transcendentals=0)


def prune(weight, kept_ref, row_tile, columns):
    strips = []
    for a in range(weight.shape[0] // TILE):
        row = kept_ref[row_tile + a : row_tile + a + 1, columns]
        kept = jnp.broadcast_to(row, (16, row.shape[1])).astype(weight.dtype)
        strip = weight[a * TILE : (a + 1) * TILE, :]
        strips.append(strip * jnp.concatenate([kept] * (TILE // 16), axis=0))
    return jnp.concatenate(strips, axis=0)


def cut_kernel(own_hbm, *refs):
    *piece_refs, sems = refs
    copies, column = [], 0
    for i, ref in enumerate(piece_refs):
        width = ref.shape[-1]
        source = own_hbm.at[:, :, column : column + width]
        copies.append(pltpu.make_async_copy(source, ref, sems.at[i]))
        column += width
    for copy in copies:
        copy.start()
    for copy in copies:
        copy.wait()


def cut(own):
    shapes = [own.shape[:2] + ((last - first) * HD,) for first, last in HALOS]
    return pl.pallas_call(
        cut_kernel,
        in_specs=[HBM],
        out_specs=[VMEM for _ in shapes],
        out_shape=[jax.ShapeDtypeStruct(shape, own.dtype) for shape in shapes],
        scratch_shapes=[pltpu.SemaphoreType.DMA((len(shapes),))],
        compiler_params=params(),
        cost_estimate=cost(CUT_FLOPS),
        name="cut",
    )(pltpu.with_memory_space_constraint(own, pltpu.HBM))


def d_attended_kernel(mask_ref, cot_ref, q_ref, weight_ref, out_ref, turned_ref, kept_ref):
    tiles = mask_ref.shape[0]
    width = kept_ref.shape[1]
    tile = lax.broadcasted_iota(jnp.int32, (tiles, width), 1) // TILE
    spread = (tile == lax.broadcasted_iota(jnp.int32, (tiles, width), 0)).astype(jnp.float32)
    kept_ref[...] = f32_dot((mask_ref[...] > 0).astype(jnp.float32), spread)
    rows = 4 * TILE
    for row in range(0, width, rows):
        weight = prune(weight_ref[row : row + rows, :], kept_ref, row // TILE, slice(None))
        part = f32_dot(cot_ref[...], weight, NT).astype(jnp.bfloat16)
        out_ref[:, row : row + rows] = part
        turned_ref[2, row : row + rows, :] = part.T
    turned_ref[0] = cot_ref[...].T
    turned_ref[1] = q_ref[...].T


def d_attended_of(cot, queries, weight, mask):
    tok, width = cot.shape
    return pl.pallas_call(
        d_attended_kernel,
        in_specs=[VMEM, VMEM, VMEM, VMEM],
        out_specs=[VMEM, VMEM, VMEM],
        out_shape=[
            jax.ShapeDtypeStruct((tok, width), jnp.bfloat16),
            jax.ShapeDtypeStruct((3, width, tok), jnp.bfloat16),
            jax.ShapeDtypeStruct((mask.shape[0], width), jnp.float32),
        ],
        compiler_params=params(),
        cost_estimate=cost(1),
        name="d_attended",
    )(mask, cot, queries, weight)


def pick_kernel(cuts, shard_ref, own_ref, far_ref, after_ref, *out_refs):
    odd = shard_ref[0] % 2 == 1

    def copy_from(source_ref):
        refs = list(out_refs)
        for start, width, split in cuts:
            at = slice(start, start + width)
            if split:
                for index in range(2):
                    refs.pop(0)[...] = source_ref[index, :, at]
            else:
                refs.pop(0)[...] = source_ref[:, :, at]

    @pl.when(odd)
    def _():
        copy_from(far_ref)

    @pl.when(jnp.logical_not(odd))
    def _():
        copy_from(own_ref)


def pick(shard, own, far, after, cuts):
    shapes = []
    for _, width, split in cuts:
        shape = (own.shape[1], width)
        shapes += [shape, shape] if split else [(2,) + shape]
    return pl.pallas_call(
        functools.partial(pick_kernel, cuts),
        in_specs=[SMEM, VMEM, VMEM, pl.BlockSpec(memory_space=pl.ANY)],
        out_specs=[VMEM for _ in shapes],
        out_shape=[jax.ShapeDtypeStruct(shape, own.dtype) for shape in shapes],
        compiler_params=params(),
        cost_estimate=cost(1),
        name="pick",
    )(shard, own, far, after)


def store_piece(piece, column, turned_ref, whole_ref, sem):
    turned_ref[...] = piece.T
    store = pltpu.make_async_copy(
        turned_ref, whole_ref.at[:, column : column + turned_ref.shape[1]], sem
    )
    store.start()
    return store


def behind_kernel(column, shard_ref, piece_ref, given_ref, far_ref, *refs):
    *beside_refs, whole_ref, out_ref, turned_ref, sem = refs
    store = store_piece(piece_ref[...], column, turned_ref, whole_ref, sem)
    for index, beside_ref in enumerate(beside_refs):
        far = far_ref[index].astype(jnp.float32)
        both = far + beside_ref[...].astype(jnp.float32)
        out_ref[index] = jnp.where(shard_ref[0] % 2 == 1, both, far).astype(jnp.bfloat16)
    store.wait()


def behind_of(shard, piece, given, far, beside):
    return pl.pallas_call(
        functools.partial(behind_kernel, piece[1]),
        in_specs=[SMEM, VMEM, HBM, VMEM] + [VMEM] * len(beside),
        out_specs=[HBM, VMEM],
        out_shape=[
            jax.ShapeDtypeStruct(given.shape, given.dtype),
            jax.ShapeDtypeStruct(far.shape, far.dtype),
        ],
        scratch_shapes=[pltpu.VMEM(piece[0].shape[::-1], jnp.bfloat16), pltpu.SemaphoreType.DMA],
        input_output_aliases={2: 0},
        compiler_params=params(),
        cost_estimate=cost(1),
        name="behind",
    )(shard, piece[0], given, far, *beside)


def stacked(parts, axis=0):
    return jnp.concatenate(parts, axis=axis)


def blocks_of(own_ref, near_refs, far_ref, index, at, near_head):
    near_at = slice(near_head * HD, (near_head + 1) * HD)
    near = near_refs[index][:, near_at] if len(near_refs) == 2 else near_refs[0][index, :, near_at]
    return stacked([own_ref[index, :, at], near, far_ref[index, :, at]])


def in_grad_group(near_ok, far_ok, q_columns, d_columns, keys, values):
    tok = keys.shape[0] // 3
    scaling = HD ** (-0.5)
    factor = scaling * math.log2(math.e)
    floor = jnp.float32(-1e30)
    key_at = lax.broadcasted_iota(jnp.int32, (tok, tok), 0)
    row_at = lax.broadcasted_iota(jnp.int32, (tok, tok), 1)
    causal = key_at <= row_at
    lower = causal.astype(jnp.float32).astype(jnp.bfloat16)
    upper = (1.0 - causal.astype(jnp.float32)).astype(jnp.bfloat16)
    logits = f32_dot(keys, q_columns)
    d_probs = f32_dot(values, d_columns)
    own_l, near_l, far_l = (logits[i * tok : (i + 1) * tok] for i in range(3))
    own_d, near_d, far_d = (d_probs[i * tok : (i + 1) * tok] for i in range(3))
    parts = []
    for h in range(q_columns.shape[1] // tok):
        at = slice(h * tok, (h + 1) * tok)
        edge = jnp.where(causal, own_l[:, at], jnp.where(far_ok, far_l[:, at], floor))
        near = jnp.where(near_ok, near_l[:, at], floor)
        top = jnp.max(jnp.maximum(edge, near), axis=0, keepdims=True)
        edge = jnp.exp2((edge - top) * factor)
        near = jnp.exp2((near - top) * factor)
        inverse = 1.0 / jnp.sum(edge + near, axis=0, keepdims=True)
        edge = edge * inverse
        near = near * inverse
        edge_d = jnp.where(causal, own_d[:, at], far_d[:, at])
        row_dot = jnp.sum(edge * edge_d + near * near_d[:, at], axis=0, keepdims=True)
        d_edge = (edge * (edge_d - row_dot)).astype(jnp.bfloat16)
        d_near = (near * (near_d[:, at] - row_dot)).astype(jnp.bfloat16)
        edge = edge.astype(jnp.bfloat16)
        parts.append(
            (
                stacked([edge * lower, near.astype(jnp.bfloat16), edge * upper]),
                stacked([d_edge * lower, d_near, d_edge * upper]),
            )
        )
    probs = stacked([p for p, _ in parts], axis=1)
    d_logits = stacked([d for _, d in parts], axis=1)
    return f32_dot(keys.T, d_logits) * scaling, probs, d_logits


def in_grad_kernel(low, first, last, group, nears, shard_ref, turned_ref, *refs):
    own_ref, *refs = refs
    near_refs, far_ref = refs[:nears], refs[nears]
    grad_ref, probs_ref, d_logits_ref = refs[-3:]
    tok = own_ref.shape[1]
    shard = shard_ref[0]
    for g in range(first, last):
        at = slice((g - low) * HD, (g - low + 1) * HD)
        rows = [slice(g * group + c, g * group + c + HD) for c in range(0, group, HD)]
        d_queries, probs, d_logits = in_grad_group(
            shard >= 1,
            shard >= 2,
            stacked([turned_ref[1, row, :] for row in rows], axis=1),
            stacked([turned_ref[2, row, :] for row in rows], axis=1),
            blocks_of(own_ref, near_refs, far_ref, 0, at, g - first),
            blocks_of(own_ref, near_refs, far_ref, 1, at, g - first),
        )
        probs_ref[g - first] = probs
        d_logits_ref[g - first] = d_logits
        for h, row in enumerate(rows):
            out = slice(row.start - first * group, row.stop - first * group)
            grad_ref[out, :] = (
                turned_ref[0, row, :].astype(jnp.float32) + d_queries[:, h * tok : (h + 1) * tok]
            ).astype(jnp.bfloat16)


def in_grad_of(shard, turned, block, low, first, last, group, after):
    tok = turned.shape[-1]
    count = last - first
    inside = jax.ShapeDtypeStruct((count, 3 * tok, tok * group // HD), jnp.bfloat16)
    own, near, far = block
    return pl.pallas_call(
        functools.partial(in_grad_kernel, low, first, last, group, len(near)),
        in_specs=[SMEM] + [VMEM] * (3 + len(near)) + [pl.BlockSpec(memory_space=pl.ANY)] * len(after),
        out_specs=[VMEM] * 3,
        out_shape=[jax.ShapeDtypeStruct((count * group, tok), jnp.bfloat16), inside, inside],
        compiler_params=params(),
        cost_estimate=cost(ATT_FLOPS[first]),
        name="in_grad",
    )(shard, turned, own, *near, far, *after)


def mixed_columns(attended, weight_ref, kept_ref, q_ref, out_ref):
    step = 4 * TILE
    for column in range(0, out_ref.shape[1], step):
        at = slice(column, column + step)
        weight = prune(weight_ref[:, at], kept_ref, 0, at)
        mixed = f32_dot(attended, weight)
        out_ref[:, at] = (q_ref[:, at].astype(jnp.float32) + mixed).astype(jnp.bfloat16)


def layer_out_kernel(group, nears, *refs):
    kept_ref, q_ref, weight_ref, *refs = refs
    owns, refs = refs[: len(HALOS)], refs[len(HALOS) :]
    fars, refs = refs[: len(HALOS)], refs[len(HALOS) :]
    near_refs = []
    for count in nears:
        near_refs.append(refs[:count])
        refs = refs[count:]
    *probs_refs, out_ref, attended_ref = refs
    tok = q_ref.shape[0]
    for i, (first, last) in enumerate(CHUNKS):
        for g in range(first, last):
            halo = [j for j, (low, high) in enumerate(HALOS) if low <= g < high][0]
            at = slice((g - HALOS[halo][0]) * HD, (g - HALOS[halo][0] + 1) * HD)
            values = blocks_of(owns[halo], near_refs[i], fars[halo], 1, at, g - first)
            attended = f32_dot(values.T, probs_refs[i][g - first]).astype(jnp.bfloat16)
            for h in range(group // HD):
                c = g * group + h * HD
                attended_ref[:, c : c + HD] = attended[:, h * tok : (h + 1) * tok].T
    mixed_columns(attended_ref[...], weight_ref, kept_ref, q_ref, out_ref)


def layer_out(kept, queries, weight, owns, fars, nears, probs, group):
    tok, width = queries.shape
    operands = [kept, queries, weight, *owns, *fars, *[x for near in nears for x in near], *probs]
    return pl.pallas_call(
        functools.partial(layer_out_kernel, group, [len(near) for near in nears]),
        in_specs=[VMEM] * len(operands),
        out_specs=[VMEM, VMEM],
        out_shape=[
            jax.ShapeDtypeStruct((tok, width), jnp.bfloat16),
            jax.ShapeDtypeStruct((tok, width), jnp.bfloat16),
        ],
        compiler_params=params(),
        cost_estimate=cost(1),
        name="layer_out",
    )(*operands)


def kv_grads_kernel(group, stored, *refs):
    after_ref, q_ref, d_ref, *refs = refs
    piece_refs, refs = refs[: len(stored)], refs[len(stored) :]
    probs_refs, refs = refs[: len(CHUNKS)], refs[len(CHUNKS) :]
    d_logits_refs, refs = refs[: len(CHUNKS)], refs[len(CHUNKS) :]
    whole_ref, own_grad_ref, *near_grad_refs, far_grad_ref = refs[:5]
    *turned_refs, sems = refs[5:]
    tok = q_ref.shape[0]
    scaling = HD ** (-0.5)
    stores = [
        store_piece(piece_ref[...], column, turned_ref, whole_ref, sems.at[i])
        for i, (piece_ref, column, turned_ref) in enumerate(zip(piece_refs, stored, turned_refs))
    ]
    for i, (first, last) in enumerate(CHUNKS):
        for g in range(first, last):
            at_kv = slice(g * HD, (g + 1) * HD)
            columns = [g * group + c for c in range(0, group, HD)]
            d_rows = stacked([d_ref[:, c : c + HD] for c in columns])
            q_rows = stacked([q_ref[:, c : c + HD] for c in columns])
            d_keys = f32_dot(d_logits_refs[i][g - first], q_rows) * scaling
            d_values = f32_dot(probs_refs[i][g - first], d_rows)
            for index, grad in enumerate((d_keys, d_values)):
                own_grad_ref[index, :, at_kv] = grad[:tok]
                near_grad_refs[index][:, at_kv] = grad[tok : 2 * tok].astype(jnp.bfloat16)
                far_grad_ref[index, :, at_kv] = grad[2 * tok :].astype(jnp.bfloat16)
    for store in stores:
        store.wait()


def kv_grads_of(after, queries, d_attended, pieces, probs, d_logits, group):
    tok, width = queries.shape
    kv_width = width // group * HD
    operands = [queries, d_attended, *[p for p, _ in pieces], *probs, *d_logits]
    near_grad = jax.ShapeDtypeStruct((tok, kv_width), jnp.bfloat16)
    own_grad, far_grad = (jax.ShapeDtypeStruct((2, tok, kv_width), t) for t in (jnp.float32, jnp.bfloat16))
    return pl.pallas_call(
        functools.partial(kv_grads_kernel, group, [c for _, c in pieces]),
        in_specs=[pl.BlockSpec(memory_space=pl.ANY)] + [VMEM] * len(operands),
        out_specs=[HBM] + [VMEM] * 4,
        out_shape=[
            jax.ShapeDtypeStruct((tok, width), jnp.bfloat16), own_grad, near_grad, near_grad, far_grad,
        ],
        scratch_shapes=[pltpu.VMEM(p.shape[::-1], jnp.bfloat16) for p, _ in pieces]
        + [pltpu.SemaphoreType.DMA((len(pieces),))],
        compiler_params=params(),
        cost_estimate=cost(1),
        name="kv_grads",
    )(after, *operands)


def kv_total_kernel(shard_ref, own_ref, ahead_ref, *refs):
    *beside_refs, kv_ref, sum_ref, sem = refs
    for index, beside_ref in enumerate(beside_refs):
        total = own_ref[index] + ahead_ref[index].astype(jnp.float32)
        both = total + beside_ref[...].astype(jnp.float32)
        sum_ref[index] = jnp.where(shard_ref[0] % 2 == 0, both, total)
    store = pltpu.make_async_copy(sum_ref, kv_ref, sem)
    store.start()
    store.wait()


def kv_total_of(shard, own, ahead, beside):
    return pl.pallas_call(
        kv_total_kernel,
        in_specs=[SMEM] + [VMEM] * (2 + len(beside)),
        out_specs=HBM,
        out_shape=jax.ShapeDtypeStruct(own.shape, own.dtype),
        scratch_shapes=[pltpu.VMEM(own.shape, own.dtype), pltpu.SemaphoreType.DMA],
        compiler_params=params(),
        cost_estimate=cost(1),
        name="kv_total",
    )(shard, own, ahead, *beside)


def store_last_kernel(piece_ref, *refs):
    *_, whole_ref, _, _, sem = refs
    store = pltpu.make_async_copy(piece_ref, whole_ref, sem)
    store.start()
    store.wait()


def store_last(piece, *kept):
    return pl.pallas_call(
        store_last_kernel,
        in_specs=[VMEM, HBM, HBM],
        out_specs=[HBM, HBM, HBM],
        out_shape=[jax.ShapeDtypeStruct(x.shape, x.dtype) for x in (piece, *kept)],
        scratch_shapes=[pltpu.SemaphoreType.DMA],
        input_output_aliases={1: 1, 2: 2},
        compiler_params=params(),
        cost_estimate=cost(1),
        name="store_last",
    )(piece, *kept)


def core_swap(value, axis):
    return lax.ppermute(value, axis, [(i, i ^ 1) for i in range(lax.axis_size(axis))])


def per_device(stream_in, keys_values, out_weight, tile_mask, cotangent):
    queries, own, mask, cot = stream_in[0], keys_values[0], tile_mask[0], cotangent[0]
    weight = pltpu.with_memory_space_constraint(out_weight[0], pltpu.VMEM)
    width = queries.shape[1]
    group = width // (own.shape[-1] // HD)
    shard = lax.axis_index("seq").astype(jnp.int32).reshape(1)
    owns = cut(own)
    fars = [around(piece, "seq", 2) for piece in owns]
    d_attended, turned, kept = d_attended_of(cot, queries, weight, mask)
    pieces, probs, d_logits, nears = [], [], [], []
    after = d_attended
    for halo, (low, high) in enumerate(HALOS):
        chunks = [(first, last) for first, last in CHUNKS if low <= first < high]
        cuts = [((first - low) * HD, (last - first) * HD, last - first > 1) for first, last in chunks]
        picked = pick(shard, owns[halo], fars[halo], after, cuts)
        swapped = [core_swap(x, "seq") for x in picked]
        for first, last in chunks:
            near, swapped = swapped[: 1 + (last - first > 1)], swapped[1 + (last - first > 1) :]
            grad, p, d = in_grad_of(
                shard, turned, (owns[halo], near, fars[halo]), low, first, last, group,
                [pieces[0][0]] if first == CHUNKS[-1][0] else [],
            )
            nears.append(near)
            probs.append(p)
            d_logits.append(d)
            pieces.append((around(grad, "section", -1), first * group))
            after = grad
    result, attended = layer_out(kept, queries, weight, owns, fars, nears, probs, group)
    next_input = around(result, "section", 1)
    prev_grad, own_grad, *near_grad, far_grad = kv_grads_of(
        attended, queries, d_attended, pieces[:2], probs, d_logits, group
    )
    beside = [core_swap(x, "seq") for x in near_grad]
    prev_grad, behind = behind_of(shard, pieces[2], prev_grad, far_grad, beside)
    ahead = around(behind, "seq", -2)
    kv_total = kv_total_of(shard, own_grad, ahead, beside)
    next_input, prev_grad, kv_total = store_last(next_input, prev_grad, kv_total)
    return (next_input[None], prev_grad[None], kv_total[None])


def solution(mesh):
    return jax.shard_map(
        per_device,
        mesh=mesh,
        in_specs=(
            P("section", "seq", None),
            P("section", None, "seq", None),
            P("section", None, None),
            P("section", None, None),
            P("section", "seq", None),
        ),
        out_specs=(
            P("section", "seq", None),
            P("section", "seq", None),
            P("section", None, "seq", None),
        ),
        check_vma=False,
    )
```

```python
import functools
import math

import jax
import jax.numpy as jnp
from jax import lax
from jax.experimental import pallas as pl
from jax.experimental.pallas import tpu as pltpu
from jax.sharding import PartitionSpec as P

HD = 128
TILE = 128
HALOS = ((0, 1), (1, 4))
CHUNKS = ((0, 1), (1, 2), (2, 4))
CUT_FLOPS = 10**10
FLOOR = -1e30
ATT_FLOPS = {0: 2 * 10**8, 1: 1, 2: 10**10}
VMEM = pl.BlockSpec(memory_space=pltpu.VMEM)
HBM = pl.BlockSpec(memory_space=pltpu.HBM)
SMEM = pl.BlockSpec(memory_space=pltpu.SMEM)
VMEM_LIMIT = 32 * 1024 * 1024
NT = (((1,), (1,)), ((), ()))


def around(value, axis, by):
    length = lax.axis_size(axis)
    return lax.ppermute(value, axis, [(i, (i + by) % length) for i in range(length)])


def f32_dot(a, b, dims=(((1,), (0,)), ((), ()))):
    return lax.dot_general(a, b, dims, preferred_element_type=jnp.float32)


def params():
    return pltpu.CompilerParams(vmem_limit_bytes=VMEM_LIMIT)


def cost(flops):
    return pl.CostEstimate(flops=flops, bytes_accessed=1, transcendentals=0)


def prune(weight, kept_ref, row_tile, columns):
    strips = []
    for a in range(weight.shape[0] // TILE):
        row = kept_ref[row_tile + a : row_tile + a + 1, columns]
        kept = jnp.broadcast_to(row, (16, row.shape[1])).astype(weight.dtype)
        strip = weight[a * TILE : (a + 1) * TILE, :]
        strips.append(strip * jnp.concatenate([kept] * (TILE // 16), axis=0))
    return jnp.concatenate(strips, axis=0)


def cut_kernel(own_hbm, *refs):
    *piece_refs, sems = refs
    copies, column = [], 0
    for i, ref in enumerate(piece_refs):
        width = ref.shape[-1]
        source = own_hbm.at[:, :, column : column + width]
        copies.append(pltpu.make_async_copy(source, ref, sems.at[i]))
        column += width
    for copy in copies:
        copy.start()
    for copy in copies:
        copy.wait()


def cut(own):
    shapes = [own.shape[:2] + ((last - first) * HD,) for first, last in HALOS]
    return pl.pallas_call(
        cut_kernel,
        in_specs=[HBM],
        out_specs=[VMEM for _ in shapes],
        out_shape=[jax.ShapeDtypeStruct(shape, own.dtype) for shape in shapes],
        scratch_shapes=[pltpu.SemaphoreType.DMA((len(shapes),))],
        compiler_params=params(),
        cost_estimate=cost(CUT_FLOPS),
        name="cut",
    )(pltpu.with_memory_space_constraint(own, pltpu.HBM))


def d_attended_kernel(mask_ref, cot_ref, q_ref, weight_ref, out_ref, turned_ref, kept_ref):
    tiles = mask_ref.shape[0]
    width = kept_ref.shape[1]
    tile = lax.broadcasted_iota(jnp.int32, (tiles, width), 1) // TILE
    spread = (tile == lax.broadcasted_iota(jnp.int32, (tiles, width), 0)).astype(jnp.float32)
    kept_ref[...] = f32_dot((mask_ref[...] > 0).astype(jnp.float32), spread)
    rows = 4 * TILE
    for row in range(0, width, rows):
        weight = prune(weight_ref[row : row + rows, :], kept_ref, row // TILE, slice(None))
        part = f32_dot(cot_ref[...], weight, NT).astype(jnp.bfloat16)
        out_ref[:, row : row + rows] = part
        turned_ref[2, row : row + rows, :] = part.T
    turned_ref[0] = cot_ref[...].T
    turned_ref[1] = q_ref[...].T


def d_attended_of(cot, queries, weight, mask):
    tok, width = cot.shape
    return pl.pallas_call(
        d_attended_kernel,
        in_specs=[VMEM, VMEM, VMEM, VMEM],
        out_specs=[VMEM, VMEM, VMEM],
        out_shape=[
            jax.ShapeDtypeStruct((tok, width), jnp.bfloat16),
            jax.ShapeDtypeStruct((3, width, tok), jnp.bfloat16),
            jax.ShapeDtypeStruct((mask.shape[0], width), jnp.float32),
        ],
        compiler_params=params(),
        cost_estimate=cost(1),
        name="d_attended",
    )(mask, cot, queries, weight)


def pick_kernel(cuts, shard_ref, own_ref, far_ref, after_ref, *out_refs):
    odd = shard_ref[0] % 2 == 1

    def copy_from(source_ref):
        refs = list(out_refs)
        for start, width, split in cuts:
            at = slice(start, start + width)
            if split:
                for index in range(2):
                    refs.pop(0)[...] = source_ref[index, :, at]
            else:
                refs.pop(0)[...] = source_ref[:, :, at]

    @pl.when(odd)
    def _():
        copy_from(far_ref)

    @pl.when(jnp.logical_not(odd))
    def _():
        copy_from(own_ref)


def pick(shard, own, far, after, cuts):
    shapes = []
    for _, width, split in cuts:
        shape = (own.shape[1], width)
        shapes += [shape, shape] if split else [(2,) + shape]
    return pl.pallas_call(
        functools.partial(pick_kernel, cuts),
        in_specs=[SMEM, VMEM, VMEM, pl.BlockSpec(memory_space=pl.ANY)],
        out_specs=[VMEM for _ in shapes],
        out_shape=[jax.ShapeDtypeStruct(shape, own.dtype) for shape in shapes],
        compiler_params=params(),
        cost_estimate=cost(1),
        name="pick",
    )(shard, own, far, after)


def store_piece(piece, column, turned_ref, whole_ref, sem):
    turned_ref[...] = piece.T
    store = pltpu.make_async_copy(
        turned_ref, whole_ref.at[:, column : column + turned_ref.shape[1]], sem
    )
    store.start()
    return store


def behind_kernel(column, shard_ref, piece_ref, given_ref, far_ref, *refs):
    *beside_refs, whole_ref, out_ref, turned_ref, sem = refs
    store = store_piece(piece_ref[...], column, turned_ref, whole_ref, sem)
    for index, beside_ref in enumerate(beside_refs):
        far = far_ref[index].astype(jnp.float32)
        both = far + beside_ref[...].astype(jnp.float32)
        out_ref[index] = jnp.where(shard_ref[0] % 2 == 1, both, far).astype(jnp.bfloat16)
    store.wait()


def behind_of(shard, piece, given, far, beside):
    return pl.pallas_call(
        functools.partial(behind_kernel, piece[1]),
        in_specs=[SMEM, VMEM, HBM, VMEM] + [VMEM] * len(beside),
        out_specs=[HBM, VMEM],
        out_shape=[
            jax.ShapeDtypeStruct(given.shape, given.dtype),
            jax.ShapeDtypeStruct(far.shape, far.dtype),
        ],
        scratch_shapes=[pltpu.VMEM(piece[0].shape[::-1], jnp.bfloat16), pltpu.SemaphoreType.DMA],
        input_output_aliases={2: 0},
        compiler_params=params(),
        cost_estimate=cost(1),
        name="behind",
    )(shard, piece[0], given, far, *beside)


def stacked(parts, axis=0):
    return jnp.concatenate(parts, axis=axis)


def blocks_of(own_ref, near_refs, far_ref, index, at, near_head):
    near_at = slice(near_head * HD, (near_head + 1) * HD)
    near = near_refs[index][:, near_at] if len(near_refs) == 2 else near_refs[0][index, :, near_at]
    return stacked([own_ref[index, :, at], near, far_ref[index, :, at]])


def causal_mask(tok):
    key_at = lax.broadcasted_iota(jnp.int32, (tok, tok), 0)
    row_at = lax.broadcasted_iota(jnp.int32, (tok, tok), 1)
    return key_at <= row_at


def edge_group(far_ok, q_columns, d_columns, keys, values):
    tok = keys.shape[0] // 2
    heads = q_columns.shape[1] // tok
    causal = jnp.concatenate([causal_mask(tok)] * heads, axis=1)
    logits = f32_dot(keys, q_columns)
    d_probs = f32_dot(values, d_columns)
    far_logits = jnp.where(far_ok, logits[tok:], jnp.float32(FLOOR))
    return (
        jnp.where(causal, logits[:tok], far_logits),
        jnp.where(causal, d_probs[:tok], d_probs[tok:]),
    )


def in_grad_group(near_ok, edge_l, edge_d, q_columns, d_columns, near_k, near_v, keys):
    tok = near_k.shape[0]
    scaling = HD ** (-0.5)
    factor = scaling * math.log2(math.e)
    causal = causal_mask(tok).astype(jnp.float32)
    lower = causal.astype(jnp.bfloat16)
    upper = (1.0 - causal).astype(jnp.bfloat16)
    near_l = f32_dot(near_k, q_columns)
    near_d = f32_dot(near_v, d_columns)
    parts = []
    for h in range(q_columns.shape[1] // tok):
        at = slice(h * tok, (h + 1) * tok)
        edge = edge_l[:, at]
        near = jnp.where(near_ok, near_l[:, at], jnp.float32(FLOOR))
        top = jnp.max(jnp.maximum(edge, near), axis=0, keepdims=True)
        edge = jnp.exp2((edge - top) * factor)
        near = jnp.exp2((near - top) * factor)
        inverse = 1.0 / jnp.sum(edge + near, axis=0, keepdims=True)
        edge = edge * inverse
        near = near * inverse
        row_dot = jnp.sum(edge * edge_d[:, at] + near * near_d[:, at], axis=0, keepdims=True)
        d_edge = (edge * (edge_d[:, at] - row_dot)).astype(jnp.bfloat16)
        d_near = (near * (near_d[:, at] - row_dot)).astype(jnp.bfloat16)
        edge = edge.astype(jnp.bfloat16)
        parts.append(
            (
                stacked([edge * lower, near.astype(jnp.bfloat16), edge * upper]),
                stacked([d_edge * lower, d_near, d_edge * upper]),
            )
        )
    probs = stacked([p for p, _ in parts], axis=1)
    d_logits = stacked([d for _, d in parts], axis=1)
    return f32_dot(keys.T, d_logits) * scaling, probs, d_logits


def head_columns(turned_ref, g, group):
    rows = [slice(g * group + c, g * group + c + HD) for c in range(0, group, HD)]
    q_columns = stacked([turned_ref[1, row, :] for row in rows], axis=1)
    d_columns = stacked([turned_ref[2, row, :] for row in rows], axis=1)
    return rows, q_columns, d_columns


def edge_of_head(shard, own_ref, far_ref, at, q_columns, d_columns):
    keys, values = (stacked([own_ref[i, :, at], far_ref[i, :, at]]) for i in range(2))
    return edge_group(shard >= 2, q_columns, d_columns, keys, values)


def edge_kernel(low, first, last, group, shard_ref, turned_ref, own_ref, far_ref, logits_ref, d_probs_ref):
    for g in range(first, last):
        at = slice((g - low) * HD, (g - low + 1) * HD)
        _, q_columns, d_columns = head_columns(turned_ref, g, group)
        logits_ref[g - first], d_probs_ref[g - first] = edge_of_head(
            shard_ref[0], own_ref, far_ref, at, q_columns, d_columns
        )


def edge_of(shard, turned, own, far, low, first, last, group):
    tok = turned.shape[-1]
    inside = jax.ShapeDtypeStruct((last - first, tok, tok * group // HD), jnp.float32)
    return pl.pallas_call(
        functools.partial(edge_kernel, low, first, last, group),
        in_specs=[SMEM] + [VMEM] * 3,
        out_specs=[VMEM] * 2,
        out_shape=[inside, inside],
        compiler_params=params(),
        cost_estimate=cost(1),
        name="edge",
    )(shard, turned, own, far)


def in_grad_kernel(low, first, last, group, nears, edges, shard_ref, turned_ref, *refs):
    own_ref, *refs = refs
    near_refs, far_ref, *refs = refs[:nears], *refs[nears:]
    edge_refs = refs[:edges]
    grad_ref, probs_ref, d_logits_ref = refs[-3:]
    tok = own_ref.shape[1]
    shard = shard_ref[0]
    for g in range(first, last):
        at = slice((g - low) * HD, (g - low + 1) * HD)
        rows, q_columns, d_columns = head_columns(turned_ref, g, group)
        if edges:
            edge_l, edge_d = (ref[g - first] for ref in edge_refs)
        else:
            edge_l, edge_d = edge_of_head(shard, own_ref, far_ref, at, q_columns, d_columns)
        keys = blocks_of(own_ref, near_refs, far_ref, 0, at, g - first)
        values = blocks_of(own_ref, near_refs, far_ref, 1, at, g - first)
        d_queries, probs, d_logits = in_grad_group(
            shard >= 1, edge_l, edge_d, q_columns, d_columns,
            keys[tok : 2 * tok], values[tok : 2 * tok], keys,
        )
        probs_ref[g - first] = probs
        d_logits_ref[g - first] = d_logits
        for h, row in enumerate(rows):
            out = slice(row.start - first * group, row.stop - first * group)
            grad_ref[out, :] = (
                turned_ref[0, row, :].astype(jnp.float32) + d_queries[:, h * tok : (h + 1) * tok]
            ).astype(jnp.bfloat16)


def in_grad_of(shard, turned, block, edge, low, first, last, group, after):
    tok = turned.shape[-1]
    count = last - first
    inside = jax.ShapeDtypeStruct((count, 3 * tok, tok * group // HD), jnp.bfloat16)
    own, near, far = block
    return pl.pallas_call(
        functools.partial(in_grad_kernel, low, first, last, group, len(near), len(edge)),
        in_specs=[SMEM] + [VMEM] * (3 + len(near) + len(edge)) + [pl.BlockSpec(memory_space=pl.ANY)] * len(after),
        out_specs=[VMEM] * 3,
        out_shape=[jax.ShapeDtypeStruct((count * group, tok), jnp.bfloat16), inside, inside],
        compiler_params=params(),
        cost_estimate=cost(ATT_FLOPS[first]),
        name="in_grad",
    )(shard, turned, own, *near, far, *edge, *after)


def mixed_columns(attended, weight_ref, kept_ref, q_ref, out_ref):
    step = 4 * TILE
    for column in range(0, out_ref.shape[1], step):
        at = slice(column, column + step)
        weight = prune(weight_ref[:, at], kept_ref, 0, at)
        mixed = f32_dot(attended, weight)
        out_ref[:, at] = (q_ref[:, at].astype(jnp.float32) + mixed).astype(jnp.bfloat16)


def layer_out_kernel(group, nears, *refs):
    kept_ref, q_ref, weight_ref, *refs = refs
    owns, refs = refs[: len(HALOS)], refs[len(HALOS) :]
    fars, refs = refs[: len(HALOS)], refs[len(HALOS) :]
    near_refs = []
    for count in nears:
        near_refs.append(refs[:count])
        refs = refs[count:]
    *probs_refs, out_ref, attended_ref = refs
    tok = q_ref.shape[0]
    for i, (first, last) in enumerate(CHUNKS):
        for g in range(first, last):
            halo = [j for j, (low, high) in enumerate(HALOS) if low <= g < high][0]
            at = slice((g - HALOS[halo][0]) * HD, (g - HALOS[halo][0] + 1) * HD)
            values = blocks_of(owns[halo], near_refs[i], fars[halo], 1, at, g - first)
            attended = f32_dot(values.T, probs_refs[i][g - first]).astype(jnp.bfloat16)
            for h in range(group // HD):
                c = g * group + h * HD
                attended_ref[:, c : c + HD] = attended[:, h * tok : (h + 1) * tok].T
    mixed_columns(attended_ref[...], weight_ref, kept_ref, q_ref, out_ref)


def layer_out(kept, queries, weight, owns, fars, nears, probs, group):
    tok, width = queries.shape
    operands = [kept, queries, weight, *owns, *fars, *[x for near in nears for x in near], *probs]
    return pl.pallas_call(
        functools.partial(layer_out_kernel, group, [len(near) for near in nears]),
        in_specs=[VMEM] * len(operands),
        out_specs=[VMEM, VMEM],
        out_shape=[
            jax.ShapeDtypeStruct((tok, width), jnp.bfloat16),
            jax.ShapeDtypeStruct((tok, width), jnp.bfloat16),
        ],
        compiler_params=params(),
        cost_estimate=cost(1),
        name="layer_out",
    )(*operands)


def kv_grads_kernel(group, stored, *refs):
    after_ref, q_ref, d_ref, *refs = refs
    piece_refs, refs = refs[: len(stored)], refs[len(stored) :]
    probs_refs, refs = refs[: len(CHUNKS)], refs[len(CHUNKS) :]
    d_logits_refs, refs = refs[: len(CHUNKS)], refs[len(CHUNKS) :]
    whole_ref, own_grad_ref, *near_grad_refs, far_grad_ref = refs[:5]
    *turned_refs, sems = refs[5:]
    tok = q_ref.shape[0]
    scaling = HD ** (-0.5)
    stores = [
        store_piece(piece_ref[...], column, turned_ref, whole_ref, sems.at[i])
        for i, (piece_ref, column, turned_ref) in enumerate(zip(piece_refs, stored, turned_refs))
    ]
    for i, (first, last) in enumerate(CHUNKS):
        for g in range(first, last):
            at_kv = slice(g * HD, (g + 1) * HD)
            columns = [g * group + c for c in range(0, group, HD)]
            d_rows = stacked([d_ref[:, c : c + HD] for c in columns])
            q_rows = stacked([q_ref[:, c : c + HD] for c in columns])
            d_keys = f32_dot(d_logits_refs[i][g - first], q_rows) * scaling
            d_values = f32_dot(probs_refs[i][g - first], d_rows)
            for index, grad in enumerate((d_keys, d_values)):
                own_grad_ref[index, :, at_kv] = grad[:tok]
                near_grad_refs[index][:, at_kv] = grad[tok : 2 * tok].astype(jnp.bfloat16)
                far_grad_ref[index, :, at_kv] = grad[2 * tok :].astype(jnp.bfloat16)
    for store in stores:
        store.wait()


def kv_grads_of(after, queries, d_attended, pieces, probs, d_logits, group):
    tok, width = queries.shape
    kv_width = width // group * HD
    operands = [queries, d_attended, *[p for p, _ in pieces], *probs, *d_logits]
    near_grad = jax.ShapeDtypeStruct((tok, kv_width), jnp.bfloat16)
    own_grad, far_grad = (jax.ShapeDtypeStruct((2, tok, kv_width), t) for t in (jnp.float32, jnp.bfloat16))
    return pl.pallas_call(
        functools.partial(kv_grads_kernel, group, [c for _, c in pieces]),
        in_specs=[pl.BlockSpec(memory_space=pl.ANY)] + [VMEM] * len(operands),
        out_specs=[HBM] + [VMEM] * 4,
        out_shape=[
            jax.ShapeDtypeStruct((tok, width), jnp.bfloat16), own_grad, near_grad, near_grad, far_grad,
        ],
        scratch_shapes=[pltpu.VMEM(p.shape[::-1], jnp.bfloat16) for p, _ in pieces]
        + [pltpu.SemaphoreType.DMA((len(pieces),))],
        compiler_params=params(),
        cost_estimate=cost(1),
        name="kv_grads",
    )(after, *operands)


def kv_total_kernel(shard_ref, own_ref, ahead_ref, *refs):
    *beside_refs, kv_ref, sum_ref, sem = refs
    for index, beside_ref in enumerate(beside_refs):
        total = own_ref[index] + ahead_ref[index].astype(jnp.float32)
        both = total + beside_ref[...].astype(jnp.float32)
        sum_ref[index] = jnp.where(shard_ref[0] % 2 == 0, both, total)
    store = pltpu.make_async_copy(sum_ref, kv_ref, sem)
    store.start()
    store.wait()


def kv_total_of(shard, own, ahead, beside):
    return pl.pallas_call(
        kv_total_kernel,
        in_specs=[SMEM] + [VMEM] * (2 + len(beside)),
        out_specs=HBM,
        out_shape=jax.ShapeDtypeStruct(own.shape, own.dtype),
        scratch_shapes=[pltpu.VMEM(own.shape, own.dtype), pltpu.SemaphoreType.DMA],
        compiler_params=params(),
        cost_estimate=cost(1),
        name="kv_total",
    )(shard, own, ahead, *beside)


def store_last_kernel(piece_ref, *refs):
    *_, whole_ref, _, _, sem = refs
    store = pltpu.make_async_copy(piece_ref, whole_ref, sem)
    store.start()
    store.wait()


def store_last(piece, *kept):
    return pl.pallas_call(
        store_last_kernel,
        in_specs=[VMEM, HBM, HBM],
        out_specs=[HBM, HBM, HBM],
        out_shape=[jax.ShapeDtypeStruct(x.shape, x.dtype) for x in (piece, *kept)],
        scratch_shapes=[pltpu.SemaphoreType.DMA],
        input_output_aliases={1: 1, 2: 2},
        compiler_params=params(),
        cost_estimate=cost(1),
        name="store_last",
    )(piece, *kept)


def core_swap(value, axis):
    return lax.ppermute(value, axis, [(i, i ^ 1) for i in range(lax.axis_size(axis))])


def per_device(stream_in, keys_values, out_weight, tile_mask, cotangent):
    queries, own, mask, cot = stream_in[0], keys_values[0], tile_mask[0], cotangent[0]
    weight = pltpu.with_memory_space_constraint(out_weight[0], pltpu.VMEM)
    width = queries.shape[1]
    group = width // (own.shape[-1] // HD)
    shard = lax.axis_index("seq").astype(jnp.int32).reshape(1)
    owns = cut(own)
    fars = [around(piece, "seq", 2) for piece in owns]
    d_attended, turned, kept = d_attended_of(cot, queries, weight, mask)
    pieces, probs, d_logits, nears = [], [], [], []
    after = d_attended
    for halo, (low, high) in enumerate(HALOS):
        chunks = [(first, last) for first, last in CHUNKS if low <= first < high]
        cuts = [((first - low) * HD, (last - first) * HD, last - first > 1) for first, last in chunks]
        picked = pick(shard, owns[halo], fars[halo], after, cuts)
        swapped = [core_swap(x, "seq") for x in picked]
        for first, last in chunks:
            near, swapped = swapped[: 1 + (last - first > 1)], swapped[1 + (last - first > 1) :]
            edge = []
            if first != CHUNKS[-1][0]:
                edge = edge_of(shard, turned, owns[halo], fars[halo], low, first, last, group)
            grad, p, d = in_grad_of(
                shard, turned, (owns[halo], near, fars[halo]), edge, low, first, last, group,
                [pieces[0][0]] if first == CHUNKS[-1][0] else [],
            )
            nears.append(near)
            probs.append(p)
            d_logits.append(d)
            pieces.append((around(grad, "section", -1), first * group))
            after = grad
    result, attended = layer_out(kept, queries, weight, owns, fars, nears, probs, group)
    next_input = around(result, "section", 1)
    prev_grad, own_grad, *near_grad, far_grad = kv_grads_of(
        attended, queries, d_attended, pieces[:2], probs, d_logits, group
    )
    beside = [core_swap(x, "seq") for x in near_grad]
    prev_grad, behind = behind_of(shard, pieces[2], prev_grad, far_grad, beside)
    ahead = around(behind, "seq", -2)
    kv_total = kv_total_of(shard, own_grad, ahead, beside)
    next_input, prev_grad, kv_total = store_last(next_input, prev_grad, kv_total)
    return (next_input[None], prev_grad[None], kv_total[None])


def solution(mesh):
    return jax.shard_map(
        per_device,
        mesh=mesh,
        in_specs=(
            P("section", "seq", None),
            P("section", None, "seq", None),
            P("section", None, None),
            P("section", None, None),
            P("section", "seq", None),
        ),
        out_specs=(
            P("section", "seq", None),
            P("section", "seq", None),
            P("section", None, "seq", None),
        ),
        check_vma=False,
    )
```

```python
import functools
import math

import jax
import jax.numpy as jnp
from jax import lax
from jax.experimental import pallas as pl
from jax.experimental.pallas import tpu as pltpu
from jax.sharding import PartitionSpec as P

HD = 128
TILE = 128
HALOS = ((0, 1), (1, 2), (2, 4))
CHUNKS = ((0, 1), (1, 2), (2, 4))
CUT_FLOPS = 10**10
SPLIT = ((0, 1), (2, 4))
ATT_FLOPS = {0: 5 * 10**7, 1: 1, 2: 10**10}
VMEM = pl.BlockSpec(memory_space=pltpu.VMEM)
HBM = pl.BlockSpec(memory_space=pltpu.HBM)
SMEM = pl.BlockSpec(memory_space=pltpu.SMEM)
VMEM_LIMIT = 32 * 1024 * 1024
NT = (((1,), (1,)), ((), ()))


def around(value, axis, by):
    length = lax.axis_size(axis)
    return lax.ppermute(value, axis, [(i, (i + by) % length) for i in range(length)])


def f32_dot(a, b, dims=(((1,), (0,)), ((), ()))):
    return lax.dot_general(a, b, dims, preferred_element_type=jnp.float32)


def params():
    return pltpu.CompilerParams(vmem_limit_bytes=VMEM_LIMIT)


def cost(flops):
    return pl.CostEstimate(flops=flops, bytes_accessed=1, transcendentals=0)


def prune(weight, kept_ref, row_tile, columns):
    strips = []
    for a in range(weight.shape[0] // TILE):
        row = kept_ref[row_tile + a : row_tile + a + 1, columns]
        kept = jnp.broadcast_to(row, (16, row.shape[1])).astype(weight.dtype)
        strip = weight[a * TILE : (a + 1) * TILE, :]
        strips.append(strip * jnp.concatenate([kept] * (TILE // 16), axis=0))
    return jnp.concatenate(strips, axis=0)


def cut_kernel(own_hbm, *refs):
    *piece_refs, sems = refs
    copies, column = [], 0
    for i, ref in enumerate(piece_refs):
        width = ref.shape[-1]
        source = own_hbm.at[:, :, column : column + width]
        copies.append(pltpu.make_async_copy(source, ref, sems.at[i]))
        column += width
    for copy in copies:
        copy.start()
    for copy in copies:
        copy.wait()


def cut(own):
    shapes = [own.shape[:2] + ((last - first) * HD,) for first, last in HALOS]
    return pl.pallas_call(
        cut_kernel,
        in_specs=[HBM],
        out_specs=[VMEM for _ in shapes],
        out_shape=[jax.ShapeDtypeStruct(shape, own.dtype) for shape in shapes],
        scratch_shapes=[pltpu.SemaphoreType.DMA((len(shapes),))],
        compiler_params=params(),
        cost_estimate=cost(CUT_FLOPS),
        name="cut",
    )(pltpu.with_memory_space_constraint(own, pltpu.HBM))


def d_attended_kernel(mask_ref, cot_ref, q_ref, weight_ref, out_ref, turned_ref, kept_ref):
    tiles = mask_ref.shape[0]
    width = kept_ref.shape[1]
    tile = lax.broadcasted_iota(jnp.int32, (tiles, width), 1) // TILE
    spread = (tile == lax.broadcasted_iota(jnp.int32, (tiles, width), 0)).astype(jnp.float32)
    kept_ref[...] = f32_dot((mask_ref[...] > 0).astype(jnp.float32), spread)
    rows = 4 * TILE
    for row in range(0, width, rows):
        weight = prune(weight_ref[row : row + rows, :], kept_ref, row // TILE, slice(None))
        part = f32_dot(cot_ref[...], weight, NT).astype(jnp.bfloat16)
        out_ref[:, row : row + rows] = part
        turned_ref[2, row : row + rows, :] = part.T
    turned_ref[0] = cot_ref[...].T
    turned_ref[1] = q_ref[...].T


def d_attended_of(cot, queries, weight, mask):
    tok, width = cot.shape
    return pl.pallas_call(
        d_attended_kernel,
        in_specs=[VMEM, VMEM, VMEM, VMEM],
        out_specs=[VMEM, VMEM, VMEM],
        out_shape=[
            jax.ShapeDtypeStruct((tok, width), jnp.bfloat16),
            jax.ShapeDtypeStruct((3, width, tok), jnp.bfloat16),
            jax.ShapeDtypeStruct((mask.shape[0], width), jnp.float32),
        ],
        compiler_params=params(),
        cost_estimate=cost(1),
        name="d_attended",
    )(mask, cot, queries, weight)


def pick_kernel(cuts, shard_ref, own_ref, far_ref, after_ref, *out_refs):
    odd = shard_ref[0] % 2 == 1

    def copy_from(source_ref):
        refs = list(out_refs)
        for start, width, split in cuts:
            at = slice(start, start + width)
            if split:
                for index in range(2):
                    refs.pop(0)[...] = source_ref[index, :, at]
            else:
                refs.pop(0)[...] = source_ref[:, :, at]

    @pl.when(odd)
    def _():
        copy_from(far_ref)

    @pl.when(jnp.logical_not(odd))
    def _():
        copy_from(own_ref)


def pick(shard, own, far, after, cuts):
    shapes = []
    for _, width, split in cuts:
        shape = (own.shape[1], width)
        shapes += [shape, shape] if split else [(2,) + shape]
    return pl.pallas_call(
        functools.partial(pick_kernel, cuts),
        in_specs=[SMEM, VMEM, VMEM, pl.BlockSpec(memory_space=pl.ANY)],
        out_specs=[VMEM for _ in shapes],
        out_shape=[jax.ShapeDtypeStruct(shape, own.dtype) for shape in shapes],
        compiler_params=params(),
        cost_estimate=cost(1),
        name="pick",
    )(shard, own, far, after)


def store_piece(piece, column, turned_ref, whole_ref, sem):
    turned_ref[...] = piece.T
    store = pltpu.make_async_copy(
        turned_ref, whole_ref.at[:, column : column + turned_ref.shape[1]], sem
    )
    store.start()
    return store


def behind_kernel(column, shard_ref, piece_ref, given_ref, far_ref, *refs):
    *beside_refs, whole_ref, out_ref, turned_ref, sem = refs
    store = store_piece(piece_ref[...], column, turned_ref, whole_ref, sem)
    for index, beside_ref in enumerate(beside_refs):
        far = far_ref[index].astype(jnp.float32)
        both = far + beside_ref[...].astype(jnp.float32)
        out_ref[index] = jnp.where(shard_ref[0] % 2 == 1, both, far).astype(jnp.bfloat16)
    store.wait()


def behind_of(shard, piece, given, far, beside):
    return pl.pallas_call(
        functools.partial(behind_kernel, piece[1]),
        in_specs=[SMEM, VMEM, HBM, VMEM] + [VMEM] * len(beside),
        out_specs=[HBM, VMEM],
        out_shape=[
            jax.ShapeDtypeStruct(given.shape, given.dtype),
            jax.ShapeDtypeStruct(far.shape, far.dtype),
        ],
        scratch_shapes=[pltpu.VMEM(piece[0].shape[::-1], jnp.bfloat16), pltpu.SemaphoreType.DMA],
        input_output_aliases={2: 0},
        compiler_params=params(),
        cost_estimate=cost(1),
        name="behind",
    )(shard, piece[0], given, far, *beside)


def stacked(parts, axis=0):
    return jnp.concatenate(parts, axis=axis)


def blocks_of(own_ref, near_refs, far_ref, index, at, near_head):
    near_at = slice(near_head * HD, (near_head + 1) * HD)
    near = near_refs[index][:, near_at] if len(near_refs) == 2 else near_refs[0][index, :, near_at]
    return stacked([own_ref[index, :, at], near, far_ref[index, :, at]])


def in_grad_group(near_ok, far_ok, q_columns, d_columns, keys, values):
    tok = keys.shape[0] // 3
    scaling = HD ** (-0.5)
    factor = scaling * math.log2(math.e)
    floor = jnp.float32(-1e30)
    key_at = lax.broadcasted_iota(jnp.int32, (tok, tok), 0)
    row_at = lax.broadcasted_iota(jnp.int32, (tok, tok), 1)
    causal = key_at <= row_at
    lower = causal.astype(jnp.float32).astype(jnp.bfloat16)
    upper = (1.0 - causal.astype(jnp.float32)).astype(jnp.bfloat16)
    logits = f32_dot(keys, q_columns)
    d_probs = f32_dot(values, d_columns)
    own_l, near_l, far_l = (logits[i * tok : (i + 1) * tok] for i in range(3))
    own_d, near_d, far_d = (d_probs[i * tok : (i + 1) * tok] for i in range(3))
    parts = []
    for h in range(q_columns.shape[1] // tok):
        at = slice(h * tok, (h + 1) * tok)
        edge = jnp.where(causal, own_l[:, at], jnp.where(far_ok, far_l[:, at], floor))
        near = jnp.where(near_ok, near_l[:, at], floor)
        top = jnp.max(jnp.maximum(edge, near), axis=0, keepdims=True)
        edge = jnp.exp2((edge - top) * factor)
        near = jnp.exp2((near - top) * factor)
        inverse = 1.0 / jnp.sum(edge + near, axis=0, keepdims=True)
        edge = edge * inverse
        near = near * inverse
        edge_d = jnp.where(causal, own_d[:, at], far_d[:, at])
        row_dot = jnp.sum(edge * edge_d + near * near_d[:, at], axis=0, keepdims=True)
        d_edge = (edge * (edge_d - row_dot)).astype(jnp.bfloat16)
        d_near = (near * (near_d[:, at] - row_dot)).astype(jnp.bfloat16)
        edge = edge.astype(jnp.bfloat16)
        parts.append(
            (
                stacked([edge * lower, near.astype(jnp.bfloat16), edge * upper]),
                stacked([d_edge * lower, d_near, d_edge * upper]),
            )
        )
    probs = stacked([p for p, _ in parts], axis=1)
    d_logits = stacked([d for _, d in parts], axis=1)
    return f32_dot(keys.T, d_logits) * scaling, probs, d_logits


def in_grad_kernel(low, first, last, group, nears, shard_ref, turned_ref, *refs):
    own_ref, *refs = refs
    near_refs, far_ref = refs[:nears], refs[nears]
    grad_ref, probs_ref, d_logits_ref = refs[-3:]
    tok = own_ref.shape[1]
    shard = shard_ref[0]
    for g in range(first, last):
        at = slice((g - low) * HD, (g - low + 1) * HD)
        rows = [slice(g * group + c, g * group + c + HD) for c in range(0, group, HD)]
        d_queries, probs, d_logits = in_grad_group(
            shard >= 1,
            shard >= 2,
            stacked([turned_ref[1, row, :] for row in rows], axis=1),
            stacked([turned_ref[2, row, :] for row in rows], axis=1),
            blocks_of(own_ref, near_refs, far_ref, 0, at, g - first),
            blocks_of(own_ref, near_refs, far_ref, 1, at, g - first),
        )
        probs_ref[g - first] = probs
        d_logits_ref[g - first] = d_logits
        for h, row in enumerate(rows):
            out = slice(row.start - first * group, row.stop - first * group)
            grad_ref[out, :] = (
                turned_ref[0, row, :].astype(jnp.float32) + d_queries[:, h * tok : (h + 1) * tok]
            ).astype(jnp.bfloat16)


def in_grad_of(shard, turned, block, low, first, last, group, after):
    tok = turned.shape[-1]
    count = last - first
    inside = jax.ShapeDtypeStruct((count, 3 * tok, tok * group // HD), jnp.bfloat16)
    own, near, far = block
    return pl.pallas_call(
        functools.partial(in_grad_kernel, low, first, last, group, len(near)),
        in_specs=[SMEM] + [VMEM] * (3 + len(near)) + [pl.BlockSpec(memory_space=pl.ANY)] * len(after),
        out_specs=[VMEM] * 3,
        out_shape=[jax.ShapeDtypeStruct((count * group, tok), jnp.bfloat16), inside, inside],
        compiler_params=params(),
        cost_estimate=cost(ATT_FLOPS[first]),
        name="in_grad",
    )(shard, turned, own, *near, far, *after)


def mixed_columns(attended, weight_ref, kept_ref, q_ref, out_ref):
    step = 4 * TILE
    for column in range(0, out_ref.shape[1], step):
        at = slice(column, column + step)
        weight = prune(weight_ref[:, at], kept_ref, 0, at)
        mixed = f32_dot(attended, weight)
        out_ref[:, at] = (q_ref[:, at].astype(jnp.float32) + mixed).astype(jnp.bfloat16)


def layer_out_kernel(group, nears, *refs):
    kept_ref, q_ref, weight_ref, *refs = refs
    owns, refs = refs[: len(HALOS)], refs[len(HALOS) :]
    fars, refs = refs[: len(HALOS)], refs[len(HALOS) :]
    near_refs = []
    for count in nears:
        near_refs.append(refs[:count])
        refs = refs[count:]
    *probs_refs, out_ref, attended_ref = refs
    tok = q_ref.shape[0]
    for i, (first, last) in enumerate(CHUNKS):
        for g in range(first, last):
            halo = [j for j, (low, high) in enumerate(HALOS) if low <= g < high][0]
            at = slice((g - HALOS[halo][0]) * HD, (g - HALOS[halo][0] + 1) * HD)
            values = blocks_of(owns[halo], near_refs[i], fars[halo], 1, at, g - first)
            attended = f32_dot(values.T, probs_refs[i][g - first]).astype(jnp.bfloat16)
            for h in range(group // HD):
                c = g * group + h * HD
                attended_ref[:, c : c + HD] = attended[:, h * tok : (h + 1) * tok].T
    mixed_columns(attended_ref[...], weight_ref, kept_ref, q_ref, out_ref)


def layer_out(kept, queries, weight, owns, fars, nears, probs, group):
    tok, width = queries.shape
    operands = [kept, queries, weight, *owns, *fars, *[x for near in nears for x in near], *probs]
    return pl.pallas_call(
        functools.partial(layer_out_kernel, group, [len(near) for near in nears]),
        in_specs=[VMEM] * len(operands),
        out_specs=[VMEM, VMEM],
        out_shape=[
            jax.ShapeDtypeStruct((tok, width), jnp.bfloat16),
            jax.ShapeDtypeStruct((tok, width), jnp.bfloat16),
        ],
        compiler_params=params(),
        cost_estimate=cost(1),
        name="layer_out",
    )(*operands)


def kv_grads_kernel(group, stored, *refs):
    after_ref, q_ref, d_ref, *refs = refs
    piece_refs, refs = refs[: len(stored)], refs[len(stored) :]
    probs_refs, refs = refs[: len(CHUNKS)], refs[len(CHUNKS) :]
    d_logits_refs, refs = refs[: len(CHUNKS)], refs[len(CHUNKS) :]
    whole_ref, own_grad_ref, *near_grad_refs, far_grad_ref = refs[:5]
    *turned_refs, sems = refs[5:]
    tok = q_ref.shape[0]
    scaling = HD ** (-0.5)
    stores = [
        store_piece(piece_ref[...], column, turned_ref, whole_ref, sems.at[i])
        for i, (piece_ref, column, turned_ref) in enumerate(zip(piece_refs, stored, turned_refs))
    ]
    for i, (first, last) in enumerate(CHUNKS):
        for g in range(first, last):
            at_kv = slice(g * HD, (g + 1) * HD)
            columns = [g * group + c for c in range(0, group, HD)]
            d_rows = stacked([d_ref[:, c : c + HD] for c in columns])
            q_rows = stacked([q_ref[:, c : c + HD] for c in columns])
            d_keys = f32_dot(d_logits_refs[i][g - first], q_rows) * scaling
            d_values = f32_dot(probs_refs[i][g - first], d_rows)
            for index, grad in enumerate((d_keys, d_values)):
                own_grad_ref[index, :, at_kv] = grad[:tok]
                near_grad_refs[index][:, at_kv] = grad[tok : 2 * tok].astype(jnp.bfloat16)
                far_grad_ref[index, :, at_kv] = grad[2 * tok :].astype(jnp.bfloat16)
    for store in stores:
        store.wait()


def kv_grads_of(after, queries, d_attended, pieces, probs, d_logits, group):
    tok, width = queries.shape
    kv_width = width // group * HD
    operands = [queries, d_attended, *[p for p, _ in pieces], *probs, *d_logits]
    near_grad = jax.ShapeDtypeStruct((tok, kv_width), jnp.bfloat16)
    own_grad, far_grad = (jax.ShapeDtypeStruct((2, tok, kv_width), t) for t in (jnp.float32, jnp.bfloat16))
    return pl.pallas_call(
        functools.partial(kv_grads_kernel, group, [c for _, c in pieces]),
        in_specs=[pl.BlockSpec(memory_space=pl.ANY)] + [VMEM] * len(operands),
        out_specs=[HBM] + [VMEM] * 4,
        out_shape=[
            jax.ShapeDtypeStruct((tok, width), jnp.bfloat16), own_grad, near_grad, near_grad, far_grad,
        ],
        scratch_shapes=[pltpu.VMEM(p.shape[::-1], jnp.bfloat16) for p, _ in pieces]
        + [pltpu.SemaphoreType.DMA((len(pieces),))],
        compiler_params=params(),
        cost_estimate=cost(1),
        name="kv_grads",
    )(after, *operands)


def kv_total_kernel(shard_ref, own_ref, ahead_ref, *refs):
    *beside_refs, kv_ref, sum_ref, sem = refs
    for index, beside_ref in enumerate(beside_refs):
        total = own_ref[index] + ahead_ref[index].astype(jnp.float32)
        both = total + beside_ref[...].astype(jnp.float32)
        sum_ref[index] = jnp.where(shard_ref[0] % 2 == 0, both, total)
    store = pltpu.make_async_copy(sum_ref, kv_ref, sem)
    store.start()
    store.wait()


def kv_total_of(shard, own, ahead, beside):
    return pl.pallas_call(
        kv_total_kernel,
        in_specs=[SMEM] + [VMEM] * (2 + len(beside)),
        out_specs=HBM,
        out_shape=jax.ShapeDtypeStruct(own.shape, own.dtype),
        scratch_shapes=[pltpu.VMEM(own.shape, own.dtype), pltpu.SemaphoreType.DMA],
        compiler_params=params(),
        cost_estimate=cost(1),
        name="kv_total",
    )(shard, own, ahead, *beside)


def store_last_kernel(piece_ref, *refs):
    *_, whole_ref, _, _, sem = refs
    store = pltpu.make_async_copy(piece_ref, whole_ref, sem)
    store.start()
    store.wait()


def store_last(piece, *kept):
    return pl.pallas_call(
        store_last_kernel,
        in_specs=[VMEM, HBM, HBM],
        out_specs=[HBM, HBM, HBM],
        out_shape=[jax.ShapeDtypeStruct(x.shape, x.dtype) for x in (piece, *kept)],
        scratch_shapes=[pltpu.SemaphoreType.DMA],
        input_output_aliases={1: 1, 2: 2},
        compiler_params=params(),
        cost_estimate=cost(1),
        name="store_last",
    )(piece, *kept)


def core_swap(value, axis):
    return lax.ppermute(value, axis, [(i, i ^ 1) for i in range(lax.axis_size(axis))])


def per_device(stream_in, keys_values, out_weight, tile_mask, cotangent):
    queries, own, mask, cot = stream_in[0], keys_values[0], tile_mask[0], cotangent[0]
    weight = pltpu.with_memory_space_constraint(out_weight[0], pltpu.VMEM)
    width = queries.shape[1]
    group = width // (own.shape[-1] // HD)
    shard = lax.axis_index("seq").astype(jnp.int32).reshape(1)
    owns = cut(own)
    fars = [around(piece, "seq", 2) for piece in owns]
    d_attended, turned, kept = d_attended_of(cot, queries, weight, mask)
    pieces, probs, d_logits, nears = [], [], [], []
    after = d_attended
    for halo, (low, high) in enumerate(HALOS):
        chunks = [(first, last) for first, last in CHUNKS if low <= first < high]
        cuts = [((first - low) * HD, (last - first) * HD, (first, last) in SPLIT) for first, last in chunks]
        picked = pick(shard, owns[halo], fars[halo], after, cuts)
        swapped = [core_swap(x, "seq") for x in picked]
        for first, last in chunks:
            count = 1 + ((first, last) in SPLIT)
            near, swapped = swapped[:count], swapped[count:]
            grad, p, d = in_grad_of(
                shard, turned, (owns[halo], near, fars[halo]), low, first, last, group,
                [pieces[0][0]] if first == CHUNKS[-1][0] else [],
            )
            nears.append(near)
            probs.append(p)
            d_logits.append(d)
            pieces.append((around(grad, "section", -1), first * group))
            after = grad
    result, attended = layer_out(kept, queries, weight, owns, fars, nears, probs, group)
    next_input = around(result, "section", 1)
    prev_grad, own_grad, *near_grad, far_grad = kv_grads_of(
        attended, queries, d_attended, pieces[:2], probs, d_logits, group
    )
    beside = [core_swap(x, "seq") for x in near_grad]
    prev_grad, behind = behind_of(shard, pieces[2], prev_grad, far_grad, beside)
    ahead = around(behind, "seq", -2)
    kv_total = kv_total_of(shard, own_grad, ahead, beside)
    next_input, prev_grad, kv_total = store_last(next_input, prev_grad, kv_total)
    return (next_input[None], prev_grad[None], kv_total[None])


def solution(mesh):
    return jax.shard_map(
        per_device,
        mesh=mesh,
        in_specs=(
            P("section", "seq", None),
            P("section", None, "seq", None),
            P("section", None, None),
            P("section", None, None),
            P("section", "seq", None),
        ),
        out_specs=(
            P("section", "seq", None),
            P("section", "seq", None),
            P("section", None, "seq", None),
        ),
        check_vma=False,
    )
```

```python
import functools
import math

import jax
import jax.numpy as jnp
from jax import lax
from jax.experimental import pallas as pl
from jax.experimental.pallas import tpu as pltpu
from jax.sharding import PartitionSpec as P

HD = 128
TILE = 128
HALOS = ((0, 1), (1, 4))
CHUNKS = ((0, 1), (1, 2), (2, 4))
CUT_FLOPS = 10**10
ATT_FLOPS = {0: 6 * 10**7, 1: 1, 2: 10**10}
VMEM = pl.BlockSpec(memory_space=pltpu.VMEM)
HBM = pl.BlockSpec(memory_space=pltpu.HBM)
SMEM = pl.BlockSpec(memory_space=pltpu.SMEM)
VMEM_LIMIT = 32 * 1024 * 1024
NT = (((1,), (1,)), ((), ()))


def around(value, axis, by):
    length = lax.axis_size(axis)
    return lax.ppermute(value, axis, [(i, (i + by) % length) for i in range(length)])


def f32_dot(a, b, dims=(((1,), (0,)), ((), ()))):
    return lax.dot_general(a, b, dims, preferred_element_type=jnp.float32)


def params():
    return pltpu.CompilerParams(vmem_limit_bytes=VMEM_LIMIT)


def cost(flops):
    return pl.CostEstimate(flops=flops, bytes_accessed=1, transcendentals=0)


def prune(weight, kept_ref, row_tile, columns):
    strips = []
    for a in range(weight.shape[0] // TILE):
        row = kept_ref[row_tile + a : row_tile + a + 1, columns]
        kept = jnp.broadcast_to(row, (16, row.shape[1])).astype(weight.dtype)
        strip = weight[a * TILE : (a + 1) * TILE, :]
        strips.append(strip * jnp.concatenate([kept] * (TILE // 16), axis=0))
    return jnp.concatenate(strips, axis=0)


def cut_kernel(own_hbm, *refs):
    *piece_refs, sems = refs
    copies, column = [], 0
    for i, ref in enumerate(piece_refs):
        width = ref.shape[-1]
        source = own_hbm.at[:, :, column : column + width]
        copies.append(pltpu.make_async_copy(source, ref, sems.at[i]))
        column += width
    for copy in copies:
        copy.start()
    for copy in copies:
        copy.wait()


def cut(own):
    shapes = [own.shape[:2] + ((last - first) * HD,) for first, last in HALOS]
    return pl.pallas_call(
        cut_kernel,
        in_specs=[HBM],
        out_specs=[VMEM for _ in shapes],
        out_shape=[jax.ShapeDtypeStruct(shape, own.dtype) for shape in shapes],
        scratch_shapes=[pltpu.SemaphoreType.DMA((len(shapes),))],
        compiler_params=params(),
        cost_estimate=cost(CUT_FLOPS),
        name="cut",
    )(pltpu.with_memory_space_constraint(own, pltpu.HBM))


def d_attended_kernel(mask_ref, cot_ref, q_ref, weight_ref, out_ref, turned_ref, kept_ref):
    tiles = mask_ref.shape[0]
    width = kept_ref.shape[1]
    tile = lax.broadcasted_iota(jnp.int32, (tiles, width), 1) // TILE
    spread = (tile == lax.broadcasted_iota(jnp.int32, (tiles, width), 0)).astype(jnp.float32)
    kept_ref[...] = f32_dot((mask_ref[...] > 0).astype(jnp.float32), spread)
    rows = 4 * TILE
    for row in range(0, width, rows):
        weight = prune(weight_ref[row : row + rows, :], kept_ref, row // TILE, slice(None))
        part = f32_dot(cot_ref[...], weight, NT).astype(jnp.bfloat16)
        out_ref[:, row : row + rows] = part
        turned_ref[2, row : row + rows, :] = part.T
    turned_ref[0] = cot_ref[...].T
    turned_ref[1] = q_ref[...].T


def d_attended_of(cot, queries, weight, mask):
    tok, width = cot.shape
    return pl.pallas_call(
        d_attended_kernel,
        in_specs=[VMEM, VMEM, VMEM, VMEM],
        out_specs=[VMEM, VMEM, VMEM],
        out_shape=[
            jax.ShapeDtypeStruct((tok, width), jnp.bfloat16),
            jax.ShapeDtypeStruct((3, width, tok), jnp.bfloat16),
            jax.ShapeDtypeStruct((mask.shape[0], width), jnp.float32),
        ],
        compiler_params=params(),
        cost_estimate=cost(1),
        name="d_attended",
    )(mask, cot, queries, weight)


def pick_kernel(cuts, shard_ref, own_ref, rotated_ref, swapped_ref, after_ref, far_out_ref, *out_refs):
    shard = shard_ref[0]
    odd = shard % 2 == 1
    second_chip = shard // 2 == 1

    def copy_from(source_ref):
        refs = list(out_refs)
        for start, width, split in cuts:
            at = slice(start, start + width)
            if split:
                for index in range(2):
                    refs.pop(0)[...] = source_ref[index, :, at]
            else:
                refs.pop(0)[...] = source_ref[:, :, at]

    @pl.when(second_chip)
    def _():
        far_out_ref[...] = swapped_ref[...]

    @pl.when(jnp.logical_not(second_chip))
    def _():
        far_out_ref[...] = rotated_ref[...]

    @pl.when(odd)
    def _():
        copy_from(far_out_ref)

    @pl.when(jnp.logical_not(odd))
    def _():
        copy_from(own_ref)


def pick(shard, own, far, after, cuts):
    shapes = [own.shape]
    for _, width, split in cuts:
        shape = (own.shape[1], width)
        shapes += [shape, shape] if split else [(2,) + shape]
    return pl.pallas_call(
        functools.partial(pick_kernel, cuts),
        in_specs=[SMEM] + [VMEM] * 3 + [pl.BlockSpec(memory_space=pl.ANY)],
        out_specs=[VMEM for _ in shapes],
        out_shape=[jax.ShapeDtypeStruct(shape, own.dtype) for shape in shapes],
        compiler_params=params(),
        cost_estimate=cost(1),
        name="pick",
    )(shard, own, *far, after)


def store_piece(piece, column, turned_ref, whole_ref, sem):
    turned_ref[...] = piece.T
    store = pltpu.make_async_copy(
        turned_ref, whole_ref.at[:, column : column + turned_ref.shape[1]], sem
    )
    store.start()
    return store


def behind_kernel(column, shard_ref, piece_ref, given_ref, far_ref, *refs):
    *beside_refs, whole_ref, out_ref, turned_ref, sem = refs
    store = store_piece(piece_ref[...], column, turned_ref, whole_ref, sem)
    for index, beside_ref in enumerate(beside_refs):
        far = far_ref[index].astype(jnp.float32)
        both = far + beside_ref[...].astype(jnp.float32)
        out_ref[index] = jnp.where(shard_ref[0] % 2 == 1, both, far).astype(jnp.bfloat16)
    store.wait()


def behind_of(shard, piece, given, far, beside):
    return pl.pallas_call(
        functools.partial(behind_kernel, piece[1]),
        in_specs=[SMEM, VMEM, HBM, VMEM] + [VMEM] * len(beside),
        out_specs=[HBM, VMEM],
        out_shape=[
            jax.ShapeDtypeStruct(given.shape, given.dtype),
            jax.ShapeDtypeStruct(far.shape, far.dtype),
        ],
        scratch_shapes=[pltpu.VMEM(piece[0].shape[::-1], jnp.bfloat16), pltpu.SemaphoreType.DMA],
        input_output_aliases={2: 0},
        compiler_params=params(),
        cost_estimate=cost(1),
        name="behind",
    )(shard, piece[0], given, far, *beside)


def stacked(parts, axis=0):
    return jnp.concatenate(parts, axis=axis)


def blocks_of(own_ref, near_refs, far_ref, index, at, near_head):
    near_at = slice(near_head * HD, (near_head + 1) * HD)
    near = near_refs[index][:, near_at] if len(near_refs) == 2 else near_refs[0][index, :, near_at]
    return stacked([own_ref[index, :, at], near, far_ref[index, :, at]])


def in_grad_group(near_ok, far_ok, q_columns, d_columns, keys, values):
    tok = keys.shape[0] // 3
    scaling = HD ** (-0.5)
    factor = scaling * math.log2(math.e)
    floor = jnp.float32(-1e30)
    key_at = lax.broadcasted_iota(jnp.int32, (tok, tok), 0)
    row_at = lax.broadcasted_iota(jnp.int32, (tok, tok), 1)
    causal = key_at <= row_at
    lower = causal.astype(jnp.float32).astype(jnp.bfloat16)
    upper = (1.0 - causal.astype(jnp.float32)).astype(jnp.bfloat16)
    logits = f32_dot(keys, q_columns)
    d_probs = f32_dot(values, d_columns)
    own_l, near_l, far_l = (logits[i * tok : (i + 1) * tok] for i in range(3))
    own_d, near_d, far_d = (d_probs[i * tok : (i + 1) * tok] for i in range(3))
    parts = []
    for h in range(q_columns.shape[1] // tok):
        at = slice(h * tok, (h + 1) * tok)
        edge = jnp.where(causal, own_l[:, at], jnp.where(far_ok, far_l[:, at], floor))
        near = jnp.where(near_ok, near_l[:, at], floor)
        top = jnp.max(jnp.maximum(edge, near), axis=0, keepdims=True)
        edge = jnp.exp2((edge - top) * factor)
        near = jnp.exp2((near - top) * factor)
        inverse = 1.0 / jnp.sum(edge + near, axis=0, keepdims=True)
        edge = edge * inverse
        near = near * inverse
        edge_d = jnp.where(causal, own_d[:, at], far_d[:, at])
        row_dot = jnp.sum(edge * edge_d + near * near_d[:, at], axis=0, keepdims=True)
        d_edge = (edge * (edge_d - row_dot)).astype(jnp.bfloat16)
        d_near = (near * (near_d[:, at] - row_dot)).astype(jnp.bfloat16)
        edge = edge.astype(jnp.bfloat16)
        parts.append(
            (
                stacked([edge * lower, near.astype(jnp.bfloat16), edge * upper]),
                stacked([d_edge * lower, d_near, d_edge * upper]),
            )
        )
    probs = stacked([p for p, _ in parts], axis=1)
    d_logits = stacked([d for _, d in parts], axis=1)
    return f32_dot(keys.T, d_logits) * scaling, probs, d_logits


def in_grad_kernel(low, first, last, group, nears, shard_ref, turned_ref, *refs):
    own_ref, *refs = refs
    near_refs, far_ref = refs[:nears], refs[nears]
    grad_ref, probs_ref, d_logits_ref = refs[-3:]
    tok = own_ref.shape[1]
    shard = shard_ref[0]
    for g in range(first, last):
        at = slice((g - low) * HD, (g - low + 1) * HD)
        rows = [slice(g * group + c, g * group + c + HD) for c in range(0, group, HD)]
        d_queries, probs, d_logits = in_grad_group(
            shard >= 1,
            shard >= 2,
            stacked([turned_ref[1, row, :] for row in rows], axis=1),
            stacked([turned_ref[2, row, :] for row in rows], axis=1),
            blocks_of(own_ref, near_refs, far_ref, 0, at, g - first),
            blocks_of(own_ref, near_refs, far_ref, 1, at, g - first),
        )
        probs_ref[g - first] = probs
        d_logits_ref[g - first] = d_logits
        for h, row in enumerate(rows):
            out = slice(row.start - first * group, row.stop - first * group)
            grad_ref[out, :] = (
                turned_ref[0, row, :].astype(jnp.float32) + d_queries[:, h * tok : (h + 1) * tok]
            ).astype(jnp.bfloat16)


def in_grad_of(shard, turned, block, low, first, last, group, after):
    tok = turned.shape[-1]
    count = last - first
    inside = jax.ShapeDtypeStruct((count, 3 * tok, tok * group // HD), jnp.bfloat16)
    own, near, far = block
    return pl.pallas_call(
        functools.partial(in_grad_kernel, low, first, last, group, len(near)),
        in_specs=[SMEM] + [VMEM] * (3 + len(near)) + [pl.BlockSpec(memory_space=pl.ANY)] * len(after),
        out_specs=[VMEM] * 3,
        out_shape=[jax.ShapeDtypeStruct((count * group, tok), jnp.bfloat16), inside, inside],
        compiler_params=params(),
        cost_estimate=cost(ATT_FLOPS[first]),
        name="in_grad",
    )(shard, turned, own, *near, far, *after)


def mixed_columns(attended, weight_ref, kept_ref, q_ref, out_ref):
    step = 4 * TILE
    for column in range(0, out_ref.shape[1], step):
        at = slice(column, column + step)
        weight = prune(weight_ref[:, at], kept_ref, 0, at)
        mixed = f32_dot(attended, weight)
        out_ref[:, at] = (q_ref[:, at].astype(jnp.float32) + mixed).astype(jnp.bfloat16)


def layer_out_kernel(group, nears, *refs):
    kept_ref, q_ref, weight_ref, *refs = refs
    owns, refs = refs[: len(HALOS)], refs[len(HALOS) :]
    fars, refs = refs[: len(HALOS)], refs[len(HALOS) :]
    near_refs = []
    for count in nears:
        near_refs.append(refs[:count])
        refs = refs[count:]
    *probs_refs, out_ref, attended_ref = refs
    tok = q_ref.shape[0]
    for i, (first, last) in enumerate(CHUNKS):
        for g in range(first, last):
            halo = [j for j, (low, high) in enumerate(HALOS) if low <= g < high][0]
            at = slice((g - HALOS[halo][0]) * HD, (g - HALOS[halo][0] + 1) * HD)
            values = blocks_of(owns[halo], near_refs[i], fars[halo], 1, at, g - first)
            attended = f32_dot(values.T, probs_refs[i][g - first]).astype(jnp.bfloat16)
            for h in range(group // HD):
                c = g * group + h * HD
                attended_ref[:, c : c + HD] = attended[:, h * tok : (h + 1) * tok].T
    mixed_columns(attended_ref[...], weight_ref, kept_ref, q_ref, out_ref)


def layer_out(kept, queries, weight, owns, fars, nears, probs, group):
    tok, width = queries.shape
    operands = [kept, queries, weight, *owns, *fars, *[x for near in nears for x in near], *probs]
    return pl.pallas_call(
        functools.partial(layer_out_kernel, group, [len(near) for near in nears]),
        in_specs=[VMEM] * len(operands),
        out_specs=[VMEM, VMEM],
        out_shape=[
            jax.ShapeDtypeStruct((tok, width), jnp.bfloat16),
            jax.ShapeDtypeStruct((tok, width), jnp.bfloat16),
        ],
        compiler_params=params(),
        cost_estimate=cost(1),
        name="layer_out",
    )(*operands)


def kv_grads_kernel(group, stored, *refs):
    after_ref, q_ref, d_ref, *refs = refs
    piece_refs, refs = refs[: len(stored)], refs[len(stored) :]
    probs_refs, refs = refs[: len(CHUNKS)], refs[len(CHUNKS) :]
    d_logits_refs, refs = refs[: len(CHUNKS)], refs[len(CHUNKS) :]
    whole_ref, own_grad_ref, *near_grad_refs, far_grad_ref = refs[:5]
    *turned_refs, sems = refs[5:]
    tok = q_ref.shape[0]
    scaling = HD ** (-0.5)
    stores = [
        store_piece(piece_ref[...], column, turned_ref, whole_ref, sems.at[i])
        for i, (piece_ref, column, turned_ref) in enumerate(zip(piece_refs, stored, turned_refs))
    ]
    for i, (first, last) in enumerate(CHUNKS):
        for g in range(first, last):
            at_kv = slice(g * HD, (g + 1) * HD)
            columns = [g * group + c for c in range(0, group, HD)]
            d_rows = stacked([d_ref[:, c : c + HD] for c in columns])
            q_rows = stacked([q_ref[:, c : c + HD] for c in columns])
            d_keys = f32_dot(d_logits_refs[i][g - first], q_rows) * scaling
            d_values = f32_dot(probs_refs[i][g - first], d_rows)
            for index, grad in enumerate((d_keys, d_values)):
                own_grad_ref[index, :, at_kv] = grad[:tok]
                near_grad_refs[index][:, at_kv] = grad[tok : 2 * tok].astype(jnp.bfloat16)
                far_grad_ref[index, :, at_kv] = grad[2 * tok :].astype(jnp.bfloat16)
    for store in stores:
        store.wait()


def kv_grads_of(after, queries, d_attended, pieces, probs, d_logits, group):
    tok, width = queries.shape
    kv_width = width // group * HD
    operands = [queries, d_attended, *[p for p, _ in pieces], *probs, *d_logits]
    near_grad = jax.ShapeDtypeStruct((tok, kv_width), jnp.bfloat16)
    own_grad, far_grad = (jax.ShapeDtypeStruct((2, tok, kv_width), t) for t in (jnp.float32, jnp.bfloat16))
    return pl.pallas_call(
        functools.partial(kv_grads_kernel, group, [c for _, c in pieces]),
        in_specs=[pl.BlockSpec(memory_space=pl.ANY)] + [VMEM] * len(operands),
        out_specs=[HBM] + [VMEM] * 4,
        out_shape=[
            jax.ShapeDtypeStruct((tok, width), jnp.bfloat16), own_grad, near_grad, near_grad, far_grad,
        ],
        scratch_shapes=[pltpu.VMEM(p.shape[::-1], jnp.bfloat16) for p, _ in pieces]
        + [pltpu.SemaphoreType.DMA((len(pieces),))],
        compiler_params=params(),
        cost_estimate=cost(1),
        name="kv_grads",
    )(after, *operands)


def kv_total_kernel(shard_ref, own_ref, ahead_ref, *refs):
    *beside_refs, kv_ref, sum_ref, sem = refs
    for index, beside_ref in enumerate(beside_refs):
        total = own_ref[index] + ahead_ref[index].astype(jnp.float32)
        both = total + beside_ref[...].astype(jnp.float32)
        sum_ref[index] = jnp.where(shard_ref[0] % 2 == 0, both, total)
    store = pltpu.make_async_copy(sum_ref, kv_ref, sem)
    store.start()
    store.wait()


def kv_total_of(shard, own, ahead, beside):
    return pl.pallas_call(
        kv_total_kernel,
        in_specs=[SMEM] + [VMEM] * (2 + len(beside)),
        out_specs=HBM,
        out_shape=jax.ShapeDtypeStruct(own.shape, own.dtype),
        scratch_shapes=[pltpu.VMEM(own.shape, own.dtype), pltpu.SemaphoreType.DMA],
        compiler_params=params(),
        cost_estimate=cost(1),
        name="kv_total",
    )(shard, own, ahead, *beside)


def store_last_kernel(piece_ref, *refs):
    *_, whole_ref, _, _, sem = refs
    store = pltpu.make_async_copy(piece_ref, whole_ref, sem)
    store.start()
    store.wait()


def store_last(piece, *kept):
    return pl.pallas_call(
        store_last_kernel,
        in_specs=[VMEM, HBM, HBM],
        out_specs=[HBM, HBM, HBM],
        out_shape=[jax.ShapeDtypeStruct(x.shape, x.dtype) for x in (piece, *kept)],
        scratch_shapes=[pltpu.SemaphoreType.DMA],
        input_output_aliases={1: 1, 2: 2},
        compiler_params=params(),
        cost_estimate=cost(1),
        name="store_last",
    )(piece, *kept)


def far_blocks(value, axis):
    length = lax.axis_size(axis)
    rotated = [(i, i) for i in (0, 1)]
    rotated += [(i, i + 2 if i + 2 < length else i + 4 - length) for i in range(2, length)]
    swapped = [(i, i ^ 2 if i < 4 else i) for i in range(length)]
    return [lax.ppermute(value, axis, pairs) for pairs in (rotated, swapped)]


def core_swap(value, axis):
    return lax.ppermute(value, axis, [(i, i ^ 1) for i in range(lax.axis_size(axis))])


def per_device(stream_in, keys_values, out_weight, tile_mask, cotangent):
    queries, own, mask, cot = stream_in[0], keys_values[0], tile_mask[0], cotangent[0]
    weight = pltpu.with_memory_space_constraint(out_weight[0], pltpu.VMEM)
    width = queries.shape[1]
    group = width // (own.shape[-1] // HD)
    shard = lax.axis_index("seq").astype(jnp.int32).reshape(1)
    owns = cut(own)
    fars = [far_blocks(piece, "seq") for piece in owns]
    d_attended, turned, kept = d_attended_of(cot, queries, weight, mask)
    pieces, probs, d_logits, nears = [], [], [], []
    after = d_attended
    for halo, (low, high) in enumerate(HALOS):
        chunks = [(first, last) for first, last in CHUNKS if low <= first < high]
        cuts = [((first - low) * HD, (last - first) * HD, last - first > 1) for first, last in chunks]
        fars[halo], *picked = pick(shard, owns[halo], fars[halo], after, cuts)
        swapped = [core_swap(x, "seq") for x in picked]
        for first, last in chunks:
            near, swapped = swapped[: 1 + (last - first > 1)], swapped[1 + (last - first > 1) :]
            grad, p, d = in_grad_of(
                shard, turned, (owns[halo], near, fars[halo]), low, first, last, group,
                [pieces[0][0]] if first == CHUNKS[-1][0] else [],
            )
            nears.append(near)
            probs.append(p)
            d_logits.append(d)
            pieces.append((around(grad, "section", -1), first * group))
            after = grad
    result, attended = layer_out(kept, queries, weight, owns, fars, nears, probs, group)
    next_input = around(result, "section", 1)
    prev_grad, own_grad, *near_grad, far_grad = kv_grads_of(
        attended, queries, d_attended, pieces[:2], probs, d_logits, group
    )
    beside = [core_swap(x, "seq") for x in near_grad]
    prev_grad, behind = behind_of(shard, pieces[2], prev_grad, far_grad, beside)
    ahead = around(behind, "seq", -2)
    kv_total = kv_total_of(shard, own_grad, ahead, beside)
    next_input, prev_grad, kv_total = store_last(next_input, prev_grad, kv_total)
    return (next_input[None], prev_grad[None], kv_total[None])


def solution(mesh):
    return jax.shard_map(
        per_device,
        mesh=mesh,
        in_specs=(
            P("section", "seq", None),
            P("section", None, "seq", None),
            P("section", None, None),
            P("section", None, None),
            P("section", "seq", None),
        ),
        out_specs=(
            P("section", "seq", None),
            P("section", "seq", None),
            P("section", None, "seq", None),
        ),
        check_vma=False,
    )
```

```python
import functools
import math

import jax
import jax.numpy as jnp
from jax import lax
from jax.experimental import pallas as pl
from jax.experimental.pallas import tpu as pltpu
from jax.sharding import PartitionSpec as P

HD = 128
TILE = 128
HALOS = ((0, 1), (1, 4))
CHUNKS = ((0, 1), (1, 2), (2, 4))
CUT_FLOPS = 10**10
ATT_FLOPS = {0: 2 * 10**8, 1: 1, 2: 10**10}
VMEM = pl.BlockSpec(memory_space=pltpu.VMEM)
HBM = pl.BlockSpec(memory_space=pltpu.HBM)
SMEM = pl.BlockSpec(memory_space=pltpu.SMEM)
VMEM_LIMIT = 32 * 1024 * 1024
NT = (((1,), (1,)), ((), ()))


def around(value, axis, by):
    length = lax.axis_size(axis)
    return lax.ppermute(value, axis, [(i, (i + by) % length) for i in range(length)])


def f32_dot(a, b, dims=(((1,), (0,)), ((), ()))):
    return lax.dot_general(a, b, dims, preferred_element_type=jnp.float32)


def params():
    return pltpu.CompilerParams(vmem_limit_bytes=VMEM_LIMIT)


def cost(flops):
    return pl.CostEstimate(flops=flops, bytes_accessed=1, transcendentals=0)


def prune(weight, kept_ref, row_tile, columns):
    strips = []
    for a in range(weight.shape[0] // TILE):
        row = kept_ref[row_tile + a : row_tile + a + 1, columns]
        kept = jnp.broadcast_to(row, (16, row.shape[1])).astype(weight.dtype)
        strip = weight[a * TILE : (a + 1) * TILE, :]
        strips.append(strip * jnp.concatenate([kept] * (TILE // 16), axis=0))
    return jnp.concatenate(strips, axis=0)


def cut_kernel(own_hbm, *refs):
    *piece_refs, sems = refs
    copies, column = [], 0
    for i, ref in enumerate(piece_refs):
        width = ref.shape[-1]
        for index in range(2):
            source = own_hbm.at[index, :, column : column + width]
            copies.append(pltpu.make_async_copy(source, ref.at[index], sems.at[2 * i + index]))
        column += width
    for copy in copies:
        copy.start()
    for copy in copies:
        copy.wait()


def cut(own):
    shapes = [own.shape[:2] + ((last - first) * HD,) for first, last in HALOS]
    return pl.pallas_call(
        cut_kernel,
        in_specs=[HBM],
        out_specs=[VMEM for _ in shapes],
        out_shape=[jax.ShapeDtypeStruct(shape, own.dtype) for shape in shapes],
        scratch_shapes=[pltpu.SemaphoreType.DMA((2 * len(shapes),))],
        compiler_params=params(),
        cost_estimate=cost(CUT_FLOPS),
        name="cut",
    )(pltpu.with_memory_space_constraint(own, pltpu.HBM))


def d_attended_kernel(mask_ref, cot_ref, q_ref, weight_ref, out_ref, turned_ref, kept_ref):
    tiles = mask_ref.shape[0]
    width = kept_ref.shape[1]
    tile = lax.broadcasted_iota(jnp.int32, (tiles, width), 1) // TILE
    spread = (tile == lax.broadcasted_iota(jnp.int32, (tiles, width), 0)).astype(jnp.float32)
    kept_ref[...] = f32_dot((mask_ref[...] > 0).astype(jnp.float32), spread)
    rows = 4 * TILE
    for row in range(0, width, rows):
        weight = prune(weight_ref[row : row + rows, :], kept_ref, row // TILE, slice(None))
        part = f32_dot(cot_ref[...], weight, NT).astype(jnp.bfloat16)
        out_ref[:, row : row + rows] = part
        turned_ref[2, row : row + rows, :] = part.T
    turned_ref[0] = cot_ref[...].T
    turned_ref[1] = q_ref[...].T


def d_attended_of(cot, queries, weight, mask):
    tok, width = cot.shape
    return pl.pallas_call(
        d_attended_kernel,
        in_specs=[VMEM, VMEM, VMEM, VMEM],
        out_specs=[VMEM, VMEM, VMEM],
        out_shape=[
            jax.ShapeDtypeStruct((tok, width), jnp.bfloat16),
            jax.ShapeDtypeStruct((3, width, tok), jnp.bfloat16),
            jax.ShapeDtypeStruct((mask.shape[0], width), jnp.float32),
        ],
        compiler_params=params(),
        cost_estimate=cost(1),
        name="d_attended",
    )(mask, cot, queries, weight)


def pick_kernel(cuts, shard_ref, own_ref, far_ref, after_ref, *out_refs):
    odd = shard_ref[0] % 2 == 1

    def copy_from(source_ref):
        refs = list(out_refs)
        for start, width, split in cuts:
            at = slice(start, start + width)
            if split:
                for index in range(2):
                    refs.pop(0)[...] = source_ref[index, :, at]
            else:
                refs.pop(0)[...] = source_ref[:, :, at]

    @pl.when(odd)
    def _():
        copy_from(far_ref)

    @pl.when(jnp.logical_not(odd))
    def _():
        copy_from(own_ref)


def pick(shard, own, far, after, cuts):
    shapes = []
    for _, width, split in cuts:
        shape = (own.shape[1], width)
        shapes += [shape, shape] if split else [(2,) + shape]
    return pl.pallas_call(
        functools.partial(pick_kernel, cuts),
        in_specs=[SMEM, VMEM, VMEM, pl.BlockSpec(memory_space=pl.ANY)],
        out_specs=[VMEM for _ in shapes],
        out_shape=[jax.ShapeDtypeStruct(shape, own.dtype) for shape in shapes],
        compiler_params=params(),
        cost_estimate=cost(1),
        name="pick",
    )(shard, own, far, after)


def store_piece(piece, column, turned_ref, whole_ref, sem):
    turned_ref[...] = piece.T
    store = pltpu.make_async_copy(
        turned_ref, whole_ref.at[:, column : column + turned_ref.shape[1]], sem
    )
    store.start()
    return store


def behind_kernel(column, shard_ref, piece_ref, given_ref, far_ref, *refs):
    *beside_refs, whole_ref, out_ref, turned_ref, sem = refs
    store = store_piece(piece_ref[...], column, turned_ref, whole_ref, sem)
    for index, beside_ref in enumerate(beside_refs):
        far = far_ref[index].astype(jnp.float32)
        both = far + beside_ref[...].astype(jnp.float32)
        out_ref[index] = jnp.where(shard_ref[0] % 2 == 1, both, far).astype(jnp.bfloat16)
    store.wait()


def behind_of(shard, piece, given, far, beside):
    return pl.pallas_call(
        functools.partial(behind_kernel, piece[1]),
        in_specs=[SMEM, VMEM, HBM, VMEM] + [VMEM] * len(beside),
        out_specs=[HBM, VMEM],
        out_shape=[
            jax.ShapeDtypeStruct(given.shape, given.dtype),
            jax.ShapeDtypeStruct(far.shape, far.dtype),
        ],
        scratch_shapes=[pltpu.VMEM(piece[0].shape[::-1], jnp.bfloat16), pltpu.SemaphoreType.DMA],
        input_output_aliases={2: 0},
        compiler_params=params(),
        cost_estimate=cost(1),
        name="behind",
    )(shard, piece[0], given, far, *beside)


def stacked(parts, axis=0):
    return jnp.concatenate(parts, axis=axis)


def blocks_of(own_ref, near_refs, far_ref, index, at, near_head):
    near_at = slice(near_head * HD, (near_head + 1) * HD)
    near = near_refs[index][:, near_at] if len(near_refs) == 2 else near_refs[0][index, :, near_at]
    return stacked([own_ref[index, :, at], near, far_ref[index, :, at]])


def in_grad_group(near_ok, far_ok, q_columns, d_columns, keys, values):
    tok = keys.shape[0] // 3
    scaling = HD ** (-0.5)
    factor = scaling * math.log2(math.e)
    floor = jnp.float32(-1e30)
    key_at = lax.broadcasted_iota(jnp.int32, (tok, tok), 0)
    row_at = lax.broadcasted_iota(jnp.int32, (tok, tok), 1)
    causal = key_at <= row_at
    lower = causal.astype(jnp.float32).astype(jnp.bfloat16)
    upper = (1.0 - causal.astype(jnp.float32)).astype(jnp.bfloat16)
    logits = f32_dot(keys, q_columns)
    d_probs = f32_dot(values, d_columns)
    own_l, near_l, far_l = (logits[i * tok : (i + 1) * tok] for i in range(3))
    own_d, near_d, far_d = (d_probs[i * tok : (i + 1) * tok] for i in range(3))
    parts = []
    for h in range(q_columns.shape[1] // tok):
        at = slice(h * tok, (h + 1) * tok)
        edge = jnp.where(causal, own_l[:, at], jnp.where(far_ok, far_l[:, at], floor))
        near = jnp.where(near_ok, near_l[:, at], floor)
        top = jnp.max(jnp.maximum(edge, near), axis=0, keepdims=True)
        edge = jnp.exp2((edge - top) * factor)
        near = jnp.exp2((near - top) * factor)
        inverse = 1.0 / jnp.sum(edge + near, axis=0, keepdims=True)
        edge = edge * inverse
        near = near * inverse
        edge_d = jnp.where(causal, own_d[:, at], far_d[:, at])
        row_dot = jnp.sum(edge * edge_d + near * near_d[:, at], axis=0, keepdims=True)
        d_edge = (edge * (edge_d - row_dot)).astype(jnp.bfloat16)
        d_near = (near * (near_d[:, at] - row_dot)).astype(jnp.bfloat16)
        edge = edge.astype(jnp.bfloat16)
        parts.append(
            (
                stacked([edge * lower, near.astype(jnp.bfloat16), edge * upper]),
                stacked([d_edge * lower, d_near, d_edge * upper]),
            )
        )
    probs = stacked([p for p, _ in parts], axis=1)
    d_logits = stacked([d for _, d in parts], axis=1)
    return f32_dot(keys.T, d_logits) * scaling, probs, d_logits


def in_grad_kernel(low, first, last, group, nears, shard_ref, turned_ref, *refs):
    own_ref, *refs = refs
    near_refs, far_ref = refs[:nears], refs[nears]
    grad_ref, probs_ref, d_logits_ref = refs[-3:]
    tok = own_ref.shape[1]
    shard = shard_ref[0]
    for g in range(first, last):
        at = slice((g - low) * HD, (g - low + 1) * HD)
        rows = [slice(g * group + c, g * group + c + HD) for c in range(0, group, HD)]
        d_queries, probs, d_logits = in_grad_group(
            shard >= 1,
            shard >= 2,
            stacked([turned_ref[1, row, :] for row in rows], axis=1),
            stacked([turned_ref[2, row, :] for row in rows], axis=1),
            blocks_of(own_ref, near_refs, far_ref, 0, at, g - first),
            blocks_of(own_ref, near_refs, far_ref, 1, at, g - first),
        )
        probs_ref[g - first] = probs
        d_logits_ref[g - first] = d_logits
        for h, row in enumerate(rows):
            out = slice(row.start - first * group, row.stop - first * group)
            grad_ref[out, :] = (
                turned_ref[0, row, :].astype(jnp.float32) + d_queries[:, h * tok : (h + 1) * tok]
            ).astype(jnp.bfloat16)


def in_grad_of(shard, turned, block, low, first, last, group, after):
    tok = turned.shape[-1]
    count = last - first
    inside = jax.ShapeDtypeStruct((count, 3 * tok, tok * group // HD), jnp.bfloat16)
    own, near, far = block
    return pl.pallas_call(
        functools.partial(in_grad_kernel, low, first, last, group, len(near)),
        in_specs=[SMEM] + [VMEM] * (3 + len(near)) + [pl.BlockSpec(memory_space=pl.ANY)] * len(after),
        out_specs=[VMEM] * 3,
        out_shape=[jax.ShapeDtypeStruct((count * group, tok), jnp.bfloat16), inside, inside],
        compiler_params=params(),
        cost_estimate=cost(ATT_FLOPS[first]),
        name="in_grad",
    )(shard, turned, own, *near, far, *after)


def mixed_columns(attended, weight_ref, kept_ref, q_ref, out_ref):
    step = 4 * TILE
    for column in range(0, out_ref.shape[1], step):
        at = slice(column, column + step)
        weight = prune(weight_ref[:, at], kept_ref, 0, at)
        mixed = f32_dot(attended, weight)
        out_ref[:, at] = (q_ref[:, at].astype(jnp.float32) + mixed).astype(jnp.bfloat16)


def layer_out_kernel(group, nears, *refs):
    kept_ref, q_ref, weight_ref, *refs = refs
    owns, refs = refs[: len(HALOS)], refs[len(HALOS) :]
    fars, refs = refs[: len(HALOS)], refs[len(HALOS) :]
    near_refs = []
    for count in nears:
        near_refs.append(refs[:count])
        refs = refs[count:]
    *probs_refs, out_ref, attended_ref = refs
    tok = q_ref.shape[0]
    for i, (first, last) in enumerate(CHUNKS):
        for g in range(first, last):
            halo = [j for j, (low, high) in enumerate(HALOS) if low <= g < high][0]
            at = slice((g - HALOS[halo][0]) * HD, (g - HALOS[halo][0] + 1) * HD)
            values = blocks_of(owns[halo], near_refs[i], fars[halo], 1, at, g - first)
            attended = f32_dot(values.T, probs_refs[i][g - first]).astype(jnp.bfloat16)
            for h in range(group // HD):
                c = g * group + h * HD
                attended_ref[:, c : c + HD] = attended[:, h * tok : (h + 1) * tok].T
    mixed_columns(attended_ref[...], weight_ref, kept_ref, q_ref, out_ref)


def layer_out(kept, queries, weight, owns, fars, nears, probs, group):
    tok, width = queries.shape
    operands = [kept, queries, weight, *owns, *fars, *[x for near in nears for x in near], *probs]
    return pl.pallas_call(
        functools.partial(layer_out_kernel, group, [len(near) for near in nears]),
        in_specs=[VMEM] * len(operands),
        out_specs=[VMEM, VMEM],
        out_shape=[
            jax.ShapeDtypeStruct((tok, width), jnp.bfloat16),
            jax.ShapeDtypeStruct((tok, width), jnp.bfloat16),
        ],
        compiler_params=params(),
        cost_estimate=cost(1),
        name="layer_out",
    )(*operands)


def kv_grads_kernel(group, stored, *refs):
    after_ref, q_ref, d_ref, *refs = refs
    piece_refs, refs = refs[: len(stored)], refs[len(stored) :]
    probs_refs, refs = refs[: len(CHUNKS)], refs[len(CHUNKS) :]
    d_logits_refs, refs = refs[: len(CHUNKS)], refs[len(CHUNKS) :]
    whole_ref, own_grad_ref, *near_grad_refs, far_grad_ref = refs[:5]
    *turned_refs, sems = refs[5:]
    tok = q_ref.shape[0]
    scaling = HD ** (-0.5)
    stores = [
        store_piece(piece_ref[...], column, turned_ref, whole_ref, sems.at[i])
        for i, (piece_ref, column, turned_ref) in enumerate(zip(piece_refs, stored, turned_refs))
    ]
    for i, (first, last) in enumerate(CHUNKS):
        for g in range(first, last):
            at_kv = slice(g * HD, (g + 1) * HD)
            columns = [g * group + c for c in range(0, group, HD)]
            d_rows = stacked([d_ref[:, c : c + HD] for c in columns])
            q_rows = stacked([q_ref[:, c : c + HD] for c in columns])
            d_keys = f32_dot(d_logits_refs[i][g - first], q_rows) * scaling
            d_values = f32_dot(probs_refs[i][g - first], d_rows)
            for index, grad in enumerate((d_keys, d_values)):
                own_grad_ref[index, :, at_kv] = grad[:tok]
                near_grad_refs[index][:, at_kv] = grad[tok : 2 * tok].astype(jnp.bfloat16)
                far_grad_ref[index, :, at_kv] = grad[2 * tok :].astype(jnp.bfloat16)
    for store in stores:
        store.wait()


def kv_grads_of(after, queries, d_attended, pieces, probs, d_logits, group):
    tok, width = queries.shape
    kv_width = width // group * HD
    operands = [queries, d_attended, *[p for p, _ in pieces], *probs, *d_logits]
    near_grad = jax.ShapeDtypeStruct((tok, kv_width), jnp.bfloat16)
    own_grad, far_grad = (jax.ShapeDtypeStruct((2, tok, kv_width), t) for t in (jnp.float32, jnp.bfloat16))
    return pl.pallas_call(
        functools.partial(kv_grads_kernel, group, [c for _, c in pieces]),
        in_specs=[pl.BlockSpec(memory_space=pl.ANY)] + [VMEM] * len(operands),
        out_specs=[HBM] + [VMEM] * 4,
        out_shape=[
            jax.ShapeDtypeStruct((tok, width), jnp.bfloat16), own_grad, near_grad, near_grad, far_grad,
        ],
        scratch_shapes=[pltpu.VMEM(p.shape[::-1], jnp.bfloat16) for p, _ in pieces]
        + [pltpu.SemaphoreType.DMA((len(pieces),))],
        compiler_params=params(),
        cost_estimate=cost(1),
        name="kv_grads",
    )(after, *operands)


def kv_total_kernel(shard_ref, own_ref, ahead_ref, *refs):
    *beside_refs, kv_ref, sum_ref, sem = refs
    for index, beside_ref in enumerate(beside_refs):
        total = own_ref[index] + ahead_ref[index].astype(jnp.float32)
        both = total + beside_ref[...].astype(jnp.float32)
        sum_ref[index] = jnp.where(shard_ref[0] % 2 == 0, both, total)
    store = pltpu.make_async_copy(sum_ref, kv_ref, sem)
    store.start()
    store.wait()


def kv_total_of(shard, own, ahead, beside):
    return pl.pallas_call(
        kv_total_kernel,
        in_specs=[SMEM] + [VMEM] * (2 + len(beside)),
        out_specs=HBM,
        out_shape=jax.ShapeDtypeStruct(own.shape, own.dtype),
        scratch_shapes=[pltpu.VMEM(own.shape, own.dtype), pltpu.SemaphoreType.DMA],
        compiler_params=params(),
        cost_estimate=cost(1),
        name="kv_total",
    )(shard, own, ahead, *beside)


def store_last_kernel(piece_ref, *refs):
    *_, whole_ref, _, _, sems = refs
    count = sems.shape[0]
    rows = piece_ref.shape[0] // count
    stores = []
    for i in range(count):
        at = slice(i * rows, (i + 1) * rows)
        stores.append(pltpu.make_async_copy(piece_ref.at[at], whole_ref.at[at], sems.at[i]))
    for store in stores:
        store.start()
    for store in stores:
        store.wait()


def store_last(piece, *kept):
    return pl.pallas_call(
        store_last_kernel,
        in_specs=[VMEM, HBM, HBM],
        out_specs=[HBM, HBM, HBM],
        out_shape=[jax.ShapeDtypeStruct(x.shape, x.dtype) for x in (piece, *kept)],
        scratch_shapes=[pltpu.SemaphoreType.DMA((4,))],
        input_output_aliases={1: 1, 2: 2},
        compiler_params=params(),
        cost_estimate=cost(1),
        name="store_last",
    )(piece, *kept)


def core_swap(value, axis):
    return lax.ppermute(value, axis, [(i, i ^ 1) for i in range(lax.axis_size(axis))])


def per_device(stream_in, keys_values, out_weight, tile_mask, cotangent):
    queries, own, mask, cot = stream_in[0], keys_values[0], tile_mask[0], cotangent[0]
    weight = pltpu.with_memory_space_constraint(out_weight[0], pltpu.VMEM)
    width = queries.shape[1]
    group = width // (own.shape[-1] // HD)
    shard = lax.axis_index("seq").astype(jnp.int32).reshape(1)
    owns = cut(own)
    fars = [around(piece, "seq", 2) for piece in owns]
    d_attended, turned, kept = d_attended_of(cot, queries, weight, mask)
    pieces, probs, d_logits, nears = [], [], [], []
    after = d_attended
    for halo, (low, high) in enumerate(HALOS):
        chunks = [(first, last) for first, last in CHUNKS if low <= first < high]
        cuts = [((first - low) * HD, (last - first) * HD, last - first > 1) for first, last in chunks]
        picked = pick(shard, owns[halo], fars[halo], after, cuts)
        swapped = [core_swap(x, "seq") for x in picked]
        for first, last in chunks:
            near, swapped = swapped[: 1 + (last - first > 1)], swapped[1 + (last - first > 1) :]
            grad, p, d = in_grad_of(
                shard, turned, (owns[halo], near, fars[halo]), low, first, last, group,
                [pieces[0][0]] if first == CHUNKS[-1][0] else [],
            )
            nears.append(near)
            probs.append(p)
            d_logits.append(d)
            pieces.append((around(grad, "section", -1), first * group))
            after = grad
    result, attended = layer_out(kept, queries, weight, owns, fars, nears, probs, group)
    next_input = around(result, "section", 1)
    prev_grad, own_grad, *near_grad, far_grad = kv_grads_of(
        attended, queries, d_attended, pieces[:2], probs, d_logits, group
    )
    beside = [core_swap(x, "seq") for x in near_grad]
    prev_grad, behind = behind_of(shard, pieces[2], prev_grad, far_grad, beside)
    ahead = around(behind, "seq", -2)
    kv_total = kv_total_of(shard, own_grad, ahead, beside)
    next_input, prev_grad, kv_total = store_last(next_input, prev_grad, kv_total)
    return (next_input[None], prev_grad[None], kv_total[None])


def solution(mesh):
    return jax.shard_map(
        per_device,
        mesh=mesh,
        in_specs=(
            P("section", "seq", None),
            P("section", None, "seq", None),
            P("section", None, None),
            P("section", None, None),
            P("section", "seq", None),
        ),
        out_specs=(
            P("section", "seq", None),
            P("section", "seq", None),
            P("section", None, "seq", None),
        ),
        check_vma=False,
    )
```

```python
import functools
import math

import jax
import jax.numpy as jnp
from jax import lax
from jax.experimental import pallas as pl
from jax.experimental.pallas import tpu as pltpu
from jax.sharding import PartitionSpec as P

HD = 128
TILE = 128
HALOS = ((0, 1), (1, 4))
CHUNKS = ((0, 1), (1, 2), (2, 4))
CUT_FLOPS = 10**10
ATT_FLOPS = {0: 2 * 10**8, 1: 1, 2: 10**10}
VMEM = pl.BlockSpec(memory_space=pltpu.VMEM)
HBM = pl.BlockSpec(memory_space=pltpu.HBM)
SMEM = pl.BlockSpec(memory_space=pltpu.SMEM)
VMEM_LIMIT = 32 * 1024 * 1024
NT = (((1,), (1,)), ((), ()))


def around(value, axis, by):
    length = lax.axis_size(axis)
    return lax.ppermute(value, axis, [(i, (i + by) % length) for i in range(length)])


def f32_dot(a, b, dims=(((1,), (0,)), ((), ()))):
    return lax.dot_general(a, b, dims, preferred_element_type=jnp.float32)


def params():
    return pltpu.CompilerParams(vmem_limit_bytes=VMEM_LIMIT)


def cost(flops):
    return pl.CostEstimate(flops=flops, bytes_accessed=1, transcendentals=0)


def prune(weight, kept_ref, row_tile, columns):
    strips = []
    for a in range(weight.shape[0] // TILE):
        row = kept_ref[row_tile + a : row_tile + a + 1, columns]
        kept = jnp.broadcast_to(row, (16, row.shape[1])).astype(weight.dtype)
        strip = weight[a * TILE : (a + 1) * TILE, :]
        strips.append(strip * jnp.concatenate([kept] * (TILE // 16), axis=0))
    return jnp.concatenate(strips, axis=0)


def cut_kernel(own_hbm, *refs):
    *piece_refs, sems = refs
    copies, column = [], 0
    for i, ref in enumerate(piece_refs):
        width = ref.shape[-1]
        source = own_hbm.at[:, :, column : column + width]
        copies.append(pltpu.make_async_copy(source, ref, sems.at[i]))
        column += width
    for copy in copies:
        copy.start()
    for copy in copies:
        copy.wait()


def cut(own):
    shapes = [own.shape[:2] + ((last - first) * HD,) for first, last in HALOS]
    return pl.pallas_call(
        cut_kernel,
        in_specs=[HBM],
        out_specs=[VMEM for _ in shapes],
        out_shape=[jax.ShapeDtypeStruct(shape, own.dtype) for shape in shapes],
        scratch_shapes=[pltpu.SemaphoreType.DMA((len(shapes),))],
        compiler_params=params(),
        cost_estimate=cost(CUT_FLOPS),
        name="cut",
    )(pltpu.with_memory_space_constraint(own, pltpu.HBM))


def d_attended_kernel(mask_ref, cot_ref, q_ref, weight_ref, out_ref, turned_ref, kept_ref):
    tiles = mask_ref.shape[0]
    width = kept_ref.shape[1]
    tile = lax.broadcasted_iota(jnp.int32, (tiles, width), 1) // TILE
    spread = (tile == lax.broadcasted_iota(jnp.int32, (tiles, width), 0)).astype(jnp.float32)
    kept_ref[...] = f32_dot((mask_ref[...] > 0).astype(jnp.float32), spread)
    rows = 4 * TILE
    for row in range(0, width, rows):
        weight = prune(weight_ref[row : row + rows, :], kept_ref, row // TILE, slice(None))
        part = f32_dot(cot_ref[...], weight, NT).astype(jnp.bfloat16)
        out_ref[:, row : row + rows] = part
        turned_ref[2, row : row + rows, :] = part.T
    turned_ref[0] = cot_ref[...].T
    turned_ref[1] = q_ref[...].T


def d_attended_of(cot, queries, weight, mask):
    tok, width = cot.shape
    return pl.pallas_call(
        d_attended_kernel,
        in_specs=[VMEM, VMEM, VMEM, VMEM],
        out_specs=[VMEM, VMEM, VMEM],
        out_shape=[
            jax.ShapeDtypeStruct((tok, width), jnp.bfloat16),
            jax.ShapeDtypeStruct((3, width, tok), jnp.bfloat16),
            jax.ShapeDtypeStruct((mask.shape[0], width), jnp.float32),
        ],
        compiler_params=params(),
        cost_estimate=cost(1),
        name="d_attended",
    )(mask, cot, queries, weight)


def pick_kernel(cuts, shard_ref, own_ref, far_ref, after_ref, *out_refs):
    odd = shard_ref[0] % 2 == 1

    def copy_from(source_ref):
        refs = list(out_refs)
        for start, width, split in cuts:
            at = slice(start, start + width)
            if split:
                for index in range(2):
                    refs.pop(0)[...] = source_ref[index, :, at]
            else:
                refs.pop(0)[...] = source_ref[:, :, at]

    @pl.when(odd)
    def _():
        copy_from(far_ref)

    @pl.when(jnp.logical_not(odd))
    def _():
        copy_from(own_ref)


def pick(shard, own, far, after, cuts):
    shapes = []
    for _, width, split in cuts:
        shape = (own.shape[1], width)
        shapes += [shape, shape] if split else [(2,) + shape]
    return pl.pallas_call(
        functools.partial(pick_kernel, cuts),
        in_specs=[SMEM, VMEM, VMEM, pl.BlockSpec(memory_space=pl.ANY)],
        out_specs=[VMEM for _ in shapes],
        out_shape=[jax.ShapeDtypeStruct(shape, own.dtype) for shape in shapes],
        compiler_params=params(),
        cost_estimate=cost(1),
        name="pick",
    )(shard, own, far, after)


def store_piece(piece, column, turned_ref, whole_ref, sem):
    turned_ref[...] = piece.T
    store = pltpu.make_async_copy(
        turned_ref, whole_ref.at[:, column : column + turned_ref.shape[1]], sem
    )
    store.start()
    return store


def behind_kernel(column, shard_ref, piece_ref, given_ref, far_ref, *refs):
    *beside_refs, whole_ref, out_ref, turned_ref, sem = refs
    store = store_piece(piece_ref[...], column, turned_ref, whole_ref, sem)
    for index, beside_ref in enumerate(beside_refs):
        far = far_ref[index].astype(jnp.float32)
        both = far + beside_ref[...].astype(jnp.float32)
        out_ref[index] = jnp.where(shard_ref[0] % 2 == 1, both, far).astype(jnp.bfloat16)
    store.wait()


def behind_of(shard, piece, given, far, beside):
    return pl.pallas_call(
        functools.partial(behind_kernel, piece[1]),
        in_specs=[SMEM, VMEM, HBM, VMEM] + [VMEM] * len(beside),
        out_specs=[HBM, VMEM],
        out_shape=[
            jax.ShapeDtypeStruct(given.shape, given.dtype),
            jax.ShapeDtypeStruct(far.shape, far.dtype),
        ],
        scratch_shapes=[pltpu.VMEM(piece[0].shape[::-1], jnp.bfloat16), pltpu.SemaphoreType.DMA],
        input_output_aliases={2: 0},
        compiler_params=params(),
        cost_estimate=cost(1),
        name="behind",
    )(shard, piece[0], given, far, *beside)


def stacked(parts, axis=0):
    return jnp.concatenate(parts, axis=axis)


def blocks_of(own_ref, near_refs, far_ref, index, at, near_head):
    near_at = slice(near_head * HD, (near_head + 1) * HD)
    near = near_refs[index][:, near_at] if len(near_refs) == 2 else near_refs[0][index, :, near_at]
    return stacked([own_ref[index, :, at], near, far_ref[index, :, at]])


def in_grad_group(near_ok, far_ok, q_columns, d_columns, keys, values):
    tok = keys.shape[0] // 3
    scaling = HD ** (-0.5)
    factor = scaling * math.log2(math.e)
    floor = jnp.float32(-1e30)
    key_at = lax.broadcasted_iota(jnp.int32, (tok, 2 * tok), 0)
    row_at = lax.broadcasted_iota(jnp.int32, (tok, 2 * tok), 1) % tok
    causal = key_at <= row_at
    lower = causal.astype(jnp.float32).astype(jnp.bfloat16)
    upper = (1.0 - causal.astype(jnp.float32)).astype(jnp.bfloat16)
    turned_keys = keys.T
    d_queries, probs, d_logits = [], [], []
    wide = 2 * tok
    for column in range(0, q_columns.shape[1], wide):
        logits = f32_dot(keys, q_columns[:, column : column + wide])
        d_probs = f32_dot(values, d_columns[:, column : column + wide])
        own_l, near_l, far_l = (logits[i * tok : (i + 1) * tok] for i in range(3))
        own_d, near_d, far_d = (d_probs[i * tok : (i + 1) * tok] for i in range(3))
        edge = jnp.where(causal, own_l, jnp.where(far_ok, far_l, floor))
        near = jnp.where(near_ok, near_l, floor)
        top = jnp.max(jnp.maximum(edge, near), axis=0, keepdims=True)
        edge = jnp.exp2((edge - top) * factor)
        near = jnp.exp2((near - top) * factor)
        inverse = 1.0 / jnp.sum(edge + near, axis=0, keepdims=True)
        edge = edge * inverse
        near = near * inverse
        edge_d = jnp.where(causal, own_d, far_d)
        row_dot = jnp.sum(edge * edge_d + near * near_d, axis=0, keepdims=True)
        d_edge = (edge * (edge_d - row_dot)).astype(jnp.bfloat16)
        d_near = (near * (near_d - row_dot)).astype(jnp.bfloat16)
        edge = edge.astype(jnp.bfloat16)
        probs.append(stacked([edge * lower, near.astype(jnp.bfloat16), edge * upper]))
        d_logits.append(stacked([d_edge * lower, d_near, d_edge * upper]))
        d_queries.append(f32_dot(turned_keys, d_logits[-1]) * scaling)
    return (stacked(parts, axis=1) for parts in (d_queries, probs, d_logits))


def in_grad_kernel(low, first, last, group, nears, shard_ref, turned_ref, *refs):
    own_ref, *refs = refs
    near_refs, far_ref = refs[:nears], refs[nears]
    grad_ref, probs_ref, d_logits_ref = refs[-3:]
    tok = own_ref.shape[1]
    shard = shard_ref[0]
    for g in range(first, last):
        at = slice((g - low) * HD, (g - low + 1) * HD)
        rows = [slice(g * group + c, g * group + c + HD) for c in range(0, group, HD)]
        d_queries, probs, d_logits = in_grad_group(
            shard >= 1,
            shard >= 2,
            stacked([turned_ref[1, row, :] for row in rows], axis=1),
            stacked([turned_ref[2, row, :] for row in rows], axis=1),
            blocks_of(own_ref, near_refs, far_ref, 0, at, g - first),
            blocks_of(own_ref, near_refs, far_ref, 1, at, g - first),
        )
        probs_ref[g - first] = probs
        d_logits_ref[g - first] = d_logits
        for h, row in enumerate(rows):
            out = slice(row.start - first * group, row.stop - first * group)
            grad_ref[out, :] = (
                turned_ref[0, row, :].astype(jnp.float32) + d_queries[:, h * tok : (h + 1) * tok]
            ).astype(jnp.bfloat16)


def in_grad_of(shard, turned, block, low, first, last, group, after):
    tok = turned.shape[-1]
    count = last - first
    inside = jax.ShapeDtypeStruct((count, 3 * tok, tok * group // HD), jnp.bfloat16)
    own, near, far = block
    return pl.pallas_call(
        functools.partial(in_grad_kernel, low, first, last, group, len(near)),
        in_specs=[SMEM] + [VMEM] * (3 + len(near)) + [pl.BlockSpec(memory_space=pl.ANY)] * len(after),
        out_specs=[VMEM] * 3,
        out_shape=[jax.ShapeDtypeStruct((count * group, tok), jnp.bfloat16), inside, inside],
        compiler_params=params(),
        cost_estimate=cost(ATT_FLOPS[first]),
        name="in_grad",
    )(shard, turned, own, *near, far, *after)


def mixed_columns(attended, weight_ref, kept_ref, q_ref, out_ref):
    step = 4 * TILE
    for column in range(0, out_ref.shape[1], step):
        at = slice(column, column + step)
        weight = prune(weight_ref[:, at], kept_ref, 0, at)
        mixed = f32_dot(attended, weight)
        out_ref[:, at] = (q_ref[:, at].astype(jnp.float32) + mixed).astype(jnp.bfloat16)


def layer_out_kernel(group, nears, *refs):
    kept_ref, q_ref, weight_ref, *refs = refs
    owns, refs = refs[: len(HALOS)], refs[len(HALOS) :]
    fars, refs = refs[: len(HALOS)], refs[len(HALOS) :]
    near_refs = []
    for count in nears:
        near_refs.append(refs[:count])
        refs = refs[count:]
    *probs_refs, out_ref, attended_ref = refs
    tok = q_ref.shape[0]
    for i, (first, last) in enumerate(CHUNKS):
        for g in range(first, last):
            halo = [j for j, (low, high) in enumerate(HALOS) if low <= g < high][0]
            at = slice((g - HALOS[halo][0]) * HD, (g - HALOS[halo][0] + 1) * HD)
            values = blocks_of(owns[halo], near_refs[i], fars[halo], 1, at, g - first)
            attended = f32_dot(values.T, probs_refs[i][g - first]).astype(jnp.bfloat16)
            for h in range(group // HD):
                c = g * group + h * HD
                attended_ref[:, c : c + HD] = attended[:, h * tok : (h + 1) * tok].T
    mixed_columns(attended_ref[...], weight_ref, kept_ref, q_ref, out_ref)


def layer_out(kept, queries, weight, owns, fars, nears, probs, group):
    tok, width = queries.shape
    operands = [kept, queries, weight, *owns, *fars, *[x for near in nears for x in near], *probs]
    return pl.pallas_call(
        functools.partial(layer_out_kernel, group, [len(near) for near in nears]),
        in_specs=[VMEM] * len(operands),
        out_specs=[VMEM, VMEM],
        out_shape=[
            jax.ShapeDtypeStruct((tok, width), jnp.bfloat16),
            jax.ShapeDtypeStruct((tok, width), jnp.bfloat16),
        ],
        compiler_params=params(),
        cost_estimate=cost(1),
        name="layer_out",
    )(*operands)


def kv_grads_kernel(group, stored, *refs):
    after_ref, q_ref, d_ref, *refs = refs
    piece_refs, refs = refs[: len(stored)], refs[len(stored) :]
    probs_refs, refs = refs[: len(CHUNKS)], refs[len(CHUNKS) :]
    d_logits_refs, refs = refs[: len(CHUNKS)], refs[len(CHUNKS) :]
    whole_ref, own_grad_ref, *near_grad_refs, far_grad_ref = refs[:5]
    *turned_refs, sems = refs[5:]
    tok = q_ref.shape[0]
    scaling = HD ** (-0.5)
    stores = [
        store_piece(piece_ref[...], column, turned_ref, whole_ref, sems.at[i])
        for i, (piece_ref, column, turned_ref) in enumerate(zip(piece_refs, stored, turned_refs))
    ]
    for i, (first, last) in enumerate(CHUNKS):
        for g in range(first, last):
            at_kv = slice(g * HD, (g + 1) * HD)
            columns = [g * group + c for c in range(0, group, HD)]
            d_rows = stacked([d_ref[:, c : c + HD] for c in columns])
            q_rows = stacked([q_ref[:, c : c + HD] for c in columns])
            d_keys = f32_dot(d_logits_refs[i][g - first], q_rows) * scaling
            d_values = f32_dot(probs_refs[i][g - first], d_rows)
            for index, grad in enumerate((d_keys, d_values)):
                own_grad_ref[index, :, at_kv] = grad[:tok]
                near_grad_refs[index][:, at_kv] = grad[tok : 2 * tok].astype(jnp.bfloat16)
                far_grad_ref[index, :, at_kv] = grad[2 * tok :].astype(jnp.bfloat16)
    for store in stores:
        store.wait()


def kv_grads_of(after, queries, d_attended, pieces, probs, d_logits, group):
    tok, width = queries.shape
    kv_width = width // group * HD
    operands = [queries, d_attended, *[p for p, _ in pieces], *probs, *d_logits]
    near_grad = jax.ShapeDtypeStruct((tok, kv_width), jnp.bfloat16)
    own_grad, far_grad = (jax.ShapeDtypeStruct((2, tok, kv_width), t) for t in (jnp.float32, jnp.bfloat16))
    return pl.pallas_call(
        functools.partial(kv_grads_kernel, group, [c for _, c in pieces]),
        in_specs=[pl.BlockSpec(memory_space=pl.ANY)] + [VMEM] * len(operands),
        out_specs=[HBM] + [VMEM] * 4,
        out_shape=[
            jax.ShapeDtypeStruct((tok, width), jnp.bfloat16), own_grad, near_grad, near_grad, far_grad,
        ],
        scratch_shapes=[pltpu.VMEM(p.shape[::-1], jnp.bfloat16) for p, _ in pieces]
        + [pltpu.SemaphoreType.DMA((len(pieces),))],
        compiler_params=params(),
        cost_estimate=cost(1),
        name="kv_grads",
    )(after, *operands)


def kv_total_kernel(shard_ref, own_ref, ahead_ref, *refs):
    *beside_refs, kv_ref, sum_ref, sem = refs
    for index, beside_ref in enumerate(beside_refs):
        total = own_ref[index] + ahead_ref[index].astype(jnp.float32)
        both = total + beside_ref[...].astype(jnp.float32)
        sum_ref[index] = jnp.where(shard_ref[0] % 2 == 0, both, total)
    store = pltpu.make_async_copy(sum_ref, kv_ref, sem)
    store.start()
    store.wait()


def kv_total_of(shard, own, ahead, beside):
    return pl.pallas_call(
        kv_total_kernel,
        in_specs=[SMEM] + [VMEM] * (2 + len(beside)),
        out_specs=HBM,
        out_shape=jax.ShapeDtypeStruct(own.shape, own.dtype),
        scratch_shapes=[pltpu.VMEM(own.shape, own.dtype), pltpu.SemaphoreType.DMA],
        compiler_params=params(),
        cost_estimate=cost(1),
        name="kv_total",
    )(shard, own, ahead, *beside)


def store_last_kernel(piece_ref, *refs):
    *_, whole_ref, _, _, sem = refs
    store = pltpu.make_async_copy(piece_ref, whole_ref, sem)
    store.start()
    store.wait()


def store_last(piece, *kept):
    return pl.pallas_call(
        store_last_kernel,
        in_specs=[VMEM, HBM, HBM],
        out_specs=[HBM, HBM, HBM],
        out_shape=[jax.ShapeDtypeStruct(x.shape, x.dtype) for x in (piece, *kept)],
        scratch_shapes=[pltpu.SemaphoreType.DMA],
        input_output_aliases={1: 1, 2: 2},
        compiler_params=params(),
        cost_estimate=cost(1),
        name="store_last",
    )(piece, *kept)


def core_swap(value, axis):
    return lax.ppermute(value, axis, [(i, i ^ 1) for i in range(lax.axis_size(axis))])


def per_device(stream_in, keys_values, out_weight, tile_mask, cotangent):
    queries, own, mask, cot = stream_in[0], keys_values[0], tile_mask[0], cotangent[0]
    weight = pltpu.with_memory_space_constraint(out_weight[0], pltpu.VMEM)
    width = queries.shape[1]
    group = width // (own.shape[-1] // HD)
    shard = lax.axis_index("seq").astype(jnp.int32).reshape(1)
    owns = cut(own)
    fars = [around(piece, "seq", 2) for piece in owns]
    d_attended, turned, kept = d_attended_of(cot, queries, weight, mask)
    pieces, probs, d_logits, nears = [], [], [], []
    after = d_attended
    for halo, (low, high) in enumerate(HALOS):
        chunks = [(first, last) for first, last in CHUNKS if low <= first < high]
        cuts = [((first - low) * HD, (last - first) * HD, last - first > 1) for first, last in chunks]
        picked = pick(shard, owns[halo], fars[halo], after, cuts)
        swapped = [core_swap(x, "seq") for x in picked]
        for first, last in chunks:
            near, swapped = swapped[: 1 + (last - first > 1)], swapped[1 + (last - first > 1) :]
            grad, p, d = in_grad_of(
                shard, turned, (owns[halo], near, fars[halo]), low, first, last, group,
                [pieces[0][0]] if first == CHUNKS[-1][0] else [],
            )
            nears.append(near)
            probs.append(p)
            d_logits.append(d)
            pieces.append((around(grad, "section", -1), first * group))
            after = grad
    result, attended = layer_out(kept, queries, weight, owns, fars, nears, probs, group)
    next_input = around(result, "section", 1)
    prev_grad, own_grad, *near_grad, far_grad = kv_grads_of(
        attended, queries, d_attended, pieces[:2], probs, d_logits, group
    )
    beside = [core_swap(x, "seq") for x in near_grad]
    prev_grad, behind = behind_of(shard, pieces[2], prev_grad, far_grad, beside)
    ahead = around(behind, "seq", -2)
    kv_total = kv_total_of(shard, own_grad, ahead, beside)
    next_input, prev_grad, kv_total = store_last(next_input, prev_grad, kv_total)
    return (next_input[None], prev_grad[None], kv_total[None])


def solution(mesh):
    return jax.shard_map(
        per_device,
        mesh=mesh,
        in_specs=(
            P("section", "seq", None),
            P("section", None, "seq", None),
            P("section", None, None),
            P("section", None, None),
            P("section", "seq", None),
        ),
        out_specs=(
            P("section", "seq", None),
            P("section", "seq", None),
            P("section", None, "seq", None),
        ),
        check_vma=False,
    )
```

```python
import functools
import math

import jax
import jax.numpy as jnp
from jax import lax
from jax.experimental import pallas as pl
from jax.experimental.pallas import tpu as pltpu
from jax.sharding import PartitionSpec as P

HD = 128
TILE = 128
HALOS = ((0, 1), (1, 4))
CHUNKS = ((0, 1), (1, 2), (2, 4))
CUT_FLOPS = 10**10
ATT_FLOPS = {0: 2 * 10**8, 1: 1, 2: 10**10}
VMEM = pl.BlockSpec(memory_space=pltpu.VMEM)
HBM = pl.BlockSpec(memory_space=pltpu.HBM)
SMEM = pl.BlockSpec(memory_space=pltpu.SMEM)
VMEM_LIMIT = 32 * 1024 * 1024
NT = (((1,), (1,)), ((), ()))


def around(value, axis, by):
    length = lax.axis_size(axis)
    return lax.ppermute(value, axis, [(i, (i + by) % length) for i in range(length)])


def f32_dot(a, b, dims=(((1,), (0,)), ((), ()))):
    return lax.dot_general(a, b, dims, preferred_element_type=jnp.float32)


def params():
    return pltpu.CompilerParams(vmem_limit_bytes=VMEM_LIMIT)


def cost(flops):
    return pl.CostEstimate(flops=flops, bytes_accessed=1, transcendentals=0)


def prune(weight, kept_ref, row_tile, columns):
    strips = []
    for a in range(weight.shape[0] // TILE):
        row = kept_ref[row_tile + a : row_tile + a + 1, columns]
        kept = jnp.broadcast_to(row, (16, row.shape[1])).astype(weight.dtype)
        strip = weight[a * TILE : (a + 1) * TILE, :]
        strips.append(strip * jnp.concatenate([kept] * (TILE // 16), axis=0))
    return jnp.concatenate(strips, axis=0)


def cut_kernel(own_hbm, *refs):
    *piece_refs, sems = refs
    copies, column = [], 0
    for i, ref in enumerate(piece_refs):
        width = ref.shape[-1]
        source = own_hbm.at[:, :, column : column + width]
        copies.append(pltpu.make_async_copy(source, ref, sems.at[i]))
        column += width
    for copy in copies:
        copy.start()
    for copy in copies:
        copy.wait()


def cut(own):
    shapes = [own.shape[:2] + ((last - first) * HD,) for first, last in HALOS]
    return pl.pallas_call(
        cut_kernel,
        in_specs=[HBM],
        out_specs=[VMEM for _ in shapes],
        out_shape=[jax.ShapeDtypeStruct(shape, own.dtype) for shape in shapes],
        scratch_shapes=[pltpu.SemaphoreType.DMA((len(shapes),))],
        compiler_params=params(),
        cost_estimate=cost(CUT_FLOPS),
        name="cut",
    )(pltpu.with_memory_space_constraint(own, pltpu.HBM))


def d_attended_kernel(mask_ref, cot_ref, q_ref, weight_ref, out_ref, turned_ref, kept_ref):
    tiles = mask_ref.shape[0]
    width = kept_ref.shape[1]
    tile = lax.broadcasted_iota(jnp.int32, (tiles, width), 1) // TILE
    spread = (tile == lax.broadcasted_iota(jnp.int32, (tiles, width), 0)).astype(jnp.float32)
    kept_ref[...] = f32_dot((mask_ref[...] > 0).astype(jnp.float32), spread)
    rows = 4 * TILE
    for row in range(0, width, rows):
        weight = prune(weight_ref[row : row + rows, :], kept_ref, row // TILE, slice(None))
        part = f32_dot(cot_ref[...], weight, NT).astype(jnp.bfloat16)
        out_ref[:, row : row + rows] = part
        turned_ref[2, row : row + rows, :] = part.T
    turned_ref[0] = cot_ref[...].T
    turned_ref[1] = q_ref[...].T


def d_attended_of(cot, queries, weight, mask):
    tok, width = cot.shape
    return pl.pallas_call(
        d_attended_kernel,
        in_specs=[VMEM, VMEM, VMEM, VMEM],
        out_specs=[VMEM, VMEM, VMEM],
        out_shape=[
            jax.ShapeDtypeStruct((tok, width), jnp.bfloat16),
            jax.ShapeDtypeStruct((3, width, tok), jnp.bfloat16),
            jax.ShapeDtypeStruct((mask.shape[0], width), jnp.float32),
        ],
        compiler_params=params(),
        cost_estimate=cost(1),
        name="d_attended",
    )(mask, cot, queries, weight)


def pick_kernel(cuts, shard_ref, own_ref, far_ref, after_ref, *out_refs):
    odd = shard_ref[0] % 2 == 1

    def copy_from(source_ref):
        refs = list(out_refs)
        for start, width, split in cuts:
            at = slice(start, start + width)
            if split:
                for index in range(2):
                    refs.pop(0)[...] = source_ref[index, :, at]
            else:
                refs.pop(0)[...] = source_ref[:, :, at]

    @pl.when(odd)
    def _():
        copy_from(far_ref)

    @pl.when(jnp.logical_not(odd))
    def _():
        copy_from(own_ref)


def pick(shard, own, far, after, cuts):
    shapes = []
    for _, width, split in cuts:
        shape = (own.shape[1], width)
        shapes += [shape, shape] if split else [(2,) + shape]
    return pl.pallas_call(
        functools.partial(pick_kernel, cuts),
        in_specs=[SMEM, VMEM, VMEM, pl.BlockSpec(memory_space=pl.ANY)],
        out_specs=[VMEM for _ in shapes],
        out_shape=[jax.ShapeDtypeStruct(shape, own.dtype) for shape in shapes],
        compiler_params=params(),
        cost_estimate=cost(1),
        name="pick",
    )(shard, own, far, after)


def store_piece(piece, column, turned_ref, whole_ref, sem):
    turned_ref[...] = piece.T
    store = pltpu.make_async_copy(
        turned_ref, whole_ref.at[:, column : column + turned_ref.shape[1]], sem
    )
    store.start()
    return store


def behind_kernel(column, shard_ref, piece_ref, given_ref, far_ref, *refs):
    *beside_refs, whole_ref, out_ref, turned_ref, sem = refs
    store = store_piece(piece_ref[...], column, turned_ref, whole_ref, sem)
    for index, beside_ref in enumerate(beside_refs):
        far = far_ref[index].astype(jnp.float32)
        both = far + beside_ref[...].astype(jnp.float32)
        out_ref[index] = jnp.where(shard_ref[0] % 2 == 1, both, far).astype(jnp.bfloat16)
    store.wait()


def behind_of(shard, piece, given, far, beside):
    return pl.pallas_call(
        functools.partial(behind_kernel, piece[1]),
        in_specs=[SMEM, VMEM, HBM, VMEM] + [VMEM] * len(beside),
        out_specs=[HBM, VMEM],
        out_shape=[
            jax.ShapeDtypeStruct(given.shape, given.dtype),
            jax.ShapeDtypeStruct(far.shape, far.dtype),
        ],
        scratch_shapes=[pltpu.VMEM(piece[0].shape[::-1], jnp.bfloat16), pltpu.SemaphoreType.DMA],
        input_output_aliases={2: 0},
        compiler_params=params(),
        cost_estimate=cost(1),
        name="behind",
    )(shard, piece[0], given, far, *beside)


def stacked(parts, axis=0):
    return jnp.concatenate(parts, axis=axis)


def blocks_of(own_ref, near_refs, far_ref, index, at, near_head):
    near_at = slice(near_head * HD, (near_head + 1) * HD)
    near = near_refs[index][:, near_at] if len(near_refs) == 2 else near_refs[0][index, :, near_at]
    return stacked([own_ref[index, :, at], near, far_ref[index, :, at]])


def in_grad_group(near_ok, far_ok, q_columns, d_columns, keys, values):
    tok = keys.shape[0] // 3
    scaling = HD ** (-0.5)
    factor = scaling * math.log2(math.e)
    floor = jnp.float32(-1e30)
    key_at = lax.broadcasted_iota(jnp.int32, (tok, tok), 0)
    row_at = lax.broadcasted_iota(jnp.int32, (tok, tok), 1)
    causal = key_at <= row_at
    lower = causal.astype(jnp.float32).astype(jnp.bfloat16)
    upper = (1.0 - causal.astype(jnp.float32)).astype(jnp.bfloat16)
    logits = f32_dot(keys, q_columns)
    d_probs = f32_dot(values, d_columns)
    own_l, near_l, far_l = (logits[i * tok : (i + 1) * tok] for i in range(3))
    own_d, near_d, far_d = (d_probs[i * tok : (i + 1) * tok] for i in range(3))
    turned_keys = keys.T
    parts, d_queries = [], []
    for h in range(q_columns.shape[1] // tok):
        at = slice(h * tok, (h + 1) * tok)
        edge = jnp.where(causal, own_l[:, at], jnp.where(far_ok, far_l[:, at], floor))
        near = jnp.where(near_ok, near_l[:, at], floor)
        top = jnp.max(jnp.maximum(edge, near), axis=0, keepdims=True)
        edge = jnp.exp2((edge - top) * factor)
        near = jnp.exp2((near - top) * factor)
        inverse = 1.0 / jnp.sum(edge + near, axis=0, keepdims=True)
        edge = edge * inverse
        near = near * inverse
        edge_d = jnp.where(causal, own_d[:, at], far_d[:, at])
        row_dot = jnp.sum(edge * edge_d + near * near_d[:, at], axis=0, keepdims=True)
        d_edge = (edge * (edge_d - row_dot)).astype(jnp.bfloat16)
        d_near = (near * (near_d[:, at] - row_dot)).astype(jnp.bfloat16)
        edge = edge.astype(jnp.bfloat16)
        parts.append(
            (
                stacked([edge * lower, near.astype(jnp.bfloat16), edge * upper]),
                stacked([d_edge * lower, d_near, d_edge * upper]),
            )
        )
        d_queries.append(f32_dot(turned_keys, parts[-1][1]) * scaling)
    probs = stacked([p for p, _ in parts], axis=1)
    d_logits = stacked([d for _, d in parts], axis=1)
    return stacked(d_queries, axis=1), probs, d_logits


def in_grad_kernel(low, first, last, group, nears, shard_ref, turned_ref, *refs):
    own_ref, *refs = refs
    near_refs, far_ref = refs[:nears], refs[nears]
    grad_ref, probs_ref, d_logits_ref = refs[-3:]
    tok = own_ref.shape[1]
    shard = shard_ref[0]
    for g in range(first, last):
        at = slice((g - low) * HD, (g - low + 1) * HD)
        rows = [slice(g * group + c, g * group + c + HD) for c in range(0, group, HD)]
        d_queries, probs, d_logits = in_grad_group(
            shard >= 1,
            shard >= 2,
            stacked([turned_ref[1, row, :] for row in rows], axis=1),
            stacked([turned_ref[2, row, :] for row in rows], axis=1),
            blocks_of(own_ref, near_refs, far_ref, 0, at, g - first),
            blocks_of(own_ref, near_refs, far_ref, 1, at, g - first),
        )
        probs_ref[g - first] = probs
        d_logits_ref[g - first] = d_logits
        for h, row in enumerate(rows):
            out = slice(row.start - first * group, row.stop - first * group)
            grad_ref[out, :] = (
                turned_ref[0, row, :].astype(jnp.float32) + d_queries[:, h * tok : (h + 1) * tok]
            ).astype(jnp.bfloat16)


def in_grad_of(shard, turned, block, low, first, last, group, after):
    tok = turned.shape[-1]
    count = last - first
    inside = jax.ShapeDtypeStruct((count, 3 * tok, tok * group // HD), jnp.bfloat16)
    own, near, far = block
    return pl.pallas_call(
        functools.partial(in_grad_kernel, low, first, last, group, len(near)),
        in_specs=[SMEM] + [VMEM] * (3 + len(near)) + [pl.BlockSpec(memory_space=pl.ANY)] * len(after),
        out_specs=[VMEM] * 3,
        out_shape=[jax.ShapeDtypeStruct((count * group, tok), jnp.bfloat16), inside, inside],
        compiler_params=params(),
        cost_estimate=cost(ATT_FLOPS[first]),
        name="in_grad",
    )(shard, turned, own, *near, far, *after)


def mixed_columns(attended, weight_ref, kept_ref, q_ref, out_ref):
    step = 4 * TILE
    for column in range(0, out_ref.shape[1], step):
        at = slice(column, column + step)
        weight = prune(weight_ref[:, at], kept_ref, 0, at)
        mixed = f32_dot(attended, weight)
        out_ref[:, at] = (q_ref[:, at].astype(jnp.float32) + mixed).astype(jnp.bfloat16)


def layer_out_kernel(group, nears, *refs):
    kept_ref, q_ref, weight_ref, *refs = refs
    owns, refs = refs[: len(HALOS)], refs[len(HALOS) :]
    fars, refs = refs[: len(HALOS)], refs[len(HALOS) :]
    near_refs = []
    for count in nears:
        near_refs.append(refs[:count])
        refs = refs[count:]
    *probs_refs, out_ref, attended_ref = refs
    tok = q_ref.shape[0]
    for i, (first, last) in enumerate(CHUNKS):
        for g in range(first, last):
            halo = [j for j, (low, high) in enumerate(HALOS) if low <= g < high][0]
            at = slice((g - HALOS[halo][0]) * HD, (g - HALOS[halo][0] + 1) * HD)
            values = blocks_of(owns[halo], near_refs[i], fars[halo], 1, at, g - first)
            attended = f32_dot(values.T, probs_refs[i][g - first]).astype(jnp.bfloat16)
            for h in range(group // HD):
                c = g * group + h * HD
                attended_ref[:, c : c + HD] = attended[:, h * tok : (h + 1) * tok].T
    mixed_columns(attended_ref[...], weight_ref, kept_ref, q_ref, out_ref)


def layer_out(kept, queries, weight, owns, fars, nears, probs, group):
    tok, width = queries.shape
    operands = [kept, queries, weight, *owns, *fars, *[x for near in nears for x in near], *probs]
    return pl.pallas_call(
        functools.partial(layer_out_kernel, group, [len(near) for near in nears]),
        in_specs=[VMEM] * len(operands),
        out_specs=[VMEM, VMEM],
        out_shape=[
            jax.ShapeDtypeStruct((tok, width), jnp.bfloat16),
            jax.ShapeDtypeStruct((tok, width), jnp.bfloat16),
        ],
        compiler_params=params(),
        cost_estimate=cost(1),
        name="layer_out",
    )(*operands)


def kv_grads_kernel(group, stored, *refs):
    after_ref, q_ref, d_ref, *refs = refs
    piece_refs, refs = refs[: len(stored)], refs[len(stored) :]
    probs_refs, refs = refs[: len(CHUNKS)], refs[len(CHUNKS) :]
    d_logits_refs, refs = refs[: len(CHUNKS)], refs[len(CHUNKS) :]
    whole_ref, own_grad_ref, *near_grad_refs, far_grad_ref = refs[:5]
    *turned_refs, sems = refs[5:]
    tok = q_ref.shape[0]
    scaling = HD ** (-0.5)
    stores = [
        store_piece(piece_ref[...], column, turned_ref, whole_ref, sems.at[i])
        for i, (piece_ref, column, turned_ref) in enumerate(zip(piece_refs, stored, turned_refs))
    ]
    for i, (first, last) in enumerate(CHUNKS):
        for g in range(first, last):
            at_kv = slice(g * HD, (g + 1) * HD)
            columns = [g * group + c for c in range(0, group, HD)]
            d_rows = stacked([d_ref[:, c : c + HD] for c in columns])
            q_rows = stacked([q_ref[:, c : c + HD] for c in columns])
            d_keys = f32_dot(d_logits_refs[i][g - first], q_rows) * scaling
            d_values = f32_dot(probs_refs[i][g - first], d_rows)
            for index, grad in enumerate((d_keys, d_values)):
                own_grad_ref[index, :, at_kv] = grad[:tok]
                near_grad_refs[index][:, at_kv] = grad[tok : 2 * tok].astype(jnp.bfloat16)
                far_grad_ref[index, :, at_kv] = grad[2 * tok :].astype(jnp.bfloat16)
    for store in stores:
        store.wait()


def kv_grads_of(after, queries, d_attended, pieces, probs, d_logits, group):
    tok, width = queries.shape
    kv_width = width // group * HD
    operands = [queries, d_attended, *[p for p, _ in pieces], *probs, *d_logits]
    near_grad = jax.ShapeDtypeStruct((tok, kv_width), jnp.bfloat16)
    own_grad, far_grad = (jax.ShapeDtypeStruct((2, tok, kv_width), t) for t in (jnp.float32, jnp.bfloat16))
    return pl.pallas_call(
        functools.partial(kv_grads_kernel, group, [c for _, c in pieces]),
        in_specs=[pl.BlockSpec(memory_space=pl.ANY)] + [VMEM] * len(operands),
        out_specs=[HBM] + [VMEM] * 4,
        out_shape=[
            jax.ShapeDtypeStruct((tok, width), jnp.bfloat16), own_grad, near_grad, near_grad, far_grad,
        ],
        scratch_shapes=[pltpu.VMEM(p.shape[::-1], jnp.bfloat16) for p, _ in pieces]
        + [pltpu.SemaphoreType.DMA((len(pieces),))],
        compiler_params=params(),
        cost_estimate=cost(1),
        name="kv_grads",
    )(after, *operands)


def kv_total_kernel(shard_ref, own_ref, ahead_ref, *refs):
    *beside_refs, kv_ref, sum_ref, sem = refs
    for index, beside_ref in enumerate(beside_refs):
        total = own_ref[index] + ahead_ref[index].astype(jnp.float32)
        both = total + beside_ref[...].astype(jnp.float32)
        sum_ref[index] = jnp.where(shard_ref[0] % 2 == 0, both, total)
    store = pltpu.make_async_copy(sum_ref, kv_ref, sem)
    store.start()
    store.wait()


def kv_total_of(shard, own, ahead, beside):
    return pl.pallas_call(
        kv_total_kernel,
        in_specs=[SMEM] + [VMEM] * (2 + len(beside)),
        out_specs=HBM,
        out_shape=jax.ShapeDtypeStruct(own.shape, own.dtype),
        scratch_shapes=[pltpu.VMEM(own.shape, own.dtype), pltpu.SemaphoreType.DMA],
        compiler_params=params(),
        cost_estimate=cost(1),
        name="kv_total",
    )(shard, own, ahead, *beside)


def store_last_kernel(piece_ref, *refs):
    *_, whole_ref, _, _, sem = refs
    store = pltpu.make_async_copy(piece_ref, whole_ref, sem)
    store.start()
    store.wait()


def store_last(piece, *kept):
    return pl.pallas_call(
        store_last_kernel,
        in_specs=[VMEM, HBM, HBM],
        out_specs=[HBM, HBM, HBM],
        out_shape=[jax.ShapeDtypeStruct(x.shape, x.dtype) for x in (piece, *kept)],
        scratch_shapes=[pltpu.SemaphoreType.DMA],
        input_output_aliases={1: 1, 2: 2},
        compiler_params=params(),
        cost_estimate=cost(1),
        name="store_last",
    )(piece, *kept)


def core_swap(value, axis):
    return lax.ppermute(value, axis, [(i, i ^ 1) for i in range(lax.axis_size(axis))])


def per_device(stream_in, keys_values, out_weight, tile_mask, cotangent):
    queries, own, mask, cot = stream_in[0], keys_values[0], tile_mask[0], cotangent[0]
    weight = pltpu.with_memory_space_constraint(out_weight[0], pltpu.VMEM)
    width = queries.shape[1]
    group = width // (own.shape[-1] // HD)
    shard = lax.axis_index("seq").astype(jnp.int32).reshape(1)
    owns = cut(own)
    fars = [around(piece, "seq", 2) for piece in owns]
    d_attended, turned, kept = d_attended_of(cot, queries, weight, mask)
    pieces, probs, d_logits, nears = [], [], [], []
    after = d_attended
    for halo, (low, high) in enumerate(HALOS):
        chunks = [(first, last) for first, last in CHUNKS if low <= first < high]
        cuts = [((first - low) * HD, (last - first) * HD, last - first > 1) for first, last in chunks]
        picked = pick(shard, owns[halo], fars[halo], after, cuts)
        swapped = [core_swap(x, "seq") for x in picked]
        for first, last in chunks:
            near, swapped = swapped[: 1 + (last - first > 1)], swapped[1 + (last - first > 1) :]
            grad, p, d = in_grad_of(
                shard, turned, (owns[halo], near, fars[halo]), low, first, last, group,
                [pieces[0][0]] if first == CHUNKS[-1][0] else [],
            )
            nears.append(near)
            probs.append(p)
            d_logits.append(d)
            pieces.append((around(grad, "section", -1), first * group))
            after = grad
    result, attended = layer_out(kept, queries, weight, owns, fars, nears, probs, group)
    next_input = around(result, "section", 1)
    prev_grad, own_grad, *near_grad, far_grad = kv_grads_of(
        attended, queries, d_attended, pieces[:2], probs, d_logits, group
    )
    beside = [core_swap(x, "seq") for x in near_grad]
    prev_grad, behind = behind_of(shard, pieces[2], prev_grad, far_grad, beside)
    ahead = around(behind, "seq", -2)
    kv_total = kv_total_of(shard, own_grad, ahead, beside)
    next_input, prev_grad, kv_total = store_last(next_input, prev_grad, kv_total)
    return (next_input[None], prev_grad[None], kv_total[None])


def solution(mesh):
    return jax.shard_map(
        per_device,
        mesh=mesh,
        in_specs=(
            P("section", "seq", None),
            P("section", None, "seq", None),
            P("section", None, None),
            P("section", None, None),
            P("section", "seq", None),
        ),
        out_specs=(
            P("section", "seq", None),
            P("section", "seq", None),
            P("section", None, "seq", None),
        ),
        check_vma=False,
    )
```

```python
import functools
import math

import jax
import jax.numpy as jnp
from jax import lax
from jax.experimental import pallas as pl
from jax.experimental.pallas import tpu as pltpu
from jax.sharding import PartitionSpec as P

HD = 128
TILE = 128
HALOS = ((0, 1), (1, 4))
CHUNKS = ((0, 1), (1, 2), (2, 4))
CUT_FLOPS = 10**10
FLOOR = -1e30
ATT_FLOPS = {0: 2 * 10**8, 1: 1, 2: 10**10}
VMEM = pl.BlockSpec(memory_space=pltpu.VMEM)
HBM = pl.BlockSpec(memory_space=pltpu.HBM)
SMEM = pl.BlockSpec(memory_space=pltpu.SMEM)
VMEM_LIMIT = 32 * 1024 * 1024
NT = (((1,), (1,)), ((), ()))


def around(value, axis, by):
    length = lax.axis_size(axis)
    return lax.ppermute(value, axis, [(i, (i + by) % length) for i in range(length)])


def f32_dot(a, b, dims=(((1,), (0,)), ((), ()))):
    return lax.dot_general(a, b, dims, preferred_element_type=jnp.float32)


def params():
    return pltpu.CompilerParams(vmem_limit_bytes=VMEM_LIMIT)


def cost(flops):
    return pl.CostEstimate(flops=flops, bytes_accessed=1, transcendentals=0)


def prune(weight, kept_ref, row_tile, columns):
    strips = []
    for a in range(weight.shape[0] // TILE):
        row = kept_ref[row_tile + a : row_tile + a + 1, columns]
        kept = jnp.broadcast_to(row, (16, row.shape[1])).astype(weight.dtype)
        strip = weight[a * TILE : (a + 1) * TILE, :]
        strips.append(strip * jnp.concatenate([kept] * (TILE // 16), axis=0))
    return jnp.concatenate(strips, axis=0)


def cut_kernel(own_hbm, *refs):
    *piece_refs, sems = refs
    copies, column = [], 0
    for i, ref in enumerate(piece_refs):
        width = ref.shape[-1]
        source = own_hbm.at[:, :, column : column + width]
        copies.append(pltpu.make_async_copy(source, ref, sems.at[i]))
        column += width
    for copy in copies:
        copy.start()
    for copy in copies:
        copy.wait()


def cut(own):
    shapes = [own.shape[:2] + ((last - first) * HD,) for first, last in HALOS]
    return pl.pallas_call(
        cut_kernel,
        in_specs=[HBM],
        out_specs=[VMEM for _ in shapes],
        out_shape=[jax.ShapeDtypeStruct(shape, own.dtype) for shape in shapes],
        scratch_shapes=[pltpu.SemaphoreType.DMA((len(shapes),))],
        compiler_params=params(),
        cost_estimate=cost(CUT_FLOPS),
        name="cut",
    )(pltpu.with_memory_space_constraint(own, pltpu.HBM))


def d_attended_kernel(mask_ref, cot_ref, q_ref, weight_ref, out_ref, turned_ref, kept_ref):
    tiles = mask_ref.shape[0]
    width = kept_ref.shape[1]
    tile = lax.broadcasted_iota(jnp.int32, (tiles, width), 1) // TILE
    spread = (tile == lax.broadcasted_iota(jnp.int32, (tiles, width), 0)).astype(jnp.float32)
    kept_ref[...] = f32_dot((mask_ref[...] > 0).astype(jnp.float32), spread)
    rows = 4 * TILE
    for row in range(0, width, rows):
        weight = prune(weight_ref[row : row + rows, :], kept_ref, row // TILE, slice(None))
        part = f32_dot(cot_ref[...], weight, NT).astype(jnp.bfloat16)
        out_ref[:, row : row + rows] = part
        turned_ref[2, row : row + rows, :] = part.T
    turned_ref[0] = cot_ref[...].T
    turned_ref[1] = q_ref[...].T


def d_attended_of(cot, queries, weight, mask):
    tok, width = cot.shape
    return pl.pallas_call(
        d_attended_kernel,
        in_specs=[VMEM, VMEM, VMEM, VMEM],
        out_specs=[VMEM, VMEM, VMEM],
        out_shape=[
            jax.ShapeDtypeStruct((tok, width), jnp.bfloat16),
            jax.ShapeDtypeStruct((3, width, tok), jnp.bfloat16),
            jax.ShapeDtypeStruct((mask.shape[0], width), jnp.float32),
        ],
        compiler_params=params(),
        cost_estimate=cost(1),
        name="d_attended",
    )(mask, cot, queries, weight)


def pick_kernel(cuts, shard_ref, own_ref, far_ref, after_ref, *out_refs):
    odd = shard_ref[0] % 2 == 1

    def copy_from(source_ref):
        refs = list(out_refs)
        for start, width, split in cuts:
            at = slice(start, start + width)
            if split:
                for index in range(2):
                    refs.pop(0)[...] = source_ref[index, :, at]
            else:
                refs.pop(0)[...] = source_ref[:, :, at]

    @pl.when(odd)
    def _():
        copy_from(far_ref)

    @pl.when(jnp.logical_not(odd))
    def _():
        copy_from(own_ref)


def pick(shard, own, far, after, cuts):
    shapes = []
    for _, width, split in cuts:
        shape = (own.shape[1], width)
        shapes += [shape, shape] if split else [(2,) + shape]
    return pl.pallas_call(
        functools.partial(pick_kernel, cuts),
        in_specs=[SMEM, VMEM, VMEM, pl.BlockSpec(memory_space=pl.ANY)],
        out_specs=[VMEM for _ in shapes],
        out_shape=[jax.ShapeDtypeStruct(shape, own.dtype) for shape in shapes],
        compiler_params=params(),
        cost_estimate=cost(1),
        name="pick",
    )(shard, own, far, after)


def store_piece(piece, column, turned_ref, whole_ref, sem):
    turned_ref[...] = piece.T
    store = pltpu.make_async_copy(
        turned_ref, whole_ref.at[:, column : column + turned_ref.shape[1]], sem
    )
    store.start()
    return store


def behind_kernel(column, shard_ref, piece_ref, given_ref, far_ref, *refs):
    *beside_refs, whole_ref, out_ref, turned_ref, sem = refs
    store = store_piece(piece_ref[...], column, turned_ref, whole_ref, sem)
    for index, beside_ref in enumerate(beside_refs):
        far = far_ref[index].astype(jnp.float32)
        both = far + beside_ref[...].astype(jnp.float32)
        out_ref[index] = jnp.where(shard_ref[0] % 2 == 1, both, far).astype(jnp.bfloat16)
    store.wait()


def behind_of(shard, piece, given, far, beside):
    return pl.pallas_call(
        functools.partial(behind_kernel, piece[1]),
        in_specs=[SMEM, VMEM, HBM, VMEM] + [VMEM] * len(beside),
        out_specs=[HBM, VMEM],
        out_shape=[
            jax.ShapeDtypeStruct(given.shape, given.dtype),
            jax.ShapeDtypeStruct(far.shape, far.dtype),
        ],
        scratch_shapes=[pltpu.VMEM(piece[0].shape[::-1], jnp.bfloat16), pltpu.SemaphoreType.DMA],
        input_output_aliases={2: 0},
        compiler_params=params(),
        cost_estimate=cost(1),
        name="behind",
    )(shard, piece[0], given, far, *beside)


def stacked(parts, axis=0):
    return jnp.concatenate(parts, axis=axis)


def blocks_of(own_ref, near_refs, far_ref, index, at, near_head):
    near_at = slice(near_head * HD, (near_head + 1) * HD)
    near = near_refs[index][:, near_at] if len(near_refs) == 2 else near_refs[0][index, :, near_at]
    return stacked([own_ref[index, :, at], near, far_ref[index, :, at]])


def causal_mask(tok):
    key_at = lax.broadcasted_iota(jnp.int32, (tok, tok), 0)
    row_at = lax.broadcasted_iota(jnp.int32, (tok, tok), 1)
    return key_at <= row_at


def edge_group(far_ok, q_columns, d_columns, keys, values):
    tok = keys.shape[0] // 2
    heads = q_columns.shape[1] // tok
    causal = jnp.concatenate([causal_mask(tok)] * heads, axis=1)
    logits = f32_dot(keys, q_columns)
    d_probs = f32_dot(values, d_columns)
    far_logits = jnp.where(far_ok, logits[tok:], jnp.float32(FLOOR))
    return (
        jnp.where(causal, logits[:tok], far_logits),
        jnp.where(causal, d_probs[:tok], d_probs[tok:]),
    )


def in_grad_group(near_ok, edge_l, edge_d, q_columns, d_columns, near_k, near_v, keys):
    tok = near_k.shape[0]
    scaling = HD ** (-0.5)
    factor = scaling * math.log2(math.e)
    causal = causal_mask(tok).astype(jnp.float32)
    lower = causal.astype(jnp.bfloat16)
    upper = (1.0 - causal).astype(jnp.bfloat16)
    near_l = f32_dot(near_k, q_columns)
    near_d = f32_dot(near_v, d_columns)
    parts = []
    for h in range(q_columns.shape[1] // tok):
        at = slice(h * tok, (h + 1) * tok)
        edge = edge_l[:, at]
        near = jnp.where(near_ok, near_l[:, at], jnp.float32(FLOOR))
        top = jnp.max(jnp.maximum(edge, near), axis=0, keepdims=True)
        edge = jnp.exp2((edge - top) * factor)
        near = jnp.exp2((near - top) * factor)
        inverse = 1.0 / jnp.sum(edge + near, axis=0, keepdims=True)
        edge = edge * inverse
        near = near * inverse
        row_dot = jnp.sum(edge * edge_d[:, at] + near * near_d[:, at], axis=0, keepdims=True)
        d_edge = (edge * (edge_d[:, at] - row_dot)).astype(jnp.bfloat16)
        d_near = (near * (near_d[:, at] - row_dot)).astype(jnp.bfloat16)
        edge = edge.astype(jnp.bfloat16)
        parts.append(
            (
                stacked([edge * lower, near.astype(jnp.bfloat16), edge * upper]),
                stacked([d_edge * lower, d_near, d_edge * upper]),
            )
        )
    probs = stacked([p for p, _ in parts], axis=1)
    d_logits = stacked([d for _, d in parts], axis=1)
    return f32_dot(keys.T, d_logits) * scaling, probs, d_logits


def head_columns(turned_ref, g, group):
    rows = [slice(g * group + c, g * group + c + HD) for c in range(0, group, HD)]
    q_columns = stacked([turned_ref[1, row, :] for row in rows], axis=1)
    d_columns = stacked([turned_ref[2, row, :] for row in rows], axis=1)
    return rows, q_columns, d_columns


def edge_of_head(shard, own_ref, far_ref, at, q_columns, d_columns):
    keys, values = (stacked([own_ref[i, :, at], far_ref[i, :, at]]) for i in range(2))
    return edge_group(shard >= 2, q_columns, d_columns, keys, values)


def edge_kernel(low, first, last, group, shard_ref, turned_ref, own_ref, far_ref, logits_ref, d_probs_ref):
    for g in range(first, last):
        at = slice((g - low) * HD, (g - low + 1) * HD)
        _, q_columns, d_columns = head_columns(turned_ref, g, group)
        logits_ref[g - first], d_probs_ref[g - first] = edge_of_head(
            shard_ref[0], own_ref, far_ref, at, q_columns, d_columns
        )


def edge_of(shard, turned, own, far, low, first, last, group):
    tok = turned.shape[-1]
    inside = jax.ShapeDtypeStruct((last - first, tok, tok * group // HD), jnp.float32)
    return pl.pallas_call(
        functools.partial(edge_kernel, low, first, last, group),
        in_specs=[SMEM] + [VMEM] * 3,
        out_specs=[VMEM] * 2,
        out_shape=[inside, inside],
        compiler_params=params(),
        cost_estimate=cost(1),
        name="edge",
    )(shard, turned, own, far)


def in_grad_kernel(low, first, last, group, nears, edges, shard_ref, turned_ref, *refs):
    own_ref, *refs = refs
    near_refs, far_ref, *refs = refs[:nears], *refs[nears:]
    edge_refs = refs[:edges]
    grad_ref, probs_ref, d_logits_ref = refs[-3:]
    tok = own_ref.shape[1]
    shard = shard_ref[0]
    for g in range(first, last):
        at = slice((g - low) * HD, (g - low + 1) * HD)
        rows, q_columns, d_columns = head_columns(turned_ref, g, group)
        if edges:
            edge_l, edge_d = (ref[g - first] for ref in edge_refs)
        else:
            edge_l, edge_d = edge_of_head(shard, own_ref, far_ref, at, q_columns, d_columns)
        keys = blocks_of(own_ref, near_refs, far_ref, 0, at, g - first)
        values = blocks_of(own_ref, near_refs, far_ref, 1, at, g - first)
        d_queries, probs, d_logits = in_grad_group(
            shard >= 1, edge_l, edge_d, q_columns, d_columns,
            keys[tok : 2 * tok], values[tok : 2 * tok], keys,
        )
        probs_ref[g - first] = probs
        d_logits_ref[g - first] = d_logits
        for h, row in enumerate(rows):
            out = slice(row.start - first * group, row.stop - first * group)
            grad_ref[out, :] = (
                turned_ref[0, row, :].astype(jnp.float32) + d_queries[:, h * tok : (h + 1) * tok]
            ).astype(jnp.bfloat16)


def in_grad_of(shard, turned, block, edge, low, first, last, group, after):
    tok = turned.shape[-1]
    count = last - first
    inside = jax.ShapeDtypeStruct((count, 3 * tok, tok * group // HD), jnp.bfloat16)
    own, near, far = block
    return pl.pallas_call(
        functools.partial(in_grad_kernel, low, first, last, group, len(near), len(edge)),
        in_specs=[SMEM] + [VMEM] * (3 + len(near) + len(edge)) + [pl.BlockSpec(memory_space=pl.ANY)] * len(after),
        out_specs=[VMEM] * 3,
        out_shape=[jax.ShapeDtypeStruct((count * group, tok), jnp.bfloat16), inside, inside],
        compiler_params=params(),
        cost_estimate=cost(ATT_FLOPS[first]),
        name="in_grad",
    )(shard, turned, own, *near, far, *edge, *after)


def mixed_columns(attended, weight_ref, kept_ref, q_ref, out_ref):
    step = 4 * TILE
    for column in range(0, out_ref.shape[1], step):
        at = slice(column, column + step)
        weight = prune(weight_ref[:, at], kept_ref, 0, at)
        mixed = f32_dot(attended, weight)
        out_ref[:, at] = (q_ref[:, at].astype(jnp.float32) + mixed).astype(jnp.bfloat16)


def layer_out_kernel(group, nears, *refs):
    kept_ref, q_ref, weight_ref, *refs = refs
    owns, refs = refs[: len(HALOS)], refs[len(HALOS) :]
    fars, refs = refs[: len(HALOS)], refs[len(HALOS) :]
    near_refs = []
    for count in nears:
        near_refs.append(refs[:count])
        refs = refs[count:]
    *probs_refs, out_ref, attended_ref = refs
    tok = q_ref.shape[0]
    for i, (first, last) in enumerate(CHUNKS):
        for g in range(first, last):
            halo = [j for j, (low, high) in enumerate(HALOS) if low <= g < high][0]
            at = slice((g - HALOS[halo][0]) * HD, (g - HALOS[halo][0] + 1) * HD)
            values = blocks_of(owns[halo], near_refs[i], fars[halo], 1, at, g - first)
            attended = f32_dot(values.T, probs_refs[i][g - first]).astype(jnp.bfloat16)
            for h in range(group // HD):
                c = g * group + h * HD
                attended_ref[:, c : c + HD] = attended[:, h * tok : (h + 1) * tok].T
    mixed_columns(attended_ref[...], weight_ref, kept_ref, q_ref, out_ref)


def layer_out(kept, queries, weight, owns, fars, nears, probs, group):
    tok, width = queries.shape
    operands = [kept, queries, weight, *owns, *fars, *[x for near in nears for x in near], *probs]
    return pl.pallas_call(
        functools.partial(layer_out_kernel, group, [len(near) for near in nears]),
        in_specs=[VMEM] * len(operands),
        out_specs=[VMEM, VMEM],
        out_shape=[
            jax.ShapeDtypeStruct((tok, width), jnp.bfloat16),
            jax.ShapeDtypeStruct((tok, width), jnp.bfloat16),
        ],
        compiler_params=params(),
        cost_estimate=cost(1),
        name="layer_out",
    )(*operands)


def kv_grads_kernel(group, stored, *refs):
    after_ref, q_ref, d_ref, *refs = refs
    piece_refs, refs = refs[: len(stored)], refs[len(stored) :]
    probs_refs, refs = refs[: len(CHUNKS)], refs[len(CHUNKS) :]
    d_logits_refs, refs = refs[: len(CHUNKS)], refs[len(CHUNKS) :]
    whole_ref, own_grad_ref, *near_grad_refs, far_grad_ref = refs[:5]
    *turned_refs, sems = refs[5:]
    tok = q_ref.shape[0]
    scaling = HD ** (-0.5)
    stores = [
        store_piece(piece_ref[...], column, turned_ref, whole_ref, sems.at[i])
        for i, (piece_ref, column, turned_ref) in enumerate(zip(piece_refs, stored, turned_refs))
    ]
    for i, (first, last) in enumerate(CHUNKS):
        for g in range(first, last):
            at_kv = slice(g * HD, (g + 1) * HD)
            columns = [g * group + c for c in range(0, group, HD)]
            d_rows = stacked([d_ref[:, c : c + HD] for c in columns])
            q_rows = stacked([q_ref[:, c : c + HD] for c in columns])
            d_keys = f32_dot(d_logits_refs[i][g - first], q_rows) * scaling
            d_values = f32_dot(probs_refs[i][g - first], d_rows)
            for index, grad in enumerate((d_keys, d_values)):
                own_grad_ref[index, :, at_kv] = grad[:tok]
                near_grad_refs[index][:, at_kv] = grad[tok : 2 * tok].astype(jnp.bfloat16)
                far_grad_ref[index, :, at_kv] = grad[2 * tok :].astype(jnp.bfloat16)
    for store in stores:
        store.wait()


def kv_grads_of(after, queries, d_attended, pieces, probs, d_logits, group):
    tok, width = queries.shape
    kv_width = width // group * HD
    operands = [queries, d_attended, *[p for p, _ in pieces], *probs, *d_logits]
    near_grad = jax.ShapeDtypeStruct((tok, kv_width), jnp.bfloat16)
    own_grad, far_grad = (jax.ShapeDtypeStruct((2, tok, kv_width), t) for t in (jnp.float32, jnp.bfloat16))
    return pl.pallas_call(
        functools.partial(kv_grads_kernel, group, [c for _, c in pieces]),
        in_specs=[pl.BlockSpec(memory_space=pl.ANY)] + [VMEM] * len(operands),
        out_specs=[HBM] + [VMEM] * 4,
        out_shape=[
            jax.ShapeDtypeStruct((tok, width), jnp.bfloat16), own_grad, near_grad, near_grad, far_grad,
        ],
        scratch_shapes=[pltpu.VMEM(p.shape[::-1], jnp.bfloat16) for p, _ in pieces]
        + [pltpu.SemaphoreType.DMA((len(pieces),))],
        compiler_params=params(),
        cost_estimate=cost(1),
        name="kv_grads",
    )(after, *operands)


def kv_total_kernel(shard_ref, own_ref, ahead_ref, *refs):
    *beside_refs, kv_ref, sum_ref, sem = refs
    for index, beside_ref in enumerate(beside_refs):
        total = own_ref[index] + ahead_ref[index].astype(jnp.float32)
        both = total + beside_ref[...].astype(jnp.float32)
        sum_ref[index] = jnp.where(shard_ref[0] % 2 == 0, both, total)
    store = pltpu.make_async_copy(sum_ref, kv_ref, sem)
    store.start()
    store.wait()


def kv_total_of(shard, own, ahead, beside):
    return pl.pallas_call(
        kv_total_kernel,
        in_specs=[SMEM] + [VMEM] * (2 + len(beside)),
        out_specs=HBM,
        out_shape=jax.ShapeDtypeStruct(own.shape, own.dtype),
        scratch_shapes=[pltpu.VMEM(own.shape, own.dtype), pltpu.SemaphoreType.DMA],
        compiler_params=params(),
        cost_estimate=cost(1),
        name="kv_total",
    )(shard, own, ahead, *beside)


def store_last_kernel(piece_ref, *refs):
    *_, whole_ref, _, _, sem = refs
    store = pltpu.make_async_copy(piece_ref, whole_ref, sem)
    store.start()
    store.wait()


def store_last(piece, *kept):
    return pl.pallas_call(
        store_last_kernel,
        in_specs=[VMEM, HBM, HBM],
        out_specs=[HBM, HBM, HBM],
        out_shape=[jax.ShapeDtypeStruct(x.shape, x.dtype) for x in (piece, *kept)],
        scratch_shapes=[pltpu.SemaphoreType.DMA],
        input_output_aliases={1: 1, 2: 2},
        compiler_params=params(),
        cost_estimate=cost(1),
        name="store_last",
    )(piece, *kept)


def core_swap(value, axis):
    return lax.ppermute(value, axis, [(i, i ^ 1) for i in range(lax.axis_size(axis))])


def per_device(stream_in, keys_values, out_weight, tile_mask, cotangent):
    queries, own, mask, cot = stream_in[0], keys_values[0], tile_mask[0], cotangent[0]
    weight = pltpu.with_memory_space_constraint(out_weight[0], pltpu.VMEM)
    width = queries.shape[1]
    group = width // (own.shape[-1] // HD)
    shard = lax.axis_index("seq").astype(jnp.int32).reshape(1)
    owns = cut(own)
    fars = [around(piece, "seq", 2) for piece in owns]
    d_attended, turned, kept = d_attended_of(cot, queries, weight, mask)
    pieces, probs, d_logits, nears = [], [], [], []
    after = d_attended
    for halo, (low, high) in enumerate(HALOS):
        chunks = [(first, last) for first, last in CHUNKS if low <= first < high]
        cuts = [((first - low) * HD, (last - first) * HD, last - first > 1) for first, last in chunks]
        picked = pick(shard, owns[halo], fars[halo], after, cuts)
        swapped = [core_swap(x, "seq") for x in picked]
        ahead_of = chunks[-1]
        edges = {ahead_of[0]: edge_of(shard, turned, owns[halo], fars[halo], low, *ahead_of, group)}
        for first, last in chunks:
            near, swapped = swapped[: 1 + (last - first > 1)], swapped[1 + (last - first > 1) :]
            edge = edges.pop(first, [])
            grad, p, d = in_grad_of(
                shard, turned, (owns[halo], near, fars[halo]), edge, low, first, last, group,
                [pieces[0][0]] if first == CHUNKS[-1][0] else [x for e in edges.values() for x in e],
            )
            nears.append(near)
            probs.append(p)
            d_logits.append(d)
            pieces.append((around(grad, "section", -1), first * group))
            after = grad
    result, attended = layer_out(kept, queries, weight, owns, fars, nears, probs, group)
    next_input = around(result, "section", 1)
    prev_grad, own_grad, *near_grad, far_grad = kv_grads_of(
        attended, queries, d_attended, pieces[:2], probs, d_logits, group
    )
    beside = [core_swap(x, "seq") for x in near_grad]
    prev_grad, behind = behind_of(shard, pieces[2], prev_grad, far_grad, beside)
    ahead = around(behind, "seq", -2)
    kv_total = kv_total_of(shard, own_grad, ahead, beside)
    next_input, prev_grad, kv_total = store_last(next_input, prev_grad, kv_total)
    return (next_input[None], prev_grad[None], kv_total[None])


def solution(mesh):
    return jax.shard_map(
        per_device,
        mesh=mesh,
        in_specs=(
            P("section", "seq", None),
            P("section", None, "seq", None),
            P("section", None, None),
            P("section", None, None),
            P("section", "seq", None),
        ),
        out_specs=(
            P("section", "seq", None),
            P("section", "seq", None),
            P("section", None, "seq", None),
        ),
        check_vma=False,
    )
```

```python
import functools
import math

import jax
import jax.numpy as jnp
from jax import lax
from jax.experimental import pallas as pl
from jax.experimental.pallas import tpu as pltpu
from jax.sharding import PartitionSpec as P

HD = 128
TILE = 128
HALOS = ((0, 1), (1, 4))
CHUNKS = ((0, 1), (1, 2), (2, 4))
CUT_FLOPS = 10**10
FLOOR = -1e30
ATT_FLOPS = {0: 2 * 10**8, 1: 1, 2: 10**10}
VMEM = pl.BlockSpec(memory_space=pltpu.VMEM)
HBM = pl.BlockSpec(memory_space=pltpu.HBM)
SMEM = pl.BlockSpec(memory_space=pltpu.SMEM)
VMEM_LIMIT = 12 * 1024 * 1024
NT = (((1,), (1,)), ((), ()))


def around(value, axis, by):
    length = lax.axis_size(axis)
    return lax.ppermute(value, axis, [(i, (i + by) % length) for i in range(length)])


def f32_dot(a, b, dims=(((1,), (0,)), ((), ()))):
    return lax.dot_general(a, b, dims, preferred_element_type=jnp.float32)


def params():
    return pltpu.CompilerParams(vmem_limit_bytes=VMEM_LIMIT)


def cost(flops):
    return pl.CostEstimate(flops=flops, bytes_accessed=1, transcendentals=0)


def prune(weight, kept_ref, row_tile, columns):
    strips = []
    for a in range(weight.shape[0] // TILE):
        row = kept_ref[row_tile + a : row_tile + a + 1, columns]
        kept = jnp.broadcast_to(row, (16, row.shape[1])).astype(weight.dtype)
        strip = weight[a * TILE : (a + 1) * TILE, :]
        strips.append(strip * jnp.concatenate([kept] * (TILE // 16), axis=0))
    return jnp.concatenate(strips, axis=0)


def cut_kernel(own_hbm, *refs):
    *piece_refs, sems = refs
    copies, column = [], 0
    for i, ref in enumerate(piece_refs):
        width = ref.shape[-1]
        source = own_hbm.at[:, :, column : column + width]
        copies.append(pltpu.make_async_copy(source, ref, sems.at[i]))
        column += width
    for copy in copies:
        copy.start()
    for copy in copies:
        copy.wait()


def cut(own):
    shapes = [own.shape[:2] + ((last - first) * HD,) for first, last in HALOS]
    return pl.pallas_call(
        cut_kernel,
        in_specs=[HBM],
        out_specs=[VMEM for _ in shapes],
        out_shape=[jax.ShapeDtypeStruct(shape, own.dtype) for shape in shapes],
        scratch_shapes=[pltpu.SemaphoreType.DMA((len(shapes),))],
        compiler_params=params(),
        cost_estimate=cost(CUT_FLOPS),
        name="cut",
    )(pltpu.with_memory_space_constraint(own, pltpu.HBM))


def d_attended_kernel(mask_ref, cot_ref, q_ref, weight_ref, out_ref, turned_ref, kept_ref):
    tiles = mask_ref.shape[0]
    width = kept_ref.shape[1]
    tile = lax.broadcasted_iota(jnp.int32, (tiles, width), 1) // TILE
    spread = (tile == lax.broadcasted_iota(jnp.int32, (tiles, width), 0)).astype(jnp.float32)
    kept_ref[...] = f32_dot((mask_ref[...] > 0).astype(jnp.float32), spread)
    rows = 4 * TILE
    for row in range(0, width, rows):
        weight = prune(weight_ref[row : row + rows, :], kept_ref, row // TILE, slice(None))
        part = f32_dot(cot_ref[...], weight, NT).astype(jnp.bfloat16)
        out_ref[:, row : row + rows] = part
        turned_ref[2, row : row + rows, :] = part.T
    turned_ref[0] = cot_ref[...].T
    turned_ref[1] = q_ref[...].T


def d_attended_of(cot, queries, weight, mask):
    tok, width = cot.shape
    return pl.pallas_call(
        d_attended_kernel,
        in_specs=[VMEM, VMEM, VMEM, VMEM],
        out_specs=[VMEM, VMEM, VMEM],
        out_shape=[
            jax.ShapeDtypeStruct((tok, width), jnp.bfloat16),
            jax.ShapeDtypeStruct((3, width, tok), jnp.bfloat16),
            jax.ShapeDtypeStruct((mask.shape[0], width), jnp.float32),
        ],
        compiler_params=params(),
        cost_estimate=cost(1),
        name="d_attended",
    )(mask, cot, queries, weight)


def pick_kernel(cuts, shard_ref, own_ref, far_ref, after_ref, *out_refs):
    odd = shard_ref[0] % 2 == 1

    def copy_from(source_ref):
        refs = list(out_refs)
        for start, width, split in cuts:
            at = slice(start, start + width)
            if split:
                for index in range(2):
                    refs.pop(0)[...] = source_ref[index, :, at]
            else:
                refs.pop(0)[...] = source_ref[:, :, at]

    @pl.when(odd)
    def _():
        copy_from(far_ref)

    @pl.when(jnp.logical_not(odd))
    def _():
        copy_from(own_ref)


def pick(shard, own, far, after, cuts):
    shapes = []
    for _, width, split in cuts:
        shape = (own.shape[1], width)
        shapes += [shape, shape] if split else [(2,) + shape]
    return pl.pallas_call(
        functools.partial(pick_kernel, cuts),
        in_specs=[SMEM, VMEM, VMEM, pl.BlockSpec(memory_space=pl.ANY)],
        out_specs=[VMEM for _ in shapes],
        out_shape=[jax.ShapeDtypeStruct(shape, own.dtype) for shape in shapes],
        compiler_params=params(),
        cost_estimate=cost(1),
        name="pick",
    )(shard, own, far, after)


def store_piece(piece, column, turned_ref, whole_ref, sem):
    turned_ref[...] = piece.T
    store = pltpu.make_async_copy(
        turned_ref, whole_ref.at[:, column : column + turned_ref.shape[1]], sem
    )
    store.start()
    return store


def behind_kernel(column, shard_ref, piece_ref, given_ref, far_ref, *refs):
    *beside_refs, whole_ref, out_ref, turned_ref, sem = refs
    store = store_piece(piece_ref[...], column, turned_ref, whole_ref, sem)
    for index, beside_ref in enumerate(beside_refs):
        far = far_ref[index].astype(jnp.float32)
        both = far + beside_ref[...].astype(jnp.float32)
        out_ref[index] = jnp.where(shard_ref[0] % 2 == 1, both, far).astype(jnp.bfloat16)
    store.wait()


def behind_of(shard, piece, given, far, beside):
    return pl.pallas_call(
        functools.partial(behind_kernel, piece[1]),
        in_specs=[SMEM, VMEM, HBM, VMEM] + [VMEM] * len(beside),
        out_specs=[HBM, VMEM],
        out_shape=[
            jax.ShapeDtypeStruct(given.shape, given.dtype),
            jax.ShapeDtypeStruct(far.shape, far.dtype),
        ],
        scratch_shapes=[pltpu.VMEM(piece[0].shape[::-1], jnp.bfloat16), pltpu.SemaphoreType.DMA],
        input_output_aliases={2: 0},
        compiler_params=params(),
        cost_estimate=cost(1),
        name="behind",
    )(shard, piece[0], given, far, *beside)


def stacked(parts, axis=0):
    return jnp.concatenate(parts, axis=axis)


def blocks_of(own_ref, near_refs, far_ref, index, at, near_head):
    near_at = slice(near_head * HD, (near_head + 1) * HD)
    near = near_refs[index][:, near_at] if len(near_refs) == 2 else near_refs[0][index, :, near_at]
    return stacked([own_ref[index, :, at], near, far_ref[index, :, at]])


def causal_mask(tok):
    key_at = lax.broadcasted_iota(jnp.int32, (tok, tok), 0)
    row_at = lax.broadcasted_iota(jnp.int32, (tok, tok), 1)
    return key_at <= row_at


def edge_group(far_ok, q_columns, d_columns, keys, values):
    tok = keys.shape[0] // 2
    heads = q_columns.shape[1] // tok
    causal = jnp.concatenate([causal_mask(tok)] * heads, axis=1)
    logits = f32_dot(keys, q_columns)
    d_probs = f32_dot(values, d_columns)
    far_logits = jnp.where(far_ok, logits[tok:], jnp.float32(FLOOR))
    return (
        jnp.where(causal, logits[:tok], far_logits),
        jnp.where(causal, d_probs[:tok], d_probs[tok:]),
    )


def in_grad_group(near_ok, edge_l, edge_d, q_columns, d_columns, near_k, near_v, keys):
    tok = near_k.shape[0]
    scaling = HD ** (-0.5)
    factor = scaling * math.log2(math.e)
    causal = causal_mask(tok).astype(jnp.float32)
    lower = causal.astype(jnp.bfloat16)
    upper = (1.0 - causal).astype(jnp.bfloat16)
    near_l = f32_dot(near_k, q_columns)
    near_d = f32_dot(near_v, d_columns)
    parts = []
    for h in range(q_columns.shape[1] // tok):
        at = slice(h * tok, (h + 1) * tok)
        edge = edge_l[:, at]
        near = jnp.where(near_ok, near_l[:, at], jnp.float32(FLOOR))
        top = jnp.max(jnp.maximum(edge, near), axis=0, keepdims=True)
        edge = jnp.exp2((edge - top) * factor)
        near = jnp.exp2((near - top) * factor)
        inverse = 1.0 / jnp.sum(edge + near, axis=0, keepdims=True)
        edge = edge * inverse
        near = near * inverse
        row_dot = jnp.sum(edge * edge_d[:, at] + near * near_d[:, at], axis=0, keepdims=True)
        d_edge = (edge * (edge_d[:, at] - row_dot)).astype(jnp.bfloat16)
        d_near = (near * (near_d[:, at] - row_dot)).astype(jnp.bfloat16)
        edge = edge.astype(jnp.bfloat16)
        parts.append(
            (
                stacked([edge * lower, near.astype(jnp.bfloat16), edge * upper]),
                stacked([d_edge * lower, d_near, d_edge * upper]),
            )
        )
    probs = stacked([p for p, _ in parts], axis=1)
    d_logits = stacked([d for _, d in parts], axis=1)
    return f32_dot(keys.T, d_logits) * scaling, probs, d_logits


def head_columns(turned_ref, g, group):
    rows = [slice(g * group + c, g * group + c + HD) for c in range(0, group, HD)]
    q_columns = stacked([turned_ref[1, row, :] for row in rows], axis=1)
    d_columns = stacked([turned_ref[2, row, :] for row in rows], axis=1)
    return rows, q_columns, d_columns


def edge_of_head(shard, own_ref, far_ref, at, q_columns, d_columns):
    keys, values = (stacked([own_ref[i, :, at], far_ref[i, :, at]]) for i in range(2))
    return edge_group(shard >= 2, q_columns, d_columns, keys, values)


def edge_kernel(low, first, last, group, shard_ref, turned_ref, own_ref, far_ref, logits_ref, d_probs_ref):
    for g in range(first, last):
        at = slice((g - low) * HD, (g - low + 1) * HD)
        _, q_columns, d_columns = head_columns(turned_ref, g, group)
        logits_ref[g - first], d_probs_ref[g - first] = edge_of_head(
            shard_ref[0], own_ref, far_ref, at, q_columns, d_columns
        )


def edge_of(shard, turned, own, far, low, first, last, group):
    tok = turned.shape[-1]
    inside = jax.ShapeDtypeStruct((last - first, tok, tok * group // HD), jnp.float32)
    return pl.pallas_call(
        functools.partial(edge_kernel, low, first, last, group),
        in_specs=[SMEM] + [VMEM] * 3,
        out_specs=[VMEM] * 2,
        out_shape=[inside, inside],
        compiler_params=params(),
        cost_estimate=cost(1),
        name="edge",
    )(shard, turned, own, far)


def in_grad_kernel(low, first, last, group, nears, edges, shard_ref, turned_ref, *refs):
    own_ref, *refs = refs
    near_refs, far_ref, *refs = refs[:nears], *refs[nears:]
    edge_refs = refs[:edges]
    grad_ref, probs_ref, d_logits_ref = refs[-3:]
    tok = own_ref.shape[1]
    shard = shard_ref[0]
    for g in range(first, last):
        at = slice((g - low) * HD, (g - low + 1) * HD)
        rows, q_columns, d_columns = head_columns(turned_ref, g, group)
        if edges:
            edge_l, edge_d = (ref[g - first] for ref in edge_refs)
        else:
            edge_l, edge_d = edge_of_head(shard, own_ref, far_ref, at, q_columns, d_columns)
        keys = blocks_of(own_ref, near_refs, far_ref, 0, at, g - first)
        values = blocks_of(own_ref, near_refs, far_ref, 1, at, g - first)
        d_queries, probs, d_logits = in_grad_group(
            shard >= 1, edge_l, edge_d, q_columns, d_columns,
            keys[tok : 2 * tok], values[tok : 2 * tok], keys,
        )
        probs_ref[g - first] = probs
        d_logits_ref[g - first] = d_logits
        for h, row in enumerate(rows):
            out = slice(row.start - first * group, row.stop - first * group)
            grad_ref[out, :] = (
                turned_ref[0, row, :].astype(jnp.float32) + d_queries[:, h * tok : (h + 1) * tok]
            ).astype(jnp.bfloat16)


def in_grad_of(shard, turned, block, edge, low, first, last, group, after):
    tok = turned.shape[-1]
    count = last - first
    inside = jax.ShapeDtypeStruct((count, 3 * tok, tok * group // HD), jnp.bfloat16)
    own, near, far = block
    return pl.pallas_call(
        functools.partial(in_grad_kernel, low, first, last, group, len(near), len(edge)),
        in_specs=[SMEM] + [VMEM] * (3 + len(near) + len(edge)) + [pl.BlockSpec(memory_space=pl.ANY)] * len(after),
        out_specs=[VMEM] * 3,
        out_shape=[jax.ShapeDtypeStruct((count * group, tok), jnp.bfloat16), inside, inside],
        compiler_params=params(),
        cost_estimate=cost(ATT_FLOPS[first]),
        name="in_grad",
    )(shard, turned, own, *near, far, *edge, *after)


def mixed_columns(attended, weight_ref, kept_ref, q_ref, out_ref):
    step = 4 * TILE
    for column in range(0, out_ref.shape[1], step):
        at = slice(column, column + step)
        weight = prune(weight_ref[:, at], kept_ref, 0, at)
        mixed = f32_dot(attended, weight)
        out_ref[:, at] = (q_ref[:, at].astype(jnp.float32) + mixed).astype(jnp.bfloat16)


def layer_out_kernel(group, nears, *refs):
    kept_ref, q_ref, weight_ref, *refs = refs
    owns, refs = refs[: len(HALOS)], refs[len(HALOS) :]
    fars, refs = refs[: len(HALOS)], refs[len(HALOS) :]
    near_refs = []
    for count in nears:
        near_refs.append(refs[:count])
        refs = refs[count:]
    *probs_refs, out_ref, attended_ref = refs
    tok = q_ref.shape[0]
    for i, (first, last) in enumerate(CHUNKS):
        for g in range(first, last):
            halo = [j for j, (low, high) in enumerate(HALOS) if low <= g < high][0]
            at = slice((g - HALOS[halo][0]) * HD, (g - HALOS[halo][0] + 1) * HD)
            values = blocks_of(owns[halo], near_refs[i], fars[halo], 1, at, g - first)
            attended = f32_dot(values.T, probs_refs[i][g - first]).astype(jnp.bfloat16)
            for h in range(group // HD):
                c = g * group + h * HD
                attended_ref[:, c : c + HD] = attended[:, h * tok : (h + 1) * tok].T
    mixed_columns(attended_ref[...], weight_ref, kept_ref, q_ref, out_ref)


def layer_out(kept, queries, weight, owns, fars, nears, probs, group):
    tok, width = queries.shape
    operands = [kept, queries, weight, *owns, *fars, *[x for near in nears for x in near], *probs]
    return pl.pallas_call(
        functools.partial(layer_out_kernel, group, [len(near) for near in nears]),
        in_specs=[VMEM] * len(operands),
        out_specs=[VMEM, VMEM],
        out_shape=[
            jax.ShapeDtypeStruct((tok, width), jnp.bfloat16),
            jax.ShapeDtypeStruct((tok, width), jnp.bfloat16),
        ],
        compiler_params=params(),
        cost_estimate=cost(1),
        name="layer_out",
    )(*operands)


def kv_grads_kernel(group, stored, *refs):
    after_ref, q_ref, d_ref, *refs = refs
    piece_refs, refs = refs[: len(stored)], refs[len(stored) :]
    probs_refs, refs = refs[: len(CHUNKS)], refs[len(CHUNKS) :]
    d_logits_refs, refs = refs[: len(CHUNKS)], refs[len(CHUNKS) :]
    whole_ref, own_grad_ref, *near_grad_refs, far_grad_ref = refs[:5]
    *turned_refs, sems = refs[5:]
    tok = q_ref.shape[0]
    scaling = HD ** (-0.5)
    stores = [
        store_piece(piece_ref[...], column, turned_ref, whole_ref, sems.at[i])
        for i, (piece_ref, column, turned_ref) in enumerate(zip(piece_refs, stored, turned_refs))
    ]
    for i, (first, last) in enumerate(CHUNKS):
        for g in range(first, last):
            at_kv = slice(g * HD, (g + 1) * HD)
            columns = [g * group + c for c in range(0, group, HD)]
            d_rows = stacked([d_ref[:, c : c + HD] for c in columns])
            q_rows = stacked([q_ref[:, c : c + HD] for c in columns])
            d_keys = f32_dot(d_logits_refs[i][g - first], q_rows) * scaling
            d_values = f32_dot(probs_refs[i][g - first], d_rows)
            for index, grad in enumerate((d_keys, d_values)):
                own_grad_ref[index, :, at_kv] = grad[:tok]
                near_grad_refs[index][:, at_kv] = grad[tok : 2 * tok].astype(jnp.bfloat16)
                far_grad_ref[index, :, at_kv] = grad[2 * tok :].astype(jnp.bfloat16)
    for store in stores:
        store.wait()


def kv_grads_of(after, queries, d_attended, pieces, probs, d_logits, group):
    tok, width = queries.shape
    kv_width = width // group * HD
    operands = [queries, d_attended, *[p for p, _ in pieces], *probs, *d_logits]
    near_grad = jax.ShapeDtypeStruct((tok, kv_width), jnp.bfloat16)
    own_grad, far_grad = (jax.ShapeDtypeStruct((2, tok, kv_width), t) for t in (jnp.float32, jnp.bfloat16))
    return pl.pallas_call(
        functools.partial(kv_grads_kernel, group, [c for _, c in pieces]),
        in_specs=[pl.BlockSpec(memory_space=pl.ANY)] + [VMEM] * len(operands),
        out_specs=[HBM] + [VMEM] * 4,
        out_shape=[
            jax.ShapeDtypeStruct((tok, width), jnp.bfloat16), own_grad, near_grad, near_grad, far_grad,
        ],
        scratch_shapes=[pltpu.VMEM(p.shape[::-1], jnp.bfloat16) for p, _ in pieces]
        + [pltpu.SemaphoreType.DMA((len(pieces),))],
        compiler_params=params(),
        cost_estimate=cost(1),
        name="kv_grads",
    )(after, *operands)


def kv_total_kernel(shard_ref, own_ref, ahead_ref, *refs):
    *beside_refs, kv_ref, sum_ref, sem = refs
    for index, beside_ref in enumerate(beside_refs):
        total = own_ref[index] + ahead_ref[index].astype(jnp.float32)
        both = total + beside_ref[...].astype(jnp.float32)
        sum_ref[index] = jnp.where(shard_ref[0] % 2 == 0, both, total)
    store = pltpu.make_async_copy(sum_ref, kv_ref, sem)
    store.start()
    store.wait()


def kv_total_of(shard, own, ahead, beside):
    return pl.pallas_call(
        kv_total_kernel,
        in_specs=[SMEM] + [VMEM] * (2 + len(beside)),
        out_specs=HBM,
        out_shape=jax.ShapeDtypeStruct(own.shape, own.dtype),
        scratch_shapes=[pltpu.VMEM(own.shape, own.dtype), pltpu.SemaphoreType.DMA],
        compiler_params=params(),
        cost_estimate=cost(1),
        name="kv_total",
    )(shard, own, ahead, *beside)


def store_last_kernel(piece_ref, *refs):
    *_, whole_ref, _, _, sem = refs
    store = pltpu.make_async_copy(piece_ref, whole_ref, sem)
    store.start()
    store.wait()


def store_last(piece, *kept):
    return pl.pallas_call(
        store_last_kernel,
        in_specs=[VMEM, HBM, HBM],
        out_specs=[HBM, HBM, HBM],
        out_shape=[jax.ShapeDtypeStruct(x.shape, x.dtype) for x in (piece, *kept)],
        scratch_shapes=[pltpu.SemaphoreType.DMA],
        input_output_aliases={1: 1, 2: 2},
        compiler_params=params(),
        cost_estimate=cost(1),
        name="store_last",
    )(piece, *kept)


def core_swap(value, axis):
    return lax.ppermute(value, axis, [(i, i ^ 1) for i in range(lax.axis_size(axis))])


def per_device(stream_in, keys_values, out_weight, tile_mask, cotangent):
    queries, own, mask, cot = stream_in[0], keys_values[0], tile_mask[0], cotangent[0]
    weight = pltpu.with_memory_space_constraint(out_weight[0], pltpu.VMEM)
    width = queries.shape[1]
    group = width // (own.shape[-1] // HD)
    shard = lax.axis_index("seq").astype(jnp.int32).reshape(1)
    owns = cut(own)
    fars = [around(piece, "seq", 2) for piece in owns]
    d_attended, turned, kept = d_attended_of(cot, queries, weight, mask)
    pieces, probs, d_logits, nears = [], [], [], []
    after = d_attended
    for halo, (low, high) in enumerate(HALOS):
        chunks = [(first, last) for first, last in CHUNKS if low <= first < high]
        cuts = [((first - low) * HD, (last - first) * HD, last - first > 1) for first, last in chunks]
        picked = pick(shard, owns[halo], fars[halo], after, cuts)
        swapped = [core_swap(x, "seq") for x in picked]
        ahead_of = chunks[-1]
        edges = {ahead_of[0]: edge_of(shard, turned, owns[halo], fars[halo], low, *ahead_of, group)}
        for first, last in chunks:
            near, swapped = swapped[: 1 + (last - first > 1)], swapped[1 + (last - first > 1) :]
            edge = edges.pop(first, [])
            grad, p, d = in_grad_of(
                shard, turned, (owns[halo], near, fars[halo]), edge, low, first, last, group,
                [pieces[0][0]] if first == CHUNKS[-1][0] else [x for e in edges.values() for x in e],
            )
            nears.append(near)
            probs.append(p)
            d_logits.append(d)
            pieces.append((around(grad, "section", -1), first * group))
            after = grad
    result, attended = layer_out(kept, queries, weight, owns, fars, nears, probs, group)
    next_input = around(result, "section", 1)
    prev_grad, own_grad, *near_grad, far_grad = kv_grads_of(
        attended, queries, d_attended, pieces[:2], probs, d_logits, group
    )
    beside = [core_swap(x, "seq") for x in near_grad]
    prev_grad, behind = behind_of(shard, pieces[2], prev_grad, far_grad, beside)
    ahead = around(behind, "seq", -2)
    kv_total = kv_total_of(shard, own_grad, ahead, beside)
    next_input, prev_grad, kv_total = store_last(next_input, prev_grad, kv_total)
    return (next_input[None], prev_grad[None], kv_total[None])


def solution(mesh):
    return jax.shard_map(
        per_device,
        mesh=mesh,
        in_specs=(
            P("section", "seq", None),
            P("section", None, "seq", None),
            P("section", None, None),
            P("section", None, None),
            P("section", "seq", None),
        ),
        out_specs=(
            P("section", "seq", None),
            P("section", "seq", None),
            P("section", None, "seq", None),
        ),
        check_vma=False,
    )
```

```python
import functools
import math

import jax
import jax.numpy as jnp
from jax import lax
from jax.experimental import pallas as pl
from jax.experimental.pallas import tpu as pltpu
from jax.sharding import PartitionSpec as P

HD = 128
TILE = 128
HALOS = ((0, 1), (1, 4))
CHUNKS = ((0, 1), (1, 2), (2, 4))
CUT_FLOPS = 10**10
FLOOR = -1e30
ATT_FLOPS = {0: 2 * 10**8, 1: 1, 2: 10**10}
VMEM = pl.BlockSpec(memory_space=pltpu.VMEM)
HBM = pl.BlockSpec(memory_space=pltpu.HBM)
SMEM = pl.BlockSpec(memory_space=pltpu.SMEM)
VMEM_LIMIT = 32 * 1024 * 1024
NT = (((1,), (1,)), ((), ()))


def around(value, axis, by):
    length = lax.axis_size(axis)
    return lax.ppermute(value, axis, [(i, (i + by) % length) for i in range(length)])


def f32_dot(a, b, dims=(((1,), (0,)), ((), ()))):
    return lax.dot_general(a, b, dims, preferred_element_type=jnp.float32)


def params():
    return pltpu.CompilerParams(vmem_limit_bytes=VMEM_LIMIT)


def cost(flops):
    return pl.CostEstimate(flops=flops, bytes_accessed=1, transcendentals=0)


def prune(weight, kept_ref, row_tile, columns):
    strips = []
    for a in range(weight.shape[0] // TILE):
        row = kept_ref[row_tile + a : row_tile + a + 1, columns]
        kept = jnp.broadcast_to(row, (16, row.shape[1])).astype(weight.dtype)
        strip = weight[a * TILE : (a + 1) * TILE, :]
        strips.append(strip * jnp.concatenate([kept] * (TILE // 16), axis=0))
    return jnp.concatenate(strips, axis=0)


def cut_kernel(own_hbm, *refs):
    *piece_refs, sems = refs
    copies, column = [], 0
    for i, ref in enumerate(piece_refs):
        width = ref.shape[-1]
        source = own_hbm.at[:, :, column : column + width]
        copies.append(pltpu.make_async_copy(source, ref, sems.at[i]))
        column += width
    for copy in copies:
        copy.start()
    for copy in copies:
        copy.wait()


def cut(own):
    shapes = [own.shape[:2] + ((last - first) * HD,) for first, last in HALOS]
    return pl.pallas_call(
        cut_kernel,
        in_specs=[HBM],
        out_specs=[VMEM for _ in shapes],
        out_shape=[jax.ShapeDtypeStruct(shape, own.dtype) for shape in shapes],
        scratch_shapes=[pltpu.SemaphoreType.DMA((len(shapes),))],
        compiler_params=params(),
        cost_estimate=cost(CUT_FLOPS),
        name="cut",
    )(pltpu.with_memory_space_constraint(own, pltpu.HBM))


def d_attended_kernel(mask_ref, cot_ref, q_ref, weight_ref, out_ref, turned_ref, kept_ref):
    tiles = mask_ref.shape[0]
    width = kept_ref.shape[1]
    tile = lax.broadcasted_iota(jnp.int32, (tiles, width), 1) // TILE
    spread = (tile == lax.broadcasted_iota(jnp.int32, (tiles, width), 0)).astype(jnp.float32)
    kept_ref[...] = f32_dot((mask_ref[...] > 0).astype(jnp.float32), spread)
    rows = 4 * TILE
    for row in range(0, width, rows):
        weight = prune(weight_ref[row : row + rows, :], kept_ref, row // TILE, slice(None))
        part = f32_dot(cot_ref[...], weight, NT).astype(jnp.bfloat16)
        out_ref[:, row : row + rows] = part
        turned_ref[2, row : row + rows, :] = part.T
    turned_ref[0] = cot_ref[...].T
    turned_ref[1] = q_ref[...].T


def d_attended_of(cot, queries, weight, mask):
    tok, width = cot.shape
    return pl.pallas_call(
        d_attended_kernel,
        in_specs=[VMEM, VMEM, VMEM, VMEM],
        out_specs=[VMEM, VMEM, VMEM],
        out_shape=[
            jax.ShapeDtypeStruct((tok, width), jnp.bfloat16),
            jax.ShapeDtypeStruct((3, width, tok), jnp.bfloat16),
            jax.ShapeDtypeStruct((mask.shape[0], width), jnp.float32),
        ],
        compiler_params=params(),
        cost_estimate=cost(1),
        name="d_attended",
    )(mask, cot, queries, weight)


def pick_kernel(cuts, shard_ref, own_ref, far_ref, after_ref, *out_refs):
    odd = shard_ref[0] % 2 == 1

    def copy_from(source_ref):
        refs = list(out_refs)
        for start, width, split in cuts:
            at = slice(start, start + width)
            if split:
                for index in range(2):
                    refs.pop(0)[...] = source_ref[index, :, at]
            else:
                refs.pop(0)[...] = source_ref[:, :, at]

    @pl.when(odd)
    def _():
        copy_from(far_ref)

    @pl.when(jnp.logical_not(odd))
    def _():
        copy_from(own_ref)


def pick(shard, own, far, after, cuts):
    shapes = []
    for _, width, split in cuts:
        shape = (own.shape[1], width)
        shapes += [shape, shape] if split else [(2,) + shape]
    return pl.pallas_call(
        functools.partial(pick_kernel, cuts),
        in_specs=[SMEM, VMEM, VMEM, pl.BlockSpec(memory_space=pl.ANY)],
        out_specs=[VMEM for _ in shapes],
        out_shape=[jax.ShapeDtypeStruct(shape, own.dtype) for shape in shapes],
        compiler_params=params(),
        cost_estimate=cost(1),
        name="pick",
    )(shard, own, far, after)


def store_piece(piece, column, turned_ref, whole_ref, sem):
    turned_ref[...] = piece.T
    store = pltpu.make_async_copy(
        turned_ref, whole_ref.at[:, column : column + turned_ref.shape[1]], sem
    )
    store.start()
    return store


def behind_kernel(column, shard_ref, piece_ref, given_ref, far_ref, *refs):
    *beside_refs, whole_ref, out_ref, turned_ref, sem = refs
    store = store_piece(piece_ref[...], column, turned_ref, whole_ref, sem)
    for index, beside_ref in enumerate(beside_refs):
        far = far_ref[index].astype(jnp.float32)
        both = far + beside_ref[...].astype(jnp.float32)
        out_ref[index] = jnp.where(shard_ref[0] % 2 == 1, both, far).astype(jnp.bfloat16)
    store.wait()


def behind_of(shard, piece, given, far, beside):
    return pl.pallas_call(
        functools.partial(behind_kernel, piece[1]),
        in_specs=[SMEM, VMEM, HBM, VMEM] + [VMEM] * len(beside),
        out_specs=[HBM, VMEM],
        out_shape=[
            jax.ShapeDtypeStruct(given.shape, given.dtype),
            jax.ShapeDtypeStruct(far.shape, far.dtype),
        ],
        scratch_shapes=[pltpu.VMEM(piece[0].shape[::-1], jnp.bfloat16), pltpu.SemaphoreType.DMA],
        input_output_aliases={2: 0},
        compiler_params=params(),
        cost_estimate=cost(1),
        name="behind",
    )(shard, piece[0], given, far, *beside)


def stacked(parts, axis=0):
    return jnp.concatenate(parts, axis=axis)


def blocks_of(own_ref, near_refs, far_ref, index, at, near_head):
    near_at = slice(near_head * HD, (near_head + 1) * HD)
    near = near_refs[index][:, near_at] if len(near_refs) == 2 else near_refs[0][index, :, near_at]
    return stacked([own_ref[index, :, at], near, far_ref[index, :, at]])


def causal_mask(tok):
    key_at = lax.broadcasted_iota(jnp.int32, (tok, tok), 0)
    row_at = lax.broadcasted_iota(jnp.int32, (tok, tok), 1)
    return key_at <= row_at


def edge_group(far_ok, q_columns, d_columns, keys, values):
    tok = keys.shape[0] // 2
    heads = q_columns.shape[1] // tok
    causal = jnp.concatenate([causal_mask(tok)] * heads, axis=1)
    logits = f32_dot(keys, q_columns)
    d_probs = f32_dot(values, d_columns)
    far_logits = jnp.where(far_ok, logits[tok:], jnp.float32(FLOOR))
    return (
        jnp.where(causal, logits[:tok], far_logits),
        jnp.where(causal, d_probs[:tok], d_probs[tok:]),
    )


def in_grad_group(near_ok, edge_l, edge_d, q_columns, d_columns, near_k, near_v, keys):
    tok = near_k.shape[0]
    scaling = HD ** (-0.5)
    factor = scaling * math.log2(math.e)
    causal = causal_mask(tok).astype(jnp.float32)
    lower = causal.astype(jnp.bfloat16)
    upper = (1.0 - causal).astype(jnp.bfloat16)
    near_l = f32_dot(near_k, q_columns)
    near_d = f32_dot(near_v, d_columns)
    parts = []
    for h in range(q_columns.shape[1] // tok):
        at = slice(h * tok, (h + 1) * tok)
        edge = edge_l[:, at]
        near = jnp.where(near_ok, near_l[:, at], jnp.float32(FLOOR))
        top = jnp.max(jnp.maximum(edge, near), axis=0, keepdims=True)
        edge = jnp.exp2((edge - top) * factor)
        near = jnp.exp2((near - top) * factor)
        inverse = 1.0 / jnp.sum(edge + near, axis=0, keepdims=True)
        edge = edge * inverse
        near = near * inverse
        row_dot = jnp.sum(edge * edge_d[:, at] + near * near_d[:, at], axis=0, keepdims=True)
        d_edge = (edge * (edge_d[:, at] - row_dot)).astype(jnp.bfloat16)
        d_near = (near * (near_d[:, at] - row_dot)).astype(jnp.bfloat16)
        edge = edge.astype(jnp.bfloat16)
        parts.append(
            (
                stacked([edge * lower, near.astype(jnp.bfloat16), edge * upper]),
                stacked([d_edge * lower, d_near, d_edge * upper]),
            )
        )
    probs = stacked([p for p, _ in parts], axis=1)
    d_logits = stacked([d for _, d in parts], axis=1)
    return f32_dot(keys.T, d_logits) * scaling, probs, d_logits


def head_columns(turned_ref, g, group):
    rows = [slice(g * group + c, g * group + c + HD) for c in range(0, group, HD)]
    q_columns = stacked([turned_ref[1, row, :] for row in rows], axis=1)
    d_columns = stacked([turned_ref[2, row, :] for row in rows], axis=1)
    return rows, q_columns, d_columns


def edge_of_head(shard, own_ref, far_ref, at, q_columns, d_columns):
    keys, values = (stacked([own_ref[i, :, at], far_ref[i, :, at]]) for i in range(2))
    return edge_group(shard >= 2, q_columns, d_columns, keys, values)


def edge_kernel(low, first, last, group, shard_ref, turned_ref, own_ref, far_ref, logits_ref, d_probs_ref):
    for g in range(first, last):
        at = slice((g - low) * HD, (g - low + 1) * HD)
        _, q_columns, d_columns = head_columns(turned_ref, g, group)
        logits_ref[g - first], d_probs_ref[g - first] = edge_of_head(
            shard_ref[0], own_ref, far_ref, at, q_columns, d_columns
        )


def edge_of(shard, turned, own, far, low, first, last, group):
    tok = turned.shape[-1]
    inside = jax.ShapeDtypeStruct((last - first, tok, tok * group // HD), jnp.float32)
    return pl.pallas_call(
        functools.partial(edge_kernel, low, first, last, group),
        in_specs=[SMEM] + [VMEM] * 3,
        out_specs=[VMEM] * 2,
        out_shape=[inside, inside],
        compiler_params=params(),
        cost_estimate=cost(1),
        name="edge",
    )(shard, turned, own, far)


def in_grad_kernel(low, first, last, group, nears, edges, shard_ref, turned_ref, *refs):
    own_ref, *refs = refs
    near_refs, far_ref, *refs = refs[:nears], *refs[nears:]
    edge_refs = refs[:edges]
    grad_ref, probs_ref, d_logits_ref = refs[-3:]
    tok = own_ref.shape[1]
    shard = shard_ref[0]
    for g in range(first, last):
        at = slice((g - low) * HD, (g - low + 1) * HD)
        rows, q_columns, d_columns = head_columns(turned_ref, g, group)
        if edges:
            edge_l, edge_d = (ref[g - first] for ref in edge_refs)
        else:
            edge_l, edge_d = edge_of_head(shard, own_ref, far_ref, at, q_columns, d_columns)
        keys = blocks_of(own_ref, near_refs, far_ref, 0, at, g - first)
        values = blocks_of(own_ref, near_refs, far_ref, 1, at, g - first)
        d_queries, probs, d_logits = in_grad_group(
            shard >= 1, edge_l, edge_d, q_columns, d_columns,
            keys[tok : 2 * tok], values[tok : 2 * tok], keys,
        )
        probs_ref[g - first] = probs
        d_logits_ref[g - first] = d_logits
        for h, row in enumerate(rows):
            out = slice(row.start - first * group, row.stop - first * group)
            grad_ref[out, :] = (
                turned_ref[0, row, :].astype(jnp.float32) + d_queries[:, h * tok : (h + 1) * tok]
            ).astype(jnp.bfloat16)


def in_grad_of(shard, turned, block, edge, low, first, last, group, after):
    tok = turned.shape[-1]
    count = last - first
    inside = jax.ShapeDtypeStruct((count, 3 * tok, tok * group // HD), jnp.bfloat16)
    own, near, far = block
    return pl.pallas_call(
        functools.partial(in_grad_kernel, low, first, last, group, len(near), len(edge)),
        in_specs=[SMEM] + [VMEM] * (3 + len(near) + len(edge)) + [pl.BlockSpec(memory_space=pl.ANY)] * len(after),
        out_specs=[VMEM] * 3,
        out_shape=[jax.ShapeDtypeStruct((count * group, tok), jnp.bfloat16), inside, inside],
        compiler_params=params(),
        cost_estimate=cost(ATT_FLOPS[first]),
        name="in_grad",
    )(shard, turned, own, *near, far, *edge, *after)


def mixed_columns(attended, weight_ref, kept_ref, q_ref, out_refs):
    step = 4 * TILE
    cut_at = out_refs[0].shape[1]
    for column in range(0, q_ref.shape[1], step):
        at = slice(column, column + step)
        weight = prune(weight_ref[:, at], kept_ref, 0, at)
        mixed = f32_dot(attended, weight)
        late = column >= cut_at
        to = slice(column - late * cut_at, column - late * cut_at + step)
        out_refs[late][:, to] = (q_ref[:, at].astype(jnp.float32) + mixed).astype(jnp.bfloat16)


def layer_out_kernel(group, nears, *refs):
    kept_ref, q_ref, weight_ref, *refs = refs
    owns, refs = refs[: len(HALOS)], refs[len(HALOS) :]
    fars, refs = refs[: len(HALOS)], refs[len(HALOS) :]
    near_refs = []
    for count in nears:
        near_refs.append(refs[:count])
        refs = refs[count:]
    *probs_refs, first_ref, last_ref, attended_ref = refs
    tok = q_ref.shape[0]
    for i, (first, last) in enumerate(CHUNKS):
        for g in range(first, last):
            halo = [j for j, (low, high) in enumerate(HALOS) if low <= g < high][0]
            at = slice((g - HALOS[halo][0]) * HD, (g - HALOS[halo][0] + 1) * HD)
            values = blocks_of(owns[halo], near_refs[i], fars[halo], 1, at, g - first)
            attended = f32_dot(values.T, probs_refs[i][g - first]).astype(jnp.bfloat16)
            for h in range(group // HD):
                c = g * group + h * HD
                attended_ref[:, c : c + HD] = attended[:, h * tok : (h + 1) * tok].T
    mixed_columns(attended_ref[...], weight_ref, kept_ref, q_ref, (first_ref, last_ref))


def layer_out(kept, queries, weight, owns, fars, nears, probs, group):
    tok, width = queries.shape
    operands = [kept, queries, weight, *owns, *fars, *[x for near in nears for x in near], *probs]
    return pl.pallas_call(
        functools.partial(layer_out_kernel, group, [len(near) for near in nears]),
        in_specs=[VMEM] * len(operands),
        out_specs=[VMEM, VMEM, VMEM],
        out_shape=[
            jax.ShapeDtypeStruct((tok, width - 4 * TILE), jnp.bfloat16),
            jax.ShapeDtypeStruct((tok, 4 * TILE), jnp.bfloat16),
            jax.ShapeDtypeStruct((tok, width), jnp.bfloat16),
        ],
        compiler_params=params(),
        cost_estimate=cost(1),
        name="layer_out",
    )(*operands)


def kv_grads_kernel(group, stored, *refs):
    after_ref, q_ref, d_ref, *refs = refs
    piece_refs, refs = refs[: len(stored)], refs[len(stored) :]
    probs_refs, refs = refs[: len(CHUNKS)], refs[len(CHUNKS) :]
    d_logits_refs, refs = refs[: len(CHUNKS)], refs[len(CHUNKS) :]
    whole_ref, own_grad_ref, *near_grad_refs, far_grad_ref = refs[:5]
    *turned_refs, sems = refs[5:]
    tok = q_ref.shape[0]
    scaling = HD ** (-0.5)
    stores = [
        store_piece(piece_ref[...], column, turned_ref, whole_ref, sems.at[i])
        for i, (piece_ref, column, turned_ref) in enumerate(zip(piece_refs, stored, turned_refs))
    ]
    for i, (first, last) in enumerate(CHUNKS):
        for g in range(first, last):
            at_kv = slice(g * HD, (g + 1) * HD)
            columns = [g * group + c for c in range(0, group, HD)]
            d_rows = stacked([d_ref[:, c : c + HD] for c in columns])
            q_rows = stacked([q_ref[:, c : c + HD] for c in columns])
            d_keys = f32_dot(d_logits_refs[i][g - first], q_rows) * scaling
            d_values = f32_dot(probs_refs[i][g - first], d_rows)
            for index, grad in enumerate((d_keys, d_values)):
                own_grad_ref[index, :, at_kv] = grad[:tok]
                near_grad_refs[index][:, at_kv] = grad[tok : 2 * tok].astype(jnp.bfloat16)
                far_grad_ref[index, :, at_kv] = grad[2 * tok :].astype(jnp.bfloat16)
    for store in stores:
        store.wait()


def kv_grads_of(after, queries, d_attended, pieces, probs, d_logits, group):
    tok, width = queries.shape
    kv_width = width // group * HD
    operands = [queries, d_attended, *[p for p, _ in pieces], *probs, *d_logits]
    near_grad = jax.ShapeDtypeStruct((tok, kv_width), jnp.bfloat16)
    own_grad, far_grad = (jax.ShapeDtypeStruct((2, tok, kv_width), t) for t in (jnp.float32, jnp.bfloat16))
    return pl.pallas_call(
        functools.partial(kv_grads_kernel, group, [c for _, c in pieces]),
        in_specs=[pl.BlockSpec(memory_space=pl.ANY)] + [VMEM] * len(operands),
        out_specs=[HBM] + [VMEM] * 4,
        out_shape=[
            jax.ShapeDtypeStruct((tok, width), jnp.bfloat16), own_grad, near_grad, near_grad, far_grad,
        ],
        scratch_shapes=[pltpu.VMEM(p.shape[::-1], jnp.bfloat16) for p, _ in pieces]
        + [pltpu.SemaphoreType.DMA((len(pieces),))],
        compiler_params=params(),
        cost_estimate=cost(1),
        name="kv_grads",
    )(after, *operands)


def kv_total_kernel(shard_ref, own_ref, ahead_ref, *refs):
    *beside_refs, kv_ref, sum_ref, sem = refs
    for index, beside_ref in enumerate(beside_refs):
        total = own_ref[index] + ahead_ref[index].astype(jnp.float32)
        both = total + beside_ref[...].astype(jnp.float32)
        sum_ref[index] = jnp.where(shard_ref[0] % 2 == 0, both, total)
    store = pltpu.make_async_copy(sum_ref, kv_ref, sem)
    store.start()
    store.wait()


def kv_total_of(shard, own, ahead, beside):
    return pl.pallas_call(
        kv_total_kernel,
        in_specs=[SMEM] + [VMEM] * (2 + len(beside)),
        out_specs=HBM,
        out_shape=jax.ShapeDtypeStruct(own.shape, own.dtype),
        scratch_shapes=[pltpu.VMEM(own.shape, own.dtype), pltpu.SemaphoreType.DMA],
        compiler_params=params(),
        cost_estimate=cost(1),
        name="kv_total",
    )(shard, own, ahead, *beside)


def store_early_kernel(piece_ref, whole_ref, sem):
    store = pltpu.make_async_copy(piece_ref, whole_ref.at[:, : piece_ref.shape[1]], sem)
    store.start()
    store.wait()


def store_early(piece, width):
    return pl.pallas_call(
        store_early_kernel,
        in_specs=[VMEM],
        out_specs=HBM,
        out_shape=jax.ShapeDtypeStruct((piece.shape[0], width), piece.dtype),
        scratch_shapes=[pltpu.SemaphoreType.DMA],
        compiler_params=params(),
        cost_estimate=cost(1),
        name="store_early",
    )(piece)


def store_last_kernel(piece_ref, *refs):
    *_, whole_ref, _, _, sem = refs
    column = whole_ref.shape[1] - piece_ref.shape[1]
    store = pltpu.make_async_copy(piece_ref, whole_ref.at[:, column:], sem)
    store.start()
    store.wait()


def store_last(piece, *given):
    return pl.pallas_call(
        store_last_kernel,
        in_specs=[VMEM, HBM, HBM, HBM],
        out_specs=[HBM, HBM, HBM],
        out_shape=[jax.ShapeDtypeStruct(x.shape, x.dtype) for x in given],
        scratch_shapes=[pltpu.SemaphoreType.DMA],
        input_output_aliases={1: 0, 2: 1, 3: 2},
        compiler_params=params(),
        cost_estimate=cost(1),
        name="store_last",
    )(piece, *given)


def core_swap(value, axis):
    return lax.ppermute(value, axis, [(i, i ^ 1) for i in range(lax.axis_size(axis))])


def per_device(stream_in, keys_values, out_weight, tile_mask, cotangent):
    queries, own, mask, cot = stream_in[0], keys_values[0], tile_mask[0], cotangent[0]
    weight = pltpu.with_memory_space_constraint(out_weight[0], pltpu.VMEM)
    width = queries.shape[1]
    group = width // (own.shape[-1] // HD)
    shard = lax.axis_index("seq").astype(jnp.int32).reshape(1)
    owns = cut(own)
    fars = [around(piece, "seq", 2) for piece in owns]
    d_attended, turned, kept = d_attended_of(cot, queries, weight, mask)
    pieces, probs, d_logits, nears = [], [], [], []
    after = d_attended
    for halo, (low, high) in enumerate(HALOS):
        chunks = [(first, last) for first, last in CHUNKS if low <= first < high]
        cuts = [((first - low) * HD, (last - first) * HD, last - first > 1) for first, last in chunks]
        picked = pick(shard, owns[halo], fars[halo], after, cuts)
        swapped = [core_swap(x, "seq") for x in picked]
        ahead_of = chunks[-1]
        edges = {ahead_of[0]: edge_of(shard, turned, owns[halo], fars[halo], low, *ahead_of, group)}
        for first, last in chunks:
            near, swapped = swapped[: 1 + (last - first > 1)], swapped[1 + (last - first > 1) :]
            edge = edges.pop(first, [])
            grad, p, d = in_grad_of(
                shard, turned, (owns[halo], near, fars[halo]), edge, low, first, last, group,
                [pieces[0][0]] if first == CHUNKS[-1][0] else [x for e in edges.values() for x in e],
            )
            nears.append(near)
            probs.append(p)
            d_logits.append(d)
            pieces.append((around(grad, "section", -1), first * group))
            after = grad
    *results, attended = layer_out(kept, queries, weight, owns, fars, nears, probs, group)
    early, late = (around(x, "section", 1) for x in results)
    prev_grad, own_grad, *near_grad, far_grad = kv_grads_of(
        attended, queries, d_attended, pieces[:2], probs, d_logits, group
    )
    beside = [core_swap(x, "seq") for x in near_grad]
    prev_grad, behind = behind_of(shard, pieces[2], prev_grad, far_grad, beside)
    ahead = around(behind, "seq", -2)
    kv_total = kv_total_of(shard, own_grad, ahead, beside)
    next_input = store_early(early, width)
    next_input, prev_grad, kv_total = store_last(late, next_input, prev_grad, kv_total)
    return (next_input[None], prev_grad[None], kv_total[None])


def solution(mesh):
    return jax.shard_map(
        per_device,
        mesh=mesh,
        in_specs=(
            P("section", "seq", None),
            P("section", None, "seq", None),
            P("section", None, None),
            P("section", None, None),
            P("section", "seq", None),
        ),
        out_specs=(
            P("section", "seq", None),
            P("section", "seq", None),
            P("section", None, "seq", None),
        ),
        check_vma=False,
    )
```

```python
import functools
import math

import jax
import jax.numpy as jnp
from jax import lax
from jax.experimental import pallas as pl
from jax.experimental.pallas import tpu as pltpu
from jax.sharding import PartitionSpec as P

HD = 128
TILE = 128
HALOS = ((0, 1), (1, 4))
CHUNKS = ((0, 1), (1, 2), (2, 4))
CUT_FLOPS = 10**10
FLOOR = -1e30
ATT_FLOPS = {0: 2 * 10**8, 1: 1, 2: 10**10}
VMEM = pl.BlockSpec(memory_space=pltpu.VMEM)
HBM = pl.BlockSpec(memory_space=pltpu.HBM)
SMEM = pl.BlockSpec(memory_space=pltpu.SMEM)
VMEM_LIMIT = 32 * 1024 * 1024
NT = (((1,), (1,)), ((), ()))


def around(value, axis, by):
    length = lax.axis_size(axis)
    return lax.ppermute(value, axis, [(i, (i + by) % length) for i in range(length)])


def f32_dot(a, b, dims=(((1,), (0,)), ((), ()))):
    return lax.dot_general(a, b, dims, preferred_element_type=jnp.float32)


def params():
    return pltpu.CompilerParams(vmem_limit_bytes=VMEM_LIMIT)


def cost(flops):
    return pl.CostEstimate(flops=flops, bytes_accessed=1, transcendentals=0)


def prune(weight, kept_ref, row_tile, columns):
    strips = []
    for a in range(weight.shape[0] // TILE):
        row = kept_ref[row_tile + a : row_tile + a + 1, columns]
        kept = jnp.broadcast_to(row, (16, row.shape[1])).astype(weight.dtype)
        strip = weight[a * TILE : (a + 1) * TILE, :]
        strips.append(strip * jnp.concatenate([kept] * (TILE // 16), axis=0))
    return jnp.concatenate(strips, axis=0)


def cut_kernel(own_hbm, *refs):
    *piece_refs, sems = refs
    copies, column = [], 0
    for i, ref in enumerate(piece_refs):
        width = ref.shape[-1]
        source = own_hbm.at[:, :, column : column + width]
        copies.append(pltpu.make_async_copy(source, ref, sems.at[i]))
        column += width
    for copy in copies:
        copy.start()
    for copy in copies:
        copy.wait()


def cut(own):
    shapes = [own.shape[:2] + ((last - first) * HD,) for first, last in HALOS]
    return pl.pallas_call(
        cut_kernel,
        in_specs=[HBM],
        out_specs=[VMEM for _ in shapes],
        out_shape=[jax.ShapeDtypeStruct(shape, own.dtype) for shape in shapes],
        scratch_shapes=[pltpu.SemaphoreType.DMA((len(shapes),))],
        compiler_params=params(),
        cost_estimate=cost(CUT_FLOPS),
        name="cut",
    )(pltpu.with_memory_space_constraint(own, pltpu.HBM))


def d_attended_kernel(mask_ref, cot_ref, q_ref, weight_ref, out_ref, turned_ref, kept_ref):
    tiles = mask_ref.shape[0]
    width = kept_ref.shape[1]
    tile = lax.broadcasted_iota(jnp.int32, (tiles, width), 1) // TILE
    spread = (tile == lax.broadcasted_iota(jnp.int32, (tiles, width), 0)).astype(jnp.float32)
    kept_ref[...] = f32_dot((mask_ref[...] > 0).astype(jnp.float32), spread)
    rows = 4 * TILE
    for row in range(0, width, rows):
        weight = prune(weight_ref[row : row + rows, :], kept_ref, row // TILE, slice(None))
        part = f32_dot(cot_ref[...], weight, NT).astype(jnp.bfloat16)
        out_ref[:, row : row + rows] = part
        turned_ref[2, row : row + rows, :] = part.T
    turned_ref[0] = cot_ref[...].T
    turned_ref[1] = q_ref[...].T


def d_attended_of(cot, queries, weight, mask):
    tok, width = cot.shape
    return pl.pallas_call(
        d_attended_kernel,
        in_specs=[VMEM, VMEM, VMEM, VMEM],
        out_specs=[VMEM, VMEM, VMEM],
        out_shape=[
            jax.ShapeDtypeStruct((tok, width), jnp.bfloat16),
            jax.ShapeDtypeStruct((3, width, tok), jnp.bfloat16),
            jax.ShapeDtypeStruct((mask.shape[0], width), jnp.float32),
        ],
        compiler_params=params(),
        cost_estimate=cost(1),
        name="d_attended",
    )(mask, cot, queries, weight)


def pick_kernel(cuts, shard_ref, own_ref, far_ref, after_ref, *out_refs):
    odd = shard_ref[0] % 2 == 1

    def copy_from(source_ref):
        refs = list(out_refs)
        for start, width, split in cuts:
            at = slice(start, start + width)
            if split:
                for index in range(2):
                    refs.pop(0)[...] = source_ref[index, :, at]
            else:
                refs.pop(0)[...] = source_ref[:, :, at]

    @pl.when(odd)
    def _():
        copy_from(far_ref)

    @pl.when(jnp.logical_not(odd))
    def _():
        copy_from(own_ref)


def pick(shard, own, far, after, cuts):
    shapes = []
    for _, width, split in cuts:
        shape = (own.shape[1], width)
        shapes += [shape, shape] if split else [(2,) + shape]
    return pl.pallas_call(
        functools.partial(pick_kernel, cuts),
        in_specs=[SMEM, VMEM, VMEM, pl.BlockSpec(memory_space=pl.ANY)],
        out_specs=[VMEM for _ in shapes],
        out_shape=[jax.ShapeDtypeStruct(shape, own.dtype) for shape in shapes],
        compiler_params=params(),
        cost_estimate=cost(1),
        name="pick",
    )(shard, own, far, after)


def store_piece(piece, column, turned_ref, whole_ref, sem):
    turned_ref[...] = piece.T
    store = pltpu.make_async_copy(
        turned_ref, whole_ref.at[:, column : column + turned_ref.shape[1]], sem
    )
    store.start()
    return store


def behind_kernel(column, shard_ref, piece_ref, given_ref, far_ref, *refs):
    *beside_refs, whole_ref, out_ref, turned_ref, sem = refs
    store = store_piece(piece_ref[...], column, turned_ref, whole_ref, sem)
    for index, beside_ref in enumerate(beside_refs):
        far = far_ref[index].astype(jnp.float32)
        both = far + beside_ref[...].astype(jnp.float32)
        out_ref[index] = jnp.where(shard_ref[0] % 2 == 1, both, far).astype(jnp.bfloat16)
    store.wait()


def behind_of(shard, piece, given, far, beside):
    return pl.pallas_call(
        functools.partial(behind_kernel, piece[1]),
        in_specs=[SMEM, VMEM, HBM, VMEM] + [VMEM] * len(beside),
        out_specs=[HBM, VMEM],
        out_shape=[
            jax.ShapeDtypeStruct(given.shape, given.dtype),
            jax.ShapeDtypeStruct(far.shape, far.dtype),
        ],
        scratch_shapes=[pltpu.VMEM(piece[0].shape[::-1], jnp.bfloat16), pltpu.SemaphoreType.DMA],
        input_output_aliases={2: 0},
        compiler_params=params(),
        cost_estimate=cost(1),
        name="behind",
    )(shard, piece[0], given, far, *beside)


def stacked(parts, axis=0):
    return jnp.concatenate(parts, axis=axis)


def blocks_of(own_ref, near_refs, far_ref, index, at, near_head):
    near_at = slice(near_head * HD, (near_head + 1) * HD)
    near = near_refs[index][:, near_at] if len(near_refs) == 2 else near_refs[0][index, :, near_at]
    return stacked([own_ref[index, :, at], near, far_ref[index, :, at]])


def causal_mask(tok):
    key_at = lax.broadcasted_iota(jnp.int32, (tok, tok), 0)
    row_at = lax.broadcasted_iota(jnp.int32, (tok, tok), 1)
    return key_at <= row_at


def edge_group(far_ok, q_columns, d_columns, keys, values):
    tok = keys.shape[0] // 2
    heads = q_columns.shape[1] // tok
    causal = jnp.concatenate([causal_mask(tok)] * heads, axis=1)
    logits = f32_dot(keys, q_columns)
    d_probs = f32_dot(values, d_columns)
    far_logits = jnp.where(far_ok, logits[tok:], jnp.float32(FLOOR))
    return (
        jnp.where(causal, logits[:tok], far_logits),
        jnp.where(causal, d_probs[:tok], d_probs[tok:]),
    )


def in_grad_group(near_ok, edge_l, edge_d, q_columns, d_columns, near_k, near_v, keys):
    tok = near_k.shape[0]
    scaling = HD ** (-0.5)
    factor = scaling * math.log2(math.e)
    causal = causal_mask(tok).astype(jnp.float32)
    lower = causal.astype(jnp.bfloat16)
    upper = (1.0 - causal).astype(jnp.bfloat16)
    near_l = f32_dot(near_k, q_columns)
    near_d = f32_dot(near_v, d_columns)
    parts = []
    for h in range(q_columns.shape[1] // tok):
        at = slice(h * tok, (h + 1) * tok)
        edge = edge_l[:, at]
        near = jnp.where(near_ok, near_l[:, at], jnp.float32(FLOOR))
        top = jnp.max(jnp.maximum(edge, near), axis=0, keepdims=True)
        edge = jnp.exp2((edge - top) * factor)
        near = jnp.exp2((near - top) * factor)
        inverse = 1.0 / jnp.sum(edge + near, axis=0, keepdims=True)
        edge = edge * inverse
        near = near * inverse
        row_dot = jnp.sum(edge * edge_d[:, at] + near * near_d[:, at], axis=0, keepdims=True)
        d_edge = (edge * (edge_d[:, at] - row_dot)).astype(jnp.bfloat16)
        d_near = (near * (near_d[:, at] - row_dot)).astype(jnp.bfloat16)
        edge = edge.astype(jnp.bfloat16)
        parts.append(
            (
                stacked([edge * lower, near.astype(jnp.bfloat16), edge * upper]),
                stacked([d_edge * lower, d_near, d_edge * upper]),
            )
        )
    probs = stacked([p for p, _ in parts], axis=1)
    d_logits = stacked([d for _, d in parts], axis=1)
    return f32_dot(keys.T, d_logits) * scaling, probs, d_logits


def head_columns(turned_ref, g, group):
    rows = [slice(g * group + c, g * group + c + HD) for c in range(0, group, HD)]
    q_columns = stacked([turned_ref[1, row, :] for row in rows], axis=1)
    d_columns = stacked([turned_ref[2, row, :] for row in rows], axis=1)
    return rows, q_columns, d_columns


def edge_of_head(shard, own_ref, far_ref, at, q_columns, d_columns):
    keys, values = (stacked([own_ref[i, :, at], far_ref[i, :, at]]) for i in range(2))
    return edge_group(shard >= 2, q_columns, d_columns, keys, values)


def edge_kernel(low, first, last, group, shard_ref, turned_ref, own_ref, far_ref, logits_ref, d_probs_ref):
    for g in range(first, last):
        at = slice((g - low) * HD, (g - low + 1) * HD)
        _, q_columns, d_columns = head_columns(turned_ref, g, group)
        logits_ref[g - first], d_probs_ref[g - first] = edge_of_head(
            shard_ref[0], own_ref, far_ref, at, q_columns, d_columns
        )


def edge_of(shard, turned, own, far, low, first, last, group):
    tok = turned.shape[-1]
    inside = jax.ShapeDtypeStruct((last - first, tok, tok * group // HD), jnp.float32)
    return pl.pallas_call(
        functools.partial(edge_kernel, low, first, last, group),
        in_specs=[SMEM] + [VMEM] * 3,
        out_specs=[VMEM] * 2,
        out_shape=[inside, inside],
        compiler_params=params(),
        cost_estimate=cost(1),
        name="edge",
    )(shard, turned, own, far)


def in_grad_kernel(low, first, last, group, nears, edges, shard_ref, turned_ref, *refs):
    own_ref, *refs = refs
    near_refs, far_ref, *refs = refs[:nears], *refs[nears:]
    edge_refs = refs[:edges]
    grad_ref, probs_ref, d_logits_ref = refs[-3:]
    tok = own_ref.shape[1]
    shard = shard_ref[0]
    for g in range(first, last):
        at = slice((g - low) * HD, (g - low + 1) * HD)
        rows, q_columns, d_columns = head_columns(turned_ref, g, group)
        if edges:
            edge_l, edge_d = (ref[g - first] for ref in edge_refs)
        else:
            edge_l, edge_d = edge_of_head(shard, own_ref, far_ref, at, q_columns, d_columns)
        keys = blocks_of(own_ref, near_refs, far_ref, 0, at, g - first)
        values = blocks_of(own_ref, near_refs, far_ref, 1, at, g - first)
        d_queries, probs, d_logits = in_grad_group(
            shard >= 1, edge_l, edge_d, q_columns, d_columns,
            keys[tok : 2 * tok], values[tok : 2 * tok], keys,
        )
        probs_ref[g - first] = probs
        d_logits_ref[g - first] = d_logits
        for h, row in enumerate(rows):
            out = slice(row.start - first * group, row.stop - first * group)
            grad_ref[out, :] = (
                turned_ref[0, row, :].astype(jnp.float32) + d_queries[:, h * tok : (h + 1) * tok]
            ).astype(jnp.bfloat16)


def in_grad_of(shard, turned, block, edge, low, first, last, group, after):
    tok = turned.shape[-1]
    count = last - first
    inside = jax.ShapeDtypeStruct((count, 3 * tok, tok * group // HD), jnp.bfloat16)
    own, near, far = block
    return pl.pallas_call(
        functools.partial(in_grad_kernel, low, first, last, group, len(near), len(edge)),
        in_specs=[SMEM] + [VMEM] * (3 + len(near) + len(edge)) + [pl.BlockSpec(memory_space=pl.ANY)] * len(after),
        out_specs=[VMEM] * 3,
        out_shape=[jax.ShapeDtypeStruct((count * group, tok), jnp.bfloat16), inside, inside],
        compiler_params=params(),
        cost_estimate=cost(ATT_FLOPS[first]),
        name="in_grad",
    )(shard, turned, own, *near, far, *edge, *after)


def mixed_columns(attended, weight_ref, kept_ref, q_ref, out_refs):
    step = 2 * TILE
    cut_at = out_refs[0].shape[1]
    for column in range(0, q_ref.shape[1], step):
        at = slice(column, column + step)
        weight = prune(weight_ref[:, at], kept_ref, 0, at)
        mixed = f32_dot(attended, weight)
        late = column >= cut_at
        to = slice(column - late * cut_at, column - late * cut_at + step)
        out_refs[late][:, to] = (q_ref[:, at].astype(jnp.float32) + mixed).astype(jnp.bfloat16)


def layer_out_kernel(group, nears, *refs):
    kept_ref, q_ref, weight_ref, *refs = refs
    owns, refs = refs[: len(HALOS)], refs[len(HALOS) :]
    fars, refs = refs[: len(HALOS)], refs[len(HALOS) :]
    near_refs = []
    for count in nears:
        near_refs.append(refs[:count])
        refs = refs[count:]
    *probs_refs, first_ref, last_ref, attended_ref = refs
    tok = q_ref.shape[0]
    for i, (first, last) in enumerate(CHUNKS):
        for g in range(first, last):
            halo = [j for j, (low, high) in enumerate(HALOS) if low <= g < high][0]
            at = slice((g - HALOS[halo][0]) * HD, (g - HALOS[halo][0] + 1) * HD)
            values = blocks_of(owns[halo], near_refs[i], fars[halo], 1, at, g - first)
            attended = f32_dot(values.T, probs_refs[i][g - first]).astype(jnp.bfloat16)
            for h in range(group // HD):
                c = g * group + h * HD
                attended_ref[:, c : c + HD] = attended[:, h * tok : (h + 1) * tok].T
    mixed_columns(attended_ref[...], weight_ref, kept_ref, q_ref, (first_ref, last_ref))


def layer_out(kept, queries, weight, owns, fars, nears, probs, group):
    tok, width = queries.shape
    operands = [kept, queries, weight, *owns, *fars, *[x for near in nears for x in near], *probs]
    return pl.pallas_call(
        functools.partial(layer_out_kernel, group, [len(near) for near in nears]),
        in_specs=[VMEM] * len(operands),
        out_specs=[VMEM, VMEM, VMEM],
        out_shape=[
            jax.ShapeDtypeStruct((tok, width - 2 * TILE), jnp.bfloat16),
            jax.ShapeDtypeStruct((tok, 2 * TILE), jnp.bfloat16),
            jax.ShapeDtypeStruct((tok, width), jnp.bfloat16),
        ],
        compiler_params=params(),
        cost_estimate=cost(1),
        name="layer_out",
    )(*operands)


def kv_grads_kernel(group, stored, *refs):
    after_ref, q_ref, d_ref, *refs = refs
    piece_refs, refs = refs[: len(stored)], refs[len(stored) :]
    probs_refs, refs = refs[: len(CHUNKS)], refs[len(CHUNKS) :]
    d_logits_refs, refs = refs[: len(CHUNKS)], refs[len(CHUNKS) :]
    whole_ref, own_grad_ref, *near_grad_refs, far_grad_ref = refs[:5]
    *turned_refs, sems = refs[5:]
    tok = q_ref.shape[0]
    scaling = HD ** (-0.5)
    stores = [
        store_piece(piece_ref[...], column, turned_ref, whole_ref, sems.at[i])
        for i, (piece_ref, column, turned_ref) in enumerate(zip(piece_refs, stored, turned_refs))
    ]
    for i, (first, last) in enumerate(CHUNKS):
        for g in range(first, last):
            at_kv = slice(g * HD, (g + 1) * HD)
            columns = [g * group + c for c in range(0, group, HD)]
            d_rows = stacked([d_ref[:, c : c + HD] for c in columns])
            q_rows = stacked([q_ref[:, c : c + HD] for c in columns])
            d_keys = f32_dot(d_logits_refs[i][g - first], q_rows) * scaling
            d_values = f32_dot(probs_refs[i][g - first], d_rows)
            for index, grad in enumerate((d_keys, d_values)):
                own_grad_ref[index, :, at_kv] = grad[:tok]
                near_grad_refs[index][:, at_kv] = grad[tok : 2 * tok].astype(jnp.bfloat16)
                far_grad_ref[index, :, at_kv] = grad[2 * tok :].astype(jnp.bfloat16)
    for store in stores:
        store.wait()


def kv_grads_of(after, queries, d_attended, pieces, probs, d_logits, group):
    tok, width = queries.shape
    kv_width = width // group * HD
    operands = [queries, d_attended, *[p for p, _ in pieces], *probs, *d_logits]
    near_grad = jax.ShapeDtypeStruct((tok, kv_width), jnp.bfloat16)
    own_grad, far_grad = (jax.ShapeDtypeStruct((2, tok, kv_width), t) for t in (jnp.float32, jnp.bfloat16))
    return pl.pallas_call(
        functools.partial(kv_grads_kernel, group, [c for _, c in pieces]),
        in_specs=[pl.BlockSpec(memory_space=pl.ANY)] + [VMEM] * len(operands),
        out_specs=[HBM] + [VMEM] * 4,
        out_shape=[
            jax.ShapeDtypeStruct((tok, width), jnp.bfloat16), own_grad, near_grad, near_grad, far_grad,
        ],
        scratch_shapes=[pltpu.VMEM(p.shape[::-1], jnp.bfloat16) for p, _ in pieces]
        + [pltpu.SemaphoreType.DMA((len(pieces),))],
        compiler_params=params(),
        cost_estimate=cost(1),
        name="kv_grads",
    )(after, *operands)


def kv_total_kernel(shard_ref, own_ref, ahead_ref, *refs):
    *beside_refs, kv_ref, sum_ref, sem = refs
    for index, beside_ref in enumerate(beside_refs):
        total = own_ref[index] + ahead_ref[index].astype(jnp.float32)
        both = total + beside_ref[...].astype(jnp.float32)
        sum_ref[index] = jnp.where(shard_ref[0] % 2 == 0, both, total)
    store = pltpu.make_async_copy(sum_ref, kv_ref, sem)
    store.start()
    store.wait()


def kv_total_of(shard, own, ahead, beside):
    return pl.pallas_call(
        kv_total_kernel,
        in_specs=[SMEM] + [VMEM] * (2 + len(beside)),
        out_specs=HBM,
        out_shape=jax.ShapeDtypeStruct(own.shape, own.dtype),
        scratch_shapes=[pltpu.VMEM(own.shape, own.dtype), pltpu.SemaphoreType.DMA],
        compiler_params=params(),
        cost_estimate=cost(1),
        name="kv_total",
    )(shard, own, ahead, *beside)


def store_early_kernel(piece_ref, whole_ref, sem):
    store = pltpu.make_async_copy(piece_ref, whole_ref.at[:, : piece_ref.shape[1]], sem)
    store.start()
    store.wait()


def store_early(piece, width):
    return pl.pallas_call(
        store_early_kernel,
        in_specs=[VMEM],
        out_specs=HBM,
        out_shape=jax.ShapeDtypeStruct((piece.shape[0], width), piece.dtype),
        scratch_shapes=[pltpu.SemaphoreType.DMA],
        compiler_params=params(),
        cost_estimate=cost(1),
        name="store_early",
    )(piece)


def store_last_kernel(piece_ref, *refs):
    *_, whole_ref, _, _, sem = refs
    column = whole_ref.shape[1] - piece_ref.shape[1]
    store = pltpu.make_async_copy(piece_ref, whole_ref.at[:, column:], sem)
    store.start()
    store.wait()


def store_last(piece, *given):
    return pl.pallas_call(
        store_last_kernel,
        in_specs=[VMEM, HBM, HBM, HBM],
        out_specs=[HBM, HBM, HBM],
        out_shape=[jax.ShapeDtypeStruct(x.shape, x.dtype) for x in given],
        scratch_shapes=[pltpu.SemaphoreType.DMA],
        input_output_aliases={1: 0, 2: 1, 3: 2},
        compiler_params=params(),
        cost_estimate=cost(1),
        name="store_last",
    )(piece, *given)


def core_swap(value, axis):
    return lax.ppermute(value, axis, [(i, i ^ 1) for i in range(lax.axis_size(axis))])


def per_device(stream_in, keys_values, out_weight, tile_mask, cotangent):
    queries, own, mask, cot = stream_in[0], keys_values[0], tile_mask[0], cotangent[0]
    weight = pltpu.with_memory_space_constraint(out_weight[0], pltpu.VMEM)
    width = queries.shape[1]
    group = width // (own.shape[-1] // HD)
    shard = lax.axis_index("seq").astype(jnp.int32).reshape(1)
    owns = cut(own)
    fars = [around(piece, "seq", 2) for piece in owns]
    d_attended, turned, kept = d_attended_of(cot, queries, weight, mask)
    pieces, probs, d_logits, nears = [], [], [], []
    after = d_attended
    for halo, (low, high) in enumerate(HALOS):
        chunks = [(first, last) for first, last in CHUNKS if low <= first < high]
        cuts = [((first - low) * HD, (last - first) * HD, last - first > 1) for first, last in chunks]
        picked = pick(shard, owns[halo], fars[halo], after, cuts)
        swapped = [core_swap(x, "seq") for x in picked]
        ahead_of = chunks[-1]
        edges = {ahead_of[0]: edge_of(shard, turned, owns[halo], fars[halo], low, *ahead_of, group)}
        for first, last in chunks:
            near, swapped = swapped[: 1 + (last - first > 1)], swapped[1 + (last - first > 1) :]
            edge = edges.pop(first, [])
            grad, p, d = in_grad_of(
                shard, turned, (owns[halo], near, fars[halo]), edge, low, first, last, group,
                [pieces[0][0]] if first == CHUNKS[-1][0] else [x for e in edges.values() for x in e],
            )
            nears.append(near)
            probs.append(p)
            d_logits.append(d)
            pieces.append((around(grad, "section", -1), first * group))
            after = grad
    *results, attended = layer_out(kept, queries, weight, owns, fars, nears, probs, group)
    early, late = (around(x, "section", 1) for x in results)
    prev_grad, own_grad, *near_grad, far_grad = kv_grads_of(
        attended, queries, d_attended, pieces[:2], probs, d_logits, group
    )
    beside = [core_swap(x, "seq") for x in near_grad]
    prev_grad, behind = behind_of(shard, pieces[2], prev_grad, far_grad, beside)
    ahead = around(behind, "seq", -2)
    kv_total = kv_total_of(shard, own_grad, ahead, beside)
    next_input = store_early(early, width)
    next_input, prev_grad, kv_total = store_last(late, next_input, prev_grad, kv_total)
    return (next_input[None], prev_grad[None], kv_total[None])


def solution(mesh):
    return jax.shard_map(
        per_device,
        mesh=mesh,
        in_specs=(
            P("section", "seq", None),
            P("section", None, "seq", None),
            P("section", None, None),
            P("section", None, None),
            P("section", "seq", None),
        ),
        out_specs=(
            P("section", "seq", None),
            P("section", "seq", None),
            P("section", None, "seq", None),
        ),
        check_vma=False,
    )
```
